32 devices in a mesh: ctx: 8 (over z, y), head: 4 (over x, core).
Axes of the slice: x: 2, y: 2, z: 4, core: 2. Of those that a mesh axis runs over, the one named last changes fastest.
Arguments:
- queries: bfloat16 [2048, 2048], P('ctx', 'head'), may hold values from -6 to 6
- keys: bfloat16 [2048, 2048], P('ctx', 'head'), may hold values from -6 to 6
- values: bfloat16 [2048, 2048], P('ctx', 'head'), may hold values from -6 to 6
- directions: bfloat16 [2048, 2048], P('ctx', 'head'), may hold values from -6 to 6
- rates: float32 [16, 2048], P('head', 'ctx'), may hold values from 0.004 to 1.996
- selected: int32 [16, 4], P('ctx'), may hold values from 0 to 15, as said below
- out_weight: bfloat16 [2048, 2048], P('head'), may hold values from -0.1875 to 0.1875
Outputs:
- projected: bfloat16 [2048, 2048], P('ctx', 'head')
The draws below stay inside these ranges and needn't reach their ends.
Inputs may be any that keep to these rules, and one draw needn't show every extreme that they name: `selected`: row c lists query block c's key blocks: entry 0 is c itself; the others lie from max(c - 14, 0) to c - 1 (or are 0 when c is 0), may repeat, and the farthest distance 7 * 2 is reached in every draw.
All inputs are finite; a program needn't handle non-finite values.
Results may differ from the reference program's by a relative error of at most 0.022.
Values may be sent and summed in bfloat16 or wider, within the bound.
No kernel may reach another device: no remote copies, remote signals or barrier semaphores. Data moves between devices by JAX's collectives and lax.ppermute only.
A program may use at most 64 MiB of HBM per device.

```python
import math
import jax
import jax.numpy as jnp
from jax import lax

HEADS = 16
HEAD_DIM = 128
D = 2048
BLOCK = 128
TOPK = 4
LOOK = 7
TOK_DEV = 256
TOKENS = 2048
BLOCKS = 16
N_HEAD = 4


def query_key_pair(key):
    base = jax.random.fold_in(key, 7001)
    streams = jax.random.split(base, 2)
    shape = (TOKENS, HEADS, HEAD_DIM)
    query_all = jnp.clip(jax.random.normal(streams[0], shape, jnp.float32), -6.0, 6.0)
    key_all = jnp.clip(jax.random.normal(streams[1], shape, jnp.float32), -6.0, 6.0)
    return (query_all.reshape(TOKENS, HEADS * HEAD_DIM).astype(jnp.bfloat16), key_all.reshape(TOKENS, HEADS * HEAD_DIM).astype(jnp.bfloat16))


def draw_queries(key, part):
    return query_key_pair(key)[0]


def draw_keys(key, part):
    return query_key_pair(key)[1]


def draw_rates(key, part):
    streams = jax.random.split(jax.random.fold_in(key, 7002), 4)
    slow_share = 0.6
    slow = jax.random.uniform(streams[0], (HEADS, 1)) < slow_share
    spacing = jnp.exp(jax.random.uniform(streams[1], (HEADS, TOKENS), jnp.float32, math.log(0.004), math.log(0.12)))
    flipped = jax.random.uniform(streams[2], (HEADS, 1)) < 0.5
    slow_rate = jnp.where(flipped, 2.0 - spacing, spacing)
    fast_rate = jax.random.uniform(streams[3], (HEADS, TOKENS), jnp.float32, 0.3, 1.7)
    return jnp.where(slow, slow_rate, fast_rate).astype(jnp.float32)


def draw_selected(key, part):
    streams = jax.random.split(jax.random.fold_in(key, 7003), 2)
    reach_blocks = LOOK * (TOK_DEV // BLOCK)
    block_ids = jnp.arange(BLOCKS, dtype=jnp.int32)
    distance = jax.random.randint(streams[0], (BLOCKS, TOPK - 1), 1, reach_blocks + 1)
    farthest = (jax.random.randint(streams[1], (BLOCKS,), 0, 2) == 1) | (block_ids == BLOCKS - 1)
    first_col = jnp.where(farthest, reach_blocks, distance[:, 0])
    distance = jnp.concatenate([first_col[:, None], distance[:, 1:]], 1)
    picked = jnp.maximum(block_ids[:, None] - distance, 0)
    return jnp.concatenate([block_ids[:, None], picked], 1).astype(jnp.int32)


def with_spikes(entries, own_key, source, target, shards_of, factor):
    def block_of(dim):
        return (jnp.arange(entries.shape[dim]) // (entries.shape[dim] // shards_of)).reshape((-1,) + (1,) * (entries.ndim - 1 - dim))

    one_side = jax.random.permutation(own_key, shards_of)[block_of(target)]
    other_side = (block_of(target) + shards_of // 2) % shards_of
    return jnp.where((block_of(source) == one_side) | (block_of(source) == other_side), factor * entries, entries)


def shard_levels(key, shape, shards, low, largest):
    factor_of = 1.0
    for position, blocks in shards:
        draws = jax.random.uniform(jax.random.fold_in(jax.random.fold_in(key, 6), position), (blocks,), jnp.float32, low / len(shards), largest / len(shards))
        factor_of = factor_of * jnp.repeat(jnp.exp(draws), shape[position] // blocks).reshape((-1,) + (1,) * (len(shape) - 1 - position))
    return factor_of


def normal_values(rng, shape, deviation, most, pieces=(), kind=jnp.bfloat16):
    values = jax.random.normal(rng, shape, jnp.float32) * deviation
    if len(pieces) > 0:
        values = shard_levels(rng, shape, pieces, -0.22, 0.18) * values
    return jnp.clip(values, min=-most, max=most).astype(kind)


def heavy_noise(stream_key, dims, scale, reach, pieces, heavy, held_as=jnp.bfloat16):
    values = scale * jax.random.normal(stream_key, dims, jnp.float32)
    if pieces:
        values = values * shard_levels(stream_key, dims, pieces, -0.22, 0.18)
    return jnp.clip(with_spikes(values, jax.random.fold_in(stream_key, 3), *heavy), -reach, reach).astype(held_as)


def setup_inputs(seed: int = 0) -> dict:
    streams_of = jax.random.split(jax.random.key(seed), 8)
    return {
        "queries": draw_queries(jax.random.fold_in(streams_of[7], 71), 0),
        "keys": draw_keys(jax.random.fold_in(streams_of[7], 71), 0),
        "values": normal_values(streams_of[2], (TOKENS, HEADS * HEAD_DIM), 1.0, 6.0, ((0, 8), (1, 4))),
        "directions": normal_values(streams_of[3], (TOKENS, HEADS * HEAD_DIM), 1.0, 6.0, ((0, 8), (1, 4))),
        "rates": draw_rates(jax.random.fold_in(streams_of[7], 71), 0),
        "selected": draw_selected(jax.random.fold_in(streams_of[7], 71), 0),
        "out_weight": heavy_noise(streams_of[6], (HEADS * HEAD_DIM, D), (HEADS * HEAD_DIM) ** -0.5, 0.1875, ((0, 4),), (0, 1, 4, 2.0)),
    }


def product(left, right):
    return jnp.matmul(left, right, precision=lax.Precision.HIGHEST)

def flip_last(array):
    return jnp.swapaxes(array, -1, -2)

def block_terms(query_part, key_part, direction_part, rate_part):
    block_width = query_part.shape[-2]
    head_width = query_part.shape[-1]
    unit_vectors = direction_part * lax.rsqrt(lax.optimization_barrier(jnp.sum(direction_part * direction_part, -1, keepdims=True)) + 1e-06)
    positions = jnp.arange(block_width)
    strict_below = (positions[:, None] > positions[None, :]).astype(jnp.float32)
    at_or_below = (positions[:, None] >= positions[None, :]).astype(jnp.float32)
    identity = jnp.eye(block_width, dtype=jnp.float32)
    head_identity = jnp.eye(head_width, dtype=jnp.float32)
    gram_matrix = product(unit_vectors, flip_last(unit_vectors))
    lower_matrix = identity + rate_part[..., :, None] * gram_matrix * strict_below
    mixing = lax.linalg.triangular_solve(lower_matrix, rate_part[..., :, None] * identity, left_side=True, lower=True)
    query_proj = product(query_part, flip_last(unit_vectors)) * at_or_below
    key_proj = product(unit_vectors, flip_last(key_part)) * strict_below
    query_mix = product(query_proj, mixing)
    q_start = query_part - product(query_mix, unit_vectors)
    k_end = key_part - product(flip_last(product(mixing, key_proj)), unit_vectors)
    inner_scores = product(query_part, flip_last(key_part)) - product(query_mix, key_proj)
    block_maps = head_identity - product(product(flip_last(unit_vectors), mixing), unit_vectors)
    return (q_start, k_end, inner_scores, block_maps)

def reference(queries, keys, values, directions, rates, selected, out_weight):
    tokens = queries.shape[0]
    block_count = tokens // BLOCK
    score_scale = HEAD_DIM ** (-0.5)

    def blocked(array):
        return array.reshape(block_count, BLOCK, HEADS, HEAD_DIM).transpose(0, 2, 1, 3)
    query_blocks = blocked(queries).astype(jnp.float32)
    key_blocks = blocked(keys).astype(jnp.float32)
    direction_blocks = blocked(directions).astype(jnp.float32)
    value_blocks = blocked(values)
    rate_blocks = rates.reshape(HEADS, block_count, BLOCK).transpose(1, 0, 2)

    def one_block(packed):
        return block_terms(packed[0], packed[1], packed[2], packed[3])
    q_start, k_end, inner_scores, block_maps = lax.map(one_block, (query_blocks, key_blocks, direction_blocks, rate_blocks))
    reach_blocks = LOOK * (TOK_DEV // BLOCK)
    positions = jnp.arange(BLOCK)
    causal = (positions[:, None] >= positions[None, :])[None]

    def attend(query_block):
        listed = selected[query_block]
        score_list = [inner_scores[query_block] * score_scale]
        allowed_list = [causal & jnp.any(listed == query_block)]
        value_list = [value_blocks[query_block]]
        moving = q_start[query_block]
        for offset in range(1, reach_blocks + 1):
            earlier = query_block - offset
            source_block = jnp.maximum(earlier, 0)
            score_list.append(product(moving, flip_last(k_end[source_block])) * score_scale)
            hit = jnp.any(listed == earlier) & (earlier >= 0)
            allowed_list.append(jnp.broadcast_to(hit, (1, BLOCK, BLOCK)))
            value_list.append(value_blocks[source_block])
            moving = product(moving, block_maps[source_block])
        scores = jnp.concatenate(score_list, -1)
        allowed = jnp.concatenate(allowed_list, -1)
        highest = lax.optimization_barrier(jnp.max(jnp.where(allowed, scores, -1e+30), -1, keepdims=True))
        expos = jnp.exp(jnp.where(allowed, scores - highest, -1e+30))
        denominator = lax.optimization_barrier(jnp.sum(expos, -1, keepdims=True))
        weights = (expos / denominator).astype(jnp.bfloat16)
        values_all = jnp.concatenate(value_list, 1)
        blended = jnp.einsum('hqk,hke->hqe', weights.astype(jnp.float32), values_all.astype(jnp.float32))
        return blended.astype(jnp.bfloat16)
    attended = lax.map(attend, jnp.arange(block_count))
    attended_flat = attended.transpose(0, 2, 1, 3).reshape(tokens, HEADS * HEAD_DIM)
    group_width = HEADS * HEAD_DIM // N_HEAD
    summed = jnp.zeros((tokens, out_weight.shape[1]), jnp.float32)
    for group_index in range(N_HEAD):
        lo_col = group_index * group_width
        partial_value = jnp.dot(attended_flat[:, lo_col:lo_col + group_width].astype(jnp.float32), out_weight[lo_col:lo_col + group_width].astype(jnp.float32), preferred_element_type=jnp.float32)
        summed = summed + lax.optimization_barrier(partial_value.astype(jnp.bfloat16)).astype(jnp.float32)
    return summed.astype(jnp.bfloat16)
```

```python
import functools

import jax
import jax.numpy as jnp
from jax import lax
from jax.experimental import pallas as pl
from jax.experimental.pallas import tpu as pltpu
from jax.sharding import PartitionSpec as P

HEAD_DIM = 128
BLOCK = 128
LOOK = 7
BASE = 16
EXTRA = 16
BF16 = jnp.bfloat16
F32 = jnp.float32
VMEM = pl.BlockSpec(memory_space=pltpu.VMEM)
SMEM = pl.BlockSpec(memory_space=pltpu.SMEM)
PARAMS = pltpu.CompilerParams(vmem_limit_bytes=32 * 1024 * 1024)


def dot(left, right, left_dim, right_dim):
    return lax.dot_general(
        left, right, (((left_dim,), (right_dim,)), ((), ())), preferred_element_type=F32
    )


def nn(left, right):
    return dot(left, right, 1, 0)


def nt(left, right):
    return dot(left, right, 1, 1)


def tn(left, right):
    return dot(left, right, 0, 0)


def split(value):
    high = value.astype(BF16)
    return high, (value - high.astype(F32)).astype(BF16)


def triple(product, left, right):
    return product(left[0], right[0]) + (product(left[0], right[1]) + product(left[1], right[0]))


def square_iotas():
    rows = lax.broadcasted_iota(jnp.int32, (BLOCK, BLOCK), 0)
    columns = lax.broadcasted_iota(jnp.int32, (BLOCK, BLOCK), 1)
    return rows, columns


def pack_kernel(head_axis, ctx_axis, q_ref, k_ref, v_ref, d_ref, rates_ref, selected_ref,
                keep_d, send_d, keep_rest, send_rest):
    heads = q_ref.shape[1] // HEAD_DIM
    blocks = q_ref.shape[0] // BLOCK
    core = lax.rem(lax.axis_index(head_axis), 2)
    first_block = lax.axis_index(ctx_axis) * blocks
    row = lax.broadcasted_iota(jnp.int32, (EXTRA, HEAD_DIM), 0)
    lane = lax.broadcasted_iota(jnp.int32, (EXTRA, HEAD_DIM), 1)
    for parity, d_out, rest_out in ((core, keep_d, keep_rest), (1 - core, send_d, send_rest)):
        rows = pl.ds(pl.multiple_of(parity * BLOCK, BLOCK), BLOCK)
        rate = rates_ref[:, rows]
        rate_1 = rate.astype(BF16).astype(F32)
        rate_2 = (rate - rate_1).astype(BF16).astype(F32)
        rate_3 = (rate - rate_1) - rate_2
        away = jnp.zeros((EXTRA, HEAD_DIM), jnp.int32)
        for entry in range(selected_ref.shape[1]):
            distance = first_block + parity - selected_ref[parity, entry]
            away = jnp.where(lane == entry, distance, away)
        away = away.astype(F32)
        for head in range(heads):
            columns = slice(head * HEAD_DIM, (head + 1) * HEAD_DIM)
            d_out[head, :BLOCK] = d_ref[rows, columns]
            extra = jnp.where(row == 0, rate_1[head:head + 1], 0.0)
            extra = jnp.where(row == 1, rate_2[head:head + 1], extra)
            extra = jnp.where(row == 2, rate_3[head:head + 1], extra)
            extra = jnp.where(row == 3, away, extra)
            d_out[head, BLOCK:] = extra.astype(BF16)
            rest_out[head, 0] = k_ref[rows, columns]
            rest_out[head, 1] = q_ref[rows, columns]
            rest_out[head, 2] = v_ref[rows, columns]


def base_inverse(strict):
    count = BLOCK // BASE
    moved = [
        pltpu.roll(strict[b * BASE:(b + 1) * BASE], (BLOCK - b * BASE) % BLOCK, 1)
        if b else strict[:BASE]
        for b in range(count)
    ]
    lanes = lax.broadcasted_iota(jnp.int32, (BASE // 2, BLOCK), 1)
    rows = lax.broadcasted_iota(jnp.int32, (BASE // 2, BLOCK), 0)
    half = BASE // 2
    parts = []
    for b in range(count):
        upper = (lanes == rows + b * BASE).astype(F32)
        lower = (lanes == rows + b * BASE + half).astype(F32)
        for step in range(BASE - 1):
            if step < half:
                source = upper[step:step + 1]
                if step < half - 1:
                    upper = upper - moved[b][:half, step:step + 1] * source
            else:
                source = lower[step - half:step - half + 1]
            lower = lower - moved[b][half:, step:step + 1] * source
        parts += [upper, lower]
    return jnp.concatenate(parts, 0)


def halves(value, size):
    parts = value.reshape(BLOCK // (2 * size), 2, size, BLOCK)
    return parts[:, 0].reshape(BLOCK // 2, BLOCK), parts[:, 1].reshape(BLOCK // 2, BLOCK)


def joined(first, second, size):
    shape = (BLOCK // (2 * size), 1, size, BLOCK)
    return jnp.concatenate([first.reshape(shape), second.reshape(shape)], 1).reshape(BLOCK, BLOCK)


def mixing_kernel(d_ref, mixing_ref):
    units = d_ref.shape[0]
    rows, columns = square_iotas()
    diagonal = rows == columns
    strict, inverse, scales = [], [], []
    for unit in range(units):
        direction = d_ref[unit, :BLOCK]
        extra = d_ref[unit, BLOCK:].astype(F32)
        rate = extra[0:1] + extra[1:2] + extra[2:3]
        gram = nt(direction, direction)
        squares = jnp.sum(jnp.where(diagonal, gram, 0.0), 0, keepdims=True)
        scale = lax.rsqrt(squares + 1e-06)
        scaled_rate = rate * scale
        scale_column = jnp.sum(jnp.where(diagonal, scale, 0.0), 1, keepdims=True)
        rate_column = jnp.sum(jnp.where(diagonal, scaled_rate, 0.0), 1, keepdims=True)
        strict.append(jnp.where(rows > columns, rate_column * gram * scale, 0.0))
        scales.append((scale_column, scaled_rate))
    for unit in range(units):
        inverse.append(base_inverse(strict[unit]))
    size = BASE
    while size < BLOCK:
        row = lax.broadcasted_iota(jnp.int32, (BLOCK // 2, BLOCK), 0)
        column = lax.broadcasted_iota(jnp.int32, (BLOCK // 2, BLOCK), 1)
        inside = (row // size == column // (2 * size)) & (lax.rem(column, 2 * size) < size)
        below = []
        for unit in range(units):
            corner = jnp.where(inside, halves(strict[unit], size)[1], 0.0)
            below.append(triple(nn, split(corner), split(inverse[unit])))
        for unit in range(units):
            first, second = halves(inverse[unit], size)
            padded = joined(jnp.zeros_like(below[unit]), below[unit], size)
            second = second - triple(nn, split(second), split(padded))
            inverse[unit] = joined(first, second, size)
        size *= 2
    for unit in range(units):
        mixing_ref[unit] = scales[unit][0] * inverse[unit] * scales[unit][1]


def terms_kernel(d_ref, mixing_ref, rest_ref, start_ref, inner_ref, share_ref):
    rows, columns = square_iotas()
    identity = (rows == columns).astype(F32)
    for unit in range(d_ref.shape[0]):
        direction = d_ref[unit, :BLOCK]
        key = rest_ref[unit, 0]
        query = rest_ref[unit, 1]
        every = nt(
            jnp.concatenate([direction, query], 0), jnp.concatenate([direction, key], 0)
        )
        key_proj = split(jnp.where(rows > columns, every[:BLOCK, BLOCK:], 0.0))
        query_proj = split(jnp.where(rows >= columns, every[BLOCK:, :BLOCK], 0.0))
        mixing = split(mixing_ref[unit])
        right = jnp.concatenate([direction, key_proj[0]], 1)
        mixed = nn(mixing[0], right) + nn(mixing[1], right)
        mixed = jnp.concatenate(
            [mixed[:, :BLOCK], mixed[:, BLOCK:] + nn(mixing[0], key_proj[1])], 1
        )
        mixed = split(mixed)
        ahead = triple(nn, query_proj, mixed)
        start = split(query.astype(F32) - ahead[:, :HEAD_DIM])
        start_ref[unit, 0] = start[0]
        start_ref[unit, 1] = start[1]
        inner_ref[unit] = every[BLOCK:, BLOCK:] - ahead[:, HEAD_DIM:]
        behind = tn(mixed[0], direction) + tn(mixed[1], direction)
        end = split(key.astype(F32) - behind[BLOCK:])
        block_map = split(identity - behind[:BLOCK])
        share_ref[unit, 0] = end[0]
        share_ref[unit, 1] = end[1]
        share_ref[unit, 2] = block_map[0]
        share_ref[unit, 3] = block_map[1]


def attend_kernel(head_axis, before, away_ref, start_ref, inner_ref, *refs):
    shares = refs[:2 + 2 * (before > 0)]
    values = refs[len(shares):2 * len(shares)]
    out_ref, ends, maps, tails, moving, value_table = refs[2 * len(shares):]
    units = start_ref.shape[0]
    core = lax.rem(lax.axis_index(head_axis), 2)
    pairs = before + units
    for group in range(len(shares) // 2):
        share_own, share_other = shares[2 * group:2 * group + 2]
        value_own, value_other = values[2 * group:2 * group + 2]
        base = 0 if group else before
        for unit in range(units):
            for parity, share, value in (
                (core, share_own, value_own), (1 - core, share_other, value_other)
            ):
                place = 2 * (base + unit) + parity
                ends[place, 0] = share[unit, 0]
                ends[place, 1] = share[unit, 1]
                maps[place, 0] = share[unit, 2]
                maps[place, 1] = share[unit, 3]
                value_table[place] = value[unit]

    pair_maps = []
    for pair in range(pairs):
        odd = (maps[2 * pair + 1, 0], maps[2 * pair + 1, 1])
        left = tuple(
            jnp.concatenate([ends[2 * pair, part], maps[2 * pair, part]], 0) for part in range(2)
        )
        both = split(triple(nn, left, odd))
        for part in range(2):
            tails[2 * pair, part] = both[part][:BLOCK]
            tails[2 * pair + 1, part] = ends[2 * pair + 1, part]
        pair_maps.append((both[0][BLOCK:], both[1][BLOCK:]))

    current = []
    for unit in range(units):
        pair = before + unit
        start = (start_ref[unit, 0], start_ref[unit, 1])
        passed = triple(nt, start, (maps[2 * pair, 0], maps[2 * pair, 1]))
        whole = start[0].astype(F32) + start[1].astype(F32)
        front = split(jnp.where(core == 1, passed, whole))
        current.append(front)
        for part in range(2):
            moving[unit, 0, part] = start[part]
            moving[unit, 1, part] = front[part]
    for step in range(2, LOOK + 1):
        for unit in range(units):
            pair = before + unit - step
            if pair >= 0:
                current[unit] = split(triple(nt, current[unit], pair_maps[pair + 1]))
                for part in range(2):
                    moving[unit, step, part] = current[unit][part]

    rows, columns = square_iotas()
    scale = HEAD_DIM ** (-0.5)
    entries = away_ref.shape[1]
    for unit in range(units):
        block = 2 * (before + unit) + core
        score_list = [jnp.where(rows >= columns, inner_ref[unit] * scale, -1e30)]
        value_list = [value_table[block]]
        for entry in range(1, entries):
            away = away_ref[unit, entry]
            new = away > 0
            for other in range(1, entry):
                new = new & (away_ref[unit, other] != away)
            source = jnp.clip(block - away, 0, 2 * pairs - 1)
            step = jnp.clip(before + unit - source // 2, 0, LOOK)
            same = step == 0
            query = (moving[unit, step, 0], moving[unit, step, 1])
            key = tuple(
                jnp.where(same, ends[source, part], tails[source, part]) for part in range(2)
            )
            score_list.append(jnp.where(new, triple(nt, query, key) * scale, -1e30))
            value_list.append(value_table[source])
        scores = jnp.concatenate(score_list, 1)
        expos = jnp.exp(scores - jnp.max(scores, 1, keepdims=True))
        weights = (expos / jnp.sum(expos, 1, keepdims=True)).astype(BF16)
        out_ref[unit] = nn(weights, jnp.concatenate(value_list, 0)).astype(BF16)


def project_kernel(head_axis, offset, planes, attended_ref, own_ref, other_ref, out_ref):
    index = lax.axis_index(head_axis)
    core = lax.rem(index, 2)
    plane = lax.rem(index // 2 + offset, planes)
    width = out_ref.shape[1]
    columns = pl.ds(pl.multiple_of(plane * width, width), width)
    heads = own_ref.shape[0] // HEAD_DIM

    def group(which):
        return jnp.concatenate([attended_ref[which * heads + head] for head in range(heads)], 1)

    total = nn(group(core), own_ref[:, columns]) + nn(group(1 - core), other_ref[:, columns])
    out_ref[...] = total.astype(out_ref.dtype)


def call(kernel, outs, specs, flops, scratch=()):
    many = isinstance(outs, (list, tuple))
    return pl.pallas_call(
        kernel,
        out_shape=outs,
        in_specs=specs,
        out_specs=[VMEM] * len(outs) if many else VMEM,
        scratch_shapes=list(scratch),
        compiler_params=PARAMS,
        cost_estimate=pl.CostEstimate(flops=flops, bytes_accessed=2 ** 21, transcendentals=0),
    )


def body(ctx_size, head_size, queries, keys, values, directions, rates, selected, out_weight):
    heads = queries.shape[1] // HEAD_DIM
    group = 2 * heads
    planes = head_size // 2
    groups = ctx_size // group
    core = lax.rem(lax.axis_index("head"), 2)
    partners = [(g, g + 1 - 2 * (g % 2)) for g in range(head_size)]
    cubes = 2 * BLOCK ** 3

    def partner(value):
        return lax.ppermute(value, "head", partners)

    def exchange(value):
        members = None
        if groups > 1:
            members = [[a * group + b for b in range(group)] for a in range(groups)]
        return lax.all_to_all(value, "ctx", 0, 0, axis_index_groups=members, tiled=True)

    def ordered(own, other):
        return jnp.where(
            core == 0, jnp.concatenate([own, other], 0), jnp.concatenate([other, own], 0)
        )

    def array(shape, kind=BF16):
        return jax.ShapeDtypeStruct(shape, kind)

    d_shape = array((heads, BLOCK + EXTRA, HEAD_DIM))
    rest_shape = array((heads, 3, BLOCK, HEAD_DIM))
    keep_d, send_d, keep_rest, send_rest = call(
        functools.partial(pack_kernel, "head", "ctx"),
        [d_shape, d_shape, rest_shape, rest_shape],
        [VMEM] * 5 + [SMEM],
        cubes,
    )(queries, keys, values, directions, rates, selected)
    got_d = partner(send_d)
    got_rest = partner(send_rest)
    weight_other = partner(out_weight)
    unit_d = exchange(ordered(keep_d, got_d))
    unit_rest = exchange(ordered(keep_rest, got_rest))
    away = unit_d[:, BLOCK + 3, :selected.shape[1]].astype(jnp.int32)

    mixing = call(
        mixing_kernel, array((group, BLOCK, BLOCK), F32), [VMEM], 200 * cubes
    )(unit_d)
    value_own = unit_rest[:, 2]
    value_other = partner(value_own)
    start, inner, share = call(
        terms_kernel,
        [
            array((group, 2, BLOCK, HEAD_DIM)),
            array((group, BLOCK, BLOCK), F32),
            array((group, 4, BLOCK, HEAD_DIM)),
        ],
        [VMEM] * 3,
        200 * cubes,
    )(unit_d, mixing, unit_rest)
    share_other = partner(share)
    shares = [share, share_other]
    value_parts = [value_own, value_other]
    before = 0
    if groups > 1:
        before = group
        onward = [(i, i + group) for i in range(ctx_size - group)]
        shares += [lax.ppermute(part, "ctx", onward) for part in shares]
        value_parts += [lax.ppermute(part, "ctx", onward) for part in value_parts]
    pairs = before + group
    attended = call(
        functools.partial(attend_kernel, "head", before),
        array((group, BLOCK, HEAD_DIM)),
        [SMEM] + [VMEM] * (2 + 2 * len(shares)),
        200 * cubes,
        [
            pltpu.VMEM((2 * pairs, 2, BLOCK, HEAD_DIM), BF16),
            pltpu.VMEM((2 * pairs, 2, BLOCK, HEAD_DIM), BF16),
            pltpu.VMEM((2 * pairs, 2, BLOCK, HEAD_DIM), BF16),
            pltpu.VMEM((group, LOOK + 1, 2, BLOCK, HEAD_DIM), BF16),
            pltpu.VMEM((2 * pairs, BLOCK, HEAD_DIM), BF16),
        ],
    )(away, start, inner, *shares, *value_parts)

    local = exchange(attended)
    width = out_weight.shape[1] // planes

    def projected(offset, kind):
        return call(
            functools.partial(project_kernel, "head", offset, planes),
            array((BLOCK, width), kind),
            [VMEM] * 3,
            64 * cubes,
        )(local, out_weight, weight_other)

    arrived = []
    for offset in range(1, planes):
        pairs_of = [(g, (g + 2 * offset) % head_size) for g in range(head_size)]
        arrived.append(lax.ppermute(projected(offset, BF16), "head", pairs_of))
    total = projected(0, F32)
    for part in arrived:
        total = total + part.astype(F32)
    total = total.astype(BF16)
    half = width // 2
    mine = lax.dynamic_slice_in_dim(total, core * half, half, 1)
    theirs = lax.dynamic_slice_in_dim(total, (1 - core) * half, half, 1)
    return ordered(mine, partner(theirs))


def solution(mesh):
    in_specs = (
        P("ctx", "head"),
        P("ctx", "head"),
        P("ctx", "head"),
        P("ctx", "head"),
        P("head", "ctx"),
        P("ctx", None),
        P("head", None),
    )
    out_specs = P("ctx", "head")
    return jax.shard_map(
        functools.partial(body, mesh.shape["ctx"], mesh.shape["head"]),
        mesh=mesh,
        in_specs=in_specs,
        out_specs=out_specs,
        check_vma=False,
    )
```

```python
import functools

import jax
import jax.numpy as jnp
from jax import lax
from jax.experimental import pallas as pl
from jax.experimental.pallas import tpu as pltpu
from jax.sharding import PartitionSpec as P

HEAD_DIM = 128
BLOCK = 128
LOOK = 7
TOPK = 4
BASE = 16
EXTRA = 16
BF16 = jnp.bfloat16
F32 = jnp.float32
VMEM = pl.BlockSpec(memory_space=pltpu.VMEM)
SMEM = pl.BlockSpec(memory_space=pltpu.SMEM)
ANY = pl.BlockSpec(memory_space=pl.ANY)
HBM = pl.BlockSpec(memory_space=pltpu.HBM)
PARAMS = pltpu.CompilerParams(vmem_limit_bytes=32 * 1024 * 1024)


def dot(left, right, left_dim, right_dim):
    return lax.dot_general(
        left, right, (((left_dim,), (right_dim,)), ((), ())), preferred_element_type=F32
    )


def nn(left, right):
    return dot(left, right, 1, 0)


def nt(left, right):
    return dot(left, right, 1, 1)


def tn(left, right):
    return dot(left, right, 0, 0)


def split(value):
    high = value.astype(BF16)
    return high, (value - high.astype(F32)).astype(BF16)


def triple_nn(left, right):
    width = right[0].shape[1]
    row = jnp.concatenate(right, 1)
    both = nn(jnp.concatenate(left, 1), jnp.concatenate([row, row], 0))
    return both[:, :width] + both[:, width:]


def triple_nt(left, right):
    width = right[0].shape[0]
    column = jnp.concatenate(right, 0)
    both = nt(jnp.concatenate(left, 1), jnp.concatenate([column, column], 1))
    return both[:, :width] + both[:, width:]


def square_iotas():
    rows = lax.broadcasted_iota(jnp.int32, (BLOCK, BLOCK), 0)
    columns = lax.broadcasted_iota(jnp.int32, (BLOCK, BLOCK), 1)
    return rows, columns


def unit_slices(place, turn, blocks):
    unit = lax.bitwise_xor(place, turn)
    head, parity = unit // blocks, lax.rem(unit, blocks)
    rows = pl.ds(pl.multiple_of(parity * BLOCK, BLOCK), BLOCK)
    columns = pl.ds(pl.multiple_of(head * HEAD_DIM, HEAD_DIM), HEAD_DIM)
    return head, parity, rows, columns


def pack_kernel(axes, group, d_ref, rates_ref, selected_ref, *refs):
    outs = refs[:group]
    extra_ref, sems = refs[group:]
    blocks = d_ref.shape[0] // BLOCK
    device = lax.axis_index(axes[0])
    place = lax.rem(device, group)
    copies = []
    for turn in range(group):
        head, parity, rows, columns = unit_slices(place, turn, blocks)
        copies.append(
            pltpu.make_async_copy(
                d_ref.at[rows, columns], outs[turn].at[pl.ds(0, BLOCK)], sems.at[0, turn]
            )
        )
        copies[-1].start()
    row = lax.broadcasted_iota(jnp.int32, (EXTRA, HEAD_DIM), 0)
    lane = lax.broadcasted_iota(jnp.int32, (EXTRA, HEAD_DIM), 1)
    for turn in range(group):
        head, parity, rows, columns = unit_slices(place, turn, blocks)
        rate = rates_ref[:, rows]
        which = lax.broadcasted_iota(jnp.int32, rate.shape, 0)
        rate = jnp.sum(jnp.where(which == head, rate, 0.0), 0, keepdims=True)
        rate_1 = rate.astype(BF16).astype(F32)
        rate_2 = (rate - rate_1).astype(BF16).astype(F32)
        away = jnp.zeros((EXTRA, HEAD_DIM), jnp.int32)
        for entry in range(TOPK):
            distance = device * blocks + parity - selected_ref[parity, entry]
            away = jnp.where(lane == entry, distance, away)
        extra = jnp.where(row == 3, away.astype(F32), 0.0)
        extra = jnp.where(row == 2, (rate - rate_1) - rate_2, extra)
        extra = jnp.where(row == 1, rate_2, extra)
        extra = jnp.where(row == 0, rate_1, extra)
        extra_ref[turn] = extra.astype(BF16)
        copies.append(
            pltpu.make_async_copy(
                extra_ref.at[turn], outs[turn].at[pl.ds(BLOCK, EXTRA)], sems.at[1, turn]
            )
        )
        copies[-1].start()
    for copy in copies:
        copy.wait()


def pack_rest_kernel(axes, group, k_ref, q_ref, after, *refs):
    outs, sems = refs[:group], refs[group]
    blocks = k_ref.shape[0] // BLOCK
    place = lax.rem(lax.axis_index(axes[0]), group)
    copies = []
    for turn in range(group):
        head, parity, rows, columns = unit_slices(place, turn, blocks)
        for part, source in enumerate((k_ref, q_ref)):
            copies.append(
                pltpu.make_async_copy(
                    source.at[rows, columns], outs[turn].at[part], sems.at[part, turn]
                )
            )
            copies[-1].start()
    for copy in copies:
        copy.wait()


def fetched(sources, targets, sems):
    copies = []
    for index, (source, target) in enumerate(zip(sources, targets)):
        copies.append(pltpu.make_async_copy(source, target, sems.at[index]))
        copies[-1].start()
    return copies


def base_inverse(strict):
    count = BLOCK // BASE
    moved = [
        pltpu.roll(strict[b * BASE:(b + 1) * BASE], (BLOCK - b * BASE) % BLOCK, 1)
        if b else strict[:BASE]
        for b in range(count)
    ]
    lanes = lax.broadcasted_iota(jnp.int32, (BASE // 2, BLOCK), 1)
    rows = lax.broadcasted_iota(jnp.int32, (BASE // 2, BLOCK), 0)
    half = BASE // 2
    parts = []
    for b in range(count):
        upper = (lanes == rows + b * BASE).astype(F32)
        lower = (lanes == rows + b * BASE + half).astype(F32)
        for step in range(BASE - 1):
            if step < half:
                source = upper[step:step + 1]
                if step < half - 1:
                    upper = upper - moved[b][:half, step:step + 1] * source
            else:
                source = lower[step - half:step - half + 1]
            lower = lower - moved[b][half:, step:step + 1] * source
        parts += [upper, lower]
    return jnp.concatenate(parts, 0)


def halves(value, size):
    parts = value.reshape(BLOCK // (2 * size), 2, size, BLOCK)
    return parts[:, 0].reshape(BLOCK // 2, BLOCK), parts[:, 1].reshape(BLOCK // 2, BLOCK)


def joined(first, second, size):
    shape = (BLOCK // (2 * size), 1, size, BLOCK)
    return jnp.concatenate([first.reshape(shape), second.reshape(shape)], 1).reshape(BLOCK, BLOCK)


def mixing_kernel(axes, group, *refs):
    v_ref = refs[group]
    mixing_ref, away_ref = refs[group + 1:group + 3]
    v_outs = refs[group + 3:2 * group + 3]
    d_ref, sems, v_sems = refs[2 * group + 3:]
    units = group
    blocks = v_ref.shape[0] // BLOCK
    place = lax.rem(lax.axis_index(axes[0]), group)
    v_copies = []
    for turn in range(group):
        head, parity, v_rows, v_columns = unit_slices(place, turn, blocks)
        v_copies.append(
            pltpu.make_async_copy(v_ref.at[v_rows, v_columns], v_outs[turn], v_sems.at[turn])
        )
        v_copies[-1].start()
    copies = fetched(refs[:group], [d_ref.at[unit] for unit in range(units)], sems)
    rows, columns = square_iotas()
    diagonal = rows == columns
    strict, inverse, scales = [], [], []
    for unit in range(units):
        copies[unit].wait()
        direction = d_ref[unit, :BLOCK]
        extra = d_ref[unit, BLOCK:].astype(F32)
        rate = extra[0:1] + extra[1:2] + extra[2:3]
        away_ref[unit:unit + 1] = extra[3:4].astype(jnp.int32)
        gram = nt(direction, direction)
        squares = jnp.sum(jnp.where(diagonal, gram, 0.0), 0, keepdims=True)
        scale = lax.rsqrt(squares + 1e-06)
        scaled_rate = rate * scale
        scale_column = jnp.sum(jnp.where(diagonal, scale, 0.0), 1, keepdims=True)
        rate_column = jnp.sum(jnp.where(diagonal, scaled_rate, 0.0), 1, keepdims=True)
        strict.append(jnp.where(rows > columns, rate_column * gram * scale, 0.0))
        scales.append((scale_column, scaled_rate))
    for unit in range(units):
        inverse.append(base_inverse(strict[unit]))
    size = BASE
    while size < BLOCK:
        row = lax.broadcasted_iota(jnp.int32, (BLOCK // 2, BLOCK), 0)
        column = lax.broadcasted_iota(jnp.int32, (BLOCK // 2, BLOCK), 1)
        inside = (row // size == column // (2 * size)) & (lax.rem(column, 2 * size) < size)
        below = []
        for unit in range(units):
            corner = jnp.where(inside, halves(strict[unit], size)[1], 0.0)
            below.append(triple_nn(split(corner), split(inverse[unit])))
        for unit in range(units):
            first, second = halves(inverse[unit], size)
            padded = joined(jnp.zeros_like(below[unit]), below[unit], size)
            second = second - triple_nn(split(second), split(padded))
            inverse[unit] = joined(first, second, size)
        size *= 2
    for unit in range(units):
        mixing_ref[unit] = scales[unit][0] * inverse[unit] * scales[unit][1]
    for copy in v_copies:
        copy.wait()


def terms_kernel(group, *refs):
    start_ref, inner_ref, share_ref, d_ref, rest_ref, sems = refs[2 * group + 1:]
    mixing_ref = refs[2 * group]
    d_copies = fetched(
        [ref.at[pl.ds(0, BLOCK)] for ref in refs[:group]],
        [d_ref.at[unit] for unit in range(group)],
        sems.at[0],
    )
    rest_copies = fetched(
        refs[group:2 * group], [rest_ref.at[unit] for unit in range(group)], sems.at[1]
    )
    rows, columns = square_iotas()
    identity = (rows == columns).astype(F32)
    for unit in range(group):
        d_copies[unit].wait()
        rest_copies[unit].wait()
        direction = d_ref[unit]
        key = rest_ref[unit, 0]
        query = rest_ref[unit, 1]
        every = nt(
            jnp.concatenate([direction, query], 0), jnp.concatenate([direction, key], 0)
        )
        key_proj = split(jnp.where(rows > columns, every[:BLOCK, BLOCK:], 0.0))
        query_proj = split(jnp.where(rows >= columns, every[BLOCK:, :BLOCK], 0.0))
        mixing = jnp.concatenate(split(mixing_ref[unit]), 1)
        right = jnp.concatenate([direction, key_proj[0], key_proj[1]], 1)
        mixed = nn(mixing, jnp.concatenate([right, right], 0))
        mixed = split(
            jnp.concatenate(
                [mixed[:, :BLOCK], mixed[:, BLOCK:2 * BLOCK] + mixed[:, 2 * BLOCK:]], 1
            )
        )
        ahead = triple_nn(query_proj, mixed)
        start = split(query.astype(F32) - ahead[:, :HEAD_DIM])
        start_ref[unit, 0] = start[0]
        start_ref[unit, 1] = start[1]
        inner_ref[unit] = every[BLOCK:, BLOCK:] - ahead[:, HEAD_DIM:]
        behind = tn(jnp.concatenate(mixed, 0), jnp.concatenate([direction, direction], 0))
        end = split(key.astype(F32) - behind[BLOCK:])
        block_map = split(identity - behind[:BLOCK])
        share_ref[unit, 0] = end[0]
        share_ref[unit, 1] = end[1]
        share_ref[unit, 2] = block_map[0]
        share_ref[unit, 3] = block_map[1]


def attend_kernel(axes, before, units, away_ref, start_hbm, inner_hbm, *refs):
    count = 2 + 2 * (before > 0)
    shares, values = refs[:count], refs[count:count * (1 + units)]
    outs = refs[count * (1 + units):count * (1 + units) + units]
    (start_ref, inner_ref, ends, maps, tails, moving, value_table, results, own_sems,
     table_sems) = refs[count * (1 + units) + units:]
    core = lax.rem(lax.axis_index(axes[1]), 2)
    owner = lax.rem(lax.axis_index(axes[0]), units)
    mine = lax.rem(owner, units // 2) * 2 + core
    pairs = before + units
    copies, late_copies = [], []
    for side in range(count):
        base = 0 if side >= 2 else before
        for turn in range(units):
            unit = lax.bitwise_xor(mine, turn ^ (side % 2))
            place = 2 * (base + unit) + (core if side % 2 == 0 else 1 - core)
            index = side * units + turn
            for kind, (source, table, waiting) in enumerate((
                (shares[side].at[turn, pl.ds(0, 2)], ends, copies),
                (shares[side].at[turn, pl.ds(2, 2)], maps, copies),
                (values[index], value_table, late_copies),
            )):
                waiting.append(
                    pltpu.make_async_copy(source, table.at[place], table_sems.at[kind, index])
                )
                waiting[-1].start()
    for unit in range(units):
        turn = lax.bitwise_xor(mine, unit)
        for kind, (source, target, waiting) in enumerate((
            (start_hbm, start_ref, copies), (inner_hbm, inner_ref, late_copies)
        )):
            waiting.append(
                pltpu.make_async_copy(source.at[turn], target.at[unit], own_sems.at[kind, unit])
            )
            waiting[-1].start()
    for copy in copies:
        copy.wait()

    pair_maps = []
    for pair in range(pairs - 1):
        odd = (maps[2 * pair + 1, 0], maps[2 * pair + 1, 1])
        left = tuple(
            jnp.concatenate([ends[2 * pair, part], maps[2 * pair, part]], 0) for part in range(2)
        )
        both = split(triple_nn(left, odd))
        for part in range(2):
            tails[2 * pair, part] = both[part][:BLOCK]
            tails[2 * pair + 1, part] = ends[2 * pair + 1, part]
        pair_maps.append((both[0][BLOCK:], both[1][BLOCK:]))

    current = []
    for unit in range(units):
        pair = before + unit
        start = (start_ref[unit, 0], start_ref[unit, 1])
        passed = triple_nt(start, (maps[2 * pair, 0], maps[2 * pair, 1]))
        whole = start[0].astype(F32) + start[1].astype(F32)
        front = split(jnp.where(core == 1, passed, whole))
        current.append(front)
        for part in range(2):
            moving[unit, 0, part] = start[part]
            moving[unit, 1, part] = front[part]
    for step in range(2, LOOK + 1):
        for unit in range(units):
            pair = before + unit - step
            if pair >= 0:
                current[unit] = split(triple_nt(current[unit], pair_maps[pair + 1]))
                for part in range(2):
                    moving[unit, step, part] = current[unit][part]

    for copy in late_copies:
        copy.wait()
    rows, columns = square_iotas()
    scale = HEAD_DIM ** (-0.5)
    for unit in range(units):
        block = 2 * (before + unit) + core
        turn = lax.bitwise_xor(mine, unit)
        score_list = [jnp.where(rows >= columns, inner_ref[unit] * scale, -1e30)]
        value_list = [value_table[block]]
        for entry in range(1, TOPK):
            away = away_ref[turn, entry]
            new = away > 0
            for other in range(1, entry):
                new = new & (away_ref[turn, other] != away)
            source = jnp.clip(block - away, 0, 2 * pairs - 1)
            step = jnp.clip(before + unit - source // 2, 0, LOOK)
            same = step == 0
            query = (moving[unit, step, 0], moving[unit, step, 1])
            key = tuple(
                jnp.where(same, ends[source, part], tails[source, part]) for part in range(2)
            )
            score_list.append(jnp.where(new, triple_nt(query, key) * scale, -1e30))
            value_list.append(value_table[source])
        scores = jnp.concatenate(score_list, 1)
        expos = jnp.exp(scores - jnp.max(scores, 1, keepdims=True))
        weights = (expos / jnp.sum(expos, 1, keepdims=True)).astype(BF16)
        results[unit] = nn(weights, jnp.concatenate(value_list, 0)).astype(BF16)
    for turn in range(units):
        outs[turn][...] = results[lax.bitwise_xor(owner, turn)]


def project_kernel(axes, offset, planes, group, *refs):
    own_ref, other_ref, out_ref, attended_ref, own, other, sems = refs[group:]
    index = lax.axis_index(axes[1])
    owner = lax.rem(lax.axis_index(axes[0]), group)
    core = lax.rem(index, 2)
    plane = lax.rem(index // 2 + offset, planes)
    width = out_ref.shape[1]
    columns = pl.ds(pl.multiple_of(plane * width, width), width)
    copies = fetched(
        [own_ref.at[:, columns], other_ref.at[:, columns]], [own, other], sems
    )
    for turn in range(group):
        attended_ref[lax.bitwise_xor(owner, turn)] = refs[turn][...]
    heads = group // 2

    def half(which):
        return jnp.concatenate([attended_ref[which * heads + head] for head in range(heads)], 1)

    copies[0].wait()
    total = nn(half(core), own[...])
    copies[1].wait()
    total = total + nn(half(1 - core), other[...])
    out_ref[...] = total.astype(out_ref.dtype)


def call(kernel, outs, specs, flops, scratch=(), places=None):
    if places is None:
        places = [VMEM] * len(outs) if isinstance(outs, list) else VMEM
    return pl.pallas_call(
        kernel,
        out_shape=outs,
        in_specs=specs,
        out_specs=places,
        scratch_shapes=list(scratch),
        compiler_params=PARAMS,
        cost_estimate=pl.CostEstimate(flops=flops, bytes_accessed=2 ** 21, transcendentals=0),
    )


def body(ctx_size, head_size, queries, keys, values, directions, rates, selected, out_weight):
    heads = queries.shape[1] // HEAD_DIM
    blocks = queries.shape[0] // BLOCK
    group = blocks * heads
    planes = head_size // blocks
    groups = ctx_size // group
    axes = ("ctx", "head")
    core = lax.rem(lax.axis_index("head"), blocks)
    partners = [(g, g + 1 - 2 * (g % 2)) for g in range(head_size)]
    cubes = 2 * BLOCK ** 3

    def outward(value, turn):
        pairs = []
        for ctx in range(ctx_size):
            place = ctx % group
            unit = place ^ turn
            for g in range(head_size):
                c = g % blocks
                owner = ctx - place + heads * c + unit // blocks
                pairs.append((ctx * head_size + g, owner * head_size + g - c + unit % blocks))
        return lax.ppermute(value, axes, pairs)

    def homeward(value, turn):
        if turn == 0:
            return value
        pairs = [(i, i - i % group + (i % group ^ turn)) for i in range(ctx_size)]
        return lax.ppermute(value, "ctx", pairs)

    def partner(value):
        return lax.ppermute(value, "head", partners)

    def array(shape, kind=BF16):
        return jax.ShapeDtypeStruct(shape, kind)

    turns = range(group)
    tile = (BLOCK, HEAD_DIM)
    packed_d = call(
        functools.partial(pack_kernel, axes, group),
        [array((BLOCK + EXTRA, HEAD_DIM))] * group,
        [HBM, VMEM, SMEM],
        cubes,
        [pltpu.VMEM((group, EXTRA, HEAD_DIM), BF16), pltpu.SemaphoreType.DMA((2, group))],
        [ANY] * group,
    )(directions, rates, selected)
    unit_d = [outward(packed_d[turn], turn) for turn in turns]
    packed_rest = call(
        functools.partial(pack_rest_kernel, axes, group),
        [array((2, *tile))] * group,
        [HBM, HBM, ANY],
        cubes,
        [pltpu.SemaphoreType.DMA((2, group))],
        [ANY] * group,
    )(keys, queries, unit_d[1])
    unit_rest = [outward(packed_rest[turn], turn) for turn in turns]
    weight_other = partner(out_weight)

    mixing, away, *packed_v = call(
        functools.partial(mixing_kernel, axes, group),
        [array((group, BLOCK, BLOCK), F32), array((group, HEAD_DIM), jnp.int32)]
        + [array(tile)] * group,
        [ANY] * group + [HBM],
        200 * cubes,
        [
            pltpu.VMEM((group, BLOCK + EXTRA, HEAD_DIM), BF16),
            pltpu.SemaphoreType.DMA((group,)),
            pltpu.SemaphoreType.DMA((group,)),
        ],
        [VMEM] * 2 + [ANY] * group,
    )(*unit_d, values)
    unit_v = [outward(packed_v[turn], turn) for turn in turns]
    start, inner, share = call(
        functools.partial(terms_kernel, group),
        [
            array((group, 2, *tile)),
            array((group, BLOCK, BLOCK), F32),
            array((group, 4, *tile)),
        ],
        [ANY] * (2 * group) + [VMEM],
        200 * cubes,
        [
            pltpu.VMEM((group, *tile), BF16),
            pltpu.VMEM((group, 2, *tile), BF16),
            pltpu.SemaphoreType.DMA((2, group)),
        ],
    )(*unit_d, *unit_rest, mixing)
    share_other = partner(share)
    shares = [share, share_other]
    value_parts = unit_v + [partner(part) for part in unit_v]
    before = 0
    if groups > 1:
        before = group
        onward = [(i, i + group) for i in range(ctx_size - group)]
        shares += [lax.ppermute(part, "ctx", onward) for part in shares]
        value_parts += [lax.ppermute(part, "ctx", onward) for part in value_parts]
    pairs = before + group
    attended = call(
        functools.partial(attend_kernel, axes, before, group),
        [array(tile)] * group,
        [SMEM] + [ANY] * (2 + len(shares) + len(value_parts)),
        200 * cubes,
        [
            pltpu.VMEM((group, 2, *tile), BF16),
            pltpu.VMEM((group, BLOCK, BLOCK), F32),
            pltpu.VMEM((2 * pairs, 2, *tile), BF16),
            pltpu.VMEM((2 * pairs, 2, *tile), BF16),
            pltpu.VMEM((2 * pairs, 2, *tile), BF16),
            pltpu.VMEM((group, LOOK + 1, 2, *tile), BF16),
            pltpu.VMEM((2 * pairs, *tile), BF16),
            pltpu.VMEM((group, *tile), BF16),
            pltpu.SemaphoreType.DMA((2, group)),
            pltpu.SemaphoreType.DMA((3, 2 * pairs)),
        ],
    )(away, start, inner, *shares, *value_parts)

    local = [homeward(attended[turn], turn) for turn in turns]
    width = out_weight.shape[1] // planes

    def projected(offset, kind):
        return call(
            functools.partial(project_kernel, axes, offset, planes, group),
            array((BLOCK, width), kind),
            [VMEM] * group + [HBM] * 2,
            64 * cubes,
            [
                pltpu.VMEM((group, *tile), BF16),
                pltpu.VMEM((out_weight.shape[0], width), BF16),
                pltpu.VMEM((out_weight.shape[0], width), BF16),
                pltpu.SemaphoreType.DMA((2,)),
            ],
        )(*local, out_weight, weight_other)

    arrived = []
    for offset in range(1, planes):
        pairs_of = [(g, (g + blocks * offset) % head_size) for g in range(head_size)]
        arrived.append(lax.ppermute(projected(offset, BF16), "head", pairs_of))
    total = projected(0, F32)
    for part in arrived:
        total = total + part.astype(F32)
    total = total.astype(BF16)
    half = width // blocks
    mine = lax.dynamic_slice_in_dim(total, core * half, half, 1)
    theirs = partner(lax.dynamic_slice_in_dim(total, (1 - core) * half, half, 1))
    return jnp.where(
        core == 0,
        jnp.concatenate([mine, theirs], 0),
        jnp.concatenate([theirs, mine], 0),
    )


def solution(mesh):
    in_specs = (
        P("ctx", "head"),
        P("ctx", "head"),
        P("ctx", "head"),
        P("ctx", "head"),
        P("head", "ctx"),
        P("ctx", None),
        P("head", None),
    )
    out_specs = P("ctx", "head")
    return jax.shard_map(
        functools.partial(body, mesh.shape["ctx"], mesh.shape["head"]),
        mesh=mesh,
        in_specs=in_specs,
        out_specs=out_specs,
        check_vma=False,
    )
```

```python
import functools

import jax
import jax.numpy as jnp
from jax import lax
from jax.experimental import pallas as pl
from jax.experimental.pallas import tpu as pltpu
from jax.sharding import PartitionSpec as P

HEAD_DIM = 128
BLOCK = 128
LOOK = 7
TOPK = 4
BASE = 16
EXTRA = 16
KEY_ROW = BLOCK + EXTRA
QUERY_ROW = KEY_ROW + BLOCK
VALUE_ROW = QUERY_ROW + BLOCK
UNIT_ROWS = VALUE_ROW + BLOCK
BF16 = jnp.bfloat16
F32 = jnp.float32
VMEM = pl.BlockSpec(memory_space=pltpu.VMEM)
SMEM = pl.BlockSpec(memory_space=pltpu.SMEM)
ANY = pl.BlockSpec(memory_space=pl.ANY)
PARAMS = pltpu.CompilerParams(vmem_limit_bytes=56 * 1024 * 1024)


def dot(left, right, left_dim, right_dim):
    return lax.dot_general(
        left, right, (((left_dim,), (right_dim,)), ((), ())), preferred_element_type=F32
    )


def nn(left, right):
    return dot(left, right, 1, 0)


def nt(left, right):
    return dot(left, right, 1, 1)


def tn(left, right):
    return dot(left, right, 0, 0)


def split(value):
    high = value.astype(BF16)
    return high, (value - high.astype(F32)).astype(BF16)


def triple(product, left, right):
    rows = left[0].shape[0]
    first = product(jnp.concatenate(left, 0), right[0])
    return first[:rows] + (first[rows:] + product(left[0], right[1]))


def square_iotas():
    rows = lax.broadcasted_iota(jnp.int32, (BLOCK, BLOCK), 0)
    columns = lax.broadcasted_iota(jnp.int32, (BLOCK, BLOCK), 1)
    return rows, columns


def pack_kernel(axes, d_ref, k_ref, q_ref, v_ref, rates_ref, selected_ref, whole, send,
                extra_ref, sems):
    heads = d_ref.shape[1] // HEAD_DIM
    blocks = d_ref.shape[0] // BLOCK
    device = lax.axis_index(axes[0])
    core = lax.rem(lax.axis_index(axes[1]), blocks)
    copies = []
    targets = []
    for side, parity in enumerate((core, 1 - core)):
        rows = pl.ds(pl.multiple_of(parity * BLOCK, BLOCK), BLOCK)
        for head in range(heads):
            target = send.at[head] if side else whole.at[core * heads + head]
            targets.append((parity, head, target))
            columns = pl.ds(head * HEAD_DIM, HEAD_DIM)
            for kind, (source, place) in enumerate((
                (d_ref, 0), (k_ref, KEY_ROW), (q_ref, QUERY_ROW), (v_ref, VALUE_ROW)
            )):
                copies.append(
                    pltpu.make_async_copy(
                        source.at[rows, columns],
                        target.at[pl.ds(place, BLOCK)],
                        sems.at[side * heads + head, kind],
                    )
                )
                copies[-1].start()
    row = lax.broadcasted_iota(jnp.int32, (EXTRA, HEAD_DIM), 0)
    lane = lax.broadcasted_iota(jnp.int32, (EXTRA, HEAD_DIM), 1)
    for index, (parity, head, target) in enumerate(targets):
        rate = rates_ref[:, pl.ds(pl.multiple_of(parity * BLOCK, BLOCK), BLOCK)][head:head + 1]
        rate_1 = rate.astype(BF16).astype(F32)
        rate_2 = (rate - rate_1).astype(BF16).astype(F32)
        away = jnp.zeros((EXTRA, HEAD_DIM), jnp.int32)
        for entry in range(TOPK):
            distance = device * blocks + parity - selected_ref[parity, entry]
            away = jnp.where(lane == entry, distance, away)
        extra = jnp.where(row == 3, away.astype(F32), 0.0)
        extra = jnp.where(row == 2, (rate - rate_1) - rate_2, extra)
        extra = jnp.where(row == 1, rate_2, extra)
        extra = jnp.where(row == 0, rate_1, extra)
        extra_ref[index] = extra.astype(BF16)
        copies.append(
            pltpu.make_async_copy(
                extra_ref.at[index], target.at[pl.ds(BLOCK, EXTRA)], sems.at[index, 4]
            )
        )
        copies[-1].start()
    for copy in copies:
        copy.wait()


def place_kernel(axes, partial, got, whole, sems):
    heads = got.shape[0]
    core = lax.rem(lax.axis_index(axes[1]), 2)
    copies = []
    for head in range(heads):
        copies.append(
            pltpu.make_async_copy(
                got.at[head], whole.at[(1 - core) * heads + head], sems.at[head]
            )
        )
        copies[-1].start()
    for copy in copies:
        copy.wait()


def fetched(sources, targets, sems):
    copies = []
    for index, (source, target) in enumerate(zip(sources, targets)):
        copies.append(pltpu.make_async_copy(source, target, sems.at[index]))
        copies[-1].start()
    return copies


def base_inverse(strict):
    count = BLOCK // BASE
    moved = [
        pltpu.roll(strict[b * BASE:(b + 1) * BASE], (BLOCK - b * BASE) % BLOCK, 1)
        if b else strict[:BASE]
        for b in range(count)
    ]
    lanes = lax.broadcasted_iota(jnp.int32, (BASE // 2, BLOCK), 1)
    rows = lax.broadcasted_iota(jnp.int32, (BASE // 2, BLOCK), 0)
    half = BASE // 2
    parts = []
    for b in range(count):
        upper = (lanes == rows + b * BASE).astype(F32)
        lower = (lanes == rows + b * BASE + half).astype(F32)
        for step in range(BASE - 1):
            if step < half:
                source = upper[step:step + 1]
                if step < half - 1:
                    upper = upper - moved[b][:half, step:step + 1] * source
            else:
                source = lower[step - half:step - half + 1]
            lower = lower - moved[b][half:, step:step + 1] * source
        parts += [upper, lower]
    return jnp.concatenate(parts, 0)


def halves(value, size):
    parts = value.reshape(BLOCK // (2 * size), 2, size, BLOCK)
    return parts[:, 0].reshape(BLOCK // 2, BLOCK), parts[:, 1].reshape(BLOCK // 2, BLOCK)


def joined(first, second, size):
    shape = (BLOCK // (2 * size), 1, size, BLOCK)
    return jnp.concatenate([first.reshape(shape), second.reshape(shape)], 1).reshape(BLOCK, BLOCK)


def terms_kernel(units_ref, start_ref, inner_ref, share_ref, away_ref, unit_ref, sems):
    units = units_ref.shape[0]
    copies = fetched(
        [units_ref.at[unit] for unit in range(units)],
        [unit_ref.at[unit] for unit in range(units)],
        sems,
    )
    rows, columns = square_iotas()
    diagonal = rows == columns
    identity = diagonal.astype(F32)
    strict, inverse, scales, query_projs = [], [], [], []
    for unit in range(units):
        copies[unit].wait()
        direction = unit_ref[unit, :BLOCK]
        query = unit_ref[unit, QUERY_ROW:QUERY_ROW + BLOCK]
        extra = unit_ref[unit, BLOCK:KEY_ROW].astype(F32)
        rate = extra[0:1] + extra[1:2] + extra[2:3]
        away_ref[unit:unit + 1] = extra[3:4].astype(jnp.int32)
        over = nt(jnp.concatenate([direction, query], 0), direction)
        gram = over[:BLOCK]
        query_projs.append(jnp.where(rows >= columns, over[BLOCK:], 0.0))
        squares = jnp.sum(jnp.where(diagonal, gram, 0.0), 0, keepdims=True)
        scale = lax.rsqrt(squares + 1e-06)
        scaled_rate = rate * scale
        scale_column = jnp.sum(jnp.where(diagonal, scale, 0.0), 1, keepdims=True)
        rate_column = jnp.sum(jnp.where(diagonal, scaled_rate, 0.0), 1, keepdims=True)
        strict.append(jnp.where(rows > columns, rate_column * gram * scale, 0.0))
        scales.append((scale_column, scaled_rate))
    for unit in range(units):
        inverse.append(base_inverse(strict[unit]))
    size = BASE
    while size < BLOCK:
        row = lax.broadcasted_iota(jnp.int32, (BLOCK // 2, BLOCK), 0)
        column = lax.broadcasted_iota(jnp.int32, (BLOCK // 2, BLOCK), 1)
        inside = (row // size == column // (2 * size)) & (lax.rem(column, 2 * size) < size)
        below = []
        for unit in range(units):
            corner = jnp.where(inside, halves(strict[unit], size)[1], 0.0)
            below.append(triple(nn, split(corner), split(inverse[unit])))
        for unit in range(units):
            first, second = halves(inverse[unit], size)
            padded = joined(jnp.zeros_like(below[unit]), below[unit], size)
            second = second - triple(nn, split(second), split(padded))
            inverse[unit] = joined(first, second, size)
        size *= 2
    for unit in range(units):
        direction = unit_ref[unit, :BLOCK]
        key = unit_ref[unit, KEY_ROW:KEY_ROW + BLOCK]
        query = unit_ref[unit, QUERY_ROW:QUERY_ROW + BLOCK]
        over = nt(jnp.concatenate([direction, query], 0), key)
        key_proj = jnp.where(rows > columns, over[:BLOCK], 0.0).astype(BF16)
        mixing = split(scales[unit][0] * inverse[unit] * scales[unit][1])
        mixed = nn(jnp.concatenate(mixing, 0), jnp.concatenate([direction, key_proj], 1))
        mixed = split(mixed[:BLOCK] + mixed[BLOCK:])
        query_proj = split(query_projs[unit])
        ahead = nn(jnp.concatenate(query_proj, 0), mixed[0])
        ahead = ahead[:BLOCK] + ahead[BLOCK:]
        start = split(query.astype(F32) - ahead[:, :HEAD_DIM])
        start_ref[unit, 0] = start[0]
        start_ref[unit, 1] = start[1]
        inner_ref[unit] = over[BLOCK:] - ahead[:, HEAD_DIM:]
        behind = tn(jnp.concatenate([mixed[0], mixed[1][:, :BLOCK]], 1), direction)
        block_map = split(identity - (behind[:BLOCK] + behind[2 * BLOCK:]))
        share_ref[unit, 0] = (key.astype(F32) - behind[BLOCK:2 * BLOCK]).astype(BF16)
        share_ref[unit, 1] = block_map[0]
        share_ref[unit, 2] = block_map[1]
        share_ref[unit, 3] = unit_ref[unit, VALUE_ROW:VALUE_ROW + BLOCK]


def attend_kernel(axes, before, units, away_ref, start_ref, inner_ref, *refs):
    count = 2 + 2 * (before > 0)
    shares = refs[:count]
    out_ref, table, tails, moving, sems = refs[count:]
    core = lax.rem(lax.axis_index(axes[1]), 2)
    pairs = before + units
    copies = []
    for side in range(count):
        base = 0 if side >= 2 else before
        parity = core if side % 2 == 0 else 1 - core
        for unit in range(units):
            copies.append(
                pltpu.make_async_copy(
                    shares[side].at[unit],
                    table.at[2 * (base + unit) + parity],
                    sems.at[side, unit],
                )
            )
            copies[-1].start()
    for copy in copies:
        copy.wait()

    pair_maps = []
    for pair in range(pairs - 1):
        even, odd = 2 * pair, 2 * pair + 1
        both = nn(
            jnp.concatenate([table[even, 0], table[even, 1], table[even, 2]], 0), table[odd, 1]
        )
        tails[even] = both[:BLOCK].astype(BF16)
        tails[odd] = table[odd, 0]
        pair_maps.append(
            split(both[BLOCK:2 * BLOCK] + (both[2 * BLOCK:] + nn(table[even, 1], table[odd, 2])))
        )

    current = []
    for unit in range(units):
        pair = before + unit
        start = (start_ref[unit, 0], start_ref[unit, 1])
        passed = triple(nt, start, (table[2 * pair, 1], table[2 * pair, 2]))
        whole = start[0].astype(F32) + start[1].astype(F32)
        current.append(split(jnp.where(core == 1, passed, whole)))
        moving[unit, 0] = start[0]
        moving[unit, 1] = current[unit][0]
    for step in range(2, LOOK + 1):
        for unit in range(units):
            pair = before + unit - step
            if pair >= 0:
                current[unit] = split(triple(nt, current[unit], pair_maps[pair + 1]))
                moving[unit, step] = current[unit][0]

    rows, columns = square_iotas()
    scale = HEAD_DIM ** (-0.5)
    for unit in range(units):
        block = 2 * (before + unit) + core
        score_list = [jnp.where(rows >= columns, inner_ref[unit] * scale, -1e30)]
        value_list = [table[block, 3]]
        for entry in range(1, TOPK):
            away = away_ref[unit, entry]
            new = away > 0
            for other in range(1, entry):
                new = new & (away_ref[unit, other] != away)
            source = jnp.clip(block - away, 0, 2 * pairs - 1)
            step = jnp.clip(before + unit - source // 2, 0, LOOK)
            key = jnp.where(step == 0, table[source, 0], tails[source])
            score = nt(moving[unit, step], key) * scale
            score_list.append(jnp.where(new, score, -1e30))
            value_list.append(table[source, 3])
        scores = jnp.concatenate(score_list, 1)
        expos = jnp.exp(scores - jnp.max(scores, 1, keepdims=True))
        weights = (expos / jnp.sum(expos, 1, keepdims=True)).astype(BF16)
        out_ref[unit] = nn(weights, jnp.concatenate(value_list, 0)).astype(BF16)


def project_kernel(axes, offset, planes, attended_ref, own_ref, other_ref, out_ref, own, other,
                   sems):
    index = lax.axis_index(axes[1])
    core = lax.rem(index, 2)
    plane = lax.rem(index // 2 + offset, planes)
    width = out_ref.shape[1]
    columns = pl.ds(pl.multiple_of(plane * width, width), width)
    copies = fetched(
        [own_ref.at[:, columns], other_ref.at[:, columns]], [own, other], sems
    )
    heads = attended_ref.shape[0] // 2

    def half(which):
        return jnp.concatenate([attended_ref[which * heads + head] for head in range(heads)], 1)

    copies[0].wait()
    total = nn(half(core), own[...])
    copies[1].wait()
    total = total + nn(half(1 - core), other[...])
    out_ref[...] = total.astype(out_ref.dtype)


def call(kernel, outs, specs, flops, scratch=(), places=None, aliases=None):
    if places is None:
        places = [VMEM] * len(outs) if isinstance(outs, list) else VMEM
    return pl.pallas_call(
        kernel,
        out_shape=outs,
        in_specs=specs,
        out_specs=places,
        scratch_shapes=list(scratch),
        input_output_aliases=aliases or {},
        compiler_params=PARAMS,
        cost_estimate=pl.CostEstimate(flops=flops, bytes_accessed=2 ** 21, transcendentals=0),
    )


def body(ctx_size, head_size, queries, keys, values, directions, rates, selected, out_weight):
    heads = queries.shape[1] // HEAD_DIM
    blocks = queries.shape[0] // BLOCK
    group = blocks * heads
    planes = head_size // blocks
    groups = ctx_size // group
    axes = ("ctx", "head")
    core = lax.rem(lax.axis_index("head"), blocks)
    partners = [(g, g + 1 - 2 * (g % 2)) for g in range(head_size)]
    cubes = 2 * BLOCK ** 3

    def exchange(value):
        members = None
        if groups > 1:
            members = [[a * group + b for b in range(group)] for a in range(groups)]
        return lax.all_to_all(value, "ctx", 0, 0, axis_index_groups=members, tiled=True)

    def partner(value):
        return lax.ppermute(value, "head", partners)

    def array(shape, kind=BF16):
        return jax.ShapeDtypeStruct(shape, kind)

    tile = (BLOCK, HEAD_DIM)
    whole_shape = array((group, UNIT_ROWS, HEAD_DIM))
    whole, send = call(
        functools.partial(pack_kernel, axes),
        [whole_shape, array((heads, UNIT_ROWS, HEAD_DIM))],
        [ANY] * 4 + [VMEM, SMEM],
        cubes,
        [pltpu.VMEM((group, EXTRA, HEAD_DIM), BF16), pltpu.SemaphoreType.DMA((group, 5))],
        [ANY] * 2,
    )(directions, keys, queries, values, rates, selected)
    whole = call(
        functools.partial(place_kernel, axes),
        whole_shape,
        [ANY] * 2,
        cubes,
        [pltpu.SemaphoreType.DMA((heads,))],
        ANY,
        {0: 0},
    )(whole, partner(send))
    unit_arrays = exchange(whole)
    weight_other = partner(out_weight)

    start, inner, share, away = call(
        terms_kernel,
        [
            array((group, 2, *tile)),
            array((group, BLOCK, BLOCK), F32),
            array((group, 4, *tile)),
            array((group, HEAD_DIM), jnp.int32),
        ],
        [ANY],
        400 * cubes,
        [
            pltpu.VMEM((group, UNIT_ROWS, HEAD_DIM), BF16),
            pltpu.SemaphoreType.DMA((group,)),
        ],
    )(unit_arrays)
    shares = [share, partner(share)]
    before = 0
    if groups > 1:
        before = group
        onward = [(i, i + group) for i in range(ctx_size - group)]
        shares += [lax.ppermute(part, "ctx", onward) for part in shares]
    pairs = before + group
    attended = call(
        functools.partial(attend_kernel, axes, before, group),
        array((group, *tile)),
        [SMEM, VMEM, VMEM] + [ANY] * len(shares),
        400 * cubes,
        [
            pltpu.VMEM((2 * pairs, 4, *tile), BF16),
            pltpu.VMEM((2 * pairs, *tile), BF16),
            pltpu.VMEM((group, LOOK + 1, *tile), BF16),
            pltpu.SemaphoreType.DMA((len(shares), group)),
        ],
    )(away, start, inner, *shares)

    local = exchange(attended)
    width = out_weight.shape[1] // planes

    def projected(offset, kind):
        return call(
            functools.partial(project_kernel, axes, offset, planes),
            array((BLOCK, width), kind),
            [VMEM, ANY, ANY],
            64 * cubes,
            [
                pltpu.VMEM((out_weight.shape[0], width), BF16),
                pltpu.VMEM((out_weight.shape[0], width), BF16),
                pltpu.SemaphoreType.DMA((2,)),
            ],
        )(local, out_weight, weight_other)

    arrived = []
    for offset in range(1, planes):
        pairs_of = [(g, (g + blocks * offset) % head_size) for g in range(head_size)]
        arrived.append(lax.ppermute(projected(offset, BF16), "head", pairs_of))
    total = projected(0, F32)
    for part in arrived:
        total = total + part.astype(F32)
    total = total.astype(BF16)
    half = width // blocks
    mine = lax.dynamic_slice_in_dim(total, core * half, half, 1)
    theirs = partner(lax.dynamic_slice_in_dim(total, (1 - core) * half, half, 1))
    return jnp.where(
        core == 0,
        jnp.concatenate([mine, theirs], 0),
        jnp.concatenate([theirs, mine], 0),
    )


def solution(mesh):
    in_specs = (
        P("ctx", "head"),
        P("ctx", "head"),
        P("ctx", "head"),
        P("ctx", "head"),
        P("head", "ctx"),
        P("ctx", None),
        P("head", None),
    )
    out_specs = P("ctx", "head")
    return jax.shard_map(
        functools.partial(body, mesh.shape["ctx"], mesh.shape["head"]),
        mesh=mesh,
        in_specs=in_specs,
        out_specs=out_specs,
        check_vma=False,
    )
```

```python
import functools

import jax
import jax.numpy as jnp
from jax import lax
from jax.experimental import pallas as pl
from jax.experimental.pallas import tpu as pltpu
from jax.sharding import PartitionSpec as P

HEAD_DIM = 128
BLOCK = 128
LOOK = 7
TOPK = 4
BASE = 16
EXTRA = 16
KEY_ROW = BLOCK + EXTRA
QUERY_ROW = KEY_ROW + BLOCK
VALUE_ROW = QUERY_ROW + BLOCK
UNIT_ROWS = VALUE_ROW + BLOCK
BF16 = jnp.bfloat16
F32 = jnp.float32
VMEM = pl.BlockSpec(memory_space=pltpu.VMEM)
SMEM = pl.BlockSpec(memory_space=pltpu.SMEM)
ANY = pl.BlockSpec(memory_space=pl.ANY)


def dot(left, right, left_dim, right_dim):
    return lax.dot_general(
        left, right, (((left_dim,), (right_dim,)), ((), ())), preferred_element_type=F32
    )


def nn(left, right):
    return dot(left, right, 1, 0)


def nt(left, right):
    return dot(left, right, 1, 1)


def tn(left, right):
    return dot(left, right, 0, 0)


def split(value):
    high = value.astype(BF16)
    return high, (value - high.astype(F32)).astype(BF16)


def triple(product, left, right):
    rows = left[0].shape[0]
    first = product(jnp.concatenate(left, 0), right[0])
    return first[:rows] + (first[rows:] + product(left[0], right[1]))


def square_iotas():
    rows = lax.broadcasted_iota(jnp.int32, (BLOCK, BLOCK), 0)
    columns = lax.broadcasted_iota(jnp.int32, (BLOCK, BLOCK), 1)
    return rows, columns


def pack_kernel(axes, d_ref, k_ref, q_ref, v_ref, rates_ref, selected_ref, keep, send,
                units_ref, sems, out_sems):
    heads = d_ref.shape[1] // HEAD_DIM
    blocks = d_ref.shape[0] // BLOCK
    device = lax.axis_index(axes[0])
    core = lax.rem(lax.axis_index(axes[1]), blocks)
    copies = []
    sides = (1 - core, core)
    for side, parity in enumerate(sides):
        rows = pl.ds(pl.multiple_of(parity * BLOCK, BLOCK), BLOCK)
        for head in range(heads):
            columns = pl.ds(head * HEAD_DIM, HEAD_DIM)
            for kind, (source, place) in enumerate((
                (d_ref, 0), (k_ref, KEY_ROW), (q_ref, QUERY_ROW), (v_ref, VALUE_ROW)
            )):
                copies.append(
                    pltpu.make_async_copy(
                        source.at[rows, columns],
                        units_ref.at[side, head, pl.ds(place, BLOCK)],
                        sems.at[side * heads + head, kind],
                    )
                )
                copies[-1].start()
    row = lax.broadcasted_iota(jnp.int32, (EXTRA, HEAD_DIM), 0)
    lane = lax.broadcasted_iota(jnp.int32, (EXTRA, HEAD_DIM), 1)
    for side, parity in enumerate(sides):
        rates = rates_ref[:, pl.ds(pl.multiple_of(parity * BLOCK, BLOCK), BLOCK)]
        away = jnp.zeros((EXTRA, HEAD_DIM), jnp.int32)
        for entry in range(TOPK):
            distance = device * blocks + parity - selected_ref[parity, entry]
            away = jnp.where(lane == entry, distance, away)
        away = jnp.where(row == 3, away.astype(F32), 0.0)
        rates_1 = rates.astype(BF16).astype(F32)
        rates_2 = (rates - rates_1).astype(BF16).astype(F32)
        rates_3 = (rates - rates_1) - rates_2
        for head in range(heads):
            extra = jnp.where(row == 2, rates_3[head:head + 1], away)
            extra = jnp.where(row == 1, rates_2[head:head + 1], extra)
            extra = jnp.where(row == 0, rates_1[head:head + 1], extra)
            units_ref[side, head, BLOCK:KEY_ROW] = extra.astype(BF16)
    out_copies = []
    for side, target in enumerate((send, keep)):
        for head in range(heads):
            index = side * heads + head
            for copy in copies[4 * index:4 * index + 4]:
                copy.wait()
            out_copies.append(
                pltpu.make_async_copy(
                    units_ref.at[side, head], target.at[head], out_sems.at[index]
                )
            )
            out_copies[-1].start()
    for copy in out_copies:
        copy.wait()


def place_kernel(axes, keep, got, whole, sems):
    heads = got.shape[0]
    core = lax.rem(lax.axis_index(axes[1]), 2)
    copies = []
    for side, (source, owner) in enumerate(((keep, core), (got, 1 - core))):
        for head in range(heads):
            copies.append(
                pltpu.make_async_copy(
                    source.at[head], whole.at[owner * heads + head], sems.at[side, head]
                )
            )
            copies[-1].start()
    for copy in copies:
        copy.wait()


def fetched(sources, targets, sems):
    copies = []
    for index, (source, target) in enumerate(zip(sources, targets)):
        copies.append(pltpu.make_async_copy(source, target, sems.at[index]))
        copies[-1].start()
    return copies


def base_inverse(strict):
    count = BLOCK // BASE
    moved = [
        pltpu.roll(strict[b * BASE:(b + 1) * BASE], (BLOCK - b * BASE) % BLOCK, 1)
        if b else strict[:BASE]
        for b in range(count)
    ]
    lanes = lax.broadcasted_iota(jnp.int32, (BASE // 2, BLOCK), 1)
    rows = lax.broadcasted_iota(jnp.int32, (BASE // 2, BLOCK), 0)
    half = BASE // 2
    parts = []
    for b in range(count):
        upper = (lanes == rows + b * BASE).astype(F32)
        lower = (lanes == rows + b * BASE + half).astype(F32)
        for step in range(BASE - 1):
            if step < half:
                source = upper[step:step + 1]
                if step < half - 1:
                    upper = upper - moved[b][:half, step:step + 1] * source
            else:
                source = lower[step - half:step - half + 1]
            lower = lower - moved[b][half:, step:step + 1] * source
        parts += [upper, lower]
    return jnp.concatenate(parts, 0)


def halves(value, size):
    parts = value.reshape(BLOCK // (2 * size), 2, size, BLOCK)
    return parts[:, 0].reshape(BLOCK // 2, BLOCK), parts[:, 1].reshape(BLOCK // 2, BLOCK)


def joined(first, second, size):
    shape = (BLOCK // (2 * size), 1, size, BLOCK)
    return jnp.concatenate([first.reshape(shape), second.reshape(shape)], 1).reshape(BLOCK, BLOCK)


def terms_kernel(unit_ref, start_ref, inner_ref, share_ref, away_ref):
    units = unit_ref.shape[0]
    rows, columns = square_iotas()
    diagonal = rows == columns
    identity = diagonal.astype(F32)
    strict, inverse, scales, query_projs = [], [], [], []
    for unit in range(units):
        direction = unit_ref[unit, :BLOCK]
        query = unit_ref[unit, QUERY_ROW:QUERY_ROW + BLOCK]
        extra = unit_ref[unit, BLOCK:KEY_ROW].astype(F32)
        rate = extra[0:1] + extra[1:2] + extra[2:3]
        away_ref[unit:unit + 1] = extra[3:4].astype(jnp.int32)
        over = nt(jnp.concatenate([direction, query], 0), direction)
        gram = over[:BLOCK]
        query_projs.append(jnp.where(rows >= columns, over[BLOCK:], 0.0))
        squares = jnp.sum(jnp.where(diagonal, gram, 0.0), 0, keepdims=True)
        scale = lax.rsqrt(squares + 1e-06)
        scaled_rate = rate * scale
        scale_column = jnp.sum(jnp.where(diagonal, scale, 0.0), 1, keepdims=True)
        rate_column = jnp.sum(jnp.where(diagonal, scaled_rate, 0.0), 1, keepdims=True)
        strict.append(jnp.where(rows > columns, rate_column * gram * scale, 0.0))
        scales.append((scale_column, scaled_rate))
    for unit in range(units):
        inverse.append(base_inverse(strict[unit]))
    size = BASE
    while size < BLOCK:
        row = lax.broadcasted_iota(jnp.int32, (BLOCK // 2, BLOCK), 0)
        column = lax.broadcasted_iota(jnp.int32, (BLOCK // 2, BLOCK), 1)
        inside = (row // size == column // (2 * size)) & (lax.rem(column, 2 * size) < size)
        below = []
        for unit in range(units):
            corner = jnp.where(inside, halves(strict[unit], size)[1], 0.0)
            below.append(triple(nn, split(corner), split(inverse[unit])))
        for unit in range(units):
            first, second = halves(inverse[unit], size)
            padded = joined(jnp.zeros_like(below[unit]), below[unit], size)
            second = second - triple(nn, split(second), split(padded))
            inverse[unit] = joined(first, second, size)
        size *= 2
    for unit in range(units):
        direction = unit_ref[unit, :BLOCK]
        key = unit_ref[unit, KEY_ROW:KEY_ROW + BLOCK]
        query = unit_ref[unit, QUERY_ROW:QUERY_ROW + BLOCK]
        over = nt(jnp.concatenate([direction, query], 0), key)
        key_proj = jnp.where(rows > columns, over[:BLOCK], 0.0).astype(BF16)
        mixing = split(scales[unit][0] * inverse[unit] * scales[unit][1])
        mixed = nn(jnp.concatenate(mixing, 0), jnp.concatenate([direction, key_proj], 1))
        mixed = split(mixed[:BLOCK] + mixed[BLOCK:])
        query_proj = split(query_projs[unit])
        ahead = nn(jnp.concatenate(query_proj, 0), mixed[0])
        ahead = ahead[:BLOCK] + ahead[BLOCK:]
        start = split(query.astype(F32) - ahead[:, :HEAD_DIM])
        start_ref[unit, 0] = start[0]
        start_ref[unit, 1] = start[1]
        inner_ref[unit] = over[BLOCK:] - ahead[:, HEAD_DIM:]
        behind = tn(jnp.concatenate([mixed[0], mixed[1][:, :BLOCK]], 1), direction)
        block_map = split(identity - (behind[:BLOCK] + behind[2 * BLOCK:]))
        share_ref[unit, 0] = (key.astype(F32) - behind[BLOCK:2 * BLOCK]).astype(BF16)
        share_ref[unit, 1] = block_map[0]
        share_ref[unit, 2] = block_map[1]
        share_ref[unit, 3] = unit_ref[unit, VALUE_ROW:VALUE_ROW + BLOCK]


def attend_kernel(axes, before, units, *refs):
    core = lax.rem(lax.axis_index(axes[1]), 2)
    for parity in range(2):
        pl.when(core == parity)(functools.partial(attend, before, units, parity, *refs))


def attend(before, units, parity, away_ref, start_ref, inner_ref, *refs):
    count = 2 + 2 * (before > 0)
    tails, moving = refs[count + 1:]
    out_ref = refs[count]
    pairs = before + units
    sides = [(refs[2 * group + parity], refs[2 * group + 1 - parity]) for group in range(count // 2)]

    def fixed(odd, pair, part):
        if pair < before:
            return sides[1][odd][pair, part]
        return sides[0][odd][pair - before, part]

    def listed(odd, pair, part):
        if not before:
            return sides[0][odd][pair, part]
        return jnp.where(
            pair < before,
            sides[1][odd][jnp.minimum(pair, before - 1), part],
            sides[0][odd][jnp.maximum(pair - before, 0), part],
        )

    pair_maps = []
    for pair in range(pairs - 1):
        both = nn(
            jnp.concatenate([fixed(0, pair, 0), fixed(0, pair, 1), fixed(0, pair, 2)], 0),
            fixed(1, pair, 1),
        )
        tails[pair] = both[:BLOCK].astype(BF16)
        low = both[2 * BLOCK:] + nn(fixed(0, pair, 1), fixed(1, pair, 2))
        pair_maps.append(split(both[BLOCK:2 * BLOCK] + low))

    current = []
    for unit in range(units):
        front = (start_ref[unit, 0], start_ref[unit, 1])
        moving[unit, 0] = front[0]
        if parity:
            pair = before + unit
            front = split(triple(nt, front, (fixed(0, pair, 1), fixed(0, pair, 2))))
        moving[unit, 1] = front[0]
        current.append(front)
    for step in range(2, LOOK + 1):
        for unit in range(units):
            pair = before + unit - step
            if pair >= 0:
                current[unit] = split(triple(nt, current[unit], pair_maps[pair + 1]))
                moving[unit, step] = current[unit][0]

    rows, columns = square_iotas()
    scale = HEAD_DIM ** (-0.5)
    for unit in range(units):
        block = 2 * (before + unit) + parity
        score_list = [jnp.where(rows >= columns, inner_ref[unit] * scale, -1e30)]
        value_list = [fixed(parity, before + unit, 3)]
        for entry in range(1, TOPK):
            away = away_ref[unit, entry]
            new = away > 0
            for other in range(1, entry):
                new = new & (away_ref[unit, other] != away)
            source = jnp.clip(block - away, 0, 2 * pairs - 1)
            pair, odd = source // 2, lax.rem(source, 2) == 1
            step = jnp.clip(before + unit - pair, 0, LOOK)
            key = jnp.where(odd, listed(1, pair, 0), tails[pair])
            if parity:
                key = jnp.where(step == 0, fixed(0, before + unit, 0), key)
            score = nt(moving[unit, step], key) * scale
            score_list.append(jnp.where(new, score, -1e30))
            value_list.append(jnp.where(odd, listed(1, pair, 3), listed(0, pair, 3)))
        scores = jnp.concatenate(score_list, 1)
        expos = jnp.exp(scores - jnp.max(scores, 1, keepdims=True))
        weights = (expos / jnp.sum(expos, 1, keepdims=True)).astype(BF16)
        out_ref[unit] = nn(weights, jnp.concatenate(value_list, 0)).astype(BF16)


def project_kernel(axes, offset, planes, attended_ref, own_ref, other_ref, out_ref, own, other,
                   sems):
    index = lax.axis_index(axes[1])
    core = lax.rem(index, 2)
    plane = lax.rem(index // 2 + offset, planes)
    width = out_ref.shape[1]
    columns = pl.ds(pl.multiple_of(plane * width, width), width)
    copies = fetched(
        [own_ref.at[:, columns], other_ref.at[:, columns]], [own, other], sems
    )
    heads = attended_ref.shape[0] // 2

    def half(which):
        return jnp.concatenate([attended_ref[which * heads + head] for head in range(heads)], 1)

    copies[0].wait()
    total = nn(half(core), own[...])
    copies[1].wait()
    total = total + nn(half(1 - core), other[...])
    out_ref[...] = total.astype(out_ref.dtype)


def call(kernel, outs, specs, flops, scratch=(), places=None, space=32):
    if places is None:
        places = [VMEM] * len(outs) if isinstance(outs, list) else VMEM
    return pl.pallas_call(
        kernel,
        out_shape=outs,
        in_specs=specs,
        out_specs=places,
        scratch_shapes=list(scratch),
        compiler_params=pltpu.CompilerParams(vmem_limit_bytes=space * 2 ** 20),
        cost_estimate=pl.CostEstimate(flops=flops, bytes_accessed=2 ** 21, transcendentals=0),
    )


def body(ctx_size, head_size, queries, keys, values, directions, rates, selected, out_weight):
    heads = queries.shape[1] // HEAD_DIM
    blocks = queries.shape[0] // BLOCK
    group = blocks * heads
    planes = head_size // blocks
    groups = ctx_size // group
    axes = ("ctx", "head")
    core = lax.rem(lax.axis_index("head"), blocks)
    partners = [(g, g + 1 - 2 * (g % 2)) for g in range(head_size)]
    cubes = 2 * BLOCK ** 3

    def exchange(value):
        members = None
        if groups > 1:
            members = [[a * group + b for b in range(group)] for a in range(groups)]
        return lax.all_to_all(value, "ctx", 0, 0, axis_index_groups=members, tiled=True)

    def partner(value):
        return lax.ppermute(value, "head", partners)

    def array(shape, kind=BF16):
        return jax.ShapeDtypeStruct(shape, kind)

    tile = (BLOCK, HEAD_DIM)
    whole_shape = array((group, UNIT_ROWS, HEAD_DIM))
    half_shape = array((heads, UNIT_ROWS, HEAD_DIM))
    keep, send = call(
        functools.partial(pack_kernel, axes),
        [half_shape] * 2,
        [ANY] * 4 + [VMEM, SMEM],
        cubes,
        [
            pltpu.VMEM((2, heads, UNIT_ROWS, HEAD_DIM), BF16),
            pltpu.SemaphoreType.DMA((group, 4)),
            pltpu.SemaphoreType.DMA((group,)),
        ],
        [ANY] * 2,
        56,
    )(directions, keys, queries, values, rates, selected)
    whole = call(
        functools.partial(place_kernel, axes),
        array((group, UNIT_ROWS, HEAD_DIM)),
        [VMEM] * 2,
        cubes,
        [pltpu.SemaphoreType.DMA((2, heads))],
        ANY,
    )(keep, partner(send))
    unit_arrays = exchange(whole)
    weight_other = partner(out_weight)

    start, inner, share, away = call(
        terms_kernel,
        [
            array((group, 2, *tile)),
            array((group, BLOCK, BLOCK), F32),
            array((group, 4, *tile)),
            array((group, HEAD_DIM), jnp.int32),
        ],
        [VMEM],
        400 * cubes,
    )(unit_arrays)
    shares = [share, partner(share)]
    before = 0
    if groups > 1:
        before = group
        onward = [(i, i + group) for i in range(ctx_size - group)]
        shares += [lax.ppermute(part, "ctx", onward) for part in shares]
    pairs = before + group
    attended = call(
        functools.partial(attend_kernel, axes, before, group),
        array((group, *tile)),
        [SMEM] + [VMEM] * (2 + len(shares)),
        400 * cubes,
        [
            pltpu.VMEM((pairs, *tile), BF16),
            pltpu.VMEM((group, LOOK + 1, *tile), BF16),
        ],
    )(away, start, inner, *shares)

    local = exchange(attended)
    width = out_weight.shape[1] // planes

    def projected(offset, kind):
        return call(
            functools.partial(project_kernel, axes, offset, planes),
            array((BLOCK, width), kind),
            [VMEM, ANY, ANY],
            64 * cubes,
            [
                pltpu.VMEM((out_weight.shape[0], width), BF16),
                pltpu.VMEM((out_weight.shape[0], width), BF16),
                pltpu.SemaphoreType.DMA((2,)),
            ],
        )(local, out_weight, weight_other)

    arrived = []
    for offset in range(1, planes):
        pairs_of = [(g, (g + blocks * offset) % head_size) for g in range(head_size)]
        arrived.append(lax.ppermute(projected(offset, BF16), "head", pairs_of))
    total = projected(0, F32)
    for part in arrived:
        total = total + part.astype(F32)
    total = total.astype(BF16)
    half = width // blocks
    mine = lax.dynamic_slice_in_dim(total, core * half, half, 1)
    theirs = partner(lax.dynamic_slice_in_dim(total, (1 - core) * half, half, 1))
    return jnp.where(
        core == 0,
        jnp.concatenate([mine, theirs], 0),
        jnp.concatenate([theirs, mine], 0),
    )


def solution(mesh):
    in_specs = (
        P("ctx", "head"),
        P("ctx", "head"),
        P("ctx", "head"),
        P("ctx", "head"),
        P("head", "ctx"),
        P("ctx", None),
        P("head", None),
    )
    out_specs = P("ctx", "head")
    return jax.shard_map(
        functools.partial(body, mesh.shape["ctx"], mesh.shape["head"]),
        mesh=mesh,
        in_specs=in_specs,
        out_specs=out_specs,
        check_vma=False,
    )
```

```python
import functools

import jax
import jax.numpy as jnp
from jax import lax
from jax.experimental import pallas as pl
from jax.experimental.pallas import tpu as pltpu
from jax.sharding import PartitionSpec as P

HEAD_DIM = 128
BLOCK = 128
LOOK = 7
TOPK = 4
BASE = 16
EXTRA = 16
TERMS = 3
BF16 = jnp.bfloat16
F32 = jnp.float32
VMEM = pl.BlockSpec(memory_space=pltpu.VMEM)
SMEM = pl.BlockSpec(memory_space=pltpu.SMEM)
ANY = pl.BlockSpec(memory_space=pl.ANY)


def dot(left, right, left_dim, right_dim):
    return lax.dot_general(
        left, right, (((left_dim,), (right_dim,)), ((), ())), preferred_element_type=F32
    )


def nn(left, right):
    return dot(left, right, 1, 0)


def nt(left, right):
    return dot(left, right, 1, 1)


def tn(left, right):
    return dot(left, right, 0, 0)


def split(value):
    high = value.astype(BF16)
    return high, (value - high.astype(F32)).astype(BF16)


def triple(product, left, right):
    rows = left[0].shape[0]
    first = product(jnp.concatenate(left, 0), right[0])
    return first[:rows] + (first[rows:] + product(left[0], right[1]))


def square_iotas():
    rows = lax.broadcasted_iota(jnp.int32, (BLOCK, BLOCK), 0)
    columns = lax.broadcasted_iota(jnp.int32, (BLOCK, BLOCK), 1)
    return rows, columns


def pack_kernel(axes, d_ref, k_ref, q_ref, v_ref, rates_ref, selected_ref, out_ref, parts_ref,
                sems, out_sems):
    tokens = d_ref.shape[0]
    heads = d_ref.shape[1] // HEAD_DIM
    blocks = tokens // BLOCK
    first_block = lax.axis_index(axes[0]) * blocks
    copies = []
    for head in range(heads):
        columns = pl.ds(head * HEAD_DIM, HEAD_DIM)
        for kind, source in enumerate((d_ref, k_ref, q_ref, v_ref)):
            copies.append(
                pltpu.make_async_copy(
                    source.at[:, columns],
                    parts_ref.at[head, pl.ds(kind * tokens, tokens)],
                    sems.at[head, kind],
                )
            )
            copies[-1].start()
    row = lax.broadcasted_iota(jnp.int32, (EXTRA, HEAD_DIM), 0)
    lane = lax.broadcasted_iota(jnp.int32, (EXTRA, HEAD_DIM), 1)
    away = jnp.zeros((EXTRA, HEAD_DIM), jnp.int32)
    for block in range(blocks):
        for entry in range(TOPK):
            distance = first_block + block - selected_ref[block, entry]
            away = jnp.where((row == TERMS * blocks + block) & (lane == entry), distance, away)
    away = away.astype(F32)
    terms = []
    rest = rates_ref[...]
    for _ in range(TERMS):
        terms.append(rest.astype(BF16).astype(F32))
        rest = rest - terms[-1]
    out_copies = []
    for head in range(heads):
        extra = away
        for block in range(blocks):
            for index, term in enumerate(terms):
                piece = term[head:head + 1, block * BLOCK:(block + 1) * BLOCK]
                extra = jnp.where(row == TERMS * block + index, piece, extra)
        parts_ref[head, 4 * tokens:] = extra.astype(BF16)
        for copy in copies[4 * head:4 * head + 4]:
            copy.wait()
        out_copies.append(
            pltpu.make_async_copy(parts_ref.at[head], out_ref.at[head], out_sems.at[head])
        )
        out_copies[-1].start()
    for copy in out_copies:
        copy.wait()


def rows_of(ref, blocks, unit, kind):
    start = (kind * blocks + unit % blocks) * BLOCK
    return ref[unit // blocks, start:start + BLOCK]


def base_inverse(strict):
    count = BLOCK // BASE
    moved = [
        pltpu.roll(strict[b * BASE:(b + 1) * BASE], (BLOCK - b * BASE) % BLOCK, 1)
        if b else strict[:BASE]
        for b in range(count)
    ]
    lanes = lax.broadcasted_iota(jnp.int32, (BASE // 2, BLOCK), 1)
    rows = lax.broadcasted_iota(jnp.int32, (BASE // 2, BLOCK), 0)
    half = BASE // 2
    parts = []
    for b in range(count):
        upper = (lanes == rows + b * BASE).astype(F32)
        lower = (lanes == rows + b * BASE + half).astype(F32)
        for step in range(BASE - 1):
            if step < half:
                source = upper[step:step + 1]
                if step < half - 1:
                    upper = upper - moved[b][:half, step:step + 1] * source
            else:
                source = lower[step - half:step - half + 1]
            lower = lower - moved[b][half:, step:step + 1] * source
        parts += [upper, lower]
    return jnp.concatenate(parts, 0)


def halves(value, size):
    parts = value.reshape(BLOCK // (2 * size), 2, size, BLOCK)
    return parts[:, 0].reshape(BLOCK // 2, BLOCK), parts[:, 1].reshape(BLOCK // 2, BLOCK)


def joined(first, second, size):
    shape = (BLOCK // (2 * size), 1, size, BLOCK)
    return jnp.concatenate([first.reshape(shape), second.reshape(shape)], 1).reshape(BLOCK, BLOCK)


def keys_kernel(blocks, part_ref, end_ref, tail_ref, far_ref, even_ref, pair_ref, group_ref,
                mixed_ref, away_ref):
    units = part_ref.shape[0] * blocks
    rows, columns = square_iotas()
    diagonal = rows == columns
    identity = diagonal.astype(F32)
    strict, inverse, scales = [], [], []
    for unit in range(units):
        direction = rows_of(part_ref, blocks, unit, 0)
        extra = part_ref[unit // blocks, 4 * blocks * BLOCK:].astype(F32)
        first = TERMS * (unit % blocks)
        rate = extra[first:first + 1] + extra[first + 1:first + 2] + extra[first + 2:first + 3]
        listed = TERMS * blocks + unit % blocks
        away_ref[unit:unit + 1] = extra[listed:listed + 1].astype(jnp.int32)
        gram = nt(direction, direction)
        squares = jnp.sum(jnp.where(diagonal, gram, 0.0), 0, keepdims=True)
        scale = lax.rsqrt(squares + 1e-06)
        scaled_rate = rate * scale
        scale_column = jnp.sum(jnp.where(diagonal, scale, 0.0), 1, keepdims=True)
        rate_column = jnp.sum(jnp.where(diagonal, scaled_rate, 0.0), 1, keepdims=True)
        strict.append(jnp.where(rows > columns, rate_column * gram * scale, 0.0))
        scales.append((scale_column, scaled_rate))
    for unit in range(units):
        inverse.append(base_inverse(strict[unit]))
    size = BASE
    while size < BLOCK:
        row = lax.broadcasted_iota(jnp.int32, (BLOCK // 2, BLOCK), 0)
        column = lax.broadcasted_iota(jnp.int32, (BLOCK // 2, BLOCK), 1)
        inside = (row // size == column // (2 * size)) & (lax.rem(column, 2 * size) < size)
        below = []
        for unit in range(units):
            corner = jnp.where(inside, halves(strict[unit], size)[1], 0.0)
            below.append(triple(nn, split(corner), split(inverse[unit])))
        for unit in range(units):
            first, second = halves(inverse[unit], size)
            padded = joined(jnp.zeros_like(below[unit]), below[unit], size)
            second = second - triple(nn, split(second), split(padded))
            inverse[unit] = joined(first, second, size)
        size *= 2
    ends, maps = [], []
    for unit in range(units):
        direction = rows_of(part_ref, blocks, unit, 0)
        key = rows_of(part_ref, blocks, unit, 1)
        key_proj = jnp.where(rows > columns, nt(direction, key), 0.0).astype(BF16)
        mixing = split(scales[unit][0] * inverse[unit] * scales[unit][1])
        mixed = nn(jnp.concatenate(mixing, 0), jnp.concatenate([direction, key_proj], 1))
        mixed = split(mixed[:BLOCK] + mixed[BLOCK:])
        mixed_ref[unit] = mixed[0]
        behind = tn(jnp.concatenate([mixed[0], mixed[1][:, :BLOCK]], 1), direction)
        ends.append(key.astype(F32) - behind[BLOCK:2 * BLOCK])
        maps.append(split(identity - (behind[:BLOCK] + behind[2 * BLOCK:])))
        end_ref[unit] = ends[unit].astype(BF16)
    pair_keys, pair_maps = [], []
    for pair in range(units // 2):
        even, odd = 2 * pair, 2 * pair + 1
        even_ref[pair, 0] = maps[even][0]
        even_ref[pair, 1] = maps[even][1]
        end = split(ends[even])
        left = tuple(jnp.concatenate([end[part], maps[even][part]], 0) for part in range(2))
        both = triple(nn, left, maps[odd])
        tail_ref[even] = both[:BLOCK].astype(BF16)
        tail_ref[odd] = ends[odd].astype(BF16)
        pair_keys.append(jnp.concatenate([both[:BLOCK], ends[odd]], 0))
        pair_maps.append(split(both[BLOCK:]))
        pair_ref[pair, 0] = pair_maps[pair][0]
        pair_ref[pair, 1] = pair_maps[pair][1]
    onward = None
    for pair in reversed(range(units // 2)):
        far = pair_keys[pair]
        if onward is None:
            onward = pair_maps[pair]
        else:
            far = triple(nn, split(far), onward)
            onward = split(triple(nn, pair_maps[pair], onward))
        far_ref[2 * pair] = far[:BLOCK].astype(BF16)
        far_ref[2 * pair + 1] = far[BLOCK:].astype(BF16)
    group_ref[0] = onward[0]
    group_ref[1] = onward[1]


def queries_kernel(blocks, part_ref, mixed_ref, even_ref, pair_ref, *refs):
    inner_ref, moving_ref = refs[-2:]
    units = part_ref.shape[0] * blocks
    rows, columns = square_iotas()
    current = []
    for unit in range(units):
        direction = rows_of(part_ref, blocks, unit, 0)
        key = rows_of(part_ref, blocks, unit, 1)
        query = rows_of(part_ref, blocks, unit, 2)
        query_proj = split(jnp.where(rows >= columns, nt(query, direction), 0.0))
        ahead = nn(jnp.concatenate(query_proj, 0), mixed_ref[unit])
        ahead = ahead[:BLOCK] + ahead[BLOCK:]
        inner_ref[unit] = nt(query, key) - ahead[:, HEAD_DIM:]
        start = split(query.astype(F32) - ahead[:, :HEAD_DIM])
        moving_ref[unit, 0] = start[0]
        if unit % 2:
            pair = unit // 2
            start = split(triple(nt, start, (even_ref[pair, 0], even_ref[pair, 1])))
        moving_ref[unit, 1] = start[0]
        current.append(start)
    pairs = units // 2
    current = [
        tuple(jnp.concatenate([current[2 * pair][part], current[2 * pair + 1][part]], 0)
              for part in range(2))
        for pair in range(pairs)
    ]
    for step in range(2, pairs + 1):
        for pair in range(step - 1, pairs):
            passed = pair - step + 1
            current[pair] = split(
                triple(nt, current[pair], (pair_ref[passed, 0], pair_ref[passed, 1]))
            )
            moving_ref[2 * pair, step] = current[pair][0][:BLOCK]
            moving_ref[2 * pair + 1, step] = current[pair][0][BLOCK:]


def attend_kernel(before, away_ref, moving_ref, inner_ref, end_ref, tail_ref, *refs):
    values, far_keys = refs[:before + 1], refs[before + 1:2 * before + 1]
    group_maps = refs[2 * before + 1:3 * before]
    out_ref = refs[max(3 * before, 1)]
    units = inner_ref.shape[0]
    rows, columns = square_iotas()
    scale = HEAD_DIM ** (-0.5)
    for unit in range(units):
        pair = unit // 2
        fronts = [moving_ref[unit, pair + 1]]
        for group_map in group_maps:
            passed = nt(fronts[-1], group_map[0]) + nt(fronts[-1], group_map[1])
            fronts.append(passed.astype(BF16))
        score_list = [jnp.where(rows >= columns, inner_ref[unit] * scale, -1e30)]
        value_list = [values[0][unit]]
        for entry in range(1, TOPK):
            away = away_ref[unit, entry]
            new = away > 0
            for other in range(1, entry):
                new = new & (away_ref[unit, other] != away)
            source = unit - away
            inside = jnp.maximum(source, 0)
            step = jnp.maximum(pair - inside // 2, 0)
            query = moving_ref[unit, step]
            key = jnp.where(step == 0, end_ref[inside], tail_ref[inside])
            value = values[0][inside]
            for ahead in range(1, before + 1):
                here = source < (1 - ahead) * units
                place = jnp.clip(source + ahead * units, 0, units - 1)
                query = jnp.where(here, fronts[ahead - 1], query)
                key = jnp.where(here, far_keys[ahead - 1][place], key)
                value = jnp.where(here, values[ahead][place], value)
            score_list.append(jnp.where(new, nt(query, key) * scale, -1e30))
            value_list.append(value)
        scores = jnp.concatenate(score_list, 1)
        expos = jnp.exp(scores - jnp.max(scores, 1, keepdims=True))
        weights = (expos / jnp.sum(expos, 1, keepdims=True)).astype(BF16)
        out_ref[unit] = nn(weights, jnp.concatenate(value_list, 0)).astype(BF16)


def project_kernel(axes, other, blocks, attended_ref, weight_ref, out_ref):
    planes, _, width = out_ref.shape
    cores = weight_ref.shape[1] // (planes * width)
    core = lax.rem(lax.axis_index(axes[1]) + other, cores)
    heads = attended_ref.shape[0] // blocks
    attended = jnp.concatenate(
        [
            jnp.concatenate([attended_ref[head * blocks + block] for head in range(heads)], 1)
            for block in range(blocks)
        ],
        0,
    )
    for plane in range(planes):
        start = pl.multiple_of((plane * cores + core) * width, width)
        total = nn(attended, weight_ref[:, pl.ds(start, width)])
        out_ref[plane] = total.astype(out_ref.dtype)


def call(kernel, outs, specs, flops, scratch=(), places=None, space=32):
    if places is None:
        places = [VMEM] * len(outs) if isinstance(outs, list) else VMEM
    return pl.pallas_call(
        kernel,
        out_shape=outs,
        in_specs=specs,
        out_specs=places,
        scratch_shapes=list(scratch),
        compiler_params=pltpu.CompilerParams(vmem_limit_bytes=space * 2 ** 20),
        cost_estimate=pl.CostEstimate(flops=flops, bytes_accessed=2 ** 21, transcendentals=0),
    )


def body(ctx_size, head_size, queries, keys, values, directions, rates, selected, out_weight):
    tokens = queries.shape[0]
    blocks = tokens // BLOCK
    heads = queries.shape[1] // HEAD_DIM
    units = heads * blocks
    pairs = units // 2
    groups = ctx_size // heads
    before = min(groups - 1, -(-LOOK // heads))
    cores = 2
    planes = head_size // cores
    axes = ("ctx", "head")
    members = [[group * heads + place for place in range(heads)] for group in range(groups)]
    partners = [(g, g + 1 - 2 * (g % cores)) for g in range(head_size)]
    cubes = 2 * BLOCK ** 3
    tile = (BLOCK, HEAD_DIM)

    def exchange(value):
        return lax.all_to_all(value, "ctx", 0, 0, axis_index_groups=members, tiled=True)

    def onward(value, by):
        shift = by * heads
        return lax.ppermute(value, "ctx", [(i, i + shift) for i in range(ctx_size - shift)])

    def array(shape, kind=BF16):
        return jax.ShapeDtypeStruct(shape, kind)

    part_shape = (heads, 4 * tokens + EXTRA, HEAD_DIM)
    packed = call(
        functools.partial(pack_kernel, axes),
        array(part_shape),
        [ANY] * 4 + [VMEM, SMEM],
        cubes,
        [
            pltpu.VMEM(part_shape, BF16),
            pltpu.SemaphoreType.DMA((heads, 4)),
            pltpu.SemaphoreType.DMA((heads,)),
        ],
        ANY,
        56,
    )(directions, keys, queries, values, rates, selected)
    parts = exchange(packed)
    own_values = parts[:, 3 * tokens:4 * tokens].reshape(units, *tile)
    value_parts = [own_values] + [onward(own_values, by) for by in range(1, before + 1)]

    end, tail, far, even, pair_map, group_map, mixed, away = call(
        functools.partial(keys_kernel, blocks),
        [
            array((units, *tile)),
            array((units, *tile)),
            array((units, *tile)),
            array((pairs, 2, *tile)),
            array((pairs, 2, *tile)),
            array((2, *tile)),
            array((units, BLOCK, 2 * BLOCK)),
            array((units, HEAD_DIM), jnp.int32),
        ],
        [VMEM],
        400 * cubes,
    )(parts)
    far_parts = [onward(far, by) for by in range(1, before + 1)]
    map_parts = [onward(group_map, by) for by in range(1, before)]
    inner, moving = call(
        functools.partial(queries_kernel, blocks),
        [array((units, BLOCK, BLOCK), F32), array((units, pairs + 1, *tile))],
        [VMEM] * 4 + [ANY] * before,
        200 * cubes,
    )(parts, mixed, even, pair_map, *value_parts[1:])
    attended = call(
        functools.partial(attend_kernel, before),
        array((units, *tile)),
        [SMEM] + [VMEM] * (4 + max(3 * before, 1)),
        200 * cubes,
    )(away, moving, inner, end, tail, *value_parts, *far_parts, *map_parts)

    local = exchange(attended)
    width = out_weight.shape[1] // head_size

    def projected(other, kind):
        return call(
            functools.partial(project_kernel, axes, other, blocks),
            array((planes, tokens, width), kind),
            [VMEM] * 2,
            128 * cubes,
        )(local, out_weight)

    arrived = lax.ppermute(projected(1, BF16), "head", partners)
    total = projected(0, F32) + arrived.astype(F32)
    plane = lax.axis_index("head") // cores
    result = lax.dynamic_index_in_dim(total, plane, 0, False)
    for offset in range(1, planes):
        part = lax.dynamic_index_in_dim(total, lax.rem(plane + offset, planes), 0, False)
        turned = [(g, (g + cores * offset) % head_size) for g in range(head_size)]
        result = result + lax.ppermute(part.astype(BF16), "head", turned).astype(F32)
    return result.astype(BF16)


def solution(mesh):
    in_specs = (
        P("ctx", "head"),
        P("ctx", "head"),
        P("ctx", "head"),
        P("ctx", "head"),
        P("head", "ctx"),
        P("ctx", None),
        P("head", None),
    )
    out_specs = P("ctx", "head")
    return jax.shard_map(
        functools.partial(body, mesh.shape["ctx"], mesh.shape["head"]),
        mesh=mesh,
        in_specs=in_specs,
        out_specs=out_specs,
        check_vma=False,
    )
```

```python
import functools

import jax
import jax.numpy as jnp
from jax import lax
from jax.experimental import pallas as pl
from jax.experimental.pallas import tpu as pltpu
from jax.sharding import PartitionSpec as P

HEAD_DIM = 128
BLOCK = 128
LOOK = 7
TOPK = 4
BASE = 16
EXTRA = 16
TERMS = 3
BF16 = jnp.bfloat16
F32 = jnp.float32
VMEM = pl.BlockSpec(memory_space=pltpu.VMEM)
SMEM = pl.BlockSpec(memory_space=pltpu.SMEM)
ANY = pl.BlockSpec(memory_space=pl.ANY)


def dot(left, right, left_dim, right_dim):
    return lax.dot_general(
        left, right, (((left_dim,), (right_dim,)), ((), ())), preferred_element_type=F32
    )


def nn(left, right):
    return dot(left, right, 1, 0)


def nt(left, right):
    return dot(left, right, 1, 1)


def tn(left, right):
    return dot(left, right, 0, 0)


def split(value):
    high = value.astype(BF16)
    return high, (value - high.astype(F32)).astype(BF16)


def triple(product, left, right):
    rows = left[0].shape[0]
    first = product(jnp.concatenate(left, 0), right[0])
    return first[:rows] + (first[rows:] + product(left[0], right[1]))


def square_iotas():
    rows = lax.broadcasted_iota(jnp.int32, (BLOCK, BLOCK), 0)
    columns = lax.broadcasted_iota(jnp.int32, (BLOCK, BLOCK), 1)
    return rows, columns


def pack_kernel(axes, d_ref, k_ref, q_ref, v_ref, rates_ref, selected_ref, out_ref, parts_ref,
                sems, out_sems):
    tokens = d_ref.shape[0]
    heads = d_ref.shape[1] // HEAD_DIM
    blocks = tokens // BLOCK
    first_block = lax.axis_index(axes[0]) * blocks
    copies = []
    for head in range(heads):
        columns = pl.ds(head * HEAD_DIM, HEAD_DIM)
        for kind, source in enumerate((d_ref, k_ref, q_ref, v_ref)):
            copies.append(
                pltpu.make_async_copy(
                    source.at[:, columns],
                    parts_ref.at[head, pl.ds(kind * tokens, tokens)],
                    sems.at[head, kind],
                )
            )
            copies[-1].start()
    row = lax.broadcasted_iota(jnp.int32, (EXTRA, HEAD_DIM), 0)
    lane = lax.broadcasted_iota(jnp.int32, (EXTRA, HEAD_DIM), 1)
    away = jnp.zeros((EXTRA, HEAD_DIM), jnp.int32)
    for block in range(blocks):
        for entry in range(TOPK):
            distance = first_block + block - selected_ref[block, entry]
            away = jnp.where((row == TERMS * blocks + block) & (lane == entry), distance, away)
    away = away.astype(F32)
    terms = []
    rest = rates_ref[...]
    for _ in range(TERMS):
        terms.append(rest.astype(BF16).astype(F32))
        rest = rest - terms[-1]
    out_copies = []
    for head in range(heads):
        extra = away
        for block in range(blocks):
            for index, term in enumerate(terms):
                piece = term[head:head + 1, block * BLOCK:(block + 1) * BLOCK]
                extra = jnp.where(row == TERMS * block + index, piece, extra)
        parts_ref[head, 4 * tokens:] = extra.astype(BF16)
        for copy in copies[4 * head:4 * head + 4]:
            copy.wait()
        out_copies.append(
            pltpu.make_async_copy(parts_ref.at[head], out_ref.at[head], out_sems.at[head])
        )
        out_copies[-1].start()
    for copy in out_copies:
        copy.wait()


def rows_of(ref, blocks, unit, kind):
    start = (kind * blocks + unit % blocks) * BLOCK
    return ref[unit // blocks, start:start + BLOCK]


def base_inverse(strict):
    count = BLOCK // BASE
    moved = [
        pltpu.roll(strict[b * BASE:(b + 1) * BASE], (BLOCK - b * BASE) % BLOCK, 1)
        if b else strict[:BASE]
        for b in range(count)
    ]
    lanes = lax.broadcasted_iota(jnp.int32, (BASE // 2, BLOCK), 1)
    rows = lax.broadcasted_iota(jnp.int32, (BASE // 2, BLOCK), 0)
    half = BASE // 2
    parts = []
    for b in range(count):
        upper = (lanes == rows + b * BASE).astype(F32)
        lower = (lanes == rows + b * BASE + half).astype(F32)
        for step in range(BASE - 1):
            if step < half:
                source = upper[step:step + 1]
                if step < half - 1:
                    upper = upper - moved[b][:half, step:step + 1] * source
            else:
                source = lower[step - half:step - half + 1]
            lower = lower - moved[b][half:, step:step + 1] * source
        parts += [upper, lower]
    return jnp.concatenate(parts, 0)


def halves(value, size):
    parts = value.reshape(BLOCK // (2 * size), 2, size, BLOCK)
    return parts[:, 0].reshape(BLOCK // 2, BLOCK), parts[:, 1].reshape(BLOCK // 2, BLOCK)


def joined(first, second, size):
    shape = (BLOCK // (2 * size), 1, size, BLOCK)
    return jnp.concatenate([first.reshape(shape), second.reshape(shape)], 1).reshape(BLOCK, BLOCK)


def interleaved(steps, lag):
    running = list(steps)
    tick = 0
    while any(step is not None for step in running):
        for index, step in enumerate(running):
            if step is not None and tick >= index * lag:
                try:
                    next(step)
                except StopIteration:
                    running[index] = None
        tick += 1


def keys_kernel(blocks, part_ref, end_ref, tail_ref, far_ref, even_ref, pair_ref, group_ref,
                mixed_ref, away_ref):
    units = part_ref.shape[0] * blocks
    rows, columns = square_iotas()
    diagonal = rows == columns
    identity = diagonal.astype(F32)
    row = lax.broadcasted_iota(jnp.int32, (BLOCK // 2, BLOCK), 0)
    column = lax.broadcasted_iota(jnp.int32, (BLOCK // 2, BLOCK), 1)
    ends, maps = [None] * units, [None] * units

    def terms(unit):
        direction = rows_of(part_ref, blocks, unit, 0)
        key = rows_of(part_ref, blocks, unit, 1)
        extra = part_ref[unit // blocks, 4 * blocks * BLOCK:].astype(F32)
        first = TERMS * (unit % blocks)
        rate = extra[first:first + 1] + extra[first + 1:first + 2] + extra[first + 2:first + 3]
        listed = TERMS * blocks + unit % blocks
        away_ref[unit:unit + 1] = extra[listed:listed + 1].astype(jnp.int32)
        gram = nt(direction, direction)
        key_proj = jnp.where(rows > columns, nt(direction, key), 0.0).astype(BF16)
        squares = jnp.sum(jnp.where(diagonal, gram, 0.0), 0, keepdims=True)
        scale = lax.rsqrt(squares + 1e-06)
        scaled_rate = rate * scale
        scale_column = jnp.sum(jnp.where(diagonal, scale, 0.0), 1, keepdims=True)
        rate_column = jnp.sum(jnp.where(diagonal, scaled_rate, 0.0), 1, keepdims=True)
        strict = jnp.where(rows > columns, rate_column * gram * scale, 0.0)
        yield
        inverse = base_inverse(strict)
        yield
        size = BASE
        while size < BLOCK:
            inside = (row // size == column // (2 * size)) & (lax.rem(column, 2 * size) < size)
            corner = jnp.where(inside, halves(strict, size)[1], 0.0)
            below = triple(nn, split(corner), split(inverse))
            yield
            first_half, second = halves(inverse, size)
            padded = joined(jnp.zeros_like(below), below, size)
            second = second - triple(nn, split(second), split(padded))
            inverse = joined(first_half, second, size)
            size *= 2
            yield
        mixing = split(scale_column * inverse * scaled_rate)
        mixed = nn(jnp.concatenate(mixing, 0), jnp.concatenate([direction, key_proj], 1))
        mixed = split(mixed[:BLOCK] + mixed[BLOCK:])
        mixed_ref[unit] = mixed[0]
        yield
        behind = tn(jnp.concatenate([mixed[0], mixed[1][:, :BLOCK]], 1), direction)
        ends[unit] = key.astype(F32) - behind[BLOCK:2 * BLOCK]
        maps[unit] = split(identity - (behind[:BLOCK] + behind[2 * BLOCK:]))
        end_ref[unit] = ends[unit].astype(BF16)

    interleaved([terms(unit) for unit in range(units)], 1)
    pair_keys, pair_maps = [], []
    for pair in range(units // 2):
        even, odd = 2 * pair, 2 * pair + 1
        even_ref[pair, 0] = maps[even][0]
        even_ref[pair, 1] = maps[even][1]
        end = split(ends[even])
        left = tuple(jnp.concatenate([end[part], maps[even][part]], 0) for part in range(2))
        both = triple(nn, left, maps[odd])
        tail_ref[even] = both[:BLOCK].astype(BF16)
        tail_ref[odd] = ends[odd].astype(BF16)
        pair_keys.append(jnp.concatenate([both[:BLOCK], ends[odd]], 0))
        pair_maps.append(split(both[BLOCK:]))
        pair_ref[pair, 0] = pair_maps[pair][0]
        pair_ref[pair, 1] = pair_maps[pair][1]
    onward = None
    for pair in reversed(range(units // 2)):
        far = pair_keys[pair]
        if onward is None:
            onward = pair_maps[pair]
        else:
            far = triple(nn, split(far), onward)
            onward = split(triple(nn, pair_maps[pair], onward))
        far_ref[2 * pair] = far[:BLOCK].astype(BF16)
        far_ref[2 * pair + 1] = far[BLOCK:].astype(BF16)
    group_ref[0] = onward[0]
    group_ref[1] = onward[1]


def queries_kernel(blocks, part_ref, mixed_ref, even_ref, pair_ref, *refs):
    inner_ref, moving_ref, late_ref = refs[-3:]
    units = part_ref.shape[0] * blocks
    for unit in range(units // 2, units):
        late_ref[unit - units // 2] = rows_of(part_ref, blocks, unit, 3)
    rows, columns = square_iotas()
    current = []
    for unit in range(units):
        direction = rows_of(part_ref, blocks, unit, 0)
        key = rows_of(part_ref, blocks, unit, 1)
        query = rows_of(part_ref, blocks, unit, 2)
        query_proj = split(jnp.where(rows >= columns, nt(query, direction), 0.0))
        ahead = nn(jnp.concatenate(query_proj, 0), mixed_ref[unit])
        ahead = ahead[:BLOCK] + ahead[BLOCK:]
        inner_ref[unit] = nt(query, key) - ahead[:, HEAD_DIM:]
        start = split(query.astype(F32) - ahead[:, :HEAD_DIM])
        moving_ref[unit, 0] = start[0]
        if unit % 2:
            pair = unit // 2
            start = split(triple(nt, start, (even_ref[pair, 0], even_ref[pair, 1])))
        moving_ref[unit, 1] = start[0]
        current.append(start)
    pairs = units // 2
    current = [
        tuple(jnp.concatenate([current[2 * pair][part], current[2 * pair + 1][part]], 0)
              for part in range(2))
        for pair in range(pairs)
    ]
    for step in range(2, pairs + 1):
        for pair in range(step - 1, pairs):
            passed = pair - step + 1
            current[pair] = split(
                triple(nt, current[pair], (pair_ref[passed, 0], pair_ref[passed, 1]))
            )
            moving_ref[2 * pair, step] = current[pair][0][:BLOCK]
            moving_ref[2 * pair + 1, step] = current[pair][0][BLOCK:]


def listed_block(away_ref, unit, entry):
    away = away_ref[unit, entry]
    new = away > 0
    for other in range(1, entry):
        new = new & (away_ref[unit, other] != away)
    return unit - away, new


def earlier(source, ahead, units):
    return jnp.clip(source + ahead * units, 0, units - 1), source < (1 - ahead) * units


def weights_kernel(before, away_ref, moving_ref, inner_ref, end_ref, tail_ref, *refs):
    far_keys, group_maps = refs[:before], refs[before:-1]
    weights_ref = refs[-1]
    units = inner_ref.shape[0]
    rows, columns = square_iotas()
    scale = HEAD_DIM ** (-0.5)
    for unit in range(units):
        pair = unit // 2
        fronts = [moving_ref[unit, pair + 1]]
        for group_map in group_maps:
            passed = nt(fronts[-1], group_map[0]) + nt(fronts[-1], group_map[1])
            fronts.append(passed.astype(BF16))
        score_list = [jnp.where(rows >= columns, inner_ref[unit] * scale, -1e30)]
        for entry in range(1, TOPK):
            source, new = listed_block(away_ref, unit, entry)
            inside = jnp.maximum(source, 0)
            step = jnp.maximum(pair - inside // 2, 0)
            query = moving_ref[unit, step]
            key = jnp.where(step == 0, end_ref[inside], tail_ref[inside])
            for ahead in range(1, before + 1):
                place, here = earlier(source, ahead, units)
                query = jnp.where(here, fronts[ahead - 1], query)
                key = jnp.where(here, far_keys[ahead - 1][place], key)
            score_list.append(jnp.where(new, nt(query, key) * scale, -1e30))
        scores = jnp.concatenate(score_list, 1)
        expos = jnp.exp(scores - jnp.max(scores, 1, keepdims=True))
        weights_ref[unit] = (expos / jnp.sum(expos, 1, keepdims=True)).astype(BF16)


def blend_kernel(before, blocks, away_ref, weights_ref, part_ref, *refs):
    early, late, out_ref = refs[:before], refs[before:2 * before], refs[2 * before]
    units = weights_ref.shape[0]
    half = units // 2
    for unit in range(units):
        value_list = [rows_of(part_ref, blocks, unit, 3)]
        for entry in range(1, TOPK):
            source, _ = listed_block(away_ref, unit, entry)
            inside = jnp.maximum(source, 0)
            start = pl.multiple_of((3 * blocks + lax.rem(inside, blocks)) * BLOCK, BLOCK)
            value = part_ref[inside // blocks, pl.ds(start, BLOCK)]
            for ahead in range(1, before + 1):
                place, here = earlier(source, ahead, units)
                value = jnp.where(here, early[ahead - 1][jnp.minimum(place, half - 1)], value)
                value = jnp.where(
                    here & (place >= half), late[ahead - 1][jnp.maximum(place - half, 0)], value
                )
            value_list.append(value)
        blended = nn(weights_ref[unit], jnp.concatenate(value_list, 0)).astype(BF16)
        for plane in range(out_ref.shape[1]):
            out_ref[unit // blocks, plane, unit % blocks] = blended


def project_kernel(axes, other, cores, attended_ref, own_ref, *refs):
    other_refs, out_ref = refs[:-1], refs[-1]
    heads, planes, blocks = attended_ref.shape[:3]
    index = lax.axis_index(axes[1])
    core, plane = lax.rem(index + other, cores), index // cores
    width = out_ref.shape[1]
    total = None
    for offset in range(planes):
        source = lax.rem(plane + offset, planes)
        attended = jnp.concatenate(
            [
                jnp.concatenate(
                    [attended_ref[head, source, block] for head in range(heads)], 1
                )
                for block in range(blocks)
            ],
            0,
        )
        if offset:
            start = pl.multiple_of(core * width, width)
            weight = other_refs[offset - 1][:, pl.ds(start, width)]
        else:
            start = pl.multiple_of((plane * cores + core) * width, width)
            weight = own_ref[:, pl.ds(start, width)]
        product = nn(attended, weight)
        total = product if total is None else total + product
    out_ref[...] = total.astype(out_ref.dtype)


def call(kernel, outs, specs, flops, scratch=(), places=None, space=32):
    if places is None:
        places = [VMEM] * len(outs) if isinstance(outs, list) else VMEM
    return pl.pallas_call(
        kernel,
        out_shape=outs,
        in_specs=specs,
        out_specs=places,
        scratch_shapes=list(scratch),
        compiler_params=pltpu.CompilerParams(vmem_limit_bytes=space * 2 ** 20),
        cost_estimate=pl.CostEstimate(flops=flops, bytes_accessed=2 ** 21, transcendentals=0),
    )


def body(ctx_size, head_size, queries, keys, values, directions, rates, selected, out_weight):
    tokens = queries.shape[0]
    blocks = tokens // BLOCK
    heads = queries.shape[1] // HEAD_DIM
    units = heads * blocks
    pairs = units // 2
    groups = ctx_size // heads
    before = min(groups - 1, -(-LOOK // heads))
    cores = 2
    planes = head_size // cores
    axes = ("ctx", "head")
    members = [[group * heads + place for place in range(heads)] for group in range(groups)]
    partners = [(g, g + 1 - 2 * (g % cores)) for g in range(head_size)]
    cubes = 2 * BLOCK ** 3
    tile = (BLOCK, HEAD_DIM)

    def exchange(value):
        return lax.all_to_all(value, "ctx", 0, 0, axis_index_groups=members, tiled=True)

    def onward(value, by):
        shift = by * heads
        return lax.ppermute(value, "ctx", [(i, i + shift) for i in range(ctx_size - shift)])

    def array(shape, kind=BF16):
        return jax.ShapeDtypeStruct(shape, kind)

    part_shape = (heads, 4 * tokens + EXTRA, HEAD_DIM)
    packed = call(
        functools.partial(pack_kernel, axes),
        array(part_shape),
        [ANY] * 4 + [VMEM, SMEM],
        cubes,
        [
            pltpu.VMEM(part_shape, BF16),
            pltpu.SemaphoreType.DMA((heads, 4)),
            pltpu.SemaphoreType.DMA((heads,)),
        ],
        ANY,
        56,
    )(directions, keys, queries, values, rates, selected)
    plane = lax.axis_index("head") // cores
    width = out_weight.shape[1] // planes
    weight_parts = []
    for offset in range(1, planes):
        start = lax.rem(plane + planes - offset, planes) * width
        turned = [(g, (g + head_size - cores * offset) % head_size) for g in range(head_size)]
        piece = lax.dynamic_slice_in_dim(out_weight, start, width, 1)
        weight_parts.append(lax.ppermute(piece, "head", turned))
    parts = exchange(packed)
    early = parts[:heads // 2, 3 * tokens:4 * tokens].reshape(units // 2, *tile)
    early_parts = [onward(early, by) for by in range(1, before + 1)]

    end, tail, far, even, pair_map, group_map, mixed, away = call(
        functools.partial(keys_kernel, blocks),
        [
            array((units, *tile)),
            array((units, *tile)),
            array((units, *tile)),
            array((pairs, 2, *tile)),
            array((pairs, 2, *tile)),
            array((2, *tile)),
            array((units, BLOCK, 2 * BLOCK)),
            array((units, HEAD_DIM), jnp.int32),
        ],
        [VMEM],
        400 * cubes,
    )(parts)
    far_parts = [onward(far, by) for by in range(1, before + 1)]
    map_parts = [onward(group_map, by) for by in range(1, before)]
    inner, moving, late = call(
        functools.partial(queries_kernel, blocks),
        [
            array((units, BLOCK, BLOCK), F32),
            array((units, pairs + 1, *tile)),
            array((units - units // 2, *tile)),
        ],
        [VMEM] * 4 + [ANY] * (before + len(weight_parts)),
        200 * cubes,
    )(parts, mixed, even, pair_map, *early_parts, *weight_parts)
    late_parts = [onward(late, by) for by in range(1, before + 1)]
    weights = call(
        functools.partial(weights_kernel, before),
        array((units, BLOCK, TOPK * BLOCK)),
        [SMEM] + [VMEM] * (4 + before + len(map_parts)),
        100 * cubes,
    )(away, moving, inner, end, tail, *far_parts, *map_parts)
    attended = call(
        functools.partial(blend_kernel, before, blocks),
        array((heads, planes, blocks, *tile)),
        [SMEM] + [VMEM] * (2 + 2 * before),
        100 * cubes,
    )(away, weights, parts, *early_parts, *late_parts)

    returns = [
        [
            (group * heads + place) * head_size + p * cores + core
            for place in range(heads)
            for p in range(planes)
        ]
        for group in range(groups)
        for core in range(cores)
    ]
    local = lax.all_to_all(
        attended.reshape(heads * planes, blocks, *tile),
        axes, 0, 0, axis_index_groups=returns, tiled=True,
    ).reshape(heads, planes, blocks, *tile)

    def projected(other, kind):
        return call(
            functools.partial(project_kernel, axes, other, cores),
            array((tokens, width // cores), kind),
            [VMEM] * (1 + planes),
            128 * cubes,
        )(local, out_weight, *weight_parts)

    arrived = lax.ppermute(projected(1, BF16), "head", partners)
    return (projected(0, F32) + arrived.astype(F32)).astype(BF16)


def solution(mesh):
    in_specs = (
        P("ctx", "head"),
        P("ctx", "head"),
        P("ctx", "head"),
        P("ctx", "head"),
        P("head", "ctx"),
        P("ctx", None),
        P("head", None),
    )
    out_specs = P("ctx", "head")
    return jax.shard_map(
        functools.partial(body, mesh.shape["ctx"], mesh.shape["head"]),
        mesh=mesh,
        in_specs=in_specs,
        out_specs=out_specs,
        check_vma=False,
    )
```

```python
import functools

import jax
import jax.numpy as jnp
from jax import lax
from jax.experimental import pallas as pl
from jax.experimental.pallas import tpu as pltpu
from jax.sharding import PartitionSpec as P

HEAD_DIM = 128
BLOCK = 128
LOOK = 7
TOPK = 4
BASE = 16
EXTRA = 16
TERMS = 3
BF16 = jnp.bfloat16
F32 = jnp.float32
VMEM = pl.BlockSpec(memory_space=pltpu.VMEM)
SMEM = pl.BlockSpec(memory_space=pltpu.SMEM)
ANY = pl.BlockSpec(memory_space=pl.ANY)


def dot(left, right, left_dim, right_dim):
    return lax.dot_general(
        left, right, (((left_dim,), (right_dim,)), ((), ())), preferred_element_type=F32
    )


def nn(left, right):
    return dot(left, right, 1, 0)


def nt(left, right):
    return dot(left, right, 1, 1)


def tn(left, right):
    return dot(left, right, 0, 0)


def split(value):
    high = value.astype(BF16)
    return high, (value - high.astype(F32)).astype(BF16)


def triple(product, left, right):
    rows = left[0].shape[0]
    first = product(jnp.concatenate(left, 0), right[0])
    return first[:rows] + (first[rows:] + product(left[0], right[1]))


def square_iotas():
    rows = lax.broadcasted_iota(jnp.int32, (BLOCK, BLOCK), 0)
    columns = lax.broadcasted_iota(jnp.int32, (BLOCK, BLOCK), 1)
    return rows, columns


def fetched(sources, targets, sems):
    copies = []
    for index, (source, target) in enumerate(zip(sources, targets)):
        copies.append(pltpu.make_async_copy(source, target, sems.at[index]))
        copies[-1].start()
    return copies


def pack_kernel(axes, d_ref, k_ref, v_ref, rates_hbm, selected_hbm, out_ref, parts_ref,
                rates_ref, selected_ref, sems, few_sems, out_sems):
    tokens = d_ref.shape[0]
    heads = d_ref.shape[1] // HEAD_DIM
    blocks = tokens // BLOCK
    first_block = lax.axis_index(axes[0]) * blocks
    few_copies = fetched([rates_hbm, selected_hbm], [rates_ref, selected_ref], few_sems)
    sources = (d_ref, k_ref, v_ref)
    copies = []
    for head in range(heads):
        columns = pl.ds(head * HEAD_DIM, HEAD_DIM)
        for kind, source in enumerate(sources):
            copies.append(
                pltpu.make_async_copy(
                    source.at[:, columns],
                    parts_ref.at[head, pl.ds(kind * tokens, tokens)],
                    sems.at[head, kind],
                )
            )
            copies[-1].start()
    for copy in few_copies:
        copy.wait()
    row = lax.broadcasted_iota(jnp.int32, (EXTRA, HEAD_DIM), 0)
    lane = lax.broadcasted_iota(jnp.int32, (EXTRA, HEAD_DIM), 1)
    away = jnp.zeros((EXTRA, HEAD_DIM), jnp.int32)
    for block in range(blocks):
        for entry in range(TOPK):
            distance = first_block + block - selected_ref[block, entry]
            away = jnp.where((row == TERMS * blocks + block) & (lane == entry), distance, away)
    away = away.astype(F32)
    terms = []
    rest = rates_ref[...]
    for _ in range(TERMS):
        terms.append(rest.astype(BF16).astype(F32))
        rest = rest - terms[-1]
    out_copies = []
    for head in range(heads):
        extra = away
        for block in range(blocks):
            for index, term in enumerate(terms):
                piece = term[head:head + 1, block * BLOCK:(block + 1) * BLOCK]
                extra = jnp.where(row == TERMS * block + index, piece, extra)
        parts_ref[head, len(sources) * tokens:] = extra.astype(BF16)
        for copy in copies[len(sources) * head:len(sources) * (head + 1)]:
            copy.wait()
        out_copies.append(
            pltpu.make_async_copy(parts_ref.at[head], out_ref.at[head], out_sems.at[head])
        )
        out_copies[-1].start()
    for copy in out_copies:
        copy.wait()


def rows_of(ref, blocks, unit, kind):
    start = (kind * blocks + unit % blocks) * BLOCK
    return ref[unit // blocks, start:start + BLOCK]


def base_inverse(strict):
    count = BLOCK // BASE
    moved = [
        pltpu.roll(strict[b * BASE:(b + 1) * BASE], (BLOCK - b * BASE) % BLOCK, 1)
        if b else strict[:BASE]
        for b in range(count)
    ]
    lanes = lax.broadcasted_iota(jnp.int32, (BASE // 2, BLOCK), 1)
    rows = lax.broadcasted_iota(jnp.int32, (BASE // 2, BLOCK), 0)
    half = BASE // 2
    parts = []
    for b in range(count):
        upper = (lanes == rows + b * BASE).astype(F32)
        lower = (lanes == rows + b * BASE + half).astype(F32)
        for step in range(BASE - 1):
            if step < half:
                source = upper[step:step + 1]
                if step < half - 1:
                    upper = upper - moved[b][:half, step:step + 1] * source
            else:
                source = lower[step - half:step - half + 1]
            lower = lower - moved[b][half:, step:step + 1] * source
        parts += [upper, lower]
    return jnp.concatenate(parts, 0)


def halves(value, size):
    parts = value.reshape(BLOCK // (2 * size), 2, size, BLOCK)
    return parts[:, 0].reshape(BLOCK // 2, BLOCK), parts[:, 1].reshape(BLOCK // 2, BLOCK)


def joined(first, second, size):
    shape = (BLOCK // (2 * size), 1, size, BLOCK)
    return jnp.concatenate([first.reshape(shape), second.reshape(shape)], 1).reshape(BLOCK, BLOCK)


def interleaved(steps, lag):
    running = list(steps)
    tick = 0
    while any(step is not None for step in running):
        for index, step in enumerate(running):
            if step is not None and tick >= index * lag:
                try:
                    next(step)
                except StopIteration:
                    running[index] = None
        tick += 1


def keys_kernel(blocks, part_ref, queries_ref, end_ref, tail_ref, far_ref, even_ref, pair_ref,
                group_ref, mixed_ref, away_ref, out_ref, cut_ref, sems, out_sems):
    heads = part_ref.shape[0]
    units = heads * blocks
    query_copies = fetched(
        [queries_ref.at[:, pl.ds(head * HEAD_DIM, HEAD_DIM)] for head in range(heads)],
        [cut_ref.at[head] for head in range(heads)],
        sems,
    )
    rows, columns = square_iotas()
    diagonal = rows == columns
    identity = diagonal.astype(F32)
    row = lax.broadcasted_iota(jnp.int32, (BLOCK // 2, BLOCK), 0)
    column = lax.broadcasted_iota(jnp.int32, (BLOCK // 2, BLOCK), 1)
    ends, maps = [None] * units, [None] * units

    def terms(unit):
        direction = rows_of(part_ref, blocks, unit, 0)
        key = rows_of(part_ref, blocks, unit, 1)
        extra = part_ref[unit // blocks, 3 * blocks * BLOCK:].astype(F32)
        first = TERMS * (unit % blocks)
        rate = extra[first:first + 1] + extra[first + 1:first + 2] + extra[first + 2:first + 3]
        listed = TERMS * blocks + unit % blocks
        away_ref[unit:unit + 1] = extra[listed:listed + 1].astype(jnp.int32)
        gram = nt(direction, direction)
        key_proj = jnp.where(rows > columns, nt(direction, key), 0.0).astype(BF16)
        squares = jnp.sum(jnp.where(diagonal, gram, 0.0), 0, keepdims=True)
        scale = lax.rsqrt(squares + 1e-06)
        scaled_rate = rate * scale
        scale_column = jnp.sum(jnp.where(diagonal, scale, 0.0), 1, keepdims=True)
        rate_column = jnp.sum(jnp.where(diagonal, scaled_rate, 0.0), 1, keepdims=True)
        strict = jnp.where(rows > columns, rate_column * gram * scale, 0.0)
        yield
        inverse = base_inverse(strict)
        yield
        size = BASE
        while size < BLOCK:
            inside = (row // size == column // (2 * size)) & (lax.rem(column, 2 * size) < size)
            corner = jnp.where(inside, halves(strict, size)[1], 0.0)
            below = triple(nn, split(corner), split(inverse))
            yield
            first_half, second = halves(inverse, size)
            padded = joined(jnp.zeros_like(below), below, size)
            second = second - triple(nn, split(second), split(padded))
            inverse = joined(first_half, second, size)
            size *= 2
            yield
        mixing = split(scale_column * inverse * scaled_rate)
        mixed = nn(jnp.concatenate(mixing, 0), jnp.concatenate([direction, key_proj], 1))
        mixed = split(mixed[:BLOCK] + mixed[BLOCK:])
        mixed_ref[unit] = mixed[0]
        yield
        behind = tn(jnp.concatenate([mixed[0], mixed[1][:, :BLOCK]], 1), direction)
        ends[unit] = key.astype(F32) - behind[BLOCK:2 * BLOCK]
        maps[unit] = split(identity - (behind[:BLOCK] + behind[2 * BLOCK:]))
        end_ref[unit] = ends[unit].astype(BF16)

    interleaved([terms(unit) for unit in range(units)], 1)
    out_copies = []
    for head in range(heads):
        query_copies[head].wait()
        out_copies.append(
            pltpu.make_async_copy(cut_ref.at[head], out_ref.at[head], out_sems.at[head])
        )
        out_copies[-1].start()
    pair_keys, pair_maps = [], []
    for pair in range(units // 2):
        even, odd = 2 * pair, 2 * pair + 1
        even_ref[pair, 0] = maps[even][0]
        even_ref[pair, 1] = maps[even][1]
        end = split(ends[even])
        left = tuple(jnp.concatenate([end[part], maps[even][part]], 0) for part in range(2))
        both = triple(nn, left, maps[odd])
        tail_ref[even] = both[:BLOCK].astype(BF16)
        tail_ref[odd] = ends[odd].astype(BF16)
        pair_keys.append(jnp.concatenate([both[:BLOCK], ends[odd]], 0))
        pair_maps.append(split(both[BLOCK:]))
        pair_ref[pair, 0] = pair_maps[pair][0]
        pair_ref[pair, 1] = pair_maps[pair][1]
    onward = None
    for pair in reversed(range(units // 2)):
        far = pair_keys[pair]
        if onward is None:
            onward = pair_maps[pair]
        else:
            far = triple(nn, split(far), onward)
            onward = split(triple(nn, pair_maps[pair], onward))
        far_ref[2 * pair] = far[:BLOCK].astype(BF16)
        far_ref[2 * pair + 1] = far[BLOCK:].astype(BF16)
    group_ref[0] = onward[0]
    group_ref[1] = onward[1]
    for copy in out_copies:
        copy.wait()


def queries_kernel(blocks, count, part_ref, query_ref, mixed_ref, even_ref, pair_ref, *refs):
    inner_ref, moving_ref = refs[-3 - count:-1 - count]
    units = part_ref.shape[0] * blocks
    copies = fetched(refs[:count], refs[-1 - count:-1], refs[-1])
    rows, columns = square_iotas()
    current = []
    for unit in range(units):
        direction = rows_of(part_ref, blocks, unit, 0)
        key = rows_of(part_ref, blocks, unit, 1)
        query = rows_of(query_ref, blocks, unit, 0)
        query_proj = split(jnp.where(rows >= columns, nt(query, direction), 0.0))
        ahead = nn(jnp.concatenate(query_proj, 0), mixed_ref[unit])
        ahead = ahead[:BLOCK] + ahead[BLOCK:]
        inner_ref[unit] = nt(query, key) - ahead[:, HEAD_DIM:]
        start = split(query.astype(F32) - ahead[:, :HEAD_DIM])
        moving_ref[unit, 0] = start[0]
        if unit % 2:
            pair = unit // 2
            start = split(triple(nt, start, (even_ref[pair, 0], even_ref[pair, 1])))
        moving_ref[unit, 1] = start[0]
        current.append(start)
    pairs = units // 2
    current = [
        tuple(jnp.concatenate([current[2 * pair][part], current[2 * pair + 1][part]], 0)
              for part in range(2))
        for pair in range(pairs)
    ]
    for step in range(2, pairs + 1):
        for pair in range(step - 1, pairs):
            passed = pair - step + 1
            current[pair] = split(
                triple(nt, current[pair], (pair_ref[passed, 0], pair_ref[passed, 1]))
            )
            moving_ref[2 * pair, step] = current[pair][0][:BLOCK]
            moving_ref[2 * pair + 1, step] = current[pair][0][BLOCK:]
    for copy in copies:
        copy.wait()


def listed_block(away_ref, unit, entry):
    away = away_ref[unit, entry]
    new = away > 0
    for other in range(1, entry):
        new = new & (away_ref[unit, other] != away)
    return unit - away, new


def earlier(source, ahead, units):
    return jnp.clip(source + ahead * units, 0, units - 1), source < (1 - ahead) * units


def attend_kernel(before, blocks, away_ref, moving_ref, inner_ref, end_ref, tail_ref, part_ref,
                  *refs):
    values, far_keys = refs[:before], refs[before:2 * before]
    group_maps, out_ref = refs[2 * before:-1], refs[-1]
    units = inner_ref.shape[0]
    rows, columns = square_iotas()
    scale = HEAD_DIM ** (-0.5)

    def steps(unit):
        pair = unit // 2
        fronts = [moving_ref[unit, pair + 1]]
        for group_map in group_maps:
            passed = nt(fronts[-1], group_map[0]) + nt(fronts[-1], group_map[1])
            fronts.append(passed.astype(BF16))
        score_list = [jnp.where(rows >= columns, inner_ref[unit] * scale, -1e30)]
        value_list = [rows_of(part_ref, blocks, unit, 2)]
        for entry in range(1, TOPK):
            source, new = listed_block(away_ref, unit, entry)
            inside = jnp.maximum(source, 0)
            step = jnp.maximum(pair - inside // 2, 0)
            start = pl.multiple_of((2 * blocks + lax.rem(inside, blocks)) * BLOCK, BLOCK)
            query = moving_ref[unit, step]
            key = jnp.where(step == 0, end_ref[inside], tail_ref[inside])
            value = part_ref[inside // blocks, pl.ds(start, BLOCK)]
            for ahead in range(1, before + 1):
                place, here = earlier(source, ahead, units)
                query = jnp.where(here, fronts[ahead - 1], query)
                key = jnp.where(here, far_keys[ahead - 1][place], key)
                value = jnp.where(here, values[ahead - 1][place], value)
            score_list.append(jnp.where(new, nt(query, key) * scale, -1e30))
            value_list.append(value)
        yield
        scores = jnp.concatenate(score_list, 1)
        expos = jnp.exp(scores - jnp.max(scores, 1, keepdims=True))
        weights = (expos / jnp.sum(expos, 1, keepdims=True)).astype(BF16)
        yield
        blended = nn(weights, jnp.concatenate(value_list, 0)).astype(BF16)
        for plane in range(out_ref.shape[1]):
            out_ref[unit // blocks, plane, unit % blocks] = blended

    interleaved([steps(unit) for unit in range(units)], 1)


def project_kernel(axes, other, cores, attended_ref, own_ref, *refs):
    other_refs, out_ref = refs[:-1], refs[-1]
    heads, planes, blocks = attended_ref.shape[:3]
    index = lax.axis_index(axes[1])
    core, plane = lax.rem(index + other, cores), index // cores
    width = out_ref.shape[1]
    total = None
    for offset in range(planes):
        source = lax.rem(plane + offset, planes)
        attended = jnp.concatenate(
            [
                jnp.concatenate(
                    [attended_ref[head, source, block] for head in range(heads)], 1
                )
                for block in range(blocks)
            ],
            0,
        )
        if offset:
            start = pl.multiple_of(core * width, width)
            weight = other_refs[offset - 1][:, pl.ds(start, width)]
        else:
            start = pl.multiple_of((plane * cores + core) * width, width)
            weight = own_ref[:, pl.ds(start, width)]
        product = nn(attended, weight)
        total = product if total is None else total + product
    out_ref[...] = total.astype(out_ref.dtype)


def call(kernel, outs, specs, flops, scratch=(), places=None, space=32):
    if places is None:
        places = [VMEM] * len(outs) if isinstance(outs, list) else VMEM
    return pl.pallas_call(
        kernel,
        out_shape=outs,
        in_specs=specs,
        out_specs=places,
        scratch_shapes=list(scratch),
        compiler_params=pltpu.CompilerParams(vmem_limit_bytes=space * 2 ** 20),
        cost_estimate=pl.CostEstimate(flops=flops, bytes_accessed=2 ** 21, transcendentals=0),
    )


def body(ctx_size, head_size, queries, keys, values, directions, rates, selected, out_weight):
    tokens = queries.shape[0]
    blocks = tokens // BLOCK
    heads = queries.shape[1] // HEAD_DIM
    units = heads * blocks
    pairs = units // 2
    groups = ctx_size // heads
    before = min(groups - 1, -(-LOOK // heads))
    cores = 2
    planes = head_size // cores
    axes = ("ctx", "head")
    members = [[group * heads + place for place in range(heads)] for group in range(groups)]
    partners = [(g, g + 1 - 2 * (g % cores)) for g in range(head_size)]
    cubes = 2 * BLOCK ** 3
    tile = (BLOCK, HEAD_DIM)

    def exchange(value):
        return lax.all_to_all(value, "ctx", 0, 0, axis_index_groups=members, tiled=True)

    def onward(value, by):
        shift = by * heads
        return lax.ppermute(value, "ctx", [(i, i + shift) for i in range(ctx_size - shift)])

    def array(shape, kind=BF16):
        return jax.ShapeDtypeStruct(shape, kind)

    part_shape = (heads, 3 * tokens + EXTRA, HEAD_DIM)
    packed = call(
        functools.partial(pack_kernel, axes),
        array(part_shape),
        [ANY] * 5,
        cubes,
        [
            pltpu.VMEM(part_shape, BF16),
            pltpu.VMEM(rates.shape, F32),
            pltpu.SMEM(selected.shape, jnp.int32),
            pltpu.SemaphoreType.DMA((heads, 3)),
            pltpu.SemaphoreType.DMA((2,)),
            pltpu.SemaphoreType.DMA((heads,)),
        ],
        ANY,
        56,
    )(directions, keys, values, rates, selected)
    plane = lax.axis_index("head") // cores
    width = out_weight.shape[1] // planes
    weight_parts = []
    for offset in range(1, planes):
        start = lax.rem(plane + planes - offset, planes) * width
        turned = [(g, (g + head_size - cores * offset) % head_size) for g in range(head_size)]
        piece = lax.dynamic_slice_in_dim(out_weight, start, width, 1)
        weight_parts.append(lax.ppermute(piece, "head", turned))
    parts = exchange(packed)
    own_values = parts[:, 2 * tokens:3 * tokens].reshape(units, *tile)
    value_parts = [onward(own_values, by) for by in range(1, before + 1)]

    end, tail, far, even, pair_map, group_map, mixed, away, cut = call(
        functools.partial(keys_kernel, blocks),
        [
            array((units, *tile)),
            array((units, *tile)),
            array((units, *tile)),
            array((pairs, 2, *tile)),
            array((pairs, 2, *tile)),
            array((2, *tile)),
            array((units, BLOCK, 2 * BLOCK)),
            array((units, HEAD_DIM), jnp.int32),
            array((heads, tokens, HEAD_DIM)),
        ],
        [VMEM, ANY],
        400 * cubes,
        [
            pltpu.VMEM((heads, tokens, HEAD_DIM), BF16),
            pltpu.SemaphoreType.DMA((heads,)),
            pltpu.SemaphoreType.DMA((heads,)),
        ],
        [VMEM] * 8 + [ANY],
    )(parts, queries)
    far_parts = [onward(far, by) for by in range(1, before + 1)]
    map_parts = [onward(group_map, by) for by in range(1, before)]
    query_parts = exchange(cut)
    inner, moving, *weight_parts = call(
        functools.partial(queries_kernel, blocks, len(weight_parts)),
        [array((units, BLOCK, BLOCK), F32), array((units, pairs + 1, *tile))]
        + [array(part.shape) for part in weight_parts],
        [VMEM] * 5 + [ANY] * (len(weight_parts) + before),
        200 * cubes,
        [pltpu.SemaphoreType.DMA((max(len(weight_parts), 1),))],
    )(parts, query_parts, mixed, even, pair_map, *weight_parts, *value_parts)
    attended = call(
        functools.partial(attend_kernel, before, blocks),
        array((heads, planes, blocks, *tile)),
        [SMEM] + [VMEM] * (5 + 2 * before + len(map_parts)),
        200 * cubes,
    )(away, moving, inner, end, tail, parts, *value_parts, *far_parts, *map_parts)

    returns = [
        [
            (group * heads + place) * head_size + p * cores + core
            for place in range(heads)
            for p in range(planes)
        ]
        for group in range(groups)
        for core in range(cores)
    ]
    local = lax.all_to_all(
        attended.reshape(heads * planes, blocks, *tile),
        axes, 0, 0, axis_index_groups=returns, tiled=True,
    ).reshape(heads, planes, blocks, *tile)

    def projected(other, kind):
        return call(
            functools.partial(project_kernel, axes, other, cores),
            array((tokens, width // cores), kind),
            [VMEM] * (1 + planes),
            128 * cubes,
        )(local, out_weight, *weight_parts)

    arrived = lax.ppermute(projected(1, BF16), "head", partners)
    return (projected(0, F32) + arrived.astype(F32)).astype(BF16)


def solution(mesh):
    in_specs = (
        P("ctx", "head"),
        P("ctx", "head"),
        P("ctx", "head"),
        P("ctx", "head"),
        P("head", "ctx"),
        P("ctx", None),
        P("head", None),
    )
    out_specs = P("ctx", "head")
    return jax.shard_map(
        functools.partial(body, mesh.shape["ctx"], mesh.shape["head"]),
        mesh=mesh,
        in_specs=in_specs,
        out_specs=out_specs,
        check_vma=False,
    )
```

```python
import functools

import jax
import jax.numpy as jnp
from jax import lax
from jax.experimental import pallas as pl
from jax.experimental.pallas import tpu as pltpu
from jax.sharding import PartitionSpec as P

HEAD_DIM = 128
BLOCK = 128
LOOK = 7
TOPK = 4
BASE = 16
EXTRA = 16
TERMS = 3
BF16 = jnp.bfloat16
F32 = jnp.float32
VMEM = pl.BlockSpec(memory_space=pltpu.VMEM)
SMEM = pl.BlockSpec(memory_space=pltpu.SMEM)
ANY = pl.BlockSpec(memory_space=pl.ANY)


def dot(left, right, left_dim, right_dim):
    return lax.dot_general(
        left, right, (((left_dim,), (right_dim,)), ((), ())), preferred_element_type=F32
    )


def nn(left, right):
    return dot(left, right, 1, 0)


def nt(left, right):
    return dot(left, right, 1, 1)


def tn(left, right):
    return dot(left, right, 0, 0)


def split(value):
    high = value.astype(BF16)
    return high, (value - high.astype(F32)).astype(BF16)


def triple(product, left, right):
    rows = left[0].shape[0]
    first = product(jnp.concatenate(left, 0), right[0])
    return first[:rows] + (first[rows:] + product(left[0], right[1]))


def square_iotas():
    rows = lax.broadcasted_iota(jnp.int32, (BLOCK, BLOCK), 0)
    columns = lax.broadcasted_iota(jnp.int32, (BLOCK, BLOCK), 1)
    return rows, columns


def fetched(sources, targets, sems):
    copies = []
    for index, (source, target) in enumerate(zip(sources, targets)):
        copies.append(pltpu.make_async_copy(source, target, sems.at[index]))
        copies[-1].start()
    return copies


def pack_kernel(axes, d_ref, k_ref, v_ref, rates_hbm, selected_hbm, out_ref, parts_ref,
                rates_ref, selected_ref, sems, few_sems, out_sems):
    tokens = d_ref.shape[0]
    heads = d_ref.shape[1] // HEAD_DIM
    blocks = tokens // BLOCK
    first_block = lax.axis_index(axes[0]) * blocks
    few_copies = fetched([rates_hbm, selected_hbm], [rates_ref, selected_ref], few_sems)
    sources = (d_ref, k_ref, v_ref)
    copies = []
    for head in range(heads):
        columns = pl.ds(head * HEAD_DIM, HEAD_DIM)
        for kind, source in enumerate(sources):
            copies.append(
                pltpu.make_async_copy(
                    source.at[:, columns],
                    parts_ref.at[head, pl.ds(kind * tokens, tokens)],
                    sems.at[head, kind],
                )
            )
            copies[-1].start()
    for copy in few_copies:
        copy.wait()
    row = lax.broadcasted_iota(jnp.int32, (EXTRA, HEAD_DIM), 0)
    lane = lax.broadcasted_iota(jnp.int32, (EXTRA, HEAD_DIM), 1)
    away = jnp.zeros((EXTRA, HEAD_DIM), jnp.int32)
    for block in range(blocks):
        for entry in range(TOPK):
            distance = first_block + block - selected_ref[block, entry]
            away = jnp.where((row == TERMS * blocks + block) & (lane == entry), distance, away)
    away = away.astype(F32)
    terms = []
    rest = rates_ref[...]
    for _ in range(TERMS):
        terms.append(rest.astype(BF16).astype(F32))
        rest = rest - terms[-1]
    out_copies = []
    for head in range(heads):
        extra = away
        for block in range(blocks):
            for index, term in enumerate(terms):
                piece = term[head:head + 1, block * BLOCK:(block + 1) * BLOCK]
                extra = jnp.where(row == TERMS * block + index, piece, extra)
        parts_ref[head, len(sources) * tokens:] = extra.astype(BF16)
        for copy in copies[len(sources) * head:len(sources) * (head + 1)]:
            copy.wait()
        out_copies.append(
            pltpu.make_async_copy(parts_ref.at[head], out_ref.at[head], out_sems.at[head])
        )
        out_copies[-1].start()
    for copy in out_copies:
        copy.wait()


def rows_of(ref, blocks, unit, kind):
    start = (kind * blocks + unit % blocks) * BLOCK
    return ref[unit // blocks, start:start + BLOCK]


def base_inverse(strict):
    count = BLOCK // BASE
    moved = [
        pltpu.roll(strict[b * BASE:(b + 1) * BASE], (BLOCK - b * BASE) % BLOCK, 1)
        if b else strict[:BASE]
        for b in range(count)
    ]
    lanes = lax.broadcasted_iota(jnp.int32, (BASE // 2, BLOCK), 1)
    rows = lax.broadcasted_iota(jnp.int32, (BASE // 2, BLOCK), 0)
    half = BASE // 2
    parts = []
    for b in range(count):
        upper = (lanes == rows + b * BASE).astype(F32)
        lower = (lanes == rows + b * BASE + half).astype(F32)
        for step in range(BASE - 1):
            if step < half:
                source = upper[step:step + 1]
                if step < half - 1:
                    upper = upper - moved[b][:half, step:step + 1] * source
            else:
                source = lower[step - half:step - half + 1]
            lower = lower - moved[b][half:, step:step + 1] * source
        parts += [upper, lower]
    return jnp.concatenate(parts, 0)


def halves(value, size):
    parts = value.reshape(BLOCK // (2 * size), 2, size, BLOCK)
    return parts[:, 0].reshape(BLOCK // 2, BLOCK), parts[:, 1].reshape(BLOCK // 2, BLOCK)


def joined(first, second, size):
    shape = (BLOCK // (2 * size), 1, size, BLOCK)
    return jnp.concatenate([first.reshape(shape), second.reshape(shape)], 1).reshape(BLOCK, BLOCK)


def interleaved(steps, lag):
    running = list(steps)
    tick = 0
    while any(step is not None for step in running):
        for index, step in enumerate(running):
            if step is not None and tick >= index * lag:
                try:
                    next(step)
                except StopIteration:
                    running[index] = None
        tick += 1


def keys_kernel(axes, blocks, part_ref, queries_ref, end_ref, tail_ref, far_ref, even_ref,
                pair_ref, group_ref, mixed_ref, away_ref, *refs):
    heads = part_ref.shape[0]
    units = heads * blocks
    out_refs = refs[:heads]
    cut_ref, sems, out_sems = refs[heads:]
    place = lax.rem(lax.axis_index(axes[0]), heads)
    cuts = [
        pl.multiple_of(lax.bitwise_xor(place, turn) * HEAD_DIM, HEAD_DIM) for turn in range(heads)
    ]
    query_copies = fetched(
        [queries_ref.at[:, pl.ds(cut, HEAD_DIM)] for cut in cuts],
        [cut_ref.at[turn] for turn in range(heads)],
        sems,
    )
    rows, columns = square_iotas()
    diagonal = rows == columns
    identity = diagonal.astype(F32)
    row = lax.broadcasted_iota(jnp.int32, (BLOCK // 2, BLOCK), 0)
    column = lax.broadcasted_iota(jnp.int32, (BLOCK // 2, BLOCK), 1)
    ends, maps = [None] * units, [None] * units

    def terms(unit):
        direction = rows_of(part_ref, blocks, unit, 0)
        key = rows_of(part_ref, blocks, unit, 1)
        extra = part_ref[unit // blocks, 3 * blocks * BLOCK:].astype(F32)
        first = TERMS * (unit % blocks)
        rate = extra[first:first + 1] + extra[first + 1:first + 2] + extra[first + 2:first + 3]
        listed = TERMS * blocks + unit % blocks
        away_ref[unit:unit + 1] = extra[listed:listed + 1].astype(jnp.int32)
        gram = nt(direction, direction)
        key_proj = jnp.where(rows > columns, nt(direction, key), 0.0).astype(BF16)
        squares = jnp.sum(jnp.where(diagonal, gram, 0.0), 0, keepdims=True)
        scale = lax.rsqrt(squares + 1e-06)
        scaled_rate = rate * scale
        scale_column = jnp.sum(jnp.where(diagonal, scale, 0.0), 1, keepdims=True)
        rate_column = jnp.sum(jnp.where(diagonal, scaled_rate, 0.0), 1, keepdims=True)
        strict = jnp.where(rows > columns, rate_column * gram * scale, 0.0)
        yield
        inverse = base_inverse(strict)
        yield
        size = BASE
        while size < BLOCK:
            inside = (row // size == column // (2 * size)) & (lax.rem(column, 2 * size) < size)
            corner = jnp.where(inside, halves(strict, size)[1], 0.0)
            below = triple(nn, split(corner), split(inverse))
            yield
            first_half, second = halves(inverse, size)
            padded = joined(jnp.zeros_like(below), below, size)
            second = second - triple(nn, split(second), split(padded))
            inverse = joined(first_half, second, size)
            size *= 2
            yield
        mixing = split(scale_column * inverse * scaled_rate)
        mixed = nn(jnp.concatenate(mixing, 0), jnp.concatenate([direction, key_proj], 1))
        mixed = split(mixed[:BLOCK] + mixed[BLOCK:])
        mixed_ref[unit] = mixed[0]
        yield
        behind = tn(jnp.concatenate([mixed[0], mixed[1][:, :BLOCK]], 1), direction)
        ends[unit] = key.astype(F32) - behind[BLOCK:2 * BLOCK]
        maps[unit] = split(identity - (behind[:BLOCK] + behind[2 * BLOCK:]))
        end_ref[unit] = ends[unit].astype(BF16)

    interleaved([terms(unit) for unit in range(units)], 1)
    out_copies = []
    for turn in range(heads):
        query_copies[turn].wait()
        out_copies.append(
            pltpu.make_async_copy(cut_ref.at[turn], out_refs[turn], out_sems.at[turn])
        )
        out_copies[-1].start()
    pair_keys, pair_maps = [], []
    for pair in range(units // 2):
        even, odd = 2 * pair, 2 * pair + 1
        even_ref[pair, 0] = maps[even][0]
        even_ref[pair, 1] = maps[even][1]
        end = split(ends[even])
        left = tuple(jnp.concatenate([end[part], maps[even][part]], 0) for part in range(2))
        both = triple(nn, left, maps[odd])
        tail_ref[even] = both[:BLOCK].astype(BF16)
        tail_ref[odd] = ends[odd].astype(BF16)
        pair_keys.append(jnp.concatenate([both[:BLOCK], ends[odd]], 0))
        pair_maps.append(split(both[BLOCK:]))
        pair_ref[pair, 0] = pair_maps[pair][0]
        pair_ref[pair, 1] = pair_maps[pair][1]
    onward = None
    for pair in reversed(range(units // 2)):
        far = pair_keys[pair]
        if onward is None:
            onward = pair_maps[pair]
        else:
            far = triple(nn, split(far), onward)
            onward = split(triple(nn, pair_maps[pair], onward))
        far_ref[2 * pair] = far[:BLOCK].astype(BF16)
        far_ref[2 * pair + 1] = far[BLOCK:].astype(BF16)
    group_ref[0] = onward[0]
    group_ref[1] = onward[1]
    for copy in out_copies:
        copy.wait()


def queries_kernel(axes, blocks, count, part_ref, mixed_ref, even_ref, pair_ref, *refs):
    heads = part_ref.shape[0]
    units = heads * blocks
    arrived, weights = refs[:heads], refs[heads:heads + count]
    inner_ref, moving_ref, *weight_refs = refs[-5 - count:-3]
    query_ref, sems, query_sems = refs[-3:]
    place = lax.rem(lax.axis_index(axes[0]), heads)
    query_copies = fetched(
        arrived,
        [query_ref.at[lax.bitwise_xor(place, turn)] for turn in range(heads)],
        query_sems,
    )
    copies = fetched(weights, weight_refs, sems)
    for copy in query_copies:
        copy.wait()
    rows, columns = square_iotas()
    current = []
    for unit in range(units):
        direction = rows_of(part_ref, blocks, unit, 0)
        key = rows_of(part_ref, blocks, unit, 1)
        query = rows_of(query_ref, blocks, unit, 0)
        query_proj = split(jnp.where(rows >= columns, nt(query, direction), 0.0))
        ahead = nn(jnp.concatenate(query_proj, 0), mixed_ref[unit])
        ahead = ahead[:BLOCK] + ahead[BLOCK:]
        inner_ref[unit] = nt(query, key) - ahead[:, HEAD_DIM:]
        start = split(query.astype(F32) - ahead[:, :HEAD_DIM])
        moving_ref[unit, 0] = start[0]
        if unit % 2:
            pair = unit // 2
            start = split(triple(nt, start, (even_ref[pair, 0], even_ref[pair, 1])))
        moving_ref[unit, 1] = start[0]
        current.append(start)
    pairs = units // 2
    current = [
        tuple(jnp.concatenate([current[2 * pair][part], current[2 * pair + 1][part]], 0)
              for part in range(2))
        for pair in range(pairs)
    ]
    for step in range(2, pairs + 1):
        for pair in range(step - 1, pairs):
            passed = pair - step + 1
            current[pair] = split(
                triple(nt, current[pair], (pair_ref[passed, 0], pair_ref[passed, 1]))
            )
            moving_ref[2 * pair, step] = current[pair][0][:BLOCK]
            moving_ref[2 * pair + 1, step] = current[pair][0][BLOCK:]
    for copy in copies:
        copy.wait()


def listed_block(away_ref, unit, entry):
    away = away_ref[unit, entry]
    new = away > 0
    for other in range(1, entry):
        new = new & (away_ref[unit, other] != away)
    return unit - away, new


def earlier(source, ahead, units):
    return jnp.clip(source + ahead * units, 0, units - 1), source < (1 - ahead) * units


def attend_kernel(before, blocks, away_ref, moving_ref, inner_ref, end_ref, tail_ref, part_ref,
                  *refs):
    values, far_keys = refs[:before], refs[before:2 * before]
    group_maps, out_ref = refs[2 * before:-1], refs[-1]
    units = inner_ref.shape[0]
    rows, columns = square_iotas()
    scale = HEAD_DIM ** (-0.5)

    def steps(unit):
        pair = unit // 2
        fronts = [moving_ref[unit, pair + 1]]
        for group_map in group_maps:
            passed = nt(fronts[-1], group_map[0]) + nt(fronts[-1], group_map[1])
            fronts.append(passed.astype(BF16))
        score_list = [jnp.where(rows >= columns, inner_ref[unit] * scale, -1e30)]
        value_list = [rows_of(part_ref, blocks, unit, 2)]
        for entry in range(1, TOPK):
            source, new = listed_block(away_ref, unit, entry)
            inside = jnp.maximum(source, 0)
            step = jnp.maximum(pair - inside // 2, 0)
            start = pl.multiple_of((2 * blocks + lax.rem(inside, blocks)) * BLOCK, BLOCK)
            query = moving_ref[unit, step]
            key = jnp.where(step == 0, end_ref[inside], tail_ref[inside])
            value = part_ref[inside // blocks, pl.ds(start, BLOCK)]
            for ahead in range(1, before + 1):
                place, here = earlier(source, ahead, units)
                query = jnp.where(here, fronts[ahead - 1], query)
                key = jnp.where(here, far_keys[ahead - 1][place], key)
                value = jnp.where(here, values[ahead - 1][place], value)
            score_list.append(jnp.where(new, nt(query, key) * scale, -1e30))
            value_list.append(value)
        yield
        scores = jnp.concatenate(score_list, 1)
        expos = jnp.exp(scores - jnp.max(scores, 1, keepdims=True))
        weights = (expos / jnp.sum(expos, 1, keepdims=True)).astype(BF16)
        yield
        blended = nn(weights, jnp.concatenate(value_list, 0)).astype(BF16)
        for plane in range(out_ref.shape[1]):
            out_ref[unit // blocks, plane, unit % blocks] = blended

    interleaved([steps(unit) for unit in range(units)], 1)


def project_kernel(axes, other, cores, attended_ref, own_ref, *refs):
    other_refs, out_ref = refs[:-1], refs[-1]
    heads, planes, blocks = attended_ref.shape[:3]
    index = lax.axis_index(axes[1])
    core, plane = lax.rem(index + other, cores), index // cores
    width = out_ref.shape[1]
    total = None
    for offset in range(planes):
        source = lax.rem(plane + offset, planes)
        attended = jnp.concatenate(
            [
                jnp.concatenate(
                    [attended_ref[head, source, block] for head in range(heads)], 1
                )
                for block in range(blocks)
            ],
            0,
        )
        if offset:
            start = pl.multiple_of(core * width, width)
            weight = other_refs[offset - 1][:, pl.ds(start, width)]
        else:
            start = pl.multiple_of((plane * cores + core) * width, width)
            weight = own_ref[:, pl.ds(start, width)]
        product = nn(attended, weight)
        total = product if total is None else total + product
    out_ref[...] = total.astype(out_ref.dtype)


def call(kernel, outs, specs, flops, scratch=(), places=None, space=32):
    if places is None:
        places = [VMEM] * len(outs) if isinstance(outs, list) else VMEM
    return pl.pallas_call(
        kernel,
        out_shape=outs,
        in_specs=specs,
        out_specs=places,
        scratch_shapes=list(scratch),
        compiler_params=pltpu.CompilerParams(vmem_limit_bytes=space * 2 ** 20),
        cost_estimate=pl.CostEstimate(flops=flops, bytes_accessed=2 ** 21, transcendentals=0),
    )


def body(ctx_size, head_size, queries, keys, values, directions, rates, selected, out_weight):
    tokens = queries.shape[0]
    blocks = tokens // BLOCK
    heads = queries.shape[1] // HEAD_DIM
    units = heads * blocks
    pairs = units // 2
    groups = ctx_size // heads
    before = min(groups - 1, -(-LOOK // heads))
    cores = 2
    planes = head_size // cores
    axes = ("ctx", "head")
    members = [[group * heads + place for place in range(heads)] for group in range(groups)]
    partners = [(g, g + 1 - 2 * (g % cores)) for g in range(head_size)]
    cubes = 2 * BLOCK ** 3
    tile = (BLOCK, HEAD_DIM)

    def exchange(value):
        return lax.all_to_all(value, "ctx", 0, 0, axis_index_groups=members, tiled=True)

    def onward(value, by):
        shift = by * heads
        return lax.ppermute(value, "ctx", [(i, i + shift) for i in range(ctx_size - shift)])

    def crossed(value, turn):
        pairs = [(i, i - i % heads + (i % heads ^ turn)) for i in range(ctx_size)]
        return lax.ppermute(value, "ctx", pairs) if turn else value

    def array(shape, kind=BF16):
        return jax.ShapeDtypeStruct(shape, kind)

    part_shape = (heads, 3 * tokens + EXTRA, HEAD_DIM)
    packed = call(
        functools.partial(pack_kernel, axes),
        array(part_shape),
        [ANY] * 5,
        cubes,
        [
            pltpu.VMEM(part_shape, BF16),
            pltpu.VMEM(rates.shape, F32),
            pltpu.SMEM(selected.shape, jnp.int32),
            pltpu.SemaphoreType.DMA((heads, 3)),
            pltpu.SemaphoreType.DMA((2,)),
            pltpu.SemaphoreType.DMA((heads,)),
        ],
        ANY,
        56,
    )(directions, keys, values, rates, selected)
    plane = lax.axis_index("head") // cores
    width = out_weight.shape[1] // planes
    weight_parts = []
    for offset in range(1, planes):
        start = lax.rem(plane + planes - offset, planes) * width
        turned = [(g, (g + head_size - cores * offset) % head_size) for g in range(head_size)]
        piece = lax.dynamic_slice_in_dim(out_weight, start, width, 1)
        weight_parts.append(lax.ppermute(piece, "head", turned))
    parts = exchange(packed)
    own_values = parts[:, 2 * tokens:3 * tokens].reshape(units, *tile)
    value_parts = [onward(own_values, by) for by in range(1, before + 1)]

    end, tail, far, even, pair_map, group_map, mixed, away, *cut = call(
        functools.partial(keys_kernel, axes, blocks),
        [
            array((units, *tile)),
            array((units, *tile)),
            array((units, *tile)),
            array((pairs, 2, *tile)),
            array((pairs, 2, *tile)),
            array((2, *tile)),
            array((units, BLOCK, 2 * BLOCK)),
            array((units, HEAD_DIM), jnp.int32),
        ]
        + [array((tokens, HEAD_DIM))] * heads,
        [VMEM, ANY],
        400 * cubes,
        [
            pltpu.VMEM((heads, tokens, HEAD_DIM), BF16),
            pltpu.SemaphoreType.DMA((heads,)),
            pltpu.SemaphoreType.DMA((heads,)),
        ],
        [VMEM] * 8 + [ANY] * heads,
    )(parts, queries)
    far_parts = [onward(far, by) for by in range(1, before + 1)]
    map_parts = [onward(group_map, by) for by in range(1, before)]
    query_parts = [crossed(cut[turn], turn) for turn in range(heads)]
    inner, moving, *weight_parts = call(
        functools.partial(queries_kernel, axes, blocks, len(weight_parts)),
        [array((units, BLOCK, BLOCK), F32), array((units, pairs + 1, *tile))]
        + [array(part.shape) for part in weight_parts],
        [VMEM] * 4 + [ANY] * (heads + len(weight_parts) + before),
        200 * cubes,
        [
            pltpu.VMEM((heads, tokens, HEAD_DIM), BF16),
            pltpu.SemaphoreType.DMA((max(len(weight_parts), 1),)),
            pltpu.SemaphoreType.DMA((heads,)),
        ],
    )(parts, mixed, even, pair_map, *query_parts, *weight_parts, *value_parts)
    attended = call(
        functools.partial(attend_kernel, before, blocks),
        array((heads, planes, blocks, *tile)),
        [SMEM] + [VMEM] * (5 + 2 * before + len(map_parts)),
        200 * cubes,
    )(away, moving, inner, end, tail, parts, *value_parts, *far_parts, *map_parts)

    returns = [
        [
            (group * heads + place) * head_size + p * cores + core
            for place in range(heads)
            for p in range(planes)
        ]
        for group in range(groups)
        for core in range(cores)
    ]
    local = lax.all_to_all(
        attended.reshape(heads * planes, blocks, *tile),
        axes, 0, 0, axis_index_groups=returns, tiled=True,
    ).reshape(heads, planes, blocks, *tile)

    def projected(other, kind):
        return call(
            functools.partial(project_kernel, axes, other, cores),
            array((tokens, width // cores), kind),
            [VMEM] * (1 + planes),
            128 * cubes,
        )(local, out_weight, *weight_parts)

    arrived = lax.ppermute(projected(1, BF16), "head", partners)
    return (projected(0, F32) + arrived.astype(F32)).astype(BF16)


def solution(mesh):
    in_specs = (
        P("ctx", "head"),
        P("ctx", "head"),
        P("ctx", "head"),
        P("ctx", "head"),
        P("head", "ctx"),
        P("ctx", None),
        P("head", None),
    )
    out_specs = P("ctx", "head")
    return jax.shard_map(
        functools.partial(body, mesh.shape["ctx"], mesh.shape["head"]),
        mesh=mesh,
        in_specs=in_specs,
        out_specs=out_specs,
        check_vma=False,
    )
```

```python
import functools

import jax
import jax.numpy as jnp
from jax import lax
from jax.experimental import pallas as pl
from jax.experimental.pallas import tpu as pltpu
from jax.sharding import PartitionSpec as P

HEAD_DIM = 128
BLOCK = 128
LOOK = 7
TOPK = 4
BASE = 16
EXTRA = 16
TERMS = 3
BF16 = jnp.bfloat16
F32 = jnp.float32
VMEM = pl.BlockSpec(memory_space=pltpu.VMEM)
SMEM = pl.BlockSpec(memory_space=pltpu.SMEM)
ANY = pl.BlockSpec(memory_space=pl.ANY)


def dot(left, right, left_dim, right_dim):
    return lax.dot_general(
        left, right, (((left_dim,), (right_dim,)), ((), ())), preferred_element_type=F32
    )


def nn(left, right):
    return dot(left, right, 1, 0)


def nt(left, right):
    return dot(left, right, 1, 1)


def tn(left, right):
    return dot(left, right, 0, 0)


def split(value):
    high = value.astype(BF16)
    return high, (value - high.astype(F32)).astype(BF16)


def triple(product, left, right):
    rows = left[0].shape[0]
    first = product(jnp.concatenate(left, 0), right[0])
    return first[:rows] + (first[rows:] + product(left[0], right[1]))


def square_iotas():
    rows = lax.broadcasted_iota(jnp.int32, (BLOCK, BLOCK), 0)
    columns = lax.broadcasted_iota(jnp.int32, (BLOCK, BLOCK), 1)
    return rows, columns


def fetched(sources, targets, sems):
    copies = []
    for index, (source, target) in enumerate(zip(sources, targets)):
        copies.append(pltpu.make_async_copy(source, target, sems.at[index]))
        copies[-1].start()
    return copies


def pack_kernel(axes, d_ref, k_ref, rates_hbm, selected_hbm, out_ref, parts_ref,
                rates_ref, selected_ref, sems, few_sems, out_sems):
    tokens = d_ref.shape[0]
    heads = d_ref.shape[1] // HEAD_DIM
    blocks = tokens // BLOCK
    first_block = lax.axis_index(axes[0]) * blocks
    few_copies = fetched([rates_hbm, selected_hbm], [rates_ref, selected_ref], few_sems)
    sources = (d_ref, k_ref)
    copies = []
    for head in range(heads):
        columns = pl.ds(head * HEAD_DIM, HEAD_DIM)
        for kind, source in enumerate(sources):
            copies.append(
                pltpu.make_async_copy(
                    source.at[:, columns],
                    parts_ref.at[head, pl.ds(kind * tokens, tokens)],
                    sems.at[head, kind],
                )
            )
            copies[-1].start()
    for copy in few_copies:
        copy.wait()
    row = lax.broadcasted_iota(jnp.int32, (EXTRA, HEAD_DIM), 0)
    lane = lax.broadcasted_iota(jnp.int32, (EXTRA, HEAD_DIM), 1)
    away = jnp.zeros((EXTRA, HEAD_DIM), jnp.int32)
    for block in range(blocks):
        for entry in range(TOPK):
            distance = first_block + block - selected_ref[block, entry]
            away = jnp.where((row == TERMS * blocks + block) & (lane == entry), distance, away)
    away = away.astype(F32)
    terms = []
    rest = rates_ref[...]
    for _ in range(TERMS):
        terms.append(rest.astype(BF16).astype(F32))
        rest = rest - terms[-1]
    out_copies = []
    for head in range(heads):
        extra = away
        for block in range(blocks):
            for index, term in enumerate(terms):
                piece = term[head:head + 1, block * BLOCK:(block + 1) * BLOCK]
                extra = jnp.where(row == TERMS * block + index, piece, extra)
        parts_ref[head, len(sources) * tokens:] = extra.astype(BF16)
        for copy in copies[len(sources) * head:len(sources) * (head + 1)]:
            copy.wait()
        out_copies.append(
            pltpu.make_async_copy(parts_ref.at[head], out_ref.at[head], out_sems.at[head])
        )
        out_copies[-1].start()
    for copy in out_copies:
        copy.wait()


def early_kernel(axes, cores, weight_ref, values_ref, after, *refs):
    count = (len(refs) - 5) // 2 + 1
    weight_outs, values_out = refs[:count], refs[count]
    weight_bufs, values_buf = refs[count + 1:2 * count + 1], refs[2 * count + 1]
    sems, out_sems = refs[2 * count + 2:]
    width = weight_outs[0].shape[1]
    planes = weight_ref.shape[1] // width
    plane = lax.axis_index(axes[1]) // cores
    sources = [values_ref]
    for offset in range(1, planes):
        start = lax.rem(plane + planes - offset, planes) * width
        sources.append(weight_ref.at[:, pl.ds(pl.multiple_of(start, width), width)])
    buffers = [values_buf, *weight_bufs]
    copies = fetched(sources, buffers, sems)
    out_copies = []
    for index, target in enumerate([values_out, *weight_outs]):
        copies[index].wait()
        out_copies += fetched([buffers[index]], [target], out_sems.at[pl.ds(index, 1)])
    for copy in out_copies:
        copy.wait()


def cut_kernel(axes, *refs):
    sems = refs[-1]
    parts = refs[-1 - sems.shape[0]:-1]
    sources = refs[:sems.shape[1]]
    heads = sems.shape[0]
    place = lax.rem(lax.axis_index(axes[0]), heads)
    copies = []
    for turn in range(heads):
        cut = pl.multiple_of(lax.bitwise_xor(place, turn) * HEAD_DIM, HEAD_DIM)
        copies += fetched(
            [source.at[:, pl.ds(cut, HEAD_DIM)] for source in sources],
            [parts[turn].at[kind] for kind in range(len(sources))],
            sems.at[turn],
        )
    for copy in copies:
        copy.wait()


def order_kernel(axes, *refs):
    values_ref, sems = refs[-2:]
    kinds, heads = values_ref.shape[:2]
    place = lax.rem(lax.axis_index(axes[0]), heads)
    copies = []
    for turn in range(heads):
        source = lax.bitwise_xor(place, turn)
        parts = [refs[turn].at[1]]
        parts += [refs[heads + turn].at[kind] for kind in range(kinds - 1)]
        copies += fetched(
            parts, [values_ref.at[kind, source] for kind in range(kinds)], sems.at[turn]
        )
    for copy in copies:
        copy.wait()


def rows_of(ref, blocks, unit, kind):
    start = (kind * blocks + unit % blocks) * BLOCK
    return ref[unit // blocks, start:start + BLOCK]


def base_inverse(strict):
    count = BLOCK // BASE
    moved = [
        pltpu.roll(strict[b * BASE:(b + 1) * BASE], (BLOCK - b * BASE) % BLOCK, 1)
        if b else strict[:BASE]
        for b in range(count)
    ]
    lanes = lax.broadcasted_iota(jnp.int32, (BASE // 2, BLOCK), 1)
    rows = lax.broadcasted_iota(jnp.int32, (BASE // 2, BLOCK), 0)
    half = BASE // 2
    parts = []
    for b in range(count):
        upper = (lanes == rows + b * BASE).astype(F32)
        lower = (lanes == rows + b * BASE + half).astype(F32)
        for step in range(BASE - 1):
            if step < half:
                source = upper[step:step + 1]
                if step < half - 1:
                    upper = upper - moved[b][:half, step:step + 1] * source
            else:
                source = lower[step - half:step - half + 1]
            lower = lower - moved[b][half:, step:step + 1] * source
        parts += [upper, lower]
    return jnp.concatenate(parts, 0)


def halves(value, size):
    parts = value.reshape(BLOCK // (2 * size), 2, size, BLOCK)
    return parts[:, 0].reshape(BLOCK // 2, BLOCK), parts[:, 1].reshape(BLOCK // 2, BLOCK)


def joined(first, second, size):
    shape = (BLOCK // (2 * size), 1, size, BLOCK)
    return jnp.concatenate([first.reshape(shape), second.reshape(shape)], 1).reshape(BLOCK, BLOCK)


def interleaved(steps, lag):
    running = list(steps)
    tick = 0
    while any(step is not None for step in running):
        for index, step in enumerate(running):
            if step is not None and tick >= index * lag:
                try:
                    next(step)
                except StopIteration:
                    running[index] = None
        tick += 1


def keys_kernel(axes, blocks, part_ref, queries_ref, values_ref, end_ref, tail_ref, far_ref, even_ref,
                pair_ref, group_ref, mixed_ref, away_ref, *refs):
    heads = part_ref.shape[0]
    units = heads * blocks
    out_refs = refs[:heads]
    cut_ref, sems, out_sems = refs[heads:]
    place = lax.rem(lax.axis_index(axes[0]), heads)
    cuts = [
        pl.multiple_of(lax.bitwise_xor(place, turn) * HEAD_DIM, HEAD_DIM) for turn in range(heads)
    ]
    cut_copies = [
        fetched(
            [ref.at[:, pl.ds(cut, HEAD_DIM)] for ref in (queries_ref, values_ref)],
            [cut_ref.at[turn, 0], cut_ref.at[turn, 1]],
            sems.at[turn],
        )
        for turn, cut in enumerate(cuts)
    ]
    rows, columns = square_iotas()
    diagonal = rows == columns
    identity = diagonal.astype(F32)
    row = lax.broadcasted_iota(jnp.int32, (BLOCK // 2, BLOCK), 0)
    column = lax.broadcasted_iota(jnp.int32, (BLOCK // 2, BLOCK), 1)
    ends, maps = [None] * units, [None] * units

    def terms(unit):
        direction = rows_of(part_ref, blocks, unit, 0)
        key = rows_of(part_ref, blocks, unit, 1)
        extra = part_ref[unit // blocks, 2 * blocks * BLOCK:].astype(F32)
        first = TERMS * (unit % blocks)
        rate = extra[first:first + 1] + extra[first + 1:first + 2] + extra[first + 2:first + 3]
        listed = TERMS * blocks + unit % blocks
        away_ref[unit:unit + 1] = extra[listed:listed + 1].astype(jnp.int32)
        gram = nt(direction, direction)
        key_proj = jnp.where(rows > columns, nt(direction, key), 0.0).astype(BF16)
        squares = jnp.sum(jnp.where(diagonal, gram, 0.0), 0, keepdims=True)
        scale = lax.rsqrt(squares + 1e-06)
        scaled_rate = rate * scale
        scale_column = jnp.sum(jnp.where(diagonal, scale, 0.0), 1, keepdims=True)
        rate_column = jnp.sum(jnp.where(diagonal, scaled_rate, 0.0), 1, keepdims=True)
        strict = jnp.where(rows > columns, rate_column * gram * scale, 0.0)
        yield
        inverse = base_inverse(strict)
        yield
        size = BASE
        while size < BLOCK:
            inside = (row // size == column // (2 * size)) & (lax.rem(column, 2 * size) < size)
            corner = jnp.where(inside, halves(strict, size)[1], 0.0)
            below = triple(nn, split(corner), split(inverse))
            yield
            first_half, second = halves(inverse, size)
            padded = joined(jnp.zeros_like(below), below, size)
            second = second - triple(nn, split(second), split(padded))
            inverse = joined(first_half, second, size)
            size *= 2
            yield
        mixing = split(scale_column * inverse * scaled_rate)
        mixed = nn(jnp.concatenate(mixing, 0), jnp.concatenate([direction, key_proj], 1))
        mixed = split(mixed[:BLOCK] + mixed[BLOCK:])
        mixed_ref[unit] = mixed[0]
        yield
        behind = tn(jnp.concatenate([mixed[0], mixed[1][:, :BLOCK]], 1), direction)
        ends[unit] = key.astype(F32) - behind[BLOCK:2 * BLOCK]
        maps[unit] = split(identity - (behind[:BLOCK] + behind[2 * BLOCK:]))
        end_ref[unit] = ends[unit].astype(BF16)

    interleaved([terms(unit) for unit in range(units)], 1)
    out_copies = []
    for turn in range(heads):
        for copy in cut_copies[turn]:
            copy.wait()
        out_copies += fetched([cut_ref.at[turn]], [out_refs[turn]], out_sems.at[pl.ds(turn, 1)])
    pair_keys, pair_maps = [], []
    for pair in range(units // 2):
        even, odd = 2 * pair, 2 * pair + 1
        even_ref[pair, 0] = maps[even][0]
        even_ref[pair, 1] = maps[even][1]
        left = jnp.concatenate([ends[even].astype(BF16), *maps[even]], 0)
        both = nn(left, maps[odd][0])
        tail_ref[even] = both[:BLOCK].astype(BF16)
        tail_ref[odd] = ends[odd].astype(BF16)
        pair_keys.append(jnp.concatenate([both[:BLOCK], ends[odd]], 0))
        low = both[2 * BLOCK:] + nn(maps[even][0], maps[odd][1])
        pair_maps.append(split(both[BLOCK:2 * BLOCK] + low))
        pair_ref[pair, 0] = pair_maps[pair][0]
        pair_ref[pair, 1] = pair_maps[pair][1]
    onward = None
    for pair in reversed(range(units // 2)):
        far = pair_keys[pair]
        if onward is None:
            onward = pair_maps[pair]
        else:
            far = nn(far.astype(BF16), onward[0])
            onward = split(triple(nn, pair_maps[pair], onward))
        far_ref[2 * pair] = far[:BLOCK].astype(BF16)
        far_ref[2 * pair + 1] = far[BLOCK:].astype(BF16)
    group_ref[0] = onward[0]
    group_ref[1] = onward[1]
    for copy in out_copies:
        copy.wait()


def queries_kernel(axes, blocks, count, part_ref, mixed_ref, even_ref, pair_ref, *refs):
    heads = part_ref.shape[0]
    units = heads * blocks
    arrived, weights = refs[:heads], refs[heads:heads + count]
    inner_ref, moving_ref, *weight_refs = refs[heads + count:-3]
    query_ref, sems, query_sems = refs[-3:]
    place = lax.rem(lax.axis_index(axes[0]), heads)
    query_copies = fetched(
        [part.at[0] for part in arrived],
        [query_ref.at[lax.bitwise_xor(place, turn)] for turn in range(heads)],
        query_sems,
    )
    copies = fetched(weights, weight_refs, sems)
    for copy in query_copies:
        copy.wait()
    rows, columns = square_iotas()
    current = []
    for unit in range(units):
        direction = rows_of(part_ref, blocks, unit, 0)
        key = rows_of(part_ref, blocks, unit, 1)
        query = rows_of(query_ref, blocks, unit, 0)
        query_proj = split(jnp.where(rows >= columns, nt(query, direction), 0.0))
        ahead = nn(jnp.concatenate(query_proj, 0), mixed_ref[unit])
        ahead = ahead[:BLOCK] + ahead[BLOCK:]
        inner_ref[unit] = nt(query, key) - ahead[:, HEAD_DIM:]
        start = split(query.astype(F32) - ahead[:, :HEAD_DIM])
        moving_ref[unit, 0] = start[0]
        if unit % 2:
            pair = unit // 2
            start = split(triple(nt, start, (even_ref[pair, 0], even_ref[pair, 1])))
        moving_ref[unit, 1] = start[0]
        current.append(start)
    pairs = units // 2
    current = [
        tuple(jnp.concatenate([current[2 * pair][part], current[2 * pair + 1][part]], 0)
              for part in range(2))
        for pair in range(pairs)
    ]
    for step in range(2, pairs + 1):
        for pair in range(step - 1, pairs):
            passed = pair - step + 1
            current[pair] = split(
                triple(nt, current[pair], (pair_ref[passed, 0], pair_ref[passed, 1]))
            )
            moving_ref[2 * pair, step] = current[pair][0][:BLOCK]
            moving_ref[2 * pair + 1, step] = current[pair][0][BLOCK:]
    for copy in copies:
        copy.wait()


def listed_block(away_ref, unit, entry):
    away = away_ref[unit, entry]
    new = away > 0
    for other in range(1, entry):
        new = new & (away_ref[unit, other] != away)
    return unit - away, new


def earlier(source, ahead, units):
    return jnp.clip(source + ahead * units, 0, units - 1), source < (1 - ahead) * units


def attend_kernel(before, blocks, away_ref, moving_ref, inner_ref, end_ref, tail_ref,
                  values_ref, *refs):
    far_keys, group_maps, out_ref = refs[:before], refs[before:-1], refs[-1]
    units = inner_ref.shape[0]
    rows, columns = square_iotas()
    scale = HEAD_DIM ** (-0.5)

    def steps(unit):
        pair = unit // 2
        fronts = [moving_ref[unit, pair + 1]]
        for group_map in group_maps:
            passed = nt(fronts[-1], group_map[0]) + nt(fronts[-1], group_map[1])
            fronts.append(passed.astype(BF16))
        score_list = [jnp.where(rows >= columns, inner_ref[unit] * scale, -1e30)]
        value_list = [values_ref[0, unit]]
        for entry in range(1, TOPK):
            source, new = listed_block(away_ref, unit, entry)
            inside = jnp.maximum(source, 0)
            step = jnp.maximum(pair - inside // 2, 0)
            query = moving_ref[unit, step]
            key = jnp.where(step == 0, end_ref[inside], tail_ref[inside])
            value = values_ref[0, inside]
            for ahead in range(1, before + 1):
                place, here = earlier(source, ahead, units)
                query = jnp.where(here, fronts[ahead - 1], query)
                key = jnp.where(here, far_keys[ahead - 1][place], key)
                value = jnp.where(here, values_ref[ahead, place], value)
            score_list.append(jnp.where(new, nt(query, key) * scale, -1e30))
            value_list.append(value)
        yield
        scores = jnp.concatenate(score_list, 1)
        expos = jnp.exp(scores - jnp.max(scores, 1, keepdims=True))
        weights = (expos / jnp.sum(expos, 1, keepdims=True)).astype(BF16)
        yield
        blended = nn(weights, jnp.concatenate(value_list, 0)).astype(BF16)
        for plane in range(out_ref.shape[1]):
            out_ref[unit // blocks, plane, unit % blocks] = blended

    interleaved([steps(unit) for unit in range(units)], 1)


def project_kernel(axes, other, cores, attended_ref, own_ref, *refs):
    other_refs, out_ref = refs[:-1], refs[-1]
    heads, planes, blocks = attended_ref.shape[:3]
    index = lax.axis_index(axes[1])
    core, plane = lax.rem(index + other, cores), index // cores
    width = out_ref.shape[1]
    total = None
    for offset in range(planes):
        source = lax.rem(plane + offset, planes)
        attended = jnp.concatenate(
            [
                jnp.concatenate(
                    [attended_ref[head, source, block] for head in range(heads)], 1
                )
                for block in range(blocks)
            ],
            0,
        )
        if offset:
            start = pl.multiple_of(core * width, width)
            weight = other_refs[offset - 1][:, pl.ds(start, width)]
        else:
            start = pl.multiple_of((plane * cores + core) * width, width)
            weight = own_ref[:, pl.ds(start, width)]
        product = nn(attended, weight)
        total = product if total is None else total + product
    out_ref[...] = total.astype(out_ref.dtype)


def call(kernel, outs, specs, flops, scratch=(), places=None, space=32):
    if places is None:
        places = [VMEM] * len(outs) if isinstance(outs, list) else VMEM
    return pl.pallas_call(
        kernel,
        out_shape=outs,
        in_specs=specs,
        out_specs=places,
        scratch_shapes=list(scratch),
        compiler_params=pltpu.CompilerParams(vmem_limit_bytes=space * 2 ** 20),
        cost_estimate=pl.CostEstimate(flops=flops, bytes_accessed=2 ** 21, transcendentals=0),
    )


def body(ctx_size, head_size, queries, keys, values, directions, rates, selected, out_weight):
    tokens = queries.shape[0]
    blocks = tokens // BLOCK
    heads = queries.shape[1] // HEAD_DIM
    units = heads * blocks
    pairs = units // 2
    groups = ctx_size // heads
    before = min(groups - 1, -(-LOOK // heads))
    cores = 2
    planes = head_size // cores
    axes = ("ctx", "head")
    members = [[group * heads + place for place in range(heads)] for group in range(groups)]
    partners = [(g, g + 1 - 2 * (g % cores)) for g in range(head_size)]
    cubes = 2 * BLOCK ** 3
    tile = (BLOCK, HEAD_DIM)

    def exchange(value):
        return lax.all_to_all(value, "ctx", 0, 0, axis_index_groups=members, tiled=True)

    def onward(value, by):
        shift = by * heads
        return lax.ppermute(value, "ctx", [(i, i + shift) for i in range(ctx_size - shift)])

    def crossed(value, turn):
        pairs = [(i, i - i % heads + (i % heads ^ turn)) for i in range(ctx_size)]
        return lax.ppermute(value, "ctx", pairs) if turn else value

    def array(shape, kind=BF16):
        return jax.ShapeDtypeStruct(shape, kind)

    part_shape = (heads, 2 * tokens + EXTRA, HEAD_DIM)
    packed = call(
        functools.partial(pack_kernel, axes),
        array(part_shape),
        [ANY] * 4,
        cubes,
        [
            pltpu.VMEM(part_shape, BF16),
            pltpu.VMEM(rates.shape, F32),
            pltpu.SMEM(selected.shape, jnp.int32),
            pltpu.SemaphoreType.DMA((heads, 2)),
            pltpu.SemaphoreType.DMA((2,)),
            pltpu.SemaphoreType.DMA((heads,)),
        ],
        ANY,
        56,
    )(directions, keys, rates, selected)
    width = out_weight.shape[1] // planes
    early_shapes = [(out_weight.shape[0], width)] * (planes - 1) + [values.shape]
    *pieces, raw_values = call(
        functools.partial(early_kernel, axes, cores),
        [array(shape) for shape in early_shapes],
        [ANY] * 3,
        cubes,
        [pltpu.VMEM(shape, BF16) for shape in early_shapes]
        + [pltpu.SemaphoreType.DMA((planes,))] * 2,
        [ANY] * planes,
        56,
    )(out_weight, values, packed)
    weight_parts = []
    for offset in range(1, planes):
        turned = [(g, (g + head_size - cores * offset) % head_size) for g in range(head_size)]
        weight_parts.append(lax.ppermute(pieces[offset - 1], "head", turned))
    value_parts = [onward(raw_values, by) for by in range(1, before + 1)]
    parts = exchange(packed)

    end, tail, far, even, pair_map, group_map, mixed, away, *cut = call(
        functools.partial(keys_kernel, axes, blocks),
        [
            array((units, *tile)),
            array((units, *tile)),
            array((units, *tile)),
            array((pairs, 2, *tile)),
            array((pairs, 2, *tile)),
            array((2, *tile)),
            array((units, BLOCK, 2 * BLOCK)),
            array((units, HEAD_DIM), jnp.int32),
        ]
        + [array((2, tokens, HEAD_DIM))] * heads,
        [VMEM, ANY, ANY],
        400 * cubes,
        [
            pltpu.VMEM((heads, 2, tokens, HEAD_DIM), BF16),
            pltpu.SemaphoreType.DMA((heads, 2)),
            pltpu.SemaphoreType.DMA((heads,)),
        ],
        [VMEM] * 8 + [ANY] * heads,
    )(parts, queries, values)
    far_parts = [onward(far, by) for by in range(1, before + 1)]
    map_parts = [onward(group_map, by) for by in range(1, before)]
    arrived = [crossed(cut[turn], turn) for turn in range(heads)]
    arrived_values = []
    if before:
        cut = call(
            functools.partial(cut_kernel, axes),
            [array((before, tokens, HEAD_DIM))] * heads,
            [ANY] * (before + 1),
            1000 * cubes,
            [pltpu.SemaphoreType.DMA((heads, before))],
        )(*value_parts, away)
        arrived_values = [crossed(cut[turn], turn) for turn in range(heads)]
    inner, moving, *weight_parts = call(
        functools.partial(queries_kernel, axes, blocks, len(weight_parts)),
        [array((units, BLOCK, BLOCK), F32), array((units, pairs + 1, *tile))]
        + [array(part.shape) for part in weight_parts],
        [VMEM] * 4 + [ANY] * (heads + len(weight_parts)),
        200 * cubes,
        [
            pltpu.VMEM((heads, tokens, HEAD_DIM), BF16),
            pltpu.SemaphoreType.DMA((max(len(weight_parts), 1),)),
            pltpu.SemaphoreType.DMA((heads,)),
        ],
    )(parts, mixed, even, pair_map, *arrived, *weight_parts)
    all_values = call(
        functools.partial(order_kernel, axes),
        array((1 + before, heads, tokens, HEAD_DIM)),
        [ANY] * (heads + len(arrived_values)),
        0,
        [pltpu.SemaphoreType.DMA((heads, 1 + before))],
    )(*arrived, *arrived_values).reshape(1 + before, units, *tile)
    attended = call(
        functools.partial(attend_kernel, before, blocks),
        array((heads, planes, blocks, *tile)),
        [SMEM] + [VMEM] * (5 + before + len(map_parts)),
        200 * cubes,
    )(away, moving, inner, end, tail, all_values, *far_parts, *map_parts)

    returns = [
        [
            (group * heads + place) * head_size + p * cores + core
            for place in range(heads)
            for p in range(planes)
        ]
        for group in range(groups)
        for core in range(cores)
    ]
    local = lax.all_to_all(
        attended.reshape(heads * planes, blocks, *tile),
        axes, 0, 0, axis_index_groups=returns, tiled=True,
    ).reshape(heads, planes, blocks, *tile)

    def projected(other, kind):
        return call(
            functools.partial(project_kernel, axes, other, cores),
            array((tokens, width // cores), kind),
            [VMEM] * (1 + planes),
            128 * cubes,
        )(local, out_weight, *weight_parts)

    arrived = lax.ppermute(projected(1, BF16), "head", partners)
    return (projected(0, F32) + arrived.astype(F32)).astype(BF16)


def solution(mesh):
    in_specs = (
        P("ctx", "head"),
        P("ctx", "head"),
        P("ctx", "head"),
        P("ctx", "head"),
        P("head", "ctx"),
        P("ctx", None),
        P("head", None),
    )
    out_specs = P("ctx", "head")
    return jax.shard_map(
        functools.partial(body, mesh.shape["ctx"], mesh.shape["head"]),
        mesh=mesh,
        in_specs=in_specs,
        out_specs=out_specs,
        check_vma=False,
    )
```

```python
import functools

import jax
import jax.numpy as jnp
from jax import lax
from jax.experimental import pallas as pl
from jax.experimental.pallas import tpu as pltpu
from jax.sharding import PartitionSpec as P

HEAD_DIM = 128
BLOCK = 128
LOOK = 7
TOPK = 4
BASE = 16
EXTRA = 16
TERMS = 3
BF16 = jnp.bfloat16
F32 = jnp.float32
VMEM = pl.BlockSpec(memory_space=pltpu.VMEM)
SMEM = pl.BlockSpec(memory_space=pltpu.SMEM)
ANY = pl.BlockSpec(memory_space=pl.ANY)


def dot(left, right, left_dim, right_dim):
    return lax.dot_general(
        left, right, (((left_dim,), (right_dim,)), ((), ())), preferred_element_type=F32
    )


def nn(left, right):
    return dot(left, right, 1, 0)


def nt(left, right):
    return dot(left, right, 1, 1)


def tn(left, right):
    return dot(left, right, 0, 0)


def split(value):
    high = value.astype(BF16)
    return high, (value - high.astype(F32)).astype(BF16)


def triple(product, left, right):
    rows = left[0].shape[0]
    first = product(jnp.concatenate(left, 0), right[0])
    return first[:rows] + (first[rows:] + product(left[0], right[1]))


def square_iotas():
    rows = lax.broadcasted_iota(jnp.int32, (BLOCK, BLOCK), 0)
    columns = lax.broadcasted_iota(jnp.int32, (BLOCK, BLOCK), 1)
    return rows, columns


def fetched(sources, targets, sems):
    copies = []
    for index, (source, target) in enumerate(zip(sources, targets)):
        copies.append(pltpu.make_async_copy(source, target, sems.at[index]))
        copies[-1].start()
    return copies


def pack_kernel(axes, d_ref, k_ref, rates_hbm, selected_hbm, out_ref, parts_ref,
                rates_ref, selected_ref, sems, few_sems, out_sems):
    tokens = d_ref.shape[0]
    heads = d_ref.shape[1] // HEAD_DIM
    blocks = tokens // BLOCK
    first_block = lax.axis_index(axes[0]) * blocks
    few_copies = fetched([rates_hbm, selected_hbm], [rates_ref, selected_ref], few_sems)
    sources = (d_ref, k_ref)
    copies = []
    for head in range(heads):
        columns = pl.ds(head * HEAD_DIM, HEAD_DIM)
        for kind, source in enumerate(sources):
            copies.append(
                pltpu.make_async_copy(
                    source.at[:, columns],
                    parts_ref.at[head, pl.ds(kind * tokens, tokens)],
                    sems.at[head, kind],
                )
            )
            copies[-1].start()
    for copy in few_copies:
        copy.wait()
    row = lax.broadcasted_iota(jnp.int32, (EXTRA, HEAD_DIM), 0)
    lane = lax.broadcasted_iota(jnp.int32, (EXTRA, HEAD_DIM), 1)
    away = jnp.zeros((EXTRA, HEAD_DIM), jnp.int32)
    for block in range(blocks):
        for entry in range(TOPK):
            distance = first_block + block - selected_ref[block, entry]
            away = jnp.where((row == TERMS * blocks + block) & (lane == entry), distance, away)
    away = away.astype(F32)
    terms = []
    rest = rates_ref[...]
    for _ in range(TERMS):
        terms.append(rest.astype(BF16).astype(F32))
        rest = rest - terms[-1]
    out_copies = []
    for head in range(heads):
        extra = away
        for block in range(blocks):
            for index, term in enumerate(terms):
                piece = term[head:head + 1, block * BLOCK:(block + 1) * BLOCK]
                extra = jnp.where(row == TERMS * block + index, piece, extra)
        parts_ref[head, len(sources) * tokens:] = extra.astype(BF16)
        for copy in copies[len(sources) * head:len(sources) * (head + 1)]:
            copy.wait()
        out_copies.append(
            pltpu.make_async_copy(parts_ref.at[head], out_ref.at[head], out_sems.at[head])
        )
        out_copies[-1].start()
    for copy in out_copies:
        copy.wait()


def values_kernel(values_ref, after, out_ref, buffer_ref, sems):
    for copy in fetched([values_ref], [buffer_ref], sems.at[pl.ds(0, 1)]):
        copy.wait()
    for copy in fetched([buffer_ref], [out_ref], sems.at[pl.ds(1, 1)]):
        copy.wait()


def weights_kernel(axes, cores, weight_ref, after, *refs):
    count = (len(refs) - 2) // 2
    outs, buffers = refs[:count], refs[count:2 * count]
    sems, out_sems = refs[2 * count:]
    width = outs[0].shape[1]
    planes = weight_ref.shape[1] // width
    plane = lax.axis_index(axes[1]) // cores
    sources = []
    for offset in range(1, planes):
        start = lax.rem(plane + planes - offset, planes) * width
        sources.append(weight_ref.at[:, pl.ds(pl.multiple_of(start, width), width)])
    copies = fetched(sources, buffers, sems)
    out_copies = []
    for index, target in enumerate(outs):
        copies[index].wait()
        out_copies += fetched([buffers[index]], [target], out_sems.at[pl.ds(index, 1)])
    for copy in out_copies:
        copy.wait()


def cut_kernel(axes, *refs):
    sems = refs[-1]
    parts = refs[-1 - sems.shape[0]:-1]
    sources = refs[:sems.shape[1]]
    heads = sems.shape[0]
    place = lax.rem(lax.axis_index(axes[0]), heads)
    copies = []
    for turn in range(heads):
        cut = pl.multiple_of(lax.bitwise_xor(place, turn) * HEAD_DIM, HEAD_DIM)
        copies += fetched(
            [source.at[:, pl.ds(cut, HEAD_DIM)] for source in sources],
            [parts[turn].at[kind] for kind in range(len(sources))],
            sems.at[turn],
        )
    for copy in copies:
        copy.wait()


def rows_of(ref, blocks, unit, kind):
    start = (kind * blocks + unit % blocks) * BLOCK
    return ref[unit // blocks, start:start + BLOCK]


def base_inverse(strict):
    count = BLOCK // BASE
    moved = [
        pltpu.roll(strict[b * BASE:(b + 1) * BASE], (BLOCK - b * BASE) % BLOCK, 1)
        if b else strict[:BASE]
        for b in range(count)
    ]
    lanes = lax.broadcasted_iota(jnp.int32, (BASE // 2, BLOCK), 1)
    rows = lax.broadcasted_iota(jnp.int32, (BASE // 2, BLOCK), 0)
    half = BASE // 2
    parts = []
    for b in range(count):
        upper = (lanes == rows + b * BASE).astype(F32)
        lower = (lanes == rows + b * BASE + half).astype(F32)
        for step in range(BASE - 1):
            if step < half:
                source = upper[step:step + 1]
                if step < half - 1:
                    upper = upper - moved[b][:half, step:step + 1] * source
            else:
                source = lower[step - half:step - half + 1]
            lower = lower - moved[b][half:, step:step + 1] * source
        parts += [upper, lower]
    return jnp.concatenate(parts, 0)


def halves(value, size):
    parts = value.reshape(BLOCK // (2 * size), 2, size, BLOCK)
    return parts[:, 0].reshape(BLOCK // 2, BLOCK), parts[:, 1].reshape(BLOCK // 2, BLOCK)


def joined(first, second, size):
    shape = (BLOCK // (2 * size), 1, size, BLOCK)
    return jnp.concatenate([first.reshape(shape), second.reshape(shape)], 1).reshape(BLOCK, BLOCK)


def interleaved(steps, lag):
    running = list(steps)
    tick = 0
    while any(step is not None for step in running):
        for index, step in enumerate(running):
            if step is not None and tick >= index * lag:
                try:
                    next(step)
                except StopIteration:
                    running[index] = None
        tick += 1


def keys_kernel(blocks, part_ref, end_ref, tail_ref, far_ref, even_ref, pair_ref, group_ref,
                mixed_ref, away_ref):
    units = part_ref.shape[0] * blocks
    rows, columns = square_iotas()
    diagonal = rows == columns
    identity = diagonal.astype(F32)
    row = lax.broadcasted_iota(jnp.int32, (BLOCK // 2, BLOCK), 0)
    column = lax.broadcasted_iota(jnp.int32, (BLOCK // 2, BLOCK), 1)
    ends, maps = [None] * units, [None] * units

    def terms(unit):
        direction = rows_of(part_ref, blocks, unit, 0)
        key = rows_of(part_ref, blocks, unit, 1)
        extra = part_ref[unit // blocks, 2 * blocks * BLOCK:].astype(F32)
        first = TERMS * (unit % blocks)
        rate = extra[first:first + 1] + extra[first + 1:first + 2] + extra[first + 2:first + 3]
        listed = TERMS * blocks + unit % blocks
        away_ref[unit:unit + 1] = extra[listed:listed + 1].astype(jnp.int32)
        gram = nt(direction, direction)
        key_proj = jnp.where(rows > columns, nt(direction, key), 0.0).astype(BF16)
        squares = jnp.sum(jnp.where(diagonal, gram, 0.0), 0, keepdims=True)
        scale = lax.rsqrt(squares + 1e-06)
        scaled_rate = rate * scale
        scale_column = jnp.sum(jnp.where(diagonal, scale, 0.0), 1, keepdims=True)
        rate_column = jnp.sum(jnp.where(diagonal, scaled_rate, 0.0), 1, keepdims=True)
        strict = jnp.where(rows > columns, rate_column * gram * scale, 0.0)
        yield
        inverse = base_inverse(strict)
        yield
        size = BASE
        while size < BLOCK:
            inside = (row // size == column // (2 * size)) & (lax.rem(column, 2 * size) < size)
            corner = jnp.where(inside, halves(strict, size)[1], 0.0)
            below = triple(nn, split(corner), split(inverse))
            yield
            first_half, second = halves(inverse, size)
            padded = joined(jnp.zeros_like(below), below, size)
            second = second - triple(nn, split(second), split(padded))
            inverse = joined(first_half, second, size)
            size *= 2
            yield
        mixing = split(scale_column * inverse * scaled_rate)
        mixed = nn(jnp.concatenate(mixing, 0), jnp.concatenate([direction, key_proj], 1))
        mixed = split(mixed[:BLOCK] + mixed[BLOCK:])
        mixed_ref[unit] = mixed[0]
        yield
        behind = tn(jnp.concatenate([mixed[0], mixed[1][:, :BLOCK]], 1), direction)
        ends[unit] = key.astype(F32) - behind[BLOCK:2 * BLOCK]
        maps[unit] = split(identity - (behind[:BLOCK] + behind[2 * BLOCK:]))
        end_ref[unit] = ends[unit].astype(BF16)

    interleaved([terms(unit) for unit in range(units)], 1)
    pair_keys, pair_maps = [], []
    for pair in range(units // 2):
        even, odd = 2 * pair, 2 * pair + 1
        even_ref[pair, 0] = maps[even][0]
        even_ref[pair, 1] = maps[even][1]
        left = jnp.concatenate([ends[even].astype(BF16), *maps[even]], 0)
        both = nn(left, maps[odd][0])
        tail_ref[even] = both[:BLOCK].astype(BF16)
        tail_ref[odd] = ends[odd].astype(BF16)
        pair_keys.append(jnp.concatenate([both[:BLOCK], ends[odd]], 0))
        low = both[2 * BLOCK:] + nn(maps[even][0], maps[odd][1])
        pair_maps.append(split(both[BLOCK:2 * BLOCK] + low))
        pair_ref[pair, 0] = pair_maps[pair][0]
        pair_ref[pair, 1] = pair_maps[pair][1]
    onward = None
    for pair in reversed(range(units // 2)):
        far = pair_keys[pair]
        if onward is None:
            onward = pair_maps[pair]
        else:
            far = nn(far.astype(BF16), onward[0])
            onward = split(triple(nn, pair_maps[pair], onward))
        far_ref[2 * pair] = far[:BLOCK].astype(BF16)
        far_ref[2 * pair + 1] = far[BLOCK:].astype(BF16)
    group_ref[0] = onward[0]
    group_ref[1] = onward[1]


def queries_kernel(axes, blocks, count, part_ref, mixed_ref, even_ref, pair_ref, *refs):
    heads = part_ref.shape[0]
    units = heads * blocks
    arrived, weights = refs[:heads], refs[heads:heads + count]
    inner_ref, moving_ref, values_ref, *weight_refs = refs[-7 - count:-4]
    query_ref, sems, query_sems, value_sems = refs[-4:]
    place = lax.rem(lax.axis_index(axes[0]), heads)
    sources = [lax.bitwise_xor(place, turn) for turn in range(heads)]
    query_copies = fetched(
        [part.at[0] for part in arrived], [query_ref.at[source] for source in sources], query_sems
    )
    copies = fetched(weights, weight_refs, sems)
    for kind in range(values_ref.shape[0]):
        copies += fetched(
            [part.at[kind + 1] for part in arrived],
            [values_ref.at[kind, source] for source in sources],
            value_sems.at[kind],
        )
    for copy in query_copies:
        copy.wait()
    rows, columns = square_iotas()
    current = []
    for unit in range(units):
        direction = rows_of(part_ref, blocks, unit, 0)
        key = rows_of(part_ref, blocks, unit, 1)
        query = rows_of(query_ref, blocks, unit, 0)
        query_proj = split(jnp.where(rows >= columns, nt(query, direction), 0.0))
        ahead = nn(jnp.concatenate(query_proj, 0), mixed_ref[unit])
        ahead = ahead[:BLOCK] + ahead[BLOCK:]
        inner_ref[unit] = nt(query, key) - ahead[:, HEAD_DIM:]
        start = split(query.astype(F32) - ahead[:, :HEAD_DIM])
        moving_ref[unit, 0] = start[0]
        if unit % 2:
            pair = unit // 2
            start = split(triple(nt, start, (even_ref[pair, 0], even_ref[pair, 1])))
        moving_ref[unit, 1] = start[0]
        current.append(start)
    pairs = units // 2
    current = [
        tuple(jnp.concatenate([current[2 * pair][part], current[2 * pair + 1][part]], 0)
              for part in range(2))
        for pair in range(pairs)
    ]
    for step in range(2, pairs + 1):
        for pair in range(step - 1, pairs):
            passed = pair - step + 1
            current[pair] = split(
                triple(nt, current[pair], (pair_ref[passed, 0], pair_ref[passed, 1]))
            )
            moving_ref[2 * pair, step] = current[pair][0][:BLOCK]
            moving_ref[2 * pair + 1, step] = current[pair][0][BLOCK:]
    for copy in copies:
        copy.wait()


def listed_block(away_ref, unit, entry):
    away = away_ref[unit, entry]
    new = away > 0
    for other in range(1, entry):
        new = new & (away_ref[unit, other] != away)
    return unit - away, new


def earlier(source, ahead, units):
    return jnp.clip(source + ahead * units, 0, units - 1), source < (1 - ahead) * units


def attend_kernel(before, blocks, away_ref, moving_ref, inner_ref, end_ref, tail_ref,
                  values_ref, *refs):
    far_keys, group_maps, out_ref = refs[:before], refs[before:-1], refs[-1]
    units = inner_ref.shape[0]
    rows, columns = square_iotas()
    scale = HEAD_DIM ** (-0.5)

    def steps(unit):
        pair = unit // 2
        fronts = [moving_ref[unit, pair + 1]]
        for group_map in group_maps:
            passed = nt(fronts[-1], group_map[0]) + nt(fronts[-1], group_map[1])
            fronts.append(passed.astype(BF16))
        score_list = [jnp.where(rows >= columns, inner_ref[unit] * scale, -1e30)]
        value_list = [values_ref[0, unit]]
        for entry in range(1, TOPK):
            source, new = listed_block(away_ref, unit, entry)
            inside = jnp.maximum(source, 0)
            step = jnp.maximum(pair - inside // 2, 0)
            query = moving_ref[unit, step]
            key = jnp.where(step == 0, end_ref[inside], tail_ref[inside])
            value = values_ref[0, inside]
            for ahead in range(1, before + 1):
                place, here = earlier(source, ahead, units)
                query = jnp.where(here, fronts[ahead - 1], query)
                key = jnp.where(here, far_keys[ahead - 1][place], key)
                value = jnp.where(here, values_ref[ahead, place], value)
            score_list.append(jnp.where(new, nt(query, key) * scale, -1e30))
            value_list.append(value)
        yield
        scores = jnp.concatenate(score_list, 1)
        expos = jnp.exp(scores - jnp.max(scores, 1, keepdims=True))
        weights = (expos / jnp.sum(expos, 1, keepdims=True)).astype(BF16)
        yield
        blended = nn(weights, jnp.concatenate(value_list, 0)).astype(BF16)
        for plane in range(out_ref.shape[1]):
            out_ref[unit // blocks, plane, unit % blocks] = blended

    interleaved([steps(unit) for unit in range(units)], 1)


def project_kernel(axes, other, cores, attended_ref, own_ref, *refs):
    other_refs, out_ref = refs[:-1], refs[-1]
    heads, planes, blocks = attended_ref.shape[:3]
    index = lax.axis_index(axes[1])
    core, plane = lax.rem(index + other, cores), index // cores
    width = out_ref.shape[1]
    total = None
    for offset in range(planes):
        source = lax.rem(plane + offset, planes)
        attended = jnp.concatenate(
            [
                jnp.concatenate(
                    [attended_ref[head, source, block] for head in range(heads)], 1
                )
                for block in range(blocks)
            ],
            0,
        )
        if offset:
            start = pl.multiple_of(core * width, width)
            weight = other_refs[offset - 1][:, pl.ds(start, width)]
        else:
            start = pl.multiple_of((plane * cores + core) * width, width)
            weight = own_ref[:, pl.ds(start, width)]
        product = nn(attended, weight)
        total = product if total is None else total + product
    out_ref[...] = total.astype(out_ref.dtype)


def call(kernel, outs, specs, flops, scratch=(), places=None, space=32):
    if places is None:
        places = [VMEM] * len(outs) if isinstance(outs, list) else VMEM
    return pl.pallas_call(
        kernel,
        out_shape=outs,
        in_specs=specs,
        out_specs=places,
        scratch_shapes=list(scratch),
        compiler_params=pltpu.CompilerParams(vmem_limit_bytes=space * 2 ** 20),
        cost_estimate=pl.CostEstimate(flops=flops, bytes_accessed=2 ** 21, transcendentals=0),
    )


def body(ctx_size, head_size, queries, keys, values, directions, rates, selected, out_weight):
    tokens = queries.shape[0]
    blocks = tokens // BLOCK
    heads = queries.shape[1] // HEAD_DIM
    units = heads * blocks
    pairs = units // 2
    groups = ctx_size // heads
    before = min(groups - 1, -(-LOOK // heads))
    cores = 2
    planes = head_size // cores
    axes = ("ctx", "head")
    members = [[group * heads + place for place in range(heads)] for group in range(groups)]
    partners = [(g, g + 1 - 2 * (g % cores)) for g in range(head_size)]
    cubes = 2 * BLOCK ** 3
    tile = (BLOCK, HEAD_DIM)

    def exchange(value):
        return lax.all_to_all(value, "ctx", 0, 0, axis_index_groups=members, tiled=True)

    def onward(value, by):
        shift = by * heads
        return lax.ppermute(value, "ctx", [(i, i + shift) for i in range(ctx_size - shift)])

    def crossed(value, turn):
        pairs = [(i, i - i % heads + (i % heads ^ turn)) for i in range(ctx_size)]
        return lax.ppermute(value, "ctx", pairs) if turn else value

    def array(shape, kind=BF16):
        return jax.ShapeDtypeStruct(shape, kind)

    part_shape = (heads, 2 * tokens + EXTRA, HEAD_DIM)
    packed = call(
        functools.partial(pack_kernel, axes),
        array(part_shape),
        [ANY] * 4,
        cubes,
        [
            pltpu.VMEM(part_shape, BF16),
            pltpu.VMEM(rates.shape, F32),
            pltpu.SMEM(selected.shape, jnp.int32),
            pltpu.SemaphoreType.DMA((heads, 2)),
            pltpu.SemaphoreType.DMA((2,)),
            pltpu.SemaphoreType.DMA((heads,)),
        ],
        ANY,
        56,
    )(directions, keys, rates, selected)
    width = out_weight.shape[1] // planes
    raw_values = call(
        values_kernel,
        array(values.shape),
        [ANY] * 2,
        cubes,
        [pltpu.VMEM(values.shape, BF16), pltpu.SemaphoreType.DMA((2,))],
        ANY,
        56,
    )(values, packed)
    value_parts = [onward(raw_values, by) for by in range(1, before + 1)]
    weight_parts = []
    if planes > 1:
        piece_shape = (out_weight.shape[0], width)
        pieces = call(
            functools.partial(weights_kernel, axes, cores),
            [array(piece_shape)] * (planes - 1),
            [ANY] * 2,
            cubes,
            [pltpu.VMEM(piece_shape, BF16)] * (planes - 1)
            + [pltpu.SemaphoreType.DMA((planes - 1,))] * 2,
            [ANY] * (planes - 1),
            56,
        )(out_weight, raw_values)
    for offset in range(1, planes):
        turned = [(g, (g + head_size - cores * offset) % head_size) for g in range(head_size)]
        weight_parts.append(lax.ppermute(pieces[offset - 1], "head", turned))
    parts = exchange(packed)

    end, tail, far, even, pair_map, group_map, mixed, away = call(
        functools.partial(keys_kernel, blocks),
        [
            array((units, *tile)),
            array((units, *tile)),
            array((units, *tile)),
            array((pairs, 2, *tile)),
            array((pairs, 2, *tile)),
            array((2, *tile)),
            array((units, BLOCK, 2 * BLOCK)),
            array((units, HEAD_DIM), jnp.int32),
        ],
        [VMEM],
        400 * cubes,
    )(parts)
    far_parts = [onward(far, by) for by in range(1, before + 1)]
    map_parts = [onward(group_map, by) for by in range(1, before)]
    kinds = 2 + before
    cut = call(
        functools.partial(cut_kernel, axes),
        [array((kinds, tokens, HEAD_DIM))] * heads,
        [ANY] * (kinds + 1),
        2000 * cubes,
        [pltpu.SemaphoreType.DMA((heads, kinds))],
    )(queries, values, *value_parts, away)
    arrived = [crossed(cut[turn], turn) for turn in range(heads)]
    inner, moving, all_values, *weight_parts = call(
        functools.partial(queries_kernel, axes, blocks, len(weight_parts)),
        [
            array((units, BLOCK, BLOCK), F32),
            array((units, pairs + 1, *tile)),
            array((1 + before, heads, tokens, HEAD_DIM)),
        ]
        + [array(part.shape) for part in weight_parts],
        [VMEM] * 4 + [ANY] * (heads + len(weight_parts)),
        0,
        [
            pltpu.VMEM((heads, tokens, HEAD_DIM), BF16),
            pltpu.SemaphoreType.DMA((max(len(weight_parts), 1),)),
            pltpu.SemaphoreType.DMA((heads,)),
            pltpu.SemaphoreType.DMA((1 + before, heads)),
        ],
    )(parts, mixed, even, pair_map, *arrived, *weight_parts)
    all_values = all_values.reshape(1 + before, units, *tile)
    attended = call(
        functools.partial(attend_kernel, before, blocks),
        array((heads, planes, blocks, *tile)),
        [SMEM] + [VMEM] * (5 + before + len(map_parts)),
        200 * cubes,
    )(away, moving, inner, end, tail, all_values, *far_parts, *map_parts)

    returns = [
        [
            (group * heads + place) * head_size + p * cores + core
            for place in range(heads)
            for p in range(planes)
        ]
        for group in range(groups)
        for core in range(cores)
    ]
    local = lax.all_to_all(
        attended.reshape(heads * planes, blocks, *tile),
        axes, 0, 0, axis_index_groups=returns, tiled=True,
    ).reshape(heads, planes, blocks, *tile)

    def projected(other, kind):
        return call(
            functools.partial(project_kernel, axes, other, cores),
            array((tokens, width // cores), kind),
            [VMEM] * (1 + planes),
            128 * cubes,
        )(local, out_weight, *weight_parts)

    arrived = lax.ppermute(projected(1, BF16), "head", partners)
    return (projected(0, F32) + arrived.astype(F32)).astype(BF16)


def solution(mesh):
    in_specs = (
        P("ctx", "head"),
        P("ctx", "head"),
        P("ctx", "head"),
        P("ctx", "head"),
        P("head", "ctx"),
        P("ctx", None),
        P("head", None),
    )
    out_specs = P("ctx", "head")
    return jax.shard_map(
        functools.partial(body, mesh.shape["ctx"], mesh.shape["head"]),
        mesh=mesh,
        in_specs=in_specs,
        out_specs=out_specs,
        check_vma=False,
    )
```

```python
import functools

import jax
import jax.numpy as jnp
from jax import lax
from jax.experimental import pallas as pl
from jax.experimental.pallas import tpu as pltpu
from jax.sharding import PartitionSpec as P

HEAD_DIM = 128
BLOCK = 128
LOOK = 7
TOPK = 4
BASE = 16
EXTRA = 16
TERMS = 3
BF16 = jnp.bfloat16
F32 = jnp.float32
VMEM = pl.BlockSpec(memory_space=pltpu.VMEM)
SMEM = pl.BlockSpec(memory_space=pltpu.SMEM)
ANY = pl.BlockSpec(memory_space=pl.ANY)


def dot(left, right, left_dim, right_dim):
    return lax.dot_general(
        left, right, (((left_dim,), (right_dim,)), ((), ())), preferred_element_type=F32
    )


def nn(left, right):
    return dot(left, right, 1, 0)


def nt(left, right):
    return dot(left, right, 1, 1)


def tn(left, right):
    return dot(left, right, 0, 0)


def split(value):
    high = value.astype(BF16)
    return high, (value - high.astype(F32)).astype(BF16)


def triple(product, left, right):
    rows = left[0].shape[0]
    first = product(jnp.concatenate(left, 0), right[0])
    return first[:rows] + (first[rows:] + product(left[0], right[1]))


def square_iotas():
    rows = lax.broadcasted_iota(jnp.int32, (BLOCK, BLOCK), 0)
    columns = lax.broadcasted_iota(jnp.int32, (BLOCK, BLOCK), 1)
    return rows, columns


def fetched(sources, targets, sems):
    copies = []
    for index, (source, target) in enumerate(zip(sources, targets)):
        copies.append(pltpu.make_async_copy(source, target, sems.at[index]))
        copies[-1].start()
    return copies


def pack_kernel(axes, cores, d_ref, k_ref, rates_hbm, selected_hbm, values_ref, weight_ref,
                *refs):
    tokens = d_ref.shape[0]
    heads = d_ref.shape[1] // HEAD_DIM
    blocks = tokens // BLOCK
    (parts_ref, rates_ref, selected_ref, cut_ref, piece_ref, sems, few_sems, out_sems, cut_sems,
     cut_out_sems, piece_sems) = refs[-11:]
    out_ref, cut_outs, piece_outs = refs[0], refs[1:1 + heads], refs[1 + heads:-11]
    planes = len(piece_outs) + 1
    width = weight_ref.shape[1] // planes
    device = lax.axis_index(axes[0])
    place = lax.rem(device, heads)
    plane = lax.axis_index(axes[1]) // cores
    first_block = device * blocks
    few_copies = fetched([rates_hbm, selected_hbm], [rates_ref, selected_ref], few_sems)
    sources = (d_ref, k_ref)
    copies = []
    for head in range(heads):
        columns = pl.ds(head * HEAD_DIM, HEAD_DIM)
        for kind, source in enumerate(sources):
            copies.append(
                pltpu.make_async_copy(
                    source.at[:, columns],
                    parts_ref.at[head, pl.ds(kind * tokens, tokens)],
                    sems.at[head, kind],
                )
            )
            copies[-1].start()
    cuts = [
        pl.multiple_of(lax.bitwise_xor(place, turn) * HEAD_DIM, HEAD_DIM) for turn in range(heads)
    ]
    cut_copies = fetched(
        [values_ref.at[:, pl.ds(cut, HEAD_DIM)] for cut in cuts],
        [cut_ref.at[turn] for turn in range(heads)],
        cut_sems,
    )
    piece_copies = []
    for offset in range(1, planes):
        start = pl.multiple_of(lax.rem(plane + planes - offset, planes) * width, width)
        piece_copies += fetched(
            [weight_ref.at[:, pl.ds(start, width)]],
            [piece_ref.at[offset - 1]],
            piece_sems.at[0, pl.ds(offset - 1, 1)],
        )
    for copy in few_copies:
        copy.wait()
    row = lax.broadcasted_iota(jnp.int32, (EXTRA, HEAD_DIM), 0)
    lane = lax.broadcasted_iota(jnp.int32, (EXTRA, HEAD_DIM), 1)
    away = jnp.zeros((EXTRA, HEAD_DIM), jnp.int32)
    for block in range(blocks):
        for entry in range(TOPK):
            distance = first_block + block - selected_ref[block, entry]
            away = jnp.where((row == TERMS * blocks + block) & (lane == entry), distance, away)
    away = away.astype(F32)
    terms = []
    rest = rates_ref[...]
    for _ in range(TERMS):
        terms.append(rest.astype(BF16).astype(F32))
        rest = rest - terms[-1]
    out_copies = []
    for head in range(heads):
        extra = away
        for block in range(blocks):
            for index, term in enumerate(terms):
                piece = term[head:head + 1, block * BLOCK:(block + 1) * BLOCK]
                extra = jnp.where(row == TERMS * block + index, piece, extra)
        parts_ref[head, len(sources) * tokens:] = extra.astype(BF16)
        for copy in copies[len(sources) * head:len(sources) * (head + 1)]:
            copy.wait()
        out_copies.append(
            pltpu.make_async_copy(parts_ref.at[head], out_ref.at[head], out_sems.at[head])
        )
        out_copies[-1].start()
    for turn in range(heads):
        cut_copies[turn].wait()
        out_copies += fetched(
            [cut_ref.at[turn]], [cut_outs[turn]], cut_out_sems.at[pl.ds(turn, 1)]
        )
    for index, copy in enumerate(piece_copies):
        copy.wait()
        out_copies += fetched(
            [piece_ref.at[index]], [piece_outs[index]], piece_sems.at[1, pl.ds(index, 1)]
        )
    for copy in out_copies:
        copy.wait()


def cut_kernel(axes, *refs):
    sems = refs[-1]
    parts = refs[-1 - sems.shape[0]:-1]
    sources = refs[:sems.shape[1]]
    heads = sems.shape[0]
    place = lax.rem(lax.axis_index(axes[0]), heads)
    copies = []
    for turn in range(heads):
        cut = pl.multiple_of(lax.bitwise_xor(place, turn) * HEAD_DIM, HEAD_DIM)
        copies += fetched(
            [source.at[:, pl.ds(cut, HEAD_DIM)] for source in sources],
            [parts[turn].at[kind] for kind in range(len(sources))],
            sems.at[turn],
        )
    for copy in copies:
        copy.wait()


def rows_of(ref, blocks, unit, kind):
    start = (kind * blocks + unit % blocks) * BLOCK
    return ref[unit // blocks, start:start + BLOCK]


def base_inverse(strict):
    count = BLOCK // BASE
    moved = [
        pltpu.roll(strict[b * BASE:(b + 1) * BASE], (BLOCK - b * BASE) % BLOCK, 1)
        if b else strict[:BASE]
        for b in range(count)
    ]
    lanes = lax.broadcasted_iota(jnp.int32, (BASE // 2, BLOCK), 1)
    rows = lax.broadcasted_iota(jnp.int32, (BASE // 2, BLOCK), 0)
    half = BASE // 2
    parts = []
    for b in range(count):
        upper = (lanes == rows + b * BASE).astype(F32)
        lower = (lanes == rows + b * BASE + half).astype(F32)
        for step in range(BASE - 1):
            if step < half:
                source = upper[step:step + 1]
                if step < half - 1:
                    upper = upper - moved[b][:half, step:step + 1] * source
            else:
                source = lower[step - half:step - half + 1]
            lower = lower - moved[b][half:, step:step + 1] * source
        parts += [upper, lower]
    return jnp.concatenate(parts, 0)


def halves(value, size):
    parts = value.reshape(BLOCK // (2 * size), 2, size, BLOCK)
    return parts[:, 0].reshape(BLOCK // 2, BLOCK), parts[:, 1].reshape(BLOCK // 2, BLOCK)


def joined(first, second, size):
    shape = (BLOCK // (2 * size), 1, size, BLOCK)
    return jnp.concatenate([first.reshape(shape), second.reshape(shape)], 1).reshape(BLOCK, BLOCK)


def interleaved(steps, lag):
    running = list(steps)
    tick = 0
    while any(step is not None for step in running):
        for index, step in enumerate(running):
            if step is not None and tick >= index * lag:
                try:
                    next(step)
                except StopIteration:
                    running[index] = None
        tick += 1


def keys_kernel(blocks, part_ref, end_ref, tail_ref, far_ref, even_ref, pair_ref, group_ref,
                mixed_ref, away_ref):
    units = part_ref.shape[0] * blocks
    rows, columns = square_iotas()
    diagonal = rows == columns
    identity = diagonal.astype(F32)
    row = lax.broadcasted_iota(jnp.int32, (BLOCK // 2, BLOCK), 0)
    column = lax.broadcasted_iota(jnp.int32, (BLOCK // 2, BLOCK), 1)
    ends, maps = [None] * units, [None] * units

    def terms(unit):
        direction = rows_of(part_ref, blocks, unit, 0)
        key = rows_of(part_ref, blocks, unit, 1)
        extra = part_ref[unit // blocks, 2 * blocks * BLOCK:].astype(F32)
        first = TERMS * (unit % blocks)
        rate = extra[first:first + 1] + extra[first + 1:first + 2] + extra[first + 2:first + 3]
        listed = TERMS * blocks + unit % blocks
        away_ref[unit:unit + 1] = extra[listed:listed + 1].astype(jnp.int32)
        gram = nt(direction, direction)
        key_proj = jnp.where(rows > columns, nt(direction, key), 0.0).astype(BF16)
        squares = jnp.sum(jnp.where(diagonal, gram, 0.0), 0, keepdims=True)
        scale = lax.rsqrt(squares + 1e-06)
        scaled_rate = rate * scale
        scale_column = jnp.sum(jnp.where(diagonal, scale, 0.0), 1, keepdims=True)
        rate_column = jnp.sum(jnp.where(diagonal, scaled_rate, 0.0), 1, keepdims=True)
        strict = jnp.where(rows > columns, rate_column * gram * scale, 0.0)
        yield
        inverse = base_inverse(strict)
        yield
        size = BASE
        while size < BLOCK:
            inside = (row // size == column // (2 * size)) & (lax.rem(column, 2 * size) < size)
            corner = jnp.where(inside, halves(strict, size)[1], 0.0)
            below = triple(nn, split(corner), split(inverse))
            yield
            first_half, second = halves(inverse, size)
            padded = joined(jnp.zeros_like(below), below, size)
            second = second - triple(nn, split(second), split(padded))
            inverse = joined(first_half, second, size)
            size *= 2
            yield
        mixing = split(scale_column * inverse * scaled_rate)
        mixed = nn(jnp.concatenate(mixing, 0), jnp.concatenate([direction, key_proj], 1))
        mixed = split(mixed[:BLOCK] + mixed[BLOCK:])
        mixed_ref[unit] = mixed[0]
        yield
        behind = tn(jnp.concatenate([mixed[0], mixed[1][:, :BLOCK]], 1), direction)
        ends[unit] = key.astype(F32) - behind[BLOCK:2 * BLOCK]
        maps[unit] = split(identity - (behind[:BLOCK] + behind[2 * BLOCK:]))
        end_ref[unit] = ends[unit].astype(BF16)

    interleaved([terms(unit) for unit in range(units)], 1)
    pair_keys, pair_maps = [], []
    for pair in range(units // 2):
        even, odd = 2 * pair, 2 * pair + 1
        even_ref[pair, 0] = maps[even][0]
        even_ref[pair, 1] = maps[even][1]
        left = jnp.concatenate([ends[even].astype(BF16), *maps[even]], 0)
        both = nn(left, maps[odd][0])
        tail_ref[even] = both[:BLOCK].astype(BF16)
        tail_ref[odd] = ends[odd].astype(BF16)
        pair_keys.append(jnp.concatenate([both[:BLOCK], ends[odd]], 0))
        low = both[2 * BLOCK:] + nn(maps[even][0], maps[odd][1])
        pair_maps.append(split(both[BLOCK:2 * BLOCK] + low))
        pair_ref[pair, 0] = pair_maps[pair][0]
        pair_ref[pair, 1] = pair_maps[pair][1]
    onward = None
    for pair in reversed(range(units // 2)):
        far = pair_keys[pair]
        if onward is None:
            onward = pair_maps[pair]
        else:
            far = nn(far.astype(BF16), onward[0])
            onward = split(triple(nn, pair_maps[pair], onward))
        far_ref[2 * pair] = far[:BLOCK].astype(BF16)
        far_ref[2 * pair + 1] = far[BLOCK:].astype(BF16)
    group_ref[0] = onward[0]
    group_ref[1] = onward[1]


def queries_kernel(axes, blocks, count, part_ref, mixed_ref, even_ref, pair_ref, *refs):
    heads = part_ref.shape[0]
    units = heads * blocks
    arrived, weights = refs[:heads], refs[heads:heads + count]
    inner_ref, moving_ref, values_ref, *weight_refs = refs[-7 - count:-4]
    query_ref, sems, query_sems, value_sems = refs[-4:]
    place = lax.rem(lax.axis_index(axes[0]), heads)
    sources = [lax.bitwise_xor(place, turn) for turn in range(heads)]
    query_copies = fetched(
        [part.at[0] for part in arrived], [query_ref.at[source] for source in sources], query_sems
    )
    copies = fetched(weights, weight_refs, sems)
    straight = refs[heads + count:-7 - count]
    for kind in range(values_ref.shape[0]):
        copies += fetched(
            straight[(kind - 1) * heads:kind * heads] if kind else [part.at[1] for part in arrived],
            [values_ref.at[kind, source] for source in sources],
            value_sems.at[kind],
        )
    for copy in query_copies:
        copy.wait()
    rows, columns = square_iotas()
    current = []
    for unit in range(units):
        direction = rows_of(part_ref, blocks, unit, 0)
        key = rows_of(part_ref, blocks, unit, 1)
        query = rows_of(query_ref, blocks, unit, 0)
        query_proj = split(jnp.where(rows >= columns, nt(query, direction), 0.0))
        ahead = nn(jnp.concatenate(query_proj, 0), mixed_ref[unit])
        ahead = ahead[:BLOCK] + ahead[BLOCK:]
        inner_ref[unit] = nt(query, key) - ahead[:, HEAD_DIM:]
        start = split(query.astype(F32) - ahead[:, :HEAD_DIM])
        moving_ref[unit, 0] = start[0]
        if unit % 2:
            pair = unit // 2
            start = split(triple(nt, start, (even_ref[pair, 0], even_ref[pair, 1])))
        moving_ref[unit, 1] = start[0]
        current.append(start)
    pairs = units // 2
    current = [
        tuple(jnp.concatenate([current[2 * pair][part], current[2 * pair + 1][part]], 0)
              for part in range(2))
        for pair in range(pairs)
    ]
    for step in range(2, pairs + 1):
        for pair in range(step - 1, pairs):
            passed = pair - step + 1
            current[pair] = split(
                triple(nt, current[pair], (pair_ref[passed, 0], pair_ref[passed, 1]))
            )
            moving_ref[2 * pair, step] = current[pair][0][:BLOCK]
            moving_ref[2 * pair + 1, step] = current[pair][0][BLOCK:]
    for copy in copies:
        copy.wait()


def listed_block(away_ref, unit, entry):
    away = away_ref[unit, entry]
    new = away > 0
    for other in range(1, entry):
        new = new & (away_ref[unit, other] != away)
    return unit - away, new


def earlier(source, ahead, units):
    return jnp.clip(source + ahead * units, 0, units - 1), source < (1 - ahead) * units


def attend_kernel(before, blocks, away_ref, moving_ref, inner_ref, end_ref, tail_ref,
                  values_ref, *refs):
    far_keys, group_maps, out_ref = refs[:before], refs[before:-1], refs[-1]
    units = inner_ref.shape[0]
    rows, columns = square_iotas()
    scale = HEAD_DIM ** (-0.5)

    def steps(unit):
        pair = unit // 2
        fronts = [moving_ref[unit, pair + 1]]
        for group_map in group_maps:
            passed = nt(fronts[-1], group_map[0]) + nt(fronts[-1], group_map[1])
            fronts.append(passed.astype(BF16))
        score_list = [jnp.where(rows >= columns, inner_ref[unit] * scale, -1e30)]
        value_list = [values_ref[0, unit]]
        for entry in range(1, TOPK):
            source, new = listed_block(away_ref, unit, entry)
            inside = jnp.maximum(source, 0)
            step = jnp.maximum(pair - inside // 2, 0)
            query = moving_ref[unit, step]
            key = jnp.where(step == 0, end_ref[inside], tail_ref[inside])
            value = values_ref[0, inside]
            for ahead in range(1, before + 1):
                place, here = earlier(source, ahead, units)
                query = jnp.where(here, fronts[ahead - 1], query)
                key = jnp.where(here, far_keys[ahead - 1][place], key)
                value = jnp.where(here, values_ref[ahead, place], value)
            score_list.append(jnp.where(new, nt(query, key) * scale, -1e30))
            value_list.append(value)
        yield
        scores = jnp.concatenate(score_list, 1)
        expos = jnp.exp(scores - jnp.max(scores, 1, keepdims=True))
        weights = (expos / jnp.sum(expos, 1, keepdims=True)).astype(BF16)
        yield
        blended = nn(weights, jnp.concatenate(value_list, 0)).astype(BF16)
        for plane in range(out_ref.shape[1]):
            out_ref[unit // blocks, plane, unit % blocks] = blended

    interleaved([steps(unit) for unit in range(units)], 1)


def project_kernel(axes, other, cores, attended_ref, own_ref, *refs):
    other_refs, out_ref = refs[:-1], refs[-1]
    heads, planes, blocks = attended_ref.shape[:3]
    index = lax.axis_index(axes[1])
    core, plane = lax.rem(index + other, cores), index // cores
    width = out_ref.shape[1]
    total = None
    for offset in range(planes):
        source = lax.rem(plane + offset, planes)
        attended = jnp.concatenate(
            [
                jnp.concatenate(
                    [attended_ref[head, source, block] for head in range(heads)], 1
                )
                for block in range(blocks)
            ],
            0,
        )
        if offset:
            start = pl.multiple_of(core * width, width)
            weight = other_refs[offset - 1][:, pl.ds(start, width)]
        else:
            start = pl.multiple_of((plane * cores + core) * width, width)
            weight = own_ref[:, pl.ds(start, width)]
        product = nn(attended, weight)
        total = product if total is None else total + product
    out_ref[...] = total.astype(out_ref.dtype)


def call(kernel, outs, specs, flops, scratch=(), places=None, space=32):
    if places is None:
        places = [VMEM] * len(outs) if isinstance(outs, list) else VMEM
    return pl.pallas_call(
        kernel,
        out_shape=outs,
        in_specs=specs,
        out_specs=places,
        scratch_shapes=list(scratch),
        compiler_params=pltpu.CompilerParams(vmem_limit_bytes=space * 2 ** 20),
        cost_estimate=pl.CostEstimate(flops=flops, bytes_accessed=2 ** 21, transcendentals=0),
    )


def body(ctx_size, head_size, queries, keys, values, directions, rates, selected, out_weight):
    tokens = queries.shape[0]
    blocks = tokens // BLOCK
    heads = queries.shape[1] // HEAD_DIM
    units = heads * blocks
    pairs = units // 2
    groups = ctx_size // heads
    before = min(groups - 1, -(-LOOK // heads))
    cores = 2
    planes = head_size // cores
    axes = ("ctx", "head")
    members = [[group * heads + place for place in range(heads)] for group in range(groups)]
    partners = [(g, g + 1 - 2 * (g % cores)) for g in range(head_size)]
    cubes = 2 * BLOCK ** 3
    tile = (BLOCK, HEAD_DIM)

    def exchange(value):
        return lax.all_to_all(value, "ctx", 0, 0, axis_index_groups=members, tiled=True)

    def onward(value, by):
        shift = by * heads
        return lax.ppermute(value, "ctx", [(i, i + shift) for i in range(ctx_size - shift)])

    def crossed(value, turn):
        pairs = [(i, i - i % heads + (i % heads ^ turn)) for i in range(ctx_size)]
        return lax.ppermute(value, "ctx", pairs) if turn else value

    def straight(value, turn, by):
        shift = by * heads
        pairs = [(i, i - i % heads + (i % heads ^ turn) + shift) for i in range(ctx_size - shift)]
        return lax.ppermute(value, "ctx", pairs)

    def array(shape, kind=BF16):
        return jax.ShapeDtypeStruct(shape, kind)

    part_shape = (heads, 2 * tokens + EXTRA, HEAD_DIM)
    width = out_weight.shape[1] // planes
    piece_shape = (out_weight.shape[0], width)
    packed, *rest = call(
        functools.partial(pack_kernel, axes, cores),
        [array(part_shape)]
        + [array((tokens, HEAD_DIM))] * heads
        + [array(piece_shape)] * (planes - 1),
        [ANY] * 6,
        cubes,
        [
            pltpu.VMEM(part_shape, BF16),
            pltpu.VMEM(rates.shape, F32),
            pltpu.SMEM(selected.shape, jnp.int32),
            pltpu.VMEM((heads, tokens, HEAD_DIM), BF16),
            pltpu.VMEM((max(planes - 1, 1), *piece_shape), BF16),
            pltpu.SemaphoreType.DMA((heads, 2)),
            pltpu.SemaphoreType.DMA((2,)),
            pltpu.SemaphoreType.DMA((heads,)),
            pltpu.SemaphoreType.DMA((heads,)),
            pltpu.SemaphoreType.DMA((heads,)),
            pltpu.SemaphoreType.DMA((2, planes)),
        ],
        [ANY] * (heads + planes),
        56,
    )(directions, keys, rates, selected, values, out_weight)
    value_cuts, pieces = rest[:heads], rest[heads:]
    value_parts = [
        straight(value_cuts[turn], turn, by) for by in range(1, before + 1) for turn in range(heads)
    ]
    weight_parts = []
    for offset in range(1, planes):
        turned = [(g, (g + head_size - cores * offset) % head_size) for g in range(head_size)]
        weight_parts.append(lax.ppermute(pieces[offset - 1], "head", turned))
    parts = exchange(packed)

    end, tail, far, even, pair_map, group_map, mixed, away = call(
        functools.partial(keys_kernel, blocks),
        [
            array((units, *tile)),
            array((units, *tile)),
            array((units, *tile)),
            array((pairs, 2, *tile)),
            array((pairs, 2, *tile)),
            array((2, *tile)),
            array((units, BLOCK, 2 * BLOCK)),
            array((units, HEAD_DIM), jnp.int32),
        ],
        [VMEM],
        400 * cubes,
    )(parts)
    far_parts = [onward(far, by) for by in range(1, before + 1)]
    map_parts = [onward(group_map, by) for by in range(1, before)]
    kinds = 2
    cut = call(
        functools.partial(cut_kernel, axes),
        [array((kinds, tokens, HEAD_DIM))] * heads,
        [ANY] * (kinds + len(value_parts) + 1),
        2000 * cubes,
        [pltpu.SemaphoreType.DMA((heads, kinds))],
    )(queries, values, *value_parts, away)
    arrived = [crossed(cut[turn], turn) for turn in range(heads)]
    inner, moving, all_values, *weight_parts = call(
        functools.partial(queries_kernel, axes, blocks, len(weight_parts)),
        [
            array((units, BLOCK, BLOCK), F32),
            array((units, pairs + 1, *tile)),
            array((1 + before, heads, tokens, HEAD_DIM)),
        ]
        + [array(part.shape) for part in weight_parts],
        [VMEM] * 4 + [ANY] * (heads + len(weight_parts) + len(value_parts)),
        0,
        [
            pltpu.VMEM((heads, tokens, HEAD_DIM), BF16),
            pltpu.SemaphoreType.DMA((max(len(weight_parts), 1),)),
            pltpu.SemaphoreType.DMA((heads,)),
            pltpu.SemaphoreType.DMA((1 + before, heads)),
        ],
    )(parts, mixed, even, pair_map, *arrived, *weight_parts, *value_parts)
    all_values = all_values.reshape(1 + before, units, *tile)
    attended = call(
        functools.partial(attend_kernel, before, blocks),
        array((heads, planes, blocks, *tile)),
        [SMEM] + [VMEM] * (5 + before + len(map_parts)),
        200 * cubes,
    )(away, moving, inner, end, tail, all_values, *far_parts, *map_parts)

    returns = [
        [
            (group * heads + place) * head_size + p * cores + core
            for place in range(heads)
            for p in range(planes)
        ]
        for group in range(groups)
        for core in range(cores)
    ]
    local = lax.all_to_all(
        attended.reshape(heads * planes, blocks, *tile),
        axes, 0, 0, axis_index_groups=returns, tiled=True,
    ).reshape(heads, planes, blocks, *tile)

    def projected(other, kind):
        return call(
            functools.partial(project_kernel, axes, other, cores),
            array((tokens, width // cores), kind),
            [VMEM] * (1 + planes),
            128 * cubes,
        )(local, out_weight, *weight_parts)

    arrived = lax.ppermute(projected(1, BF16), "head", partners)
    return (projected(0, F32) + arrived.astype(F32)).astype(BF16)


def solution(mesh):
    in_specs = (
        P("ctx", "head"),
        P("ctx", "head"),
        P("ctx", "head"),
        P("ctx", "head"),
        P("head", "ctx"),
        P("ctx", None),
        P("head", None),
    )
    out_specs = P("ctx", "head")
    return jax.shard_map(
        functools.partial(body, mesh.shape["ctx"], mesh.shape["head"]),
        mesh=mesh,
        in_specs=in_specs,
        out_specs=out_specs,
        check_vma=False,
    )
```

```python
import functools

import jax
import jax.numpy as jnp
from jax import lax
from jax.experimental import pallas as pl
from jax.experimental.pallas import tpu as pltpu
from jax.sharding import PartitionSpec as P

HEAD_DIM = 128
BLOCK = 128
LOOK = 7
TOPK = 4
BASE = 16
EXTRA = 16
TERMS = 3
BF16 = jnp.bfloat16
F32 = jnp.float32
VMEM = pl.BlockSpec(memory_space=pltpu.VMEM)
SMEM = pl.BlockSpec(memory_space=pltpu.SMEM)
ANY = pl.BlockSpec(memory_space=pl.ANY)


def dot(left, right, left_dim, right_dim):
    return lax.dot_general(
        left, right, (((left_dim,), (right_dim,)), ((), ())), preferred_element_type=F32
    )


def nn(left, right):
    return dot(left, right, 1, 0)


def nt(left, right):
    return dot(left, right, 1, 1)


def tn(left, right):
    return dot(left, right, 0, 0)


def split(value):
    high = value.astype(BF16)
    return high, (value - high.astype(F32)).astype(BF16)


def triple(product, left, right):
    rows = left[0].shape[0]
    first = product(jnp.concatenate(left, 0), right[0])
    return first[:rows] + (first[rows:] + product(left[0], right[1]))


def square_iotas():
    rows = lax.broadcasted_iota(jnp.int32, (BLOCK, BLOCK), 0)
    columns = lax.broadcasted_iota(jnp.int32, (BLOCK, BLOCK), 1)
    return rows, columns


def fetched(sources, targets, sems):
    copies = []
    for index, (source, target) in enumerate(zip(sources, targets)):
        copies.append(pltpu.make_async_copy(source, target, sems.at[index]))
        copies[-1].start()
    return copies


def pack_kernel(axes, cores, d_ref, k_ref, q_ref, rates_hbm, selected_hbm, values_ref,
                weight_ref, *refs):
    tokens = d_ref.shape[0]
    heads = d_ref.shape[1] // HEAD_DIM
    blocks = tokens // BLOCK
    (parts_ref, rates_ref, selected_ref, cut_ref, piece_ref, sems, few_sems, out_sems, cut_sems,
     cut_out_sems, piece_sems) = refs[-11:]
    out_ref, cut_outs, piece_outs = refs[0], refs[1:1 + heads], refs[1 + heads:-11]
    planes = len(piece_outs) + 1
    width = weight_ref.shape[1] // planes
    device = lax.axis_index(axes[0])
    place = lax.rem(device, heads)
    plane = lax.axis_index(axes[1]) // cores
    first_block = device * blocks
    few_copies = fetched([rates_hbm, selected_hbm], [rates_ref, selected_ref], few_sems)
    sources = (d_ref, k_ref, q_ref)
    copies = []
    for head in range(heads):
        columns = pl.ds(head * HEAD_DIM, HEAD_DIM)
        for kind, source in enumerate(sources):
            copies.append(
                pltpu.make_async_copy(
                    source.at[:, columns],
                    parts_ref.at[head, pl.ds(kind * tokens, tokens)],
                    sems.at[head, kind],
                )
            )
            copies[-1].start()
    cuts = [
        pl.multiple_of(lax.bitwise_xor(place, turn) * HEAD_DIM, HEAD_DIM) for turn in range(heads)
    ]
    cut_copies = fetched(
        [values_ref.at[:, pl.ds(cut, HEAD_DIM)] for cut in cuts],
        [cut_ref.at[turn] for turn in range(heads)],
        cut_sems,
    )
    piece_copies = []
    for offset in range(1, planes):
        start = pl.multiple_of(lax.rem(plane + planes - offset, planes) * width, width)
        piece_copies += fetched(
            [weight_ref.at[:, pl.ds(start, width)]],
            [piece_ref.at[offset - 1]],
            piece_sems.at[0, pl.ds(offset - 1, 1)],
        )
    for copy in few_copies:
        copy.wait()
    row = lax.broadcasted_iota(jnp.int32, (EXTRA, HEAD_DIM), 0)
    lane = lax.broadcasted_iota(jnp.int32, (EXTRA, HEAD_DIM), 1)
    away = jnp.zeros((EXTRA, HEAD_DIM), jnp.int32)
    for block in range(blocks):
        for entry in range(TOPK):
            distance = first_block + block - selected_ref[block, entry]
            away = jnp.where((row == TERMS * blocks + block) & (lane == entry), distance, away)
    away = away.astype(F32)
    terms = []
    rest = rates_ref[...]
    for _ in range(TERMS):
        terms.append(rest.astype(BF16).astype(F32))
        rest = rest - terms[-1]
    out_copies = []
    for head in range(heads):
        extra = away
        for block in range(blocks):
            for index, term in enumerate(terms):
                piece = term[head:head + 1, block * BLOCK:(block + 1) * BLOCK]
                extra = jnp.where(row == TERMS * block + index, piece, extra)
        parts_ref[head, len(sources) * tokens:] = extra.astype(BF16)
        for copy in copies[len(sources) * head:len(sources) * (head + 1)]:
            copy.wait()
        out_copies.append(
            pltpu.make_async_copy(parts_ref.at[head], out_ref.at[head], out_sems.at[head])
        )
        out_copies[-1].start()
    for turn in range(heads):
        cut_copies[turn].wait()
        out_copies += fetched(
            [cut_ref.at[turn]], [cut_outs[turn]], cut_out_sems.at[pl.ds(turn, 1)]
        )
    for index, copy in enumerate(piece_copies):
        copy.wait()
        out_copies += fetched(
            [piece_ref.at[index]], [piece_outs[index]], piece_sems.at[1, pl.ds(index, 1)]
        )
    for copy in out_copies:
        copy.wait()


def cut_kernel(axes, values_ref, *refs):
    sems = refs[-1]
    heads = sems.shape[0]
    place = lax.rem(lax.axis_index(axes[0]), heads)
    cuts = [
        pl.multiple_of(lax.bitwise_xor(place, turn) * HEAD_DIM, HEAD_DIM) for turn in range(heads)
    ]
    copies = fetched(
        [values_ref.at[:, pl.ds(cut, HEAD_DIM)] for cut in cuts], refs[-1 - heads:-1], sems
    )
    for copy in copies:
        copy.wait()


def rows_of(ref, blocks, unit, kind):
    start = (kind * blocks + unit % blocks) * BLOCK
    return ref[unit // blocks, start:start + BLOCK]


def base_inverse(strict):
    count = BLOCK // BASE
    moved = [
        pltpu.roll(strict[b * BASE:(b + 1) * BASE], (BLOCK - b * BASE) % BLOCK, 1)
        if b else strict[:BASE]
        for b in range(count)
    ]
    lanes = lax.broadcasted_iota(jnp.int32, (BASE // 2, BLOCK), 1)
    rows = lax.broadcasted_iota(jnp.int32, (BASE // 2, BLOCK), 0)
    half = BASE // 2
    parts = []
    for b in range(count):
        upper = (lanes == rows + b * BASE).astype(F32)
        lower = (lanes == rows + b * BASE + half).astype(F32)
        for step in range(BASE - 1):
            if step < half:
                source = upper[step:step + 1]
                if step < half - 1:
                    upper = upper - moved[b][:half, step:step + 1] * source
            else:
                source = lower[step - half:step - half + 1]
            lower = lower - moved[b][half:, step:step + 1] * source
        parts += [upper, lower]
    return jnp.concatenate(parts, 0)


def halves(value, size):
    parts = value.reshape(BLOCK // (2 * size), 2, size, BLOCK)
    return parts[:, 0].reshape(BLOCK // 2, BLOCK), parts[:, 1].reshape(BLOCK // 2, BLOCK)


def joined(first, second, size):
    shape = (BLOCK // (2 * size), 1, size, BLOCK)
    return jnp.concatenate([first.reshape(shape), second.reshape(shape)], 1).reshape(BLOCK, BLOCK)


def interleaved(steps, lag):
    running = list(steps)
    tick = 0
    while any(step is not None for step in running):
        for index, step in enumerate(running):
            if step is not None and tick >= index * lag:
                try:
                    next(step)
                except StopIteration:
                    running[index] = None
        tick += 1


def keys_kernel(blocks, part_ref, end_ref, tail_ref, far_ref, even_ref, pair_ref, group_ref,
                mixed_ref, away_ref):
    units = part_ref.shape[0] * blocks
    rows, columns = square_iotas()
    diagonal = rows == columns
    identity = diagonal.astype(F32)
    row = lax.broadcasted_iota(jnp.int32, (BLOCK // 2, BLOCK), 0)
    column = lax.broadcasted_iota(jnp.int32, (BLOCK // 2, BLOCK), 1)
    ends, maps = [None] * units, [None] * units

    def terms(unit):
        direction = rows_of(part_ref, blocks, unit, 0)
        key = rows_of(part_ref, blocks, unit, 1)
        extra = part_ref[unit // blocks, 3 * blocks * BLOCK:].astype(F32)
        first = TERMS * (unit % blocks)
        rate = extra[first:first + 1] + extra[first + 1:first + 2] + extra[first + 2:first + 3]
        listed = TERMS * blocks + unit % blocks
        away_ref[unit:unit + 1] = extra[listed:listed + 1].astype(jnp.int32)
        gram = nt(direction, direction)
        key_proj = jnp.where(rows > columns, nt(direction, key), 0.0).astype(BF16)
        squares = jnp.sum(jnp.where(diagonal, gram, 0.0), 0, keepdims=True)
        scale = lax.rsqrt(squares + 1e-06)
        scaled_rate = rate * scale
        scale_column = jnp.sum(jnp.where(diagonal, scale, 0.0), 1, keepdims=True)
        rate_column = jnp.sum(jnp.where(diagonal, scaled_rate, 0.0), 1, keepdims=True)
        strict = jnp.where(rows > columns, rate_column * gram * scale, 0.0)
        yield
        inverse = base_inverse(strict)
        yield
        size = BASE
        while size < BLOCK:
            inside = (row // size == column // (2 * size)) & (lax.rem(column, 2 * size) < size)
            corner = jnp.where(inside, halves(strict, size)[1], 0.0)
            below = triple(nn, split(corner), split(inverse))
            yield
            first_half, second = halves(inverse, size)
            padded = joined(jnp.zeros_like(below), below, size)
            second = second - triple(nn, split(second), split(padded))
            inverse = joined(first_half, second, size)
            size *= 2
            yield
        mixing = split(scale_column * inverse * scaled_rate)
        mixed = nn(jnp.concatenate(mixing, 0), jnp.concatenate([direction, key_proj], 1))
        mixed = split(mixed[:BLOCK] + mixed[BLOCK:])
        mixed_ref[unit] = mixed[0]
        yield
        behind = tn(jnp.concatenate([mixed[0], mixed[1][:, :BLOCK]], 1), direction)
        ends[unit] = key.astype(F32) - behind[BLOCK:2 * BLOCK]
        maps[unit] = split(identity - (behind[:BLOCK] + behind[2 * BLOCK:]))
        end_ref[unit] = ends[unit].astype(BF16)

    interleaved([terms(unit) for unit in range(units)], 1)
    pair_keys, pair_maps = [], []
    for pair in range(units // 2):
        even, odd = 2 * pair, 2 * pair + 1
        even_ref[pair, 0] = maps[even][0]
        even_ref[pair, 1] = maps[even][1]
        left = jnp.concatenate([ends[even].astype(BF16), *maps[even]], 0)
        both = nn(left, maps[odd][0])
        tail_ref[even] = both[:BLOCK].astype(BF16)
        tail_ref[odd] = ends[odd].astype(BF16)
        pair_keys.append(jnp.concatenate([both[:BLOCK], ends[odd]], 0))
        low = both[2 * BLOCK:] + nn(maps[even][0], maps[odd][1])
        pair_maps.append(split(both[BLOCK:2 * BLOCK] + low))
        pair_ref[pair, 0] = pair_maps[pair][0]
        pair_ref[pair, 1] = pair_maps[pair][1]
    onward = None
    for pair in reversed(range(units // 2)):
        far = pair_keys[pair]
        if onward is None:
            onward = pair_maps[pair]
        else:
            far = nn(far.astype(BF16), onward[0])
            onward = split(triple(nn, pair_maps[pair], onward))
        far_ref[2 * pair] = far[:BLOCK].astype(BF16)
        far_ref[2 * pair + 1] = far[BLOCK:].astype(BF16)
    group_ref[0] = onward[0]
    group_ref[1] = onward[1]


def queries_kernel(axes, blocks, part_ref, mixed_ref, even_ref, pair_ref, *refs):
    heads = part_ref.shape[0]
    units = heads * blocks
    inner_ref, moving_ref, values_ref, sems = refs[-4:]
    place = lax.rem(lax.axis_index(axes[0]), heads)
    copies = []
    for kind in range(values_ref.shape[0]):
        copies += fetched(
            refs[kind * heads:(kind + 1) * heads],
            [values_ref.at[kind, lax.bitwise_xor(place, turn)] for turn in range(heads)],
            sems.at[kind],
        )
    rows, columns = square_iotas()
    current = []
    for unit in range(units):
        direction = rows_of(part_ref, blocks, unit, 0)
        key = rows_of(part_ref, blocks, unit, 1)
        query = rows_of(part_ref, blocks, unit, 2)
        query_proj = split(jnp.where(rows >= columns, nt(query, direction), 0.0))
        ahead = nn(jnp.concatenate(query_proj, 0), mixed_ref[unit])
        ahead = ahead[:BLOCK] + ahead[BLOCK:]
        inner_ref[unit] = nt(query, key) - ahead[:, HEAD_DIM:]
        start = split(query.astype(F32) - ahead[:, :HEAD_DIM])
        moving_ref[unit, 0] = start[0]
        if unit % 2:
            pair = unit // 2
            start = split(triple(nt, start, (even_ref[pair, 0], even_ref[pair, 1])))
        moving_ref[unit, 1] = start[0]
        current.append(start)
    pairs = units // 2
    current = [
        tuple(jnp.concatenate([current[2 * pair][part], current[2 * pair + 1][part]], 0)
              for part in range(2))
        for pair in range(pairs)
    ]
    for step in range(2, pairs + 1):
        for pair in range(step - 1, pairs):
            passed = pair - step + 1
            current[pair] = split(
                triple(nt, current[pair], (pair_ref[passed, 0], pair_ref[passed, 1]))
            )
            moving_ref[2 * pair, step] = current[pair][0][:BLOCK]
            moving_ref[2 * pair + 1, step] = current[pair][0][BLOCK:]
    for copy in copies:
        copy.wait()


def listed_block(away_ref, unit, entry):
    away = away_ref[unit, entry]
    new = away > 0
    for other in range(1, entry):
        new = new & (away_ref[unit, other] != away)
    return unit - away, new


def earlier(source, ahead, units):
    return jnp.clip(source + ahead * units, 0, units - 1), source < (1 - ahead) * units


def attend_kernel(before, blocks, away_ref, moving_ref, inner_ref, end_ref, tail_ref,
                  values_ref, *refs):
    maps = max(before - 1, 0)
    far_keys, group_maps = refs[:before], refs[before:before + maps]
    count = (len(refs) - before - maps - 2) // 2
    out_ref, sems = refs[-2 - count], refs[-1]
    copies = fetched(refs[before + maps:before + maps + count], refs[-1 - count:-1], sems)
    units = inner_ref.shape[0]
    rows, columns = square_iotas()
    scale = HEAD_DIM ** (-0.5)

    def steps(unit):
        pair = unit // 2
        fronts = [moving_ref[unit, pair + 1]]
        for group_map in group_maps:
            passed = nt(fronts[-1], group_map[0]) + nt(fronts[-1], group_map[1])
            fronts.append(passed.astype(BF16))
        score_list = [jnp.where(rows >= columns, inner_ref[unit] * scale, -1e30)]
        value_list = [values_ref[0, unit]]
        for entry in range(1, TOPK):
            source, new = listed_block(away_ref, unit, entry)
            inside = jnp.maximum(source, 0)
            step = jnp.maximum(pair - inside // 2, 0)
            query = moving_ref[unit, step]
            key = jnp.where(step == 0, end_ref[inside], tail_ref[inside])
            value = values_ref[0, inside]
            for ahead in range(1, before + 1):
                place, here = earlier(source, ahead, units)
                query = jnp.where(here, fronts[ahead - 1], query)
                key = jnp.where(here, far_keys[ahead - 1][place], key)
                value = jnp.where(here, values_ref[ahead, place], value)
            score_list.append(jnp.where(new, nt(query, key) * scale, -1e30))
            value_list.append(value)
        yield
        scores = jnp.concatenate(score_list, 1)
        expos = jnp.exp(scores - jnp.max(scores, 1, keepdims=True))
        weights = (expos / jnp.sum(expos, 1, keepdims=True)).astype(BF16)
        yield
        blended = nn(weights, jnp.concatenate(value_list, 0)).astype(BF16)
        for plane in range(out_ref.shape[1]):
            out_ref[unit // blocks, plane, unit % blocks] = blended

    interleaved([steps(unit) for unit in range(units)], 1)
    for copy in copies:
        copy.wait()


def project_kernel(axes, other, cores, attended_ref, own_ref, *refs):
    other_refs, out_ref = refs[:-1], refs[-1]
    heads, planes, blocks = attended_ref.shape[:3]
    index = lax.axis_index(axes[1])
    core, plane = lax.rem(index + other, cores), index // cores
    width = out_ref.shape[1]
    total = None
    for offset in range(planes):
        source = lax.rem(plane + offset, planes)
        attended = jnp.concatenate(
            [
                jnp.concatenate(
                    [attended_ref[head, source, block] for head in range(heads)], 1
                )
                for block in range(blocks)
            ],
            0,
        )
        if offset:
            start = pl.multiple_of(core * width, width)
            weight = other_refs[offset - 1][:, pl.ds(start, width)]
        else:
            start = pl.multiple_of((plane * cores + core) * width, width)
            weight = own_ref[:, pl.ds(start, width)]
        product = nn(attended, weight)
        total = product if total is None else total + product
    out_ref[...] = total.astype(out_ref.dtype)


def call(kernel, outs, specs, flops, scratch=(), places=None, space=32):
    if places is None:
        places = [VMEM] * len(outs) if isinstance(outs, list) else VMEM
    return pl.pallas_call(
        kernel,
        out_shape=outs,
        in_specs=specs,
        out_specs=places,
        scratch_shapes=list(scratch),
        compiler_params=pltpu.CompilerParams(vmem_limit_bytes=space * 2 ** 20),
        cost_estimate=pl.CostEstimate(flops=flops, bytes_accessed=2 ** 21, transcendentals=0),
    )


def body(ctx_size, head_size, queries, keys, values, directions, rates, selected, out_weight):
    tokens = queries.shape[0]
    blocks = tokens // BLOCK
    heads = queries.shape[1] // HEAD_DIM
    units = heads * blocks
    pairs = units // 2
    groups = ctx_size // heads
    before = min(groups - 1, -(-LOOK // heads))
    cores = 2
    planes = head_size // cores
    axes = ("ctx", "head")
    members = [[group * heads + place for place in range(heads)] for group in range(groups)]
    partners = [(g, g + 1 - 2 * (g % cores)) for g in range(head_size)]
    cubes = 2 * BLOCK ** 3
    tile = (BLOCK, HEAD_DIM)

    def exchange(value):
        return lax.all_to_all(value, "ctx", 0, 0, axis_index_groups=members, tiled=True)

    def onward(value, by):
        shift = by * heads
        return lax.ppermute(value, "ctx", [(i, i + shift) for i in range(ctx_size - shift)])

    def crossed(value, turn):
        pairs = [(i, i - i % heads + (i % heads ^ turn)) for i in range(ctx_size)]
        return lax.ppermute(value, "ctx", pairs) if turn else value

    def straight(value, turn, by):
        shift = by * heads
        pairs = [(i, i - i % heads + (i % heads ^ turn) + shift) for i in range(ctx_size - shift)]
        return lax.ppermute(value, "ctx", pairs)

    def array(shape, kind=BF16):
        return jax.ShapeDtypeStruct(shape, kind)

    part_shape = (heads, 3 * tokens + EXTRA, HEAD_DIM)
    width = out_weight.shape[1] // planes
    piece_shape = (out_weight.shape[0], width)
    packed, *rest = call(
        functools.partial(pack_kernel, axes, cores),
        [array(part_shape)]
        + [array((tokens, HEAD_DIM))] * heads
        + [array(piece_shape)] * (planes - 1),
        [ANY] * 7,
        cubes,
        [
            pltpu.VMEM(part_shape, BF16),
            pltpu.VMEM(rates.shape, F32),
            pltpu.SMEM(selected.shape, jnp.int32),
            pltpu.VMEM((heads, tokens, HEAD_DIM), BF16),
            pltpu.VMEM((max(planes - 1, 1), *piece_shape), BF16),
            pltpu.SemaphoreType.DMA((heads, 3)),
            pltpu.SemaphoreType.DMA((2,)),
            pltpu.SemaphoreType.DMA((heads,)),
            pltpu.SemaphoreType.DMA((heads,)),
            pltpu.SemaphoreType.DMA((heads,)),
            pltpu.SemaphoreType.DMA((2, planes)),
        ],
        [ANY] * (heads + planes),
        56,
    )(directions, keys, queries, rates, selected, values, out_weight)
    value_cuts, pieces = rest[:heads], rest[heads:]
    value_parts = [
        straight(value_cuts[turn], turn, by) for by in range(1, before + 1) for turn in range(heads)
    ]
    weight_parts = []
    for offset in range(1, planes):
        turned = [(g, (g + head_size - cores * offset) % head_size) for g in range(head_size)]
        weight_parts.append(lax.ppermute(pieces[offset - 1], "head", turned))
    parts = exchange(packed)

    end, tail, far, even, pair_map, group_map, mixed, away = call(
        functools.partial(keys_kernel, blocks),
        [
            array((units, *tile)),
            array((units, *tile)),
            array((units, *tile)),
            array((pairs, 2, *tile)),
            array((pairs, 2, *tile)),
            array((2, *tile)),
            array((units, BLOCK, 2 * BLOCK)),
            array((units, HEAD_DIM), jnp.int32),
        ],
        [VMEM],
        400 * cubes,
    )(parts)
    far_parts = [onward(far, by) for by in range(1, before + 1)]
    map_parts = [onward(group_map, by) for by in range(1, before)]
    cut = call(
        functools.partial(cut_kernel, axes),
        [array((tokens, HEAD_DIM))] * heads,
        [ANY] * (len(value_parts) + 2),
        2000 * cubes,
        [pltpu.SemaphoreType.DMA((heads,))],
    )(values, *value_parts, away)
    own_parts = [crossed(cut[turn], turn) for turn in range(heads)]
    inner, moving, all_values = call(
        functools.partial(queries_kernel, axes, blocks),
        [
            array((units, BLOCK, BLOCK), F32),
            array((units, pairs + 1, *tile)),
            array((1 + before, heads, tokens, HEAD_DIM)),
        ],
        [VMEM] * 4 + [ANY] * (heads + len(value_parts)),
        0,
        [pltpu.SemaphoreType.DMA((1 + before, heads))],
    )(parts, mixed, even, pair_map, *own_parts, *value_parts)
    all_values = all_values.reshape(1 + before, units, *tile)
    attended, *weight_parts = call(
        functools.partial(attend_kernel, before, blocks),
        [array((heads, planes, blocks, *tile))] + [array(part.shape) for part in weight_parts],
        [SMEM] + [VMEM] * (5 + before + len(map_parts)) + [ANY] * len(weight_parts),
        200 * cubes,
        [pltpu.SemaphoreType.DMA((planes,))],
    )(away, moving, inner, end, tail, all_values, *far_parts, *map_parts, *weight_parts)

    returns = [
        [
            (group * heads + place) * head_size + p * cores + core
            for place in range(heads)
            for p in range(planes)
        ]
        for group in range(groups)
        for core in range(cores)
    ]
    local = lax.all_to_all(
        attended.reshape(heads * planes, blocks, *tile),
        axes, 0, 0, axis_index_groups=returns, tiled=True,
    ).reshape(heads, planes, blocks, *tile)

    def projected(other, kind):
        return call(
            functools.partial(project_kernel, axes, other, cores),
            array((tokens, width // cores), kind),
            [VMEM] * (1 + planes),
            128 * cubes,
        )(local, out_weight, *weight_parts)

    arrived = lax.ppermute(projected(1, BF16), "head", partners)
    return (projected(0, F32) + arrived.astype(F32)).astype(BF16)


def solution(mesh):
    in_specs = (
        P("ctx", "head"),
        P("ctx", "head"),
        P("ctx", "head"),
        P("ctx", "head"),
        P("head", "ctx"),
        P("ctx", None),
        P("head", None),
    )
    out_specs = P("ctx", "head")
    return jax.shard_map(
        functools.partial(body, mesh.shape["ctx"], mesh.shape["head"]),
        mesh=mesh,
        in_specs=in_specs,
        out_specs=out_specs,
        check_vma=False,
    )
```

```python
import functools

import jax
import jax.numpy as jnp
from jax import lax
from jax.experimental import pallas as pl
from jax.experimental.pallas import tpu as pltpu
from jax.sharding import PartitionSpec as P

HEAD_DIM = 128
BLOCK = 128
LOOK = 7
TOPK = 4
BASE = 16
EXTRA = 16
TERMS = 3
BF16 = jnp.bfloat16
F32 = jnp.float32
VMEM = pl.BlockSpec(memory_space=pltpu.VMEM)
SMEM = pl.BlockSpec(memory_space=pltpu.SMEM)
ANY = pl.BlockSpec(memory_space=pl.ANY)


def dot(left, right, left_dim, right_dim):
    return lax.dot_general(
        left, right, (((left_dim,), (right_dim,)), ((), ())), preferred_element_type=F32
    )


def nn(left, right):
    return dot(left, right, 1, 0)


def nt(left, right):
    return dot(left, right, 1, 1)


def tn(left, right):
    return dot(left, right, 0, 0)


def split(value):
    high = value.astype(BF16)
    return high, (value - high.astype(F32)).astype(BF16)


def triple(product, left, right):
    rows = left[0].shape[0]
    first = product(jnp.concatenate(left, 0), right[0])
    return first[:rows] + (first[rows:] + product(left[0], right[1]))


def square_iotas():
    rows = lax.broadcasted_iota(jnp.int32, (BLOCK, BLOCK), 0)
    columns = lax.broadcasted_iota(jnp.int32, (BLOCK, BLOCK), 1)
    return rows, columns


def fetched(sources, targets, sems):
    copies = []
    for index, (source, target) in enumerate(zip(sources, targets)):
        copies.append(pltpu.make_async_copy(source, target, sems.at[index]))
        copies[-1].start()
    return copies


def pack_kernel(axes, cores, d_ref, k_ref, rates_hbm, selected_hbm, values_ref, weight_ref,
                *refs):
    tokens = d_ref.shape[0]
    heads = d_ref.shape[1] // HEAD_DIM
    blocks = tokens // BLOCK
    (parts_ref, rates_ref, selected_ref, cut_ref, piece_ref, sems, few_sems, out_sems, cut_sems,
     cut_out_sems, piece_sems) = refs[-11:]
    out_ref, cut_outs, piece_outs = refs[0], refs[1:1 + heads], refs[1 + heads:-11]
    planes = len(piece_outs) + 1
    width = weight_ref.shape[1] // planes
    device = lax.axis_index(axes[0])
    place = lax.rem(device, heads)
    plane = lax.axis_index(axes[1]) // cores
    first_block = device * blocks
    few_copies = fetched([rates_hbm, selected_hbm], [rates_ref, selected_ref], few_sems)
    sources = (d_ref, k_ref)
    copies = []
    for head in range(heads):
        columns = pl.ds(head * HEAD_DIM, HEAD_DIM)
        for kind, source in enumerate(sources):
            copies.append(
                pltpu.make_async_copy(
                    source.at[:, columns],
                    parts_ref.at[head, pl.ds(kind * tokens, tokens)],
                    sems.at[head, kind],
                )
            )
            copies[-1].start()
    cuts = [
        pl.multiple_of(lax.bitwise_xor(place, turn) * HEAD_DIM, HEAD_DIM) for turn in range(heads)
    ]
    cut_copies = fetched(
        [values_ref.at[:, pl.ds(cut, HEAD_DIM)] for cut in cuts],
        [cut_ref.at[turn] for turn in range(heads)],
        cut_sems,
    )
    piece_copies = []
    for offset in range(1, planes):
        start = pl.multiple_of(lax.rem(plane + planes - offset, planes) * width, width)
        piece_copies += fetched(
            [weight_ref.at[:, pl.ds(start, width)]],
            [piece_ref.at[offset - 1]],
            piece_sems.at[0, pl.ds(offset - 1, 1)],
        )
    for copy in few_copies:
        copy.wait()
    row = lax.broadcasted_iota(jnp.int32, (EXTRA, HEAD_DIM), 0)
    lane = lax.broadcasted_iota(jnp.int32, (EXTRA, HEAD_DIM), 1)
    away = jnp.zeros((EXTRA, HEAD_DIM), jnp.int32)
    for block in range(blocks):
        for entry in range(TOPK):
            distance = first_block + block - selected_ref[block, entry]
            away = jnp.where((row == TERMS * blocks + block) & (lane == entry), distance, away)
    away = away.astype(F32)
    terms = []
    rest = rates_ref[...]
    for _ in range(TERMS):
        terms.append(rest.astype(BF16).astype(F32))
        rest = rest - terms[-1]
    out_copies = []
    for head in range(heads):
        extra = away
        for block in range(blocks):
            for index, term in enumerate(terms):
                piece = term[head:head + 1, block * BLOCK:(block + 1) * BLOCK]
                extra = jnp.where(row == TERMS * block + index, piece, extra)
        parts_ref[head, len(sources) * tokens:] = extra.astype(BF16)
        for copy in copies[len(sources) * head:len(sources) * (head + 1)]:
            copy.wait()
        out_copies.append(
            pltpu.make_async_copy(parts_ref.at[head], out_ref.at[head], out_sems.at[head])
        )
        out_copies[-1].start()
    for turn in range(heads):
        cut_copies[turn].wait()
        out_copies += fetched(
            [cut_ref.at[turn]], [cut_outs[turn]], cut_out_sems.at[pl.ds(turn, 1)]
        )
    for index, copy in enumerate(piece_copies):
        copy.wait()
        out_copies += fetched(
            [piece_ref.at[index]], [piece_outs[index]], piece_sems.at[1, pl.ds(index, 1)]
        )
    for copy in out_copies:
        copy.wait()


def cut_kernel(axes, queries_ref, values_ref, *refs):
    sems = refs[-1]
    heads = sems.shape[1]
    outs = refs[-1 - 2 * heads:-1]
    place = lax.rem(lax.axis_index(axes[0]), heads)
    cuts = [
        pl.multiple_of(lax.bitwise_xor(place, turn) * HEAD_DIM, HEAD_DIM) for turn in range(heads)
    ]
    copies = []
    for kind, source in enumerate((queries_ref, values_ref)):
        copies += fetched(
            [source.at[:, pl.ds(cut, HEAD_DIM)] for cut in cuts],
            outs[kind * heads:(kind + 1) * heads],
            sems.at[kind],
        )
    for copy in copies:
        copy.wait()


def order_kernel(axes, after, *refs):
    values_ref, sems = refs[-2:]
    kinds, heads = values_ref.shape[:2]
    place = lax.rem(lax.axis_index(axes[0]), heads)
    copies = []
    for kind in range(kinds):
        copies += fetched(
            refs[kind * heads:(kind + 1) * heads],
            [values_ref.at[kind, lax.bitwise_xor(place, turn)] for turn in range(heads)],
            sems.at[kind],
        )
    for copy in copies:
        copy.wait()


def rows_of(ref, blocks, unit, kind):
    start = (kind * blocks + unit % blocks) * BLOCK
    return ref[unit // blocks, start:start + BLOCK]


def base_inverse(strict):
    count = BLOCK // BASE
    moved = [
        pltpu.roll(strict[b * BASE:(b + 1) * BASE], (BLOCK - b * BASE) % BLOCK, 1)
        if b else strict[:BASE]
        for b in range(count)
    ]
    lanes = lax.broadcasted_iota(jnp.int32, (BASE // 2, BLOCK), 1)
    rows = lax.broadcasted_iota(jnp.int32, (BASE // 2, BLOCK), 0)
    half = BASE // 2
    parts = []
    for b in range(count):
        upper = (lanes == rows + b * BASE).astype(F32)
        lower = (lanes == rows + b * BASE + half).astype(F32)
        for step in range(BASE - 1):
            if step < half:
                source = upper[step:step + 1]
                if step < half - 1:
                    upper = upper - moved[b][:half, step:step + 1] * source
            else:
                source = lower[step - half:step - half + 1]
            lower = lower - moved[b][half:, step:step + 1] * source
        parts += [upper, lower]
    return jnp.concatenate(parts, 0)


def halves(value, size):
    parts = value.reshape(BLOCK // (2 * size), 2, size, BLOCK)
    return parts[:, 0].reshape(BLOCK // 2, BLOCK), parts[:, 1].reshape(BLOCK // 2, BLOCK)


def joined(first, second, size):
    shape = (BLOCK // (2 * size), 1, size, BLOCK)
    return jnp.concatenate([first.reshape(shape), second.reshape(shape)], 1).reshape(BLOCK, BLOCK)


def interleaved(steps, lag):
    running = list(steps)
    tick = 0
    while any(step is not None for step in running):
        for index, step in enumerate(running):
            if step is not None and tick >= index * lag:
                try:
                    next(step)
                except StopIteration:
                    running[index] = None
        tick += 1


def keys_kernel(blocks, part_ref, end_ref, tail_ref, far_ref, even_ref, pair_ref, group_ref,
                mixed_ref, away_ref):
    units = part_ref.shape[0] * blocks
    rows, columns = square_iotas()
    diagonal = rows == columns
    identity = diagonal.astype(F32)
    row = lax.broadcasted_iota(jnp.int32, (BLOCK // 2, BLOCK), 0)
    column = lax.broadcasted_iota(jnp.int32, (BLOCK // 2, BLOCK), 1)
    ends, maps = [None] * units, [None] * units

    def terms(unit):
        direction = rows_of(part_ref, blocks, unit, 0)
        key = rows_of(part_ref, blocks, unit, 1)
        extra = part_ref[unit // blocks, 2 * blocks * BLOCK:].astype(F32)
        first = TERMS * (unit % blocks)
        rate = extra[first:first + 1] + extra[first + 1:first + 2] + extra[first + 2:first + 3]
        listed = TERMS * blocks + unit % blocks
        away_ref[unit:unit + 1] = extra[listed:listed + 1].astype(jnp.int32)
        gram = nt(direction, direction)
        key_proj = jnp.where(rows > columns, nt(direction, key), 0.0).astype(BF16)
        squares = jnp.sum(jnp.where(diagonal, gram, 0.0), 0, keepdims=True)
        scale = lax.rsqrt(squares + 1e-06)
        scaled_rate = rate * scale
        scale_column = jnp.sum(jnp.where(diagonal, scale, 0.0), 1, keepdims=True)
        rate_column = jnp.sum(jnp.where(diagonal, scaled_rate, 0.0), 1, keepdims=True)
        strict = jnp.where(rows > columns, rate_column * gram * scale, 0.0)
        yield
        inverse = base_inverse(strict)
        yield
        size = BASE
        while size < BLOCK:
            inside = (row // size == column // (2 * size)) & (lax.rem(column, 2 * size) < size)
            corner = jnp.where(inside, halves(strict, size)[1], 0.0)
            below = triple(nn, split(corner), split(inverse))
            yield
            first_half, second = halves(inverse, size)
            padded = joined(jnp.zeros_like(below), below, size)
            second = second - triple(nn, split(second), split(padded))
            inverse = joined(first_half, second, size)
            size *= 2
            yield
        mixing = split(scale_column * inverse * scaled_rate)
        mixed = nn(jnp.concatenate(mixing, 0), jnp.concatenate([direction, key_proj], 1))
        mixed = split(mixed[:BLOCK] + mixed[BLOCK:])
        mixed_ref[unit] = mixed[0]
        yield
        behind = tn(jnp.concatenate([mixed[0], mixed[1][:, :BLOCK]], 1), direction)
        ends[unit] = key.astype(F32) - behind[BLOCK:2 * BLOCK]
        maps[unit] = split(identity - (behind[:BLOCK] + behind[2 * BLOCK:]))
        end_ref[unit] = ends[unit].astype(BF16)

    onward = []

    def pair_terms(pair):
        even, odd = 2 * pair, 2 * pair + 1
        running = [terms(even), terms(odd)]
        while running:
            for step in list(running):
                if next(step, running) is running:
                    running.remove(step)
            yield
        even_ref[pair, 0] = maps[even][0]
        even_ref[pair, 1] = maps[even][1]
        left = jnp.concatenate([ends[even].astype(BF16), *maps[even]], 0)
        both = nn(left, maps[odd][0])
        tail_even, tail_odd = both[:BLOCK].astype(BF16), ends[odd].astype(BF16)
        tail_ref[even] = tail_even
        tail_ref[odd] = tail_odd
        low = both[2 * BLOCK:] + nn(maps[even][0], maps[odd][1])
        pair_map = split(both[BLOCK:2 * BLOCK] + low)
        pair_ref[pair, 0] = pair_map[0]
        pair_ref[pair, 1] = pair_map[1]
        yield
        if onward:
            far = nn(jnp.concatenate([tail_even, tail_odd], 0), onward[-1][0]).astype(BF16)
            far_ref[even] = far[:BLOCK]
            far_ref[odd] = far[BLOCK:]
            pair_map = split(triple(nn, pair_map, onward[-1]))
        else:
            far_ref[even] = tail_even
            far_ref[odd] = tail_odd
        onward.append(pair_map)

    interleaved([pair_terms(pair) for pair in reversed(range(units // 2))], 1)
    group_ref[0] = onward[-1][0]
    group_ref[1] = onward[-1][1]


def queries_kernel(axes, blocks, part_ref, mixed_ref, even_ref, pair_ref, *refs):
    heads = part_ref.shape[0]
    units = heads * blocks
    inner_ref, moving_ref, query_ref, sems = refs[heads:]
    place = lax.rem(lax.axis_index(axes[0]), heads)
    copies = fetched(
        refs[:heads],
        [query_ref.at[lax.bitwise_xor(place, turn)] for turn in range(heads)],
        sems,
    )
    for copy in copies:
        copy.wait()
    rows, columns = square_iotas()
    current = []
    for unit in range(units):
        direction = rows_of(part_ref, blocks, unit, 0)
        key = rows_of(part_ref, blocks, unit, 1)
        query = rows_of(query_ref, blocks, unit, 0)
        query_proj = split(jnp.where(rows >= columns, nt(query, direction), 0.0))
        ahead = nn(jnp.concatenate(query_proj, 0), mixed_ref[unit])
        ahead = ahead[:BLOCK] + ahead[BLOCK:]
        inner_ref[unit] = nt(query, key) - ahead[:, HEAD_DIM:]
        start = split(query.astype(F32) - ahead[:, :HEAD_DIM])
        moving_ref[unit, 0] = start[0]
        if unit % 2:
            pair = unit // 2
            start = split(triple(nt, start, (even_ref[pair, 0], even_ref[pair, 1])))
        moving_ref[unit, 1] = start[0]
        current.append(start)
    pairs = units // 2
    current = [
        tuple(jnp.concatenate([current[2 * pair][part], current[2 * pair + 1][part]], 0)
              for part in range(2))
        for pair in range(pairs)
    ]
    for step in range(2, pairs + 1):
        for pair in range(step - 1, pairs):
            passed = pair - step + 1
            current[pair] = split(
                triple(nt, current[pair], (pair_ref[passed, 0], pair_ref[passed, 1]))
            )
            moving_ref[2 * pair, step] = current[pair][0][:BLOCK]
            moving_ref[2 * pair + 1, step] = current[pair][0][BLOCK:]


def listed_block(away_ref, unit, entry):
    away = away_ref[unit, entry]
    new = away > 0
    for other in range(1, entry):
        new = new & (away_ref[unit, other] != away)
    return unit - away, new


def earlier(source, ahead, units):
    return jnp.clip(source + ahead * units, 0, units - 1), source < (1 - ahead) * units


def attend_kernel(before, blocks, away_ref, moving_ref, inner_ref, end_ref, tail_ref,
                  values_ref, *refs):
    maps = max(before - 1, 0)
    far_keys, group_maps = refs[:before], refs[before:before + maps]
    count = (len(refs) - before - maps - 2) // 2
    out_ref, sems = refs[-2 - count], refs[-1]
    copies = fetched(refs[before + maps:before + maps + count], refs[-1 - count:-1], sems)
    units = inner_ref.shape[0]
    rows, columns = square_iotas()
    scale = HEAD_DIM ** (-0.5)

    def steps(unit):
        pair = unit // 2
        fronts = [moving_ref[unit, pair + 1]]
        for group_map in group_maps:
            passed = nt(fronts[-1], group_map[0]) + nt(fronts[-1], group_map[1])
            fronts.append(passed.astype(BF16))
        score_list = [jnp.where(rows >= columns, inner_ref[unit] * scale, -1e30)]
        value_list = [values_ref[0, unit]]
        for entry in range(1, TOPK):
            source, new = listed_block(away_ref, unit, entry)
            inside = jnp.maximum(source, 0)
            step = jnp.maximum(pair - inside // 2, 0)
            query = moving_ref[unit, step]
            key = jnp.where(step == 0, end_ref[inside], tail_ref[inside])
            value = values_ref[0, inside]
            for ahead in range(1, before + 1):
                place, here = earlier(source, ahead, units)
                query = jnp.where(here, fronts[ahead - 1], query)
                key = jnp.where(here, far_keys[ahead - 1][place], key)
                value = jnp.where(here, values_ref[ahead, place], value)
            score_list.append(jnp.where(new, nt(query, key) * scale, -1e30))
            value_list.append(value)
        yield
        scores = jnp.concatenate(score_list, 1)
        expos = jnp.exp(scores - jnp.max(scores, 1, keepdims=True))
        weights = (expos / jnp.sum(expos, 1, keepdims=True)).astype(BF16)
        yield
        blended = nn(weights, jnp.concatenate(value_list, 0)).astype(BF16)
        for plane in range(out_ref.shape[1]):
            out_ref[unit // blocks, plane, unit % blocks] = blended

    interleaved([steps(unit) for unit in range(units)], 1)
    for copy in copies:
        copy.wait()


def project_kernel(axes, other, cores, attended_ref, own_ref, *refs):
    other_refs, out_ref = refs[:-1], refs[-1]
    heads, planes, blocks = attended_ref.shape[:3]
    index = lax.axis_index(axes[1])
    core, plane = lax.rem(index + other, cores), index // cores
    width = out_ref.shape[1]
    total = None
    for offset in range(planes):
        source = lax.rem(plane + offset, planes)
        attended = jnp.concatenate(
            [
                jnp.concatenate(
                    [attended_ref[head, source, block] for head in range(heads)], 1
                )
                for block in range(blocks)
            ],
            0,
        )
        if offset:
            start = pl.multiple_of(core * width, width)
            weight = other_refs[offset - 1][:, pl.ds(start, width)]
        else:
            start = pl.multiple_of((plane * cores + core) * width, width)
            weight = own_ref[:, pl.ds(start, width)]
        product = nn(attended, weight)
        total = product if total is None else total + product
    out_ref[...] = total.astype(out_ref.dtype)


def call(kernel, outs, specs, flops, scratch=(), places=None, space=32):
    if places is None:
        places = [VMEM] * len(outs) if isinstance(outs, list) else VMEM
    return pl.pallas_call(
        kernel,
        out_shape=outs,
        in_specs=specs,
        out_specs=places,
        scratch_shapes=list(scratch),
        compiler_params=pltpu.CompilerParams(vmem_limit_bytes=space * 2 ** 20),
        cost_estimate=pl.CostEstimate(flops=flops, bytes_accessed=2 ** 21, transcendentals=0),
    )


def body(ctx_size, head_size, queries, keys, values, directions, rates, selected, out_weight):
    tokens = queries.shape[0]
    blocks = tokens // BLOCK
    heads = queries.shape[1] // HEAD_DIM
    units = heads * blocks
    pairs = units // 2
    groups = ctx_size // heads
    before = min(groups - 1, -(-LOOK // heads))
    cores = 2
    planes = head_size // cores
    axes = ("ctx", "head")
    members = [[group * heads + place for place in range(heads)] for group in range(groups)]
    partners = [(g, g + 1 - 2 * (g % cores)) for g in range(head_size)]
    cubes = 2 * BLOCK ** 3
    tile = (BLOCK, HEAD_DIM)

    def exchange(value):
        return lax.all_to_all(value, "ctx", 0, 0, axis_index_groups=members, tiled=True)

    def onward(value, by):
        shift = by * heads
        return lax.ppermute(value, "ctx", [(i, i + shift) for i in range(ctx_size - shift)])

    def crossed(value, turn):
        pairs = [(i, i - i % heads + (i % heads ^ turn)) for i in range(ctx_size)]
        return lax.ppermute(value, "ctx", pairs) if turn else value

    def straight(value, turn, by):
        shift = by * heads
        pairs = [(i, i - i % heads + (i % heads ^ turn) + shift) for i in range(ctx_size - shift)]
        return lax.ppermute(value, "ctx", pairs)

    def array(shape, kind=BF16):
        return jax.ShapeDtypeStruct(shape, kind)

    part_shape = (heads, 2 * tokens + EXTRA, HEAD_DIM)
    width = out_weight.shape[1] // planes
    piece_shape = (out_weight.shape[0], width)
    packed, *rest = call(
        functools.partial(pack_kernel, axes, cores),
        [array(part_shape)]
        + [array((tokens, HEAD_DIM))] * heads
        + [array(piece_shape)] * (planes - 1),
        [ANY] * 6,
        cubes,
        [
            pltpu.VMEM(part_shape, BF16),
            pltpu.VMEM(rates.shape, F32),
            pltpu.SMEM(selected.shape, jnp.int32),
            pltpu.VMEM((heads, tokens, HEAD_DIM), BF16),
            pltpu.VMEM((max(planes - 1, 1), *piece_shape), BF16),
            pltpu.SemaphoreType.DMA((heads, 2)),
            pltpu.SemaphoreType.DMA((2,)),
            pltpu.SemaphoreType.DMA((heads,)),
            pltpu.SemaphoreType.DMA((heads,)),
            pltpu.SemaphoreType.DMA((heads,)),
            pltpu.SemaphoreType.DMA((2, planes)),
        ],
        [ANY] * (heads + planes),
        56,
    )(directions, keys, rates, selected, values, out_weight)
    value_cuts, pieces = rest[:heads], rest[heads:]
    value_parts = [
        straight(value_cuts[turn], turn, by) for by in range(1, before + 1) for turn in range(heads)
    ]
    weight_parts = []
    for offset in range(1, planes):
        turned = [(g, (g + head_size - cores * offset) % head_size) for g in range(head_size)]
        weight_parts.append(lax.ppermute(pieces[offset - 1], "head", turned))
    parts = exchange(packed)

    end, tail, far, even, pair_map, group_map, mixed, away = call(
        functools.partial(keys_kernel, blocks),
        [
            array((units, *tile)),
            array((units, *tile)),
            array((units, *tile)),
            array((pairs, 2, *tile)),
            array((pairs, 2, *tile)),
            array((2, *tile)),
            array((units, BLOCK, 2 * BLOCK)),
            array((units, HEAD_DIM), jnp.int32),
        ],
        [VMEM],
        400 * cubes,
    )(parts)
    far_parts = [onward(far, by) for by in range(1, before + 1)]
    map_parts = [onward(group_map, by) for by in range(1, before)]
    cut = call(
        functools.partial(cut_kernel, axes),
        [array((tokens, HEAD_DIM))] * (2 * heads),
        [ANY] * (len(value_parts) + 3),
        2000 * cubes,
        [pltpu.SemaphoreType.DMA((2, heads))],
    )(queries, values, *value_parts, away)
    query_parts = [crossed(cut[turn], turn) for turn in range(heads)]
    own_parts = [crossed(cut[heads + turn], turn) for turn in range(heads)]
    inner, moving = call(
        functools.partial(queries_kernel, axes, blocks),
        [array((units, BLOCK, BLOCK), F32), array((units, pairs + 1, *tile))],
        [VMEM] * 4 + [ANY] * heads,
        0,
        [pltpu.VMEM((heads, tokens, HEAD_DIM), BF16), pltpu.SemaphoreType.DMA((heads,))],
    )(parts, mixed, even, pair_map, *query_parts)
    all_values = call(
        functools.partial(order_kernel, axes),
        array((1 + before, heads, tokens, HEAD_DIM)),
        [ANY] * (1 + heads + len(value_parts)),
        0,
        [pltpu.SemaphoreType.DMA((1 + before, heads))],
    )(inner, *own_parts, *value_parts).reshape(1 + before, units, *tile)
    attended, *weight_parts = call(
        functools.partial(attend_kernel, before, blocks),
        [array((heads, planes, blocks, *tile))] + [array(part.shape) for part in weight_parts],
        [SMEM] + [VMEM] * (5 + before + len(map_parts)) + [ANY] * len(weight_parts),
        200 * cubes,
        [pltpu.SemaphoreType.DMA((planes,))],
    )(away, moving, inner, end, tail, all_values, *far_parts, *map_parts, *weight_parts)

    returns = [
        [
            (group * heads + place) * head_size + p * cores + core
            for place in range(heads)
            for p in range(planes)
        ]
        for group in range(groups)
        for core in range(cores)
    ]
    local = lax.all_to_all(
        attended.reshape(heads * planes, blocks, *tile),
        axes, 0, 0, axis_index_groups=returns, tiled=True,
    ).reshape(heads, planes, blocks, *tile)

    def projected(other, kind):
        return call(
            functools.partial(project_kernel, axes, other, cores),
            array((tokens, width // cores), kind),
            [VMEM] * (1 + planes),
            128 * cubes,
        )(local, out_weight, *weight_parts)

    arrived = lax.ppermute(projected(1, BF16), "head", partners)
    return (projected(0, F32) + arrived.astype(F32)).astype(BF16)


def solution(mesh):
    in_specs = (
        P("ctx", "head"),
        P("ctx", "head"),
        P("ctx", "head"),
        P("ctx", "head"),
        P("head", "ctx"),
        P("ctx", None),
        P("head", None),
    )
    out_specs = P("ctx", "head")
    return jax.shard_map(
        functools.partial(body, mesh.shape["ctx"], mesh.shape["head"]),
        mesh=mesh,
        in_specs=in_specs,
        out_specs=out_specs,
        check_vma=False,
    )
```

```python
import functools

import jax
import jax.numpy as jnp
from jax import lax
from jax.experimental import pallas as pl
from jax.experimental.pallas import tpu as pltpu
from jax.sharding import PartitionSpec as P

HEAD_DIM = 128
BLOCK = 128
LOOK = 7
TOPK = 4
BASE = 16
EXTRA = 16
TERMS = 3
BF16 = jnp.bfloat16
F32 = jnp.float32
VMEM = pl.BlockSpec(memory_space=pltpu.VMEM)
SMEM = pl.BlockSpec(memory_space=pltpu.SMEM)
ANY = pl.BlockSpec(memory_space=pl.ANY)


def dot(left, right, left_dim, right_dim):
    return lax.dot_general(
        left, right, (((left_dim,), (right_dim,)), ((), ())), preferred_element_type=F32
    )


def nn(left, right):
    return dot(left, right, 1, 0)


def nt(left, right):
    return dot(left, right, 1, 1)


def tn(left, right):
    return dot(left, right, 0, 0)


def split(value):
    high = value.astype(BF16)
    return high, (value - high.astype(F32)).astype(BF16)


def triple(product, left, right):
    rows = left[0].shape[0]
    first = product(jnp.concatenate(left, 0), right[0])
    return first[:rows] + (first[rows:] + product(left[0], right[1]))


def square_iotas():
    rows = lax.broadcasted_iota(jnp.int32, (BLOCK, BLOCK), 0)
    columns = lax.broadcasted_iota(jnp.int32, (BLOCK, BLOCK), 1)
    return rows, columns


def fetched(sources, targets, sems):
    copies = []
    for index, (source, target) in enumerate(zip(sources, targets)):
        copies.append(pltpu.make_async_copy(source, target, sems.at[index]))
        copies[-1].start()
    return copies


def pack_kernel(axes, cores, d_ref, k_ref, rates_hbm, selected_hbm, values_ref, weight_ref,
                *refs):
    tokens = d_ref.shape[0]
    heads = d_ref.shape[1] // HEAD_DIM
    blocks = tokens // BLOCK
    (parts_ref, rates_ref, selected_ref, cut_ref, piece_ref, sems, few_sems, out_sems, cut_sems,
     cut_out_sems, piece_sems) = refs[-11:]
    out_ref, cut_outs, piece_outs = refs[0], refs[1:1 + heads], refs[1 + heads:-11]
    planes = len(piece_outs) + 1
    width = weight_ref.shape[1] // planes
    device = lax.axis_index(axes[0])
    place = lax.rem(device, heads)
    plane = lax.axis_index(axes[1]) // cores
    first_block = device * blocks
    few_copies = fetched([rates_hbm, selected_hbm], [rates_ref, selected_ref], few_sems)
    sources = (d_ref, k_ref)
    copies = []
    for head in range(heads):
        columns = pl.ds(head * HEAD_DIM, HEAD_DIM)
        for kind, source in enumerate(sources):
            copies.append(
                pltpu.make_async_copy(
                    source.at[:, columns],
                    parts_ref.at[head, pl.ds(kind * tokens, tokens)],
                    sems.at[head, kind],
                )
            )
            copies[-1].start()
    cuts = [
        pl.multiple_of(lax.bitwise_xor(place, turn) * HEAD_DIM, HEAD_DIM) for turn in range(heads)
    ]
    cut_copies = fetched(
        [values_ref.at[:, pl.ds(cut, HEAD_DIM)] for cut in cuts],
        [cut_ref.at[turn] for turn in range(heads)],
        cut_sems,
    )
    piece_copies = []
    for offset in range(1, planes):
        start = pl.multiple_of(lax.rem(plane + planes - offset, planes) * width, width)
        piece_copies += fetched(
            [weight_ref.at[:, pl.ds(start, width)]],
            [piece_ref.at[offset - 1]],
            piece_sems.at[0, pl.ds(offset - 1, 1)],
        )
    for copy in few_copies:
        copy.wait()
    row = lax.broadcasted_iota(jnp.int32, (EXTRA, HEAD_DIM), 0)
    lane = lax.broadcasted_iota(jnp.int32, (EXTRA, HEAD_DIM), 1)
    away = jnp.zeros((EXTRA, HEAD_DIM), jnp.int32)
    for block in range(blocks):
        for entry in range(TOPK):
            distance = first_block + block - selected_ref[block, entry]
            away = jnp.where((row == TERMS * blocks + block) & (lane == entry), distance, away)
    away = away.astype(F32)
    terms = []
    rest = rates_ref[...]
    for _ in range(TERMS):
        terms.append(rest.astype(BF16).astype(F32))
        rest = rest - terms[-1]
    out_copies = []
    for head in range(heads):
        extra = away
        for block in range(blocks):
            for index, term in enumerate(terms):
                piece = term[head:head + 1, block * BLOCK:(block + 1) * BLOCK]
                extra = jnp.where(row == TERMS * block + index, piece, extra)
        parts_ref[head, len(sources) * tokens:] = extra.astype(BF16)
        for copy in copies[len(sources) * head:len(sources) * (head + 1)]:
            copy.wait()
        out_copies.append(
            pltpu.make_async_copy(parts_ref.at[head], out_ref.at[head], out_sems.at[head])
        )
        out_copies[-1].start()
    for turn in range(heads):
        cut_copies[turn].wait()
        out_copies += fetched(
            [cut_ref.at[turn]], [cut_outs[turn]], cut_out_sems.at[pl.ds(turn, 1)]
        )
    for index, copy in enumerate(piece_copies):
        copy.wait()
        out_copies += fetched(
            [piece_ref.at[index]], [piece_outs[index]], piece_sems.at[1, pl.ds(index, 1)]
        )
    for copy in out_copies:
        copy.wait()


def cut_kernel(axes, queries_ref, values_ref, *refs):
    sems = refs[-1]
    heads = sems.shape[1]
    outs = refs[-1 - 2 * heads:-1]
    place = lax.rem(lax.axis_index(axes[0]), heads)
    cuts = [
        pl.multiple_of(lax.bitwise_xor(place, turn) * HEAD_DIM, HEAD_DIM) for turn in range(heads)
    ]
    copies = []
    for kind, source in enumerate((queries_ref, values_ref)):
        copies += fetched(
            [source.at[:, pl.ds(cut, HEAD_DIM)] for cut in cuts],
            outs[kind * heads:(kind + 1) * heads],
            sems.at[kind],
        )
    for copy in copies:
        copy.wait()


def rows_of(ref, blocks, unit, kind):
    start = (kind * blocks + unit % blocks) * BLOCK
    return ref[unit // blocks, start:start + BLOCK]


def base_inverse(strict):
    count = BLOCK // BASE
    moved = [
        pltpu.roll(strict[b * BASE:(b + 1) * BASE], (BLOCK - b * BASE) % BLOCK, 1)
        if b else strict[:BASE]
        for b in range(count)
    ]
    lanes = lax.broadcasted_iota(jnp.int32, (BASE // 2, BLOCK), 1)
    rows = lax.broadcasted_iota(jnp.int32, (BASE // 2, BLOCK), 0)
    half = BASE // 2
    parts = []
    for b in range(count):
        upper = (lanes == rows + b * BASE).astype(F32)
        lower = (lanes == rows + b * BASE + half).astype(F32)
        for step in range(BASE - 1):
            if step < half:
                source = upper[step:step + 1]
                if step < half - 1:
                    upper = upper - moved[b][:half, step:step + 1] * source
            else:
                source = lower[step - half:step - half + 1]
            lower = lower - moved[b][half:, step:step + 1] * source
        parts += [upper, lower]
    return jnp.concatenate(parts, 0)


def halves(value, size):
    parts = value.reshape(BLOCK // (2 * size), 2, size, BLOCK)
    return parts[:, 0].reshape(BLOCK // 2, BLOCK), parts[:, 1].reshape(BLOCK // 2, BLOCK)


def joined(first, second, size):
    shape = (BLOCK // (2 * size), 1, size, BLOCK)
    return jnp.concatenate([first.reshape(shape), second.reshape(shape)], 1).reshape(BLOCK, BLOCK)


def interleaved(steps, lag):
    running = list(steps)
    tick = 0
    while any(step is not None for step in running):
        for index, step in enumerate(running):
            if step is not None and tick >= index * lag:
                try:
                    next(step)
                except StopIteration:
                    running[index] = None
        tick += 1


def keys_kernel(blocks, part_ref, end_ref, tail_ref, far_ref, even_ref, pair_ref, group_ref,
                mixed_ref, away_ref):
    units = part_ref.shape[0] * blocks
    rows, columns = square_iotas()
    diagonal = rows == columns
    identity = diagonal.astype(F32)
    row = lax.broadcasted_iota(jnp.int32, (BLOCK // 2, BLOCK), 0)
    column = lax.broadcasted_iota(jnp.int32, (BLOCK // 2, BLOCK), 1)
    ends, maps = [None] * units, [None] * units

    def terms(unit):
        direction = rows_of(part_ref, blocks, unit, 0)
        key = rows_of(part_ref, blocks, unit, 1)
        extra = part_ref[unit // blocks, 2 * blocks * BLOCK:].astype(F32)
        first = TERMS * (unit % blocks)
        rate = extra[first:first + 1] + extra[first + 1:first + 2] + extra[first + 2:first + 3]
        listed = TERMS * blocks + unit % blocks
        away_ref[unit:unit + 1] = extra[listed:listed + 1].astype(jnp.int32)
        gram = nt(direction, direction)
        key_proj = jnp.where(rows > columns, nt(direction, key), 0.0).astype(BF16)
        squares = jnp.sum(jnp.where(diagonal, gram, 0.0), 0, keepdims=True)
        scale = lax.rsqrt(squares + 1e-06)
        scaled_rate = rate * scale
        scale_column = jnp.sum(jnp.where(diagonal, scale, 0.0), 1, keepdims=True)
        rate_column = jnp.sum(jnp.where(diagonal, scaled_rate, 0.0), 1, keepdims=True)
        strict = jnp.where(rows > columns, rate_column * gram * scale, 0.0)
        yield
        inverse = base_inverse(strict)
        yield
        size = BASE
        while size < BLOCK:
            inside = (row // size == column // (2 * size)) & (lax.rem(column, 2 * size) < size)
            corner = jnp.where(inside, halves(strict, size)[1], 0.0)
            below = triple(nn, split(corner), split(inverse))
            yield
            first_half, second = halves(inverse, size)
            padded = joined(jnp.zeros_like(below), below, size)
            second = second - triple(nn, split(second), split(padded))
            inverse = joined(first_half, second, size)
            size *= 2
            yield
        mixing = split(scale_column * inverse * scaled_rate)
        mixed = nn(jnp.concatenate(mixing, 0), jnp.concatenate([direction, key_proj], 1))
        mixed = split(mixed[:BLOCK] + mixed[BLOCK:])
        mixed_ref[unit] = mixed[0]
        yield
        behind = tn(jnp.concatenate([mixed[0], mixed[1][:, :BLOCK]], 1), direction)
        ends[unit] = key.astype(F32) - behind[BLOCK:2 * BLOCK]
        maps[unit] = split(identity - (behind[:BLOCK] + behind[2 * BLOCK:]))
        end_ref[unit] = ends[unit].astype(BF16)

    onward = []

    def pair_terms(pair):
        even, odd = 2 * pair, 2 * pair + 1
        running = [terms(even), terms(odd)]
        while running:
            for step in list(running):
                if next(step, running) is running:
                    running.remove(step)
            yield
        even_ref[pair, 0] = maps[even][0]
        even_ref[pair, 1] = maps[even][1]
        left = jnp.concatenate([ends[even].astype(BF16), *maps[even]], 0)
        both = nn(left, maps[odd][0])
        tail_even, tail_odd = both[:BLOCK].astype(BF16), ends[odd].astype(BF16)
        tail_ref[even] = tail_even
        tail_ref[odd] = tail_odd
        low = both[2 * BLOCK:] + nn(maps[even][0], maps[odd][1])
        pair_map = split(both[BLOCK:2 * BLOCK] + low)
        pair_ref[pair, 0] = pair_map[0]
        pair_ref[pair, 1] = pair_map[1]
        yield
        if onward:
            far = nn(jnp.concatenate([tail_even, tail_odd], 0), onward[-1][0]).astype(BF16)
            far_ref[even] = far[:BLOCK]
            far_ref[odd] = far[BLOCK:]
            pair_map = split(triple(nn, pair_map, onward[-1]))
        else:
            far_ref[even] = tail_even
            far_ref[odd] = tail_odd
        onward.append(pair_map)

    interleaved([pair_terms(pair) for pair in reversed(range(units // 2))], 1)
    group_ref[0] = onward[-1][0]
    group_ref[1] = onward[-1][1]


def queries_kernel(axes, blocks, part_ref, mixed_ref, even_ref, pair_ref, *refs):
    heads = part_ref.shape[0]
    units = heads * blocks
    inner_ref, moving_ref, query_ref, sems = refs[heads:]
    place = lax.rem(lax.axis_index(axes[0]), heads)
    copies = fetched(
        refs[:heads],
        [query_ref.at[lax.bitwise_xor(place, turn)] for turn in range(heads)],
        sems,
    )
    for copy in copies:
        copy.wait()
    rows, columns = square_iotas()
    current = []
    for unit in range(units):
        direction = rows_of(part_ref, blocks, unit, 0)
        key = rows_of(part_ref, blocks, unit, 1)
        query = rows_of(query_ref, blocks, unit, 0)
        query_proj = split(jnp.where(rows >= columns, nt(query, direction), 0.0))
        ahead = nn(jnp.concatenate(query_proj, 0), mixed_ref[unit])
        ahead = ahead[:BLOCK] + ahead[BLOCK:]
        inner_ref[unit] = nt(query, key) - ahead[:, HEAD_DIM:]
        start = split(query.astype(F32) - ahead[:, :HEAD_DIM])
        moving_ref[unit, 0] = start[0]
        if unit % 2:
            pair = unit // 2
            start = split(triple(nt, start, (even_ref[pair, 0], even_ref[pair, 1])))
        moving_ref[unit, 1] = start[0]
        current.append(start)
    pairs = units // 2
    current = [
        tuple(jnp.concatenate([current[2 * pair][part], current[2 * pair + 1][part]], 0)
              for part in range(2))
        for pair in range(pairs)
    ]
    for step in range(2, pairs + 1):
        for pair in range(step - 1, pairs):
            passed = pair - step + 1
            current[pair] = split(
                triple(nt, current[pair], (pair_ref[passed, 0], pair_ref[passed, 1]))
            )
            moving_ref[2 * pair, step] = current[pair][0][:BLOCK]
            moving_ref[2 * pair + 1, step] = current[pair][0][BLOCK:]


def listed_block(away_ref, unit, entry):
    away = away_ref[unit, entry]
    new = away > 0
    for other in range(1, entry):
        new = new & (away_ref[unit, other] != away)
    return unit - away, new


def earlier(source, ahead, units):
    return jnp.clip(source + ahead * units, 0, units - 1), source < (1 - ahead) * units


def weights_kernel(before, away_ref, moving_ref, inner_ref, end_ref, tail_ref, *refs):
    far_keys, group_maps, weights_ref = refs[:before], refs[before:-1], refs[-1]
    units = inner_ref.shape[0]
    rows, columns = square_iotas()
    scale = HEAD_DIM ** (-0.5)

    def steps(unit):
        pair = unit // 2
        fronts = [moving_ref[unit, pair + 1]]
        for group_map in group_maps:
            passed = nt(fronts[-1], group_map[0]) + nt(fronts[-1], group_map[1])
            fronts.append(passed.astype(BF16))
        score_list = [jnp.where(rows >= columns, inner_ref[unit] * scale, -1e30)]
        for entry in range(1, TOPK):
            source, new = listed_block(away_ref, unit, entry)
            inside = jnp.maximum(source, 0)
            step = jnp.maximum(pair - inside // 2, 0)
            query = moving_ref[unit, step]
            key = jnp.where(step == 0, end_ref[inside], tail_ref[inside])
            for ahead in range(1, before + 1):
                place, here = earlier(source, ahead, units)
                query = jnp.where(here, fronts[ahead - 1], query)
                key = jnp.where(here, far_keys[ahead - 1][place], key)
            score_list.append(jnp.where(new, nt(query, key) * scale, -1e30))
        yield
        scores = jnp.concatenate(score_list, 1)
        expos = jnp.exp(scores - jnp.max(scores, 1, keepdims=True))
        weights_ref[unit] = (expos / jnp.sum(expos, 1, keepdims=True)).astype(BF16)

    interleaved([steps(unit) for unit in range(units)], 1)


def blend_kernel(axes, before, blocks, away_ref, weights_ref, *refs):
    units = weights_ref.shape[0]
    heads = units // blocks
    count = (len(refs) - 4 - heads * (1 + before)) // 2
    arrived = refs[:heads * (1 + before)]
    out_ref, (values_ref, value_sems, sems) = refs[-4 - count], refs[-3:]
    place = lax.rem(lax.axis_index(axes[0]), heads)
    value_copies = []
    for kind in range(1 + before):
        for turn in range(heads):
            start = pl.multiple_of(lax.bitwise_xor(place, turn) * blocks * BLOCK, BLOCK)
            value_copies += fetched(
                [arrived[kind * heads + turn]],
                [values_ref.at[kind, pl.ds(start, blocks * BLOCK)]],
                value_sems.at[kind, pl.ds(turn, 1)],
            )
    copies = fetched(
        refs[heads * (1 + before):heads * (1 + before) + count], refs[-3 - count:-3], sems
    )
    for copy in value_copies:
        copy.wait()

    def value_of(kind, block):
        return values_ref[kind, pl.ds(pl.multiple_of(block * BLOCK, BLOCK), BLOCK)]

    for unit in range(units):
        value_list = [value_of(0, unit)]
        for entry in range(1, TOPK):
            source, _ = listed_block(away_ref, unit, entry)
            kind, block = 0, jnp.maximum(source, 0)
            for ahead in range(1, before + 1):
                other, here = earlier(source, ahead, units)
                kind = jnp.where(here, ahead, kind)
                block = jnp.where(here, other, block)
            value_list.append(value_of(kind, block))
        blended = nn(weights_ref[unit], jnp.concatenate(value_list, 0)).astype(BF16)
        for plane in range(out_ref.shape[1]):
            out_ref[unit // blocks, plane, unit % blocks] = blended
    for copy in copies:
        copy.wait()


def project_kernel(axes, other, cores, attended_ref, own_ref, *refs):
    other_refs, out_ref = refs[:-1], refs[-1]
    heads, planes, blocks = attended_ref.shape[:3]
    index = lax.axis_index(axes[1])
    core, plane = lax.rem(index + other, cores), index // cores
    width = out_ref.shape[1]
    total = None
    for offset in range(planes):
        source = lax.rem(plane + offset, planes)
        attended = jnp.concatenate(
            [
                jnp.concatenate(
                    [attended_ref[head, source, block] for head in range(heads)], 1
                )
                for block in range(blocks)
            ],
            0,
        )
        if offset:
            start = pl.multiple_of(core * width, width)
            weight = other_refs[offset - 1][:, pl.ds(start, width)]
        else:
            start = pl.multiple_of((plane * cores + core) * width, width)
            weight = own_ref[:, pl.ds(start, width)]
        product = nn(attended, weight)
        total = product if total is None else total + product
    out_ref[...] = total.astype(out_ref.dtype)


def call(kernel, outs, specs, flops, scratch=(), places=None, space=32):
    if places is None:
        places = [VMEM] * len(outs) if isinstance(outs, list) else VMEM
    return pl.pallas_call(
        kernel,
        out_shape=outs,
        in_specs=specs,
        out_specs=places,
        scratch_shapes=list(scratch),
        compiler_params=pltpu.CompilerParams(vmem_limit_bytes=space * 2 ** 20),
        cost_estimate=pl.CostEstimate(flops=flops, bytes_accessed=2 ** 21, transcendentals=0),
    )


def body(ctx_size, head_size, queries, keys, values, directions, rates, selected, out_weight):
    tokens = queries.shape[0]
    blocks = tokens // BLOCK
    heads = queries.shape[1] // HEAD_DIM
    units = heads * blocks
    pairs = units // 2
    groups = ctx_size // heads
    before = min(groups - 1, -(-LOOK // heads))
    cores = 2
    planes = head_size // cores
    axes = ("ctx", "head")
    members = [[group * heads + place for place in range(heads)] for group in range(groups)]
    partners = [(g, g + 1 - 2 * (g % cores)) for g in range(head_size)]
    cubes = 2 * BLOCK ** 3
    tile = (BLOCK, HEAD_DIM)

    def exchange(value):
        return lax.all_to_all(value, "ctx", 0, 0, axis_index_groups=members, tiled=True)

    def onward(value, by):
        shift = by * heads
        return lax.ppermute(value, "ctx", [(i, i + shift) for i in range(ctx_size - shift)])

    def crossed(value, turn):
        pairs = [(i, i - i % heads + (i % heads ^ turn)) for i in range(ctx_size)]
        return lax.ppermute(value, "ctx", pairs) if turn else value

    def straight(value, turn, by):
        shift = by * heads
        pairs = [(i, i - i % heads + (i % heads ^ turn) + shift) for i in range(ctx_size - shift)]
        return lax.ppermute(value, "ctx", pairs)

    def array(shape, kind=BF16):
        return jax.ShapeDtypeStruct(shape, kind)

    part_shape = (heads, 2 * tokens + EXTRA, HEAD_DIM)
    width = out_weight.shape[1] // planes
    piece_shape = (out_weight.shape[0], width)
    packed, *rest = call(
        functools.partial(pack_kernel, axes, cores),
        [array(part_shape)]
        + [array((tokens, HEAD_DIM))] * heads
        + [array(piece_shape)] * (planes - 1),
        [ANY] * 6,
        cubes,
        [
            pltpu.VMEM(part_shape, BF16),
            pltpu.VMEM(rates.shape, F32),
            pltpu.SMEM(selected.shape, jnp.int32),
            pltpu.VMEM((heads, tokens, HEAD_DIM), BF16),
            pltpu.VMEM((max(planes - 1, 1), *piece_shape), BF16),
            pltpu.SemaphoreType.DMA((heads, 2)),
            pltpu.SemaphoreType.DMA((2,)),
            pltpu.SemaphoreType.DMA((heads,)),
            pltpu.SemaphoreType.DMA((heads,)),
            pltpu.SemaphoreType.DMA((heads,)),
            pltpu.SemaphoreType.DMA((2, planes)),
        ],
        [ANY] * (heads + planes),
        56,
    )(directions, keys, rates, selected, values, out_weight)
    value_cuts, pieces = rest[:heads], rest[heads:]
    value_parts = [
        straight(value_cuts[turn], turn, by) for by in range(1, before + 1) for turn in range(heads)
    ]
    weight_parts = []
    for offset in range(1, planes):
        turned = [(g, (g + head_size - cores * offset) % head_size) for g in range(head_size)]
        weight_parts.append(lax.ppermute(pieces[offset - 1], "head", turned))
    parts = exchange(packed)

    end, tail, far, even, pair_map, group_map, mixed, away = call(
        functools.partial(keys_kernel, blocks),
        [
            array((units, *tile)),
            array((units, *tile)),
            array((units, *tile)),
            array((pairs, 2, *tile)),
            array((pairs, 2, *tile)),
            array((2, *tile)),
            array((units, BLOCK, 2 * BLOCK)),
            array((units, HEAD_DIM), jnp.int32),
        ],
        [VMEM],
        400 * cubes,
    )(parts)
    far_parts = [onward(far, by) for by in range(1, before + 1)]
    map_parts = [onward(group_map, by) for by in range(1, before)]
    cut = call(
        functools.partial(cut_kernel, axes),
        [array((tokens, HEAD_DIM))] * (2 * heads),
        [ANY] * (len(value_parts) + 3),
        2000 * cubes,
        [pltpu.SemaphoreType.DMA((2, heads))],
    )(queries, values, *value_parts, away)
    query_parts = [crossed(cut[turn], turn) for turn in range(heads)]
    own_parts = [crossed(cut[heads + turn], turn) for turn in range(heads)]
    inner, moving = call(
        functools.partial(queries_kernel, axes, blocks),
        [array((units, BLOCK, BLOCK), F32), array((units, pairs + 1, *tile))],
        [VMEM] * 4 + [ANY] * heads,
        0,
        [pltpu.VMEM((heads, tokens, HEAD_DIM), BF16), pltpu.SemaphoreType.DMA((heads,))],
    )(parts, mixed, even, pair_map, *query_parts)
    weights = call(
        functools.partial(weights_kernel, before),
        array((units, BLOCK, TOPK * BLOCK)),
        [SMEM] + [VMEM] * (4 + before + len(map_parts)),
        0,
    )(away, moving, inner, end, tail, *far_parts, *map_parts)
    attended, *weight_parts = call(
        functools.partial(blend_kernel, axes, before, blocks),
        [array((heads, planes, blocks, *tile))] + [array(part.shape) for part in weight_parts],
        [SMEM, VMEM] + [ANY] * (heads * (1 + before) + len(weight_parts)),
        0,
        [
            pltpu.VMEM((1 + before, units * BLOCK, HEAD_DIM), BF16),
            pltpu.SemaphoreType.DMA((1 + before, heads)),
            pltpu.SemaphoreType.DMA((planes,)),
        ],
    )(away, weights, *own_parts, *value_parts, *weight_parts)

    returns = [
        [
            (group * heads + place) * head_size + p * cores + core
            for place in range(heads)
            for p in range(planes)
        ]
        for group in range(groups)
        for core in range(cores)
    ]
    local = lax.all_to_all(
        attended.reshape(heads * planes, blocks, *tile),
        axes, 0, 0, axis_index_groups=returns, tiled=True,
    ).reshape(heads, planes, blocks, *tile)

    def projected(other, kind):
        return call(
            functools.partial(project_kernel, axes, other, cores),
            array((tokens, width // cores), kind),
            [VMEM] * (1 + planes),
            128 * cubes,
        )(local, out_weight, *weight_parts)

    arrived = lax.ppermute(projected(1, BF16), "head", partners)
    return (projected(0, F32) + arrived.astype(F32)).astype(BF16)


def solution(mesh):
    in_specs = (
        P("ctx", "head"),
        P("ctx", "head"),
        P("ctx", "head"),
        P("ctx", "head"),
        P("head", "ctx"),
        P("ctx", None),
        P("head", None),
    )
    out_specs = P("ctx", "head")
    return jax.shard_map(
        functools.partial(body, mesh.shape["ctx"], mesh.shape["head"]),
        mesh=mesh,
        in_specs=in_specs,
        out_specs=out_specs,
        check_vma=False,
    )
```

```python
import functools

import jax
import jax.numpy as jnp
from jax import lax
from jax.experimental import pallas as pl
from jax.experimental.pallas import tpu as pltpu
from jax.sharding import PartitionSpec as P

HEAD_DIM = 128
BLOCK = 128
LOOK = 7
TOPK = 4
BASE = 16
EXTRA = 16
TERMS = 3
BF16 = jnp.bfloat16
F32 = jnp.float32
VMEM = pl.BlockSpec(memory_space=pltpu.VMEM)
SMEM = pl.BlockSpec(memory_space=pltpu.SMEM)
ANY = pl.BlockSpec(memory_space=pl.ANY)


def dot(left, right, left_dim, right_dim):
    return lax.dot_general(
        left, right, (((left_dim,), (right_dim,)), ((), ())), preferred_element_type=F32
    )


def nn(left, right):
    return dot(left, right, 1, 0)


def nt(left, right):
    return dot(left, right, 1, 1)


def tn(left, right):
    return dot(left, right, 0, 0)


def split(value):
    high = value.astype(BF16)
    return high, (value - high.astype(F32)).astype(BF16)


def triple(product, left, right):
    rows = left[0].shape[0]
    first = product(jnp.concatenate(left, 0), right[0])
    return first[:rows] + (first[rows:] + product(left[0], right[1]))


def square_iotas():
    rows = lax.broadcasted_iota(jnp.int32, (BLOCK, BLOCK), 0)
    columns = lax.broadcasted_iota(jnp.int32, (BLOCK, BLOCK), 1)
    return rows, columns


def fetched(sources, targets, sems):
    copies = []
    for index, (source, target) in enumerate(zip(sources, targets)):
        copies.append(pltpu.make_async_copy(source, target, sems.at[index]))
        copies[-1].start()
    return copies


def pack_kernel(axes, cores, d_ref, k_ref, rates_hbm, selected_hbm, values_ref, weight_ref,
                *refs):
    tokens = d_ref.shape[0]
    heads = d_ref.shape[1] // HEAD_DIM
    blocks = tokens // BLOCK
    (parts_ref, rates_ref, selected_ref, cut_ref, piece_ref, sems, few_sems, out_sems, cut_sems,
     cut_out_sems, piece_sems) = refs[-11:]
    rounds = heads // 2
    out_ref, cut_outs, piece_outs = refs[0], refs[1:1 + rounds], refs[1 + rounds:-11]
    planes = len(piece_outs) + 1
    width = weight_ref.shape[1] // planes
    device = lax.axis_index(axes[0])
    place = lax.rem(device, heads)
    plane = lax.axis_index(axes[1]) // cores
    first_block = device * blocks
    few_copies = fetched([rates_hbm, selected_hbm], [rates_ref, selected_ref], few_sems)
    sources = (d_ref, k_ref)
    copies = []
    for head in range(heads):
        columns = pl.ds(head * HEAD_DIM, HEAD_DIM)
        for kind, source in enumerate(sources):
            copies.append(
                pltpu.make_async_copy(
                    source.at[:, columns],
                    parts_ref.at[head, pl.ds(kind * tokens, tokens)],
                    sems.at[head, kind],
                )
            )
            copies[-1].start()
    cuts = [
        pl.multiple_of(lax.bitwise_xor(place, turn) * HEAD_DIM, HEAD_DIM) for turn in range(heads)
    ]
    cut_copies = fetched(
        [values_ref.at[:, pl.ds(cut, HEAD_DIM)] for cut in cuts],
        [cut_ref.at[turn // 2, turn % 2] for turn in range(heads)],
        cut_sems,
    )
    piece_copies = []
    for offset in range(1, planes):
        start = pl.multiple_of(lax.rem(plane + planes - offset, planes) * width, width)
        piece_copies += fetched(
            [weight_ref.at[:, pl.ds(start, width)]],
            [piece_ref.at[offset - 1]],
            piece_sems.at[0, pl.ds(offset - 1, 1)],
        )
    for copy in few_copies:
        copy.wait()
    row = lax.broadcasted_iota(jnp.int32, (EXTRA, HEAD_DIM), 0)
    lane = lax.broadcasted_iota(jnp.int32, (EXTRA, HEAD_DIM), 1)
    away = jnp.zeros((EXTRA, HEAD_DIM), jnp.int32)
    for block in range(blocks):
        for entry in range(TOPK):
            distance = first_block + block - selected_ref[block, entry]
            away = jnp.where((row == TERMS * blocks + block) & (lane == entry), distance, away)
    away = away.astype(F32)
    terms = []
    rest = rates_ref[...]
    for _ in range(TERMS):
        terms.append(rest.astype(BF16).astype(F32))
        rest = rest - terms[-1]
    out_copies = []
    for head in range(heads):
        extra = away
        for block in range(blocks):
            for index, term in enumerate(terms):
                piece = term[head:head + 1, block * BLOCK:(block + 1) * BLOCK]
                extra = jnp.where(row == TERMS * block + index, piece, extra)
        parts_ref[head, len(sources) * tokens:] = extra.astype(BF16)
        for copy in copies[len(sources) * head:len(sources) * (head + 1)]:
            copy.wait()
        out_copies.append(
            pltpu.make_async_copy(parts_ref.at[head], out_ref.at[head], out_sems.at[head])
        )
        out_copies[-1].start()
    for turn in range(rounds):
        cut_copies[2 * turn].wait()
        cut_copies[2 * turn + 1].wait()
        out_copies += fetched(
            [cut_ref.at[turn]], [cut_outs[turn]], cut_out_sems.at[pl.ds(turn, 1)]
        )
    for index, copy in enumerate(piece_copies):
        copy.wait()
        out_copies += fetched(
            [piece_ref.at[index]], [piece_outs[index]], piece_sems.at[1, pl.ds(index, 1)]
        )
    for copy in out_copies:
        copy.wait()


def cut_kernel(axes, queries_ref, values_ref, *refs):
    sems, more_sems = refs[-2:]
    heads = sems.shape[1]
    outs = refs[-2 - 2 * heads:-2]
    come = refs[:-3 - 2 * heads]
    place = lax.rem(lax.axis_index(axes[0]), heads)
    cuts = [
        pl.multiple_of(lax.bitwise_xor(place, turn) * HEAD_DIM, HEAD_DIM) for turn in range(heads)
    ]
    copies = []
    for kind, source in enumerate((queries_ref, values_ref)):
        targets = list(outs[kind * heads:(kind + 1) * heads])
        if kind:
            targets[1] = targets[1].at[0]
        copies += fetched(
            [source.at[:, pl.ds(cut, HEAD_DIM)] for cut in cuts], targets, sems.at[kind]
        )
    copies += fetched(
        [part.at[1] for part in come],
        [outs[heads + 1].at[1 + index] for index in range(len(come))],
        more_sems,
    )
    for copy in copies:
        copy.wait()


def rows_of(ref, blocks, unit, kind):
    start = (kind * blocks + unit % blocks) * BLOCK
    return ref[unit // blocks, start:start + BLOCK]


def base_inverse(strict):
    count = BLOCK // BASE
    moved = [
        pltpu.roll(strict[b * BASE:(b + 1) * BASE], (BLOCK - b * BASE) % BLOCK, 1)
        if b else strict[:BASE]
        for b in range(count)
    ]
    lanes = lax.broadcasted_iota(jnp.int32, (BASE // 2, BLOCK), 1)
    rows = lax.broadcasted_iota(jnp.int32, (BASE // 2, BLOCK), 0)
    half = BASE // 2
    parts = []
    for b in range(count):
        upper = (lanes == rows + b * BASE).astype(F32)
        lower = (lanes == rows + b * BASE + half).astype(F32)
        for step in range(BASE - 1):
            if step < half:
                source = upper[step:step + 1]
                if step < half - 1:
                    upper = upper - moved[b][:half, step:step + 1] * source
            else:
                source = lower[step - half:step - half + 1]
            lower = lower - moved[b][half:, step:step + 1] * source
        parts += [upper, lower]
    return jnp.concatenate(parts, 0)


def halves(value, size):
    parts = value.reshape(BLOCK // (2 * size), 2, size, BLOCK)
    return parts[:, 0].reshape(BLOCK // 2, BLOCK), parts[:, 1].reshape(BLOCK // 2, BLOCK)


def joined(first, second, size):
    shape = (BLOCK // (2 * size), 1, size, BLOCK)
    return jnp.concatenate([first.reshape(shape), second.reshape(shape)], 1).reshape(BLOCK, BLOCK)


def interleaved(steps, lag):
    running = list(steps)
    tick = 0
    while any(step is not None for step in running):
        for index, step in enumerate(running):
            if step is not None and tick >= index * lag:
                try:
                    next(step)
                except StopIteration:
                    running[index] = None
        tick += 1


def keys_kernel(blocks, part_ref, end_ref, tail_ref, far_ref, even_ref, pair_ref, group_ref,
                mixed_ref, away_ref):
    units = part_ref.shape[0] * blocks
    rows, columns = square_iotas()
    diagonal = rows == columns
    identity = diagonal.astype(F32)
    row = lax.broadcasted_iota(jnp.int32, (BLOCK // 2, BLOCK), 0)
    column = lax.broadcasted_iota(jnp.int32, (BLOCK // 2, BLOCK), 1)
    ends, maps = [None] * units, [None] * units

    def terms(unit):
        direction = rows_of(part_ref, blocks, unit, 0)
        key = rows_of(part_ref, blocks, unit, 1)
        extra = part_ref[unit // blocks, 2 * blocks * BLOCK:].astype(F32)
        first = TERMS * (unit % blocks)
        rate = extra[first:first + 1] + extra[first + 1:first + 2] + extra[first + 2:first + 3]
        listed = TERMS * blocks + unit % blocks
        away_ref[unit:unit + 1] = extra[listed:listed + 1].astype(jnp.int32)
        gram = nt(direction, direction)
        key_proj = jnp.where(rows > columns, nt(direction, key), 0.0).astype(BF16)
        squares = jnp.sum(jnp.where(diagonal, gram, 0.0), 0, keepdims=True)
        scale = lax.rsqrt(squares + 1e-06)
        scaled_rate = rate * scale
        scale_column = jnp.sum(jnp.where(diagonal, scale, 0.0), 1, keepdims=True)
        rate_column = jnp.sum(jnp.where(diagonal, scaled_rate, 0.0), 1, keepdims=True)
        strict = jnp.where(rows > columns, rate_column * gram * scale, 0.0)
        yield
        inverse = base_inverse(strict)
        yield
        size = BASE
        while size < BLOCK:
            inside = (row // size == column // (2 * size)) & (lax.rem(column, 2 * size) < size)
            corner = jnp.where(inside, halves(strict, size)[1], 0.0)
            below = triple(nn, split(corner), split(inverse))
            yield
            first_half, second = halves(inverse, size)
            padded = joined(jnp.zeros_like(below), below, size)
            second = second - triple(nn, split(second), split(padded))
            inverse = joined(first_half, second, size)
            size *= 2
            yield
        mixing = split(scale_column * inverse * scaled_rate)
        mixed = nn(jnp.concatenate(mixing, 0), jnp.concatenate([direction, key_proj], 1))
        mixed = split(mixed[:BLOCK] + mixed[BLOCK:])
        mixed_ref[unit] = mixed[0]
        yield
        behind = tn(jnp.concatenate([mixed[0], mixed[1][:, :BLOCK]], 1), direction)
        ends[unit] = key.astype(F32) - behind[BLOCK:2 * BLOCK]
        maps[unit] = split(identity - (behind[:BLOCK] + behind[2 * BLOCK:]))
        end_ref[unit] = ends[unit].astype(BF16)

    onward = []

    def pair_terms(pair):
        even, odd = 2 * pair, 2 * pair + 1
        running = [terms(even), terms(odd)]
        while running:
            for step in list(running):
                if next(step, running) is running:
                    running.remove(step)
            yield
        even_ref[pair, 0] = maps[even][0]
        even_ref[pair, 1] = maps[even][1]
        left = jnp.concatenate([ends[even].astype(BF16), *maps[even]], 0)
        both = nn(left, maps[odd][0])
        tail_even, tail_odd = both[:BLOCK].astype(BF16), ends[odd].astype(BF16)
        tail_ref[even] = tail_even
        tail_ref[odd] = tail_odd
        low = both[2 * BLOCK:] + nn(maps[even][0], maps[odd][1])
        pair_map = split(both[BLOCK:2 * BLOCK] + low)
        pair_ref[pair, 0] = pair_map[0]
        pair_ref[pair, 1] = pair_map[1]
        yield
        if onward:
            far = nn(jnp.concatenate([tail_even, tail_odd], 0), onward[-1][0]).astype(BF16)
            far_ref[even] = far[:BLOCK]
            far_ref[odd] = far[BLOCK:]
            pair_map = split(triple(nn, pair_map, onward[-1]))
        else:
            far_ref[even] = tail_even
            far_ref[odd] = tail_odd
        onward.append(pair_map)

    interleaved([pair_terms(pair) for pair in reversed(range(units // 2))], 1)
    group_ref[0] = onward[-1][0]
    group_ref[1] = onward[-1][1]


def queries_kernel(axes, blocks, part_ref, mixed_ref, even_ref, pair_ref, *refs):
    heads = part_ref.shape[0]
    units = heads * blocks
    inner_ref, moving_ref, query_ref, sems = refs[heads:]
    place = lax.rem(lax.axis_index(axes[0]), heads)
    copies = fetched(
        refs[:heads],
        [query_ref.at[lax.bitwise_xor(place, turn)] for turn in range(heads)],
        sems,
    )
    for copy in copies:
        copy.wait()
    rows, columns = square_iotas()
    current = []
    for unit in range(units):
        direction = rows_of(part_ref, blocks, unit, 0)
        key = rows_of(part_ref, blocks, unit, 1)
        query = rows_of(query_ref, blocks, unit, 0)
        query_proj = split(jnp.where(rows >= columns, nt(query, direction), 0.0))
        ahead = nn(jnp.concatenate(query_proj, 0), mixed_ref[unit])
        ahead = ahead[:BLOCK] + ahead[BLOCK:]
        inner_ref[unit] = nt(query, key) - ahead[:, HEAD_DIM:]
        start = split(query.astype(F32) - ahead[:, :HEAD_DIM])
        moving_ref[unit, 0] = start[0]
        if unit % 2:
            pair = unit // 2
            start = split(triple(nt, start, (even_ref[pair, 0], even_ref[pair, 1])))
        moving_ref[unit, 1] = start[0]
        current.append(start)
    pairs = units // 2
    current = [
        tuple(jnp.concatenate([current[2 * pair][part], current[2 * pair + 1][part]], 0)
              for part in range(2))
        for pair in range(pairs)
    ]
    for step in range(2, pairs + 1):
        for pair in range(step - 1, pairs):
            passed = pair - step + 1
            current[pair] = split(
                triple(nt, current[pair], (pair_ref[passed, 0], pair_ref[passed, 1]))
            )
            moving_ref[2 * pair, step] = current[pair][0][:BLOCK]
            moving_ref[2 * pair + 1, step] = current[pair][0][BLOCK:]


def listed_block(away_ref, unit, entry):
    away = away_ref[unit, entry]
    new = away > 0
    for other in range(1, entry):
        new = new & (away_ref[unit, other] != away)
    return unit - away, new


def earlier(source, ahead, units):
    return jnp.clip(source + ahead * units, 0, units - 1), source < (1 - ahead) * units


def weights_kernel(before, away_ref, moving_ref, inner_ref, end_ref, tail_ref, *refs):
    far_keys, group_maps, weights_ref = refs[:before], refs[before:-1], refs[-1]
    units = inner_ref.shape[0]
    rows, columns = square_iotas()
    scale = HEAD_DIM ** (-0.5)

    def steps(unit):
        pair = unit // 2
        fronts = [moving_ref[unit, pair + 1]]
        for group_map in group_maps:
            passed = nt(fronts[-1], group_map[0]) + nt(fronts[-1], group_map[1])
            fronts.append(passed.astype(BF16))
        score_list = [jnp.where(rows >= columns, inner_ref[unit] * scale, -1e30)]
        for entry in range(1, TOPK):
            source, new = listed_block(away_ref, unit, entry)
            inside = jnp.maximum(source, 0)
            step = jnp.maximum(pair - inside // 2, 0)
            query = moving_ref[unit, step]
            key = jnp.where(step == 0, end_ref[inside], tail_ref[inside])
            for ahead in range(1, before + 1):
                place, here = earlier(source, ahead, units)
                query = jnp.where(here, fronts[ahead - 1], query)
                key = jnp.where(here, far_keys[ahead - 1][place], key)
            score_list.append(jnp.where(new, nt(query, key) * scale, -1e30))
        yield
        scores = jnp.concatenate(score_list, 1)
        expos = jnp.exp(scores - jnp.max(scores, 1, keepdims=True))
        weights_ref[unit] = (expos / jnp.sum(expos, 1, keepdims=True)).astype(BF16)

    interleaved([steps(unit) for unit in range(units)], 1)


def blend_kernel(axes, before, blocks, away_ref, weights_ref, *refs):
    units = weights_ref.shape[0]
    heads = units // blocks
    rounds = heads // 2
    own, come = refs[:heads], refs[heads:heads + rounds * before]
    count = (len(refs) - 4 - heads - rounds * before) // 2
    out_ref, (values_ref, value_sems, sems) = refs[-4 - count], refs[-3:]
    place = lax.rem(lax.axis_index(axes[0]), heads)
    value_copies = []

    def put(source, kind, turn):
        start = pl.multiple_of(lax.bitwise_xor(place, turn) * blocks * BLOCK, BLOCK)
        value_copies.extend(
            fetched(
                [source],
                [values_ref.at[kind, pl.ds(start, blocks * BLOCK)]],
                value_sems.at[kind, pl.ds(turn, 1)],
            )
        )

    for turn in range(heads):
        put(own[turn].at[0] if turn == 1 else own[turn], 0, turn)
    for index in range(rounds * before):
        kind, turn = 1 + index // rounds, 2 * (index % rounds)
        put(come[index].at[0], kind, turn)
        put(own[1].at[1 + index], kind, turn + 1)
    start = heads + rounds * before
    copies = fetched(refs[start:start + count], refs[-3 - count:-3], sems)
    for copy in value_copies:
        copy.wait()

    def value_of(kind, block):
        return values_ref[kind, pl.ds(pl.multiple_of(block * BLOCK, BLOCK), BLOCK)]

    for unit in range(units):
        value_list = [value_of(0, unit)]
        for entry in range(1, TOPK):
            source, _ = listed_block(away_ref, unit, entry)
            kind, block = 0, jnp.maximum(source, 0)
            for ahead in range(1, before + 1):
                other, here = earlier(source, ahead, units)
                kind = jnp.where(here, ahead, kind)
                block = jnp.where(here, other, block)
            value_list.append(value_of(kind, block))
        blended = nn(weights_ref[unit], jnp.concatenate(value_list, 0)).astype(BF16)
        for plane in range(out_ref.shape[1]):
            out_ref[unit // blocks, plane, unit % blocks] = blended
    for copy in copies:
        copy.wait()


def project_kernel(axes, other, cores, attended_ref, own_ref, *refs):
    other_refs, out_ref = refs[:-1], refs[-1]
    heads, planes, blocks = attended_ref.shape[:3]
    index = lax.axis_index(axes[1])
    core, plane = lax.rem(index + other, cores), index // cores
    width = out_ref.shape[1]
    total = None
    for offset in range(planes):
        source = lax.rem(plane + offset, planes)
        attended = jnp.concatenate(
            [
                jnp.concatenate(
                    [attended_ref[head, source, block] for head in range(heads)], 1
                )
                for block in range(blocks)
            ],
            0,
        )
        if offset:
            start = pl.multiple_of(core * width, width)
            weight = other_refs[offset - 1][:, pl.ds(start, width)]
        else:
            start = pl.multiple_of((plane * cores + core) * width, width)
            weight = own_ref[:, pl.ds(start, width)]
        product = nn(attended, weight)
        total = product if total is None else total + product
    out_ref[...] = total.astype(out_ref.dtype)


def call(kernel, outs, specs, flops, scratch=(), places=None, space=32):
    if places is None:
        places = [VMEM] * len(outs) if isinstance(outs, list) else VMEM
    return pl.pallas_call(
        kernel,
        out_shape=outs,
        in_specs=specs,
        out_specs=places,
        scratch_shapes=list(scratch),
        compiler_params=pltpu.CompilerParams(vmem_limit_bytes=space * 2 ** 20),
        cost_estimate=pl.CostEstimate(flops=flops, bytes_accessed=2 ** 21, transcendentals=0),
    )


def body(ctx_size, head_size, queries, keys, values, directions, rates, selected, out_weight):
    tokens = queries.shape[0]
    blocks = tokens // BLOCK
    heads = queries.shape[1] // HEAD_DIM
    units = heads * blocks
    pairs = units // 2
    groups = ctx_size // heads
    before = min(groups - 1, -(-LOOK // heads))
    cores = 2
    planes = head_size // cores
    axes = ("ctx", "head")
    members = [[group * heads + place for place in range(heads)] for group in range(groups)]
    partners = [(g, g + 1 - 2 * (g % cores)) for g in range(head_size)]
    cubes = 2 * BLOCK ** 3
    tile = (BLOCK, HEAD_DIM)

    def exchange(value):
        return lax.all_to_all(value, "ctx", 0, 0, axis_index_groups=members, tiled=True)

    def onward(value, by):
        shift = by * heads
        return lax.ppermute(value, "ctx", [(i, i + shift) for i in range(ctx_size - shift)])

    def crossed(value, turn):
        pairs = [(i, i - i % heads + (i % heads ^ turn)) for i in range(ctx_size)]
        return lax.ppermute(value, "ctx", pairs) if turn else value

    def straight(value, turn, by):
        shift = by * heads
        pairs = [(i, (i ^ 2 * turn) + shift) for i in range(ctx_size - shift)]
        return lax.ppermute(value, "ctx", pairs)

    def array(shape, kind=BF16):
        return jax.ShapeDtypeStruct(shape, kind)

    part_shape = (heads, 2 * tokens + EXTRA, HEAD_DIM)
    width = out_weight.shape[1] // planes
    piece_shape = (out_weight.shape[0], width)
    rounds = heads // 2
    packed, *rest = call(
        functools.partial(pack_kernel, axes, cores),
        [array(part_shape)]
        + [array((2, tokens, HEAD_DIM))] * rounds
        + [array(piece_shape)] * (planes - 1),
        [ANY] * 6,
        cubes,
        [
            pltpu.VMEM(part_shape, BF16),
            pltpu.VMEM(rates.shape, F32),
            pltpu.SMEM(selected.shape, jnp.int32),
            pltpu.VMEM((rounds, 2, tokens, HEAD_DIM), BF16),
            pltpu.VMEM((max(planes - 1, 1), *piece_shape), BF16),
            pltpu.SemaphoreType.DMA((heads, 2)),
            pltpu.SemaphoreType.DMA((2,)),
            pltpu.SemaphoreType.DMA((heads,)),
            pltpu.SemaphoreType.DMA((heads,)),
            pltpu.SemaphoreType.DMA((heads,)),
            pltpu.SemaphoreType.DMA((2, planes)),
        ],
        [ANY] * (rounds + planes),
        56,
    )(directions, keys, rates, selected, values, out_weight)
    value_cuts, pieces = rest[:rounds], rest[rounds:]
    value_parts = [
        straight(value_cuts[turn], turn, by)
        for by in range(1, before + 1)
        for turn in range(rounds)
    ]
    weight_parts = []
    for offset in range(1, planes):
        turned = [(g, (g + head_size - cores * offset) % head_size) for g in range(head_size)]
        weight_parts.append(lax.ppermute(pieces[offset - 1], "head", turned))
    parts = exchange(packed)

    end, tail, far, even, pair_map, group_map, mixed, away = call(
        functools.partial(keys_kernel, blocks),
        [
            array((units, *tile)),
            array((units, *tile)),
            array((units, *tile)),
            array((pairs, 2, *tile)),
            array((pairs, 2, *tile)),
            array((2, *tile)),
            array((units, BLOCK, 2 * BLOCK)),
            array((units, HEAD_DIM), jnp.int32),
        ],
        [VMEM],
        400 * cubes,
    )(parts)
    far_parts = [onward(far, by) for by in range(1, before + 1)]
    map_parts = [onward(group_map, by) for by in range(1, before)]
    cut = call(
        functools.partial(cut_kernel, axes),
        [
            array((1 + len(value_parts), tokens, HEAD_DIM) if turn == heads + 1 else (tokens, HEAD_DIM))
            for turn in range(2 * heads)
        ],
        [ANY] * (len(value_parts) + 3),
        2000 * cubes,
        [
            pltpu.SemaphoreType.DMA((2, heads)),
            pltpu.SemaphoreType.DMA((max(len(value_parts), 1),)),
        ],
    )(queries, values, *value_parts, away)
    query_parts = [crossed(cut[turn], turn) for turn in range(heads)]
    own_parts = [crossed(cut[heads + turn], turn) for turn in range(heads)]
    inner, moving = call(
        functools.partial(queries_kernel, axes, blocks),
        [array((units, BLOCK, BLOCK), F32), array((units, pairs + 1, *tile))],
        [VMEM] * 4 + [ANY] * heads,
        0,
        [pltpu.VMEM((heads, tokens, HEAD_DIM), BF16), pltpu.SemaphoreType.DMA((heads,))],
    )(parts, mixed, even, pair_map, *query_parts)
    weights = call(
        functools.partial(weights_kernel, before),
        array((units, BLOCK, TOPK * BLOCK)),
        [SMEM] + [VMEM] * (4 + before + len(map_parts)),
        0,
    )(away, moving, inner, end, tail, *far_parts, *map_parts)
    attended, *weight_parts = call(
        functools.partial(blend_kernel, axes, before, blocks),
        [array((heads, planes, blocks, *tile))] + [array(part.shape) for part in weight_parts],
        [SMEM, VMEM] + [ANY] * (heads + len(value_parts) + len(weight_parts)),
        0,
        [
            pltpu.VMEM((1 + before, units * BLOCK, HEAD_DIM), BF16),
            pltpu.SemaphoreType.DMA((1 + before, heads)),
            pltpu.SemaphoreType.DMA((planes,)),
        ],
    )(away, weights, *own_parts, *value_parts, *weight_parts)

    returns = [
        [
            (group * heads + place) * head_size + p * cores + core
            for place in range(heads)
            for p in range(planes)
        ]
        for group in range(groups)
        for core in range(cores)
    ]
    local = lax.all_to_all(
        attended.reshape(heads * planes, blocks, *tile),
        axes, 0, 0, axis_index_groups=returns, tiled=True,
    ).reshape(heads, planes, blocks, *tile)

    def projected(other, kind):
        return call(
            functools.partial(project_kernel, axes, other, cores),
            array((tokens, width // cores), kind),
            [VMEM] * (1 + planes),
            128 * cubes,
        )(local, out_weight, *weight_parts)

    arrived = lax.ppermute(projected(1, BF16), "head", partners)
    return (projected(0, F32) + arrived.astype(F32)).astype(BF16)


def solution(mesh):
    in_specs = (
        P("ctx", "head"),
        P("ctx", "head"),
        P("ctx", "head"),
        P("ctx", "head"),
        P("head", "ctx"),
        P("ctx", None),
        P("head", None),
    )
    out_specs = P("ctx", "head")
    return jax.shard_map(
        functools.partial(body, mesh.shape["ctx"], mesh.shape["head"]),
        mesh=mesh,
        in_specs=in_specs,
        out_specs=out_specs,
        check_vma=False,
    )
```

```python
import functools

import jax
import jax.numpy as jnp
from jax import lax
from jax.experimental import pallas as pl
from jax.experimental.pallas import tpu as pltpu
from jax.sharding import PartitionSpec as P

HEAD_DIM = 128
BLOCK = 128
LOOK = 7
TOPK = 4
BASE = 16
EXTRA = 16
TERMS = 3
BF16 = jnp.bfloat16
F32 = jnp.float32
VMEM = pl.BlockSpec(memory_space=pltpu.VMEM)
SMEM = pl.BlockSpec(memory_space=pltpu.SMEM)
ANY = pl.BlockSpec(memory_space=pl.ANY)


def dot(left, right, left_dim, right_dim):
    return lax.dot_general(
        left, right, (((left_dim,), (right_dim,)), ((), ())), preferred_element_type=F32
    )


def nn(left, right):
    return dot(left, right, 1, 0)


def nt(left, right):
    return dot(left, right, 1, 1)


def tn(left, right):
    return dot(left, right, 0, 0)


def split(value):
    high = value.astype(BF16)
    return high, (value - high.astype(F32)).astype(BF16)


def triple(product, left, right):
    rows = left[0].shape[0]
    first = product(jnp.concatenate(left, 0), right[0])
    return first[:rows] + (first[rows:] + product(left[0], right[1]))


def square_iotas():
    rows = lax.broadcasted_iota(jnp.int32, (BLOCK, BLOCK), 0)
    columns = lax.broadcasted_iota(jnp.int32, (BLOCK, BLOCK), 1)
    return rows, columns


def fetched(sources, targets, sems):
    copies = []
    for index, (source, target) in enumerate(zip(sources, targets)):
        copies.append(pltpu.make_async_copy(source, target, sems.at[index]))
        copies[-1].start()
    return copies


def pack_kernel(axes, cores, d_ref, k_ref, rates_hbm, selected_hbm, values_ref, weight_ref,
                *refs):
    tokens = d_ref.shape[0]
    heads = d_ref.shape[1] // HEAD_DIM
    blocks = tokens // BLOCK
    (parts_ref, rates_ref, selected_ref, cut_ref, piece_ref, sems, few_sems, out_sems, cut_sems,
     cut_out_sems, piece_sems) = refs[-11:]
    rounds = heads // 2
    out_ref, cut_outs = refs[0], refs[1:1 + rounds]
    inner_outs, piece_outs = refs[1 + rounds:rounds + heads - 1], refs[rounds + heads - 1:-11]
    planes = len(piece_outs) + 1
    width = weight_ref.shape[1] // planes
    device = lax.axis_index(axes[0])
    place = lax.rem(device, heads)
    plane = lax.axis_index(axes[1]) // cores
    first_block = device * blocks
    few_copies = fetched([rates_hbm, selected_hbm], [rates_ref, selected_ref], few_sems)
    sources = (d_ref, k_ref)
    copies = []
    for head in range(heads):
        columns = pl.ds(head * HEAD_DIM, HEAD_DIM)
        for kind, source in enumerate(sources):
            copies.append(
                pltpu.make_async_copy(
                    source.at[:, columns],
                    parts_ref.at[head, pl.ds(kind * tokens, tokens)],
                    sems.at[head, kind],
                )
            )
            copies[-1].start()
    cuts = [
        pl.multiple_of(lax.bitwise_xor(place, turn) * HEAD_DIM, HEAD_DIM) for turn in range(heads)
    ]
    cut_copies = fetched(
        [values_ref.at[:, pl.ds(cut, HEAD_DIM)] for cut in cuts],
        [cut_ref.at[turn // 2, turn % 2] for turn in range(heads)],
        cut_sems,
    )
    piece_copies = []
    for offset in range(1, planes):
        start = pl.multiple_of(lax.rem(plane + planes - offset, planes) * width, width)
        piece_copies += fetched(
            [weight_ref.at[:, pl.ds(start, width)]],
            [piece_ref.at[offset - 1]],
            piece_sems.at[0, pl.ds(offset - 1, 1)],
        )
    for copy in few_copies:
        copy.wait()
    row = lax.broadcasted_iota(jnp.int32, (EXTRA, HEAD_DIM), 0)
    lane = lax.broadcasted_iota(jnp.int32, (EXTRA, HEAD_DIM), 1)
    away = jnp.zeros((EXTRA, HEAD_DIM), jnp.int32)
    for block in range(blocks):
        for entry in range(TOPK):
            distance = first_block + block - selected_ref[block, entry]
            away = jnp.where((row == TERMS * blocks + block) & (lane == entry), distance, away)
    away = away.astype(F32)
    terms = []
    rest = rates_ref[...]
    for _ in range(TERMS):
        terms.append(rest.astype(BF16).astype(F32))
        rest = rest - terms[-1]
    out_copies = []
    for head in range(heads):
        extra = away
        for block in range(blocks):
            for index, term in enumerate(terms):
                piece = term[head:head + 1, block * BLOCK:(block + 1) * BLOCK]
                extra = jnp.where(row == TERMS * block + index, piece, extra)
        parts_ref[head, len(sources) * tokens:] = extra.astype(BF16)
        for copy in copies[len(sources) * head:len(sources) * (head + 1)]:
            copy.wait()
        out_copies.append(
            pltpu.make_async_copy(parts_ref.at[head], out_ref.at[head], out_sems.at[head])
        )
        out_copies[-1].start()
    for turn in range(rounds):
        cut_copies[2 * turn].wait()
        cut_copies[2 * turn + 1].wait()
        out_copies += fetched(
            [cut_ref.at[turn]], [cut_outs[turn]], cut_out_sems.at[0, pl.ds(turn, 1)]
        )
    out_copies += fetched(
        [cut_ref.at[turn // 2, turn % 2] for turn in range(2, heads)], inner_outs, cut_out_sems.at[1]
    )
    for index, copy in enumerate(piece_copies):
        copy.wait()
        out_copies += fetched(
            [piece_ref.at[index]], [piece_outs[index]], piece_sems.at[1, pl.ds(index, 1)]
        )
    for copy in out_copies:
        copy.wait()


def cut_kernel(axes, heads, count, queries_ref, values_ref, *refs):
    come, (stay_ref, hand_ref, sems, hand_sems) = refs[:count], refs[-4:]
    outs = refs[-4 - heads:-4]
    place = lax.rem(lax.axis_index(axes[0]), heads)
    cuts = [
        pl.multiple_of(lax.bitwise_xor(place, turn) * HEAD_DIM, HEAD_DIM) for turn in range(heads)
    ]
    copies = fetched([queries_ref.at[:, pl.ds(cut, HEAD_DIM)] for cut in cuts], outs, sems)
    copies += fetched(
        [values_ref.at[:, pl.ds(cut, HEAD_DIM)] for cut in cuts[:2]]
        + [part.at[1] for part in come],
        [stay_ref] + [hand_ref.at[index] for index in range(1 + count)],
        hand_sems,
    )
    for copy in copies:
        copy.wait()


def rows_of(ref, blocks, unit, kind):
    start = (kind * blocks + unit % blocks) * BLOCK
    return ref[unit // blocks, start:start + BLOCK]


def base_inverse(strict):
    count = BLOCK // BASE
    moved = [
        pltpu.roll(strict[b * BASE:(b + 1) * BASE], (BLOCK - b * BASE) % BLOCK, 1)
        if b else strict[:BASE]
        for b in range(count)
    ]
    lanes = lax.broadcasted_iota(jnp.int32, (BASE // 2, BLOCK), 1)
    rows = lax.broadcasted_iota(jnp.int32, (BASE // 2, BLOCK), 0)
    half = BASE // 2
    parts = []
    for b in range(count):
        upper = (lanes == rows + b * BASE).astype(F32)
        lower = (lanes == rows + b * BASE + half).astype(F32)
        for step in range(BASE - 1):
            if step < half:
                source = upper[step:step + 1]
                if step < half - 1:
                    upper = upper - moved[b][:half, step:step + 1] * source
            else:
                source = lower[step - half:step - half + 1]
            lower = lower - moved[b][half:, step:step + 1] * source
        parts += [upper, lower]
    return jnp.concatenate(parts, 0)


def halves(value, size):
    parts = value.reshape(BLOCK // (2 * size), 2, size, BLOCK)
    return parts[:, 0].reshape(BLOCK // 2, BLOCK), parts[:, 1].reshape(BLOCK // 2, BLOCK)


def joined(first, second, size):
    shape = (BLOCK // (2 * size), 1, size, BLOCK)
    return jnp.concatenate([first.reshape(shape), second.reshape(shape)], 1).reshape(BLOCK, BLOCK)


def interleaved(steps, lag):
    running = list(steps)
    tick = 0
    while any(step is not None for step in running):
        for index, step in enumerate(running):
            if step is not None and tick >= index * lag:
                try:
                    next(step)
                except StopIteration:
                    running[index] = None
        tick += 1


def keys_kernel(blocks, part_ref, end_ref, tail_ref, far_ref, even_ref, pair_ref, group_ref,
                mixed_ref, away_ref):
    units = part_ref.shape[0] * blocks
    rows, columns = square_iotas()
    diagonal = rows == columns
    identity = diagonal.astype(F32)
    row = lax.broadcasted_iota(jnp.int32, (BLOCK // 2, BLOCK), 0)
    column = lax.broadcasted_iota(jnp.int32, (BLOCK // 2, BLOCK), 1)
    ends, maps = [None] * units, [None] * units

    def terms(unit):
        direction = rows_of(part_ref, blocks, unit, 0)
        key = rows_of(part_ref, blocks, unit, 1)
        extra = part_ref[unit // blocks, 2 * blocks * BLOCK:].astype(F32)
        first = TERMS * (unit % blocks)
        rate = extra[first:first + 1] + extra[first + 1:first + 2] + extra[first + 2:first + 3]
        listed = TERMS * blocks + unit % blocks
        away_ref[unit:unit + 1] = extra[listed:listed + 1].astype(jnp.int32)
        gram = nt(direction, direction)
        key_proj = jnp.where(rows > columns, nt(direction, key), 0.0).astype(BF16)
        squares = jnp.sum(jnp.where(diagonal, gram, 0.0), 0, keepdims=True)
        scale = lax.rsqrt(squares + 1e-06)
        scaled_rate = rate * scale
        scale_column = jnp.sum(jnp.where(diagonal, scale, 0.0), 1, keepdims=True)
        rate_column = jnp.sum(jnp.where(diagonal, scaled_rate, 0.0), 1, keepdims=True)
        strict = jnp.where(rows > columns, rate_column * gram * scale, 0.0)
        yield
        inverse = base_inverse(strict)
        yield
        size = BASE
        while size < BLOCK:
            inside = (row // size == column // (2 * size)) & (lax.rem(column, 2 * size) < size)
            corner = jnp.where(inside, halves(strict, size)[1], 0.0)
            below = triple(nn, split(corner), split(inverse))
            yield
            first_half, second = halves(inverse, size)
            padded = joined(jnp.zeros_like(below), below, size)
            second = second - triple(nn, split(second), split(padded))
            inverse = joined(first_half, second, size)
            size *= 2
            yield
        mixing = split(scale_column * inverse * scaled_rate)
        mixed = nn(jnp.concatenate(mixing, 0), jnp.concatenate([direction, key_proj], 1))
        mixed = split(mixed[:BLOCK] + mixed[BLOCK:])
        mixed_ref[unit] = mixed[0]
        yield
        behind = tn(jnp.concatenate([mixed[0], mixed[1][:, :BLOCK]], 1), direction)
        ends[unit] = key.astype(F32) - behind[BLOCK:2 * BLOCK]
        maps[unit] = split(identity - (behind[:BLOCK] + behind[2 * BLOCK:]))
        end_ref[unit] = ends[unit].astype(BF16)

    onward = []

    def pair_terms(pair):
        even, odd = 2 * pair, 2 * pair + 1
        running = [terms(even), terms(odd)]
        while running:
            for step in list(running):
                if next(step, running) is running:
                    running.remove(step)
            yield
        even_ref[pair, 0] = maps[even][0]
        even_ref[pair, 1] = maps[even][1]
        left = jnp.concatenate([ends[even].astype(BF16), *maps[even]], 0)
        both = nn(left, maps[odd][0])
        tail_even, tail_odd = both[:BLOCK].astype(BF16), ends[odd].astype(BF16)
        tail_ref[even] = tail_even
        tail_ref[odd] = tail_odd
        low = both[2 * BLOCK:] + nn(maps[even][0], maps[odd][1])
        pair_map = split(both[BLOCK:2 * BLOCK] + low)
        pair_ref[pair, 0] = pair_map[0]
        pair_ref[pair, 1] = pair_map[1]
        yield
        if onward:
            far = nn(jnp.concatenate([tail_even, tail_odd], 0), onward[-1][0]).astype(BF16)
            far_ref[even] = far[:BLOCK]
            far_ref[odd] = far[BLOCK:]
            pair_map = split(triple(nn, pair_map, onward[-1]))
        else:
            far_ref[even] = tail_even
            far_ref[odd] = tail_odd
        onward.append(pair_map)

    interleaved([pair_terms(pair) for pair in reversed(range(units // 2))], 1)
    group_ref[0] = onward[-1][0]
    group_ref[1] = onward[-1][1]


def queries_kernel(axes, blocks, part_ref, mixed_ref, even_ref, pair_ref, *refs):
    heads = part_ref.shape[0]
    units = heads * blocks
    inner_ref, moving_ref, query_ref, sems = refs[heads:]
    place = lax.rem(lax.axis_index(axes[0]), heads)
    copies = fetched(
        refs[:heads],
        [query_ref.at[lax.bitwise_xor(place, turn)] for turn in range(heads)],
        sems,
    )
    for copy in copies:
        copy.wait()
    rows, columns = square_iotas()
    current = []
    for unit in range(units):
        direction = rows_of(part_ref, blocks, unit, 0)
        key = rows_of(part_ref, blocks, unit, 1)
        query = rows_of(query_ref, blocks, unit, 0)
        query_proj = split(jnp.where(rows >= columns, nt(query, direction), 0.0))
        ahead = nn(jnp.concatenate(query_proj, 0), mixed_ref[unit])
        ahead = ahead[:BLOCK] + ahead[BLOCK:]
        inner_ref[unit] = nt(query, key) - ahead[:, HEAD_DIM:]
        start = split(query.astype(F32) - ahead[:, :HEAD_DIM])
        moving_ref[unit, 0] = start[0]
        if unit % 2:
            pair = unit // 2
            start = split(triple(nt, start, (even_ref[pair, 0], even_ref[pair, 1])))
        moving_ref[unit, 1] = start[0]
        current.append(start)
    pairs = units // 2
    current = [
        tuple(jnp.concatenate([current[2 * pair][part], current[2 * pair + 1][part]], 0)
              for part in range(2))
        for pair in range(pairs)
    ]
    for step in range(2, pairs + 1):
        for pair in range(step - 1, pairs):
            passed = pair - step + 1
            current[pair] = split(
                triple(nt, current[pair], (pair_ref[passed, 0], pair_ref[passed, 1]))
            )
            moving_ref[2 * pair, step] = current[pair][0][:BLOCK]
            moving_ref[2 * pair + 1, step] = current[pair][0][BLOCK:]


def listed_block(away_ref, unit, entry):
    away = away_ref[unit, entry]
    new = away > 0
    for other in range(1, entry):
        new = new & (away_ref[unit, other] != away)
    return unit - away, new


def earlier(source, ahead, units):
    return jnp.clip(source + ahead * units, 0, units - 1), source < (1 - ahead) * units


def weights_kernel(before, away_ref, moving_ref, inner_ref, end_ref, tail_ref, *refs):
    far_keys, group_maps, weights_ref = refs[:before], refs[before:-1], refs[-1]
    units = inner_ref.shape[0]
    rows, columns = square_iotas()
    scale = HEAD_DIM ** (-0.5)

    def steps(unit):
        pair = unit // 2
        fronts = [moving_ref[unit, pair + 1]]
        for group_map in group_maps:
            passed = nt(fronts[-1], group_map[0]) + nt(fronts[-1], group_map[1])
            fronts.append(passed.astype(BF16))
        score_list = [jnp.where(rows >= columns, inner_ref[unit] * scale, -1e30)]
        for entry in range(1, TOPK):
            source, new = listed_block(away_ref, unit, entry)
            inside = jnp.maximum(source, 0)
            step = jnp.maximum(pair - inside // 2, 0)
            query = moving_ref[unit, step]
            key = jnp.where(step == 0, end_ref[inside], tail_ref[inside])
            for ahead in range(1, before + 1):
                place, here = earlier(source, ahead, units)
                query = jnp.where(here, fronts[ahead - 1], query)
                key = jnp.where(here, far_keys[ahead - 1][place], key)
            score_list.append(jnp.where(new, nt(query, key) * scale, -1e30))
        yield
        scores = jnp.concatenate(score_list, 1)
        expos = jnp.exp(scores - jnp.max(scores, 1, keepdims=True))
        weights_ref[unit] = (expos / jnp.sum(expos, 1, keepdims=True)).astype(BF16)

    interleaved([steps(unit) for unit in range(units)], 1)


def blend_kernel(axes, before, blocks, away_ref, weights_ref, *refs):
    units = weights_ref.shape[0]
    heads = units // blocks
    rounds = heads // 2
    own, come = refs[:heads], refs[heads:heads + rounds * before]
    count = (len(refs) - 4 - heads - rounds * before) // 2
    out_ref, (values_ref, value_sems, sems) = refs[-4 - count], refs[-3:]
    place = lax.rem(lax.axis_index(axes[0]), heads)
    value_copies = []

    def put(source, kind, turn):
        start = pl.multiple_of(lax.bitwise_xor(place, turn) * blocks * BLOCK, BLOCK)
        value_copies.extend(
            fetched(
                [source],
                [values_ref.at[kind, pl.ds(start, blocks * BLOCK)]],
                value_sems.at[kind, pl.ds(turn, 1)],
            )
        )

    for turn in range(heads):
        put(own[turn].at[0] if turn == 1 else own[turn], 0, turn)
    for index in range(rounds * before):
        kind, turn = 1 + index // rounds, 2 * (index % rounds)
        put(come[index].at[0], kind, turn)
        put(own[1].at[1 + index], kind, turn + 1)
    start = heads + rounds * before
    copies = fetched(refs[start:start + count], refs[-3 - count:-3], sems)
    for copy in value_copies:
        copy.wait()

    def value_of(kind, block):
        return values_ref[kind, pl.ds(pl.multiple_of(block * BLOCK, BLOCK), BLOCK)]

    for unit in range(units):
        value_list = [value_of(0, unit)]
        for entry in range(1, TOPK):
            source, _ = listed_block(away_ref, unit, entry)
            kind, block = 0, jnp.maximum(source, 0)
            for ahead in range(1, before + 1):
                other, here = earlier(source, ahead, units)
                kind = jnp.where(here, ahead, kind)
                block = jnp.where(here, other, block)
            value_list.append(value_of(kind, block))
        blended = nn(weights_ref[unit], jnp.concatenate(value_list, 0)).astype(BF16)
        for plane in range(out_ref.shape[1]):
            out_ref[unit // blocks, plane, unit % blocks] = blended
    for copy in copies:
        copy.wait()


def project_kernel(axes, other, cores, attended_ref, own_ref, *refs):
    other_refs, out_ref = refs[:-1], refs[-1]
    heads, planes, blocks = attended_ref.shape[:3]
    index = lax.axis_index(axes[1])
    core, plane = lax.rem(index + other, cores), index // cores
    width = out_ref.shape[1]
    total = None
    for offset in range(planes):
        source = lax.rem(plane + offset, planes)
        attended = jnp.concatenate(
            [
                jnp.concatenate(
                    [attended_ref[head, source, block] for head in range(heads)], 1
                )
                for block in range(blocks)
            ],
            0,
        )
        if offset:
            start = pl.multiple_of(core * width, width)
            weight = other_refs[offset - 1][:, pl.ds(start, width)]
        else:
            start = pl.multiple_of((plane * cores + core) * width, width)
            weight = own_ref[:, pl.ds(start, width)]
        product = nn(attended, weight)
        total = product if total is None else total + product
    out_ref[...] = total.astype(out_ref.dtype)


def call(kernel, outs, specs, flops, scratch=(), places=None, space=32):
    if places is None:
        places = [VMEM] * len(outs) if isinstance(outs, list) else VMEM
    return pl.pallas_call(
        kernel,
        out_shape=outs,
        in_specs=specs,
        out_specs=places,
        scratch_shapes=list(scratch),
        compiler_params=pltpu.CompilerParams(vmem_limit_bytes=space * 2 ** 20),
        cost_estimate=pl.CostEstimate(flops=flops, bytes_accessed=2 ** 21, transcendentals=0),
    )


def body(ctx_size, head_size, queries, keys, values, directions, rates, selected, out_weight):
    tokens = queries.shape[0]
    blocks = tokens // BLOCK
    heads = queries.shape[1] // HEAD_DIM
    units = heads * blocks
    pairs = units // 2
    groups = ctx_size // heads
    before = min(groups - 1, -(-LOOK // heads))
    cores = 2
    planes = head_size // cores
    axes = ("ctx", "head")
    members = [[group * heads + place for place in range(heads)] for group in range(groups)]
    partners = [(g, g + 1 - 2 * (g % cores)) for g in range(head_size)]
    cubes = 2 * BLOCK ** 3
    tile = (BLOCK, HEAD_DIM)

    def exchange(value):
        return lax.all_to_all(value, "ctx", 0, 0, axis_index_groups=members, tiled=True)

    def onward(value, by):
        shift = by * heads
        return lax.ppermute(value, "ctx", [(i, i + shift) for i in range(ctx_size - shift)])

    def crossed(value, turn):
        pairs = [(i, i - i % heads + (i % heads ^ turn)) for i in range(ctx_size)]
        return lax.ppermute(value, "ctx", pairs) if turn else value

    def straight(value, turn, by):
        shift = by * heads
        pairs = [(i, (i ^ 2 * turn) + shift) for i in range(ctx_size - shift)]
        return lax.ppermute(value, "ctx", pairs)

    def array(shape, kind=BF16):
        return jax.ShapeDtypeStruct(shape, kind)

    part_shape = (heads, 2 * tokens + EXTRA, HEAD_DIM)
    width = out_weight.shape[1] // planes
    piece_shape = (out_weight.shape[0], width)
    rounds = heads // 2
    packed, *rest = call(
        functools.partial(pack_kernel, axes, cores),
        [array(part_shape)]
        + [array((2, tokens, HEAD_DIM))] * rounds
        + [array((tokens, HEAD_DIM))] * (heads - 2)
        + [array(piece_shape)] * (planes - 1),
        [ANY] * 6,
        cubes,
        [
            pltpu.VMEM(part_shape, BF16),
            pltpu.VMEM(rates.shape, F32),
            pltpu.SMEM(selected.shape, jnp.int32),
            pltpu.VMEM((rounds, 2, tokens, HEAD_DIM), BF16),
            pltpu.VMEM((max(planes - 1, 1), *piece_shape), BF16),
            pltpu.SemaphoreType.DMA((heads, 2)),
            pltpu.SemaphoreType.DMA((2,)),
            pltpu.SemaphoreType.DMA((heads,)),
            pltpu.SemaphoreType.DMA((heads,)),
            pltpu.SemaphoreType.DMA((2, heads)),
            pltpu.SemaphoreType.DMA((2, planes)),
        ],
        [ANY] * (rounds + heads - 2 + planes),
        56,
    )(directions, keys, rates, selected, values, out_weight)
    value_cuts, inner_cuts = rest[:rounds], rest[rounds:rounds + heads - 2]
    pieces = rest[rounds + heads - 2:]
    own_parts = [crossed(part, 2 + index) for index, part in enumerate(inner_cuts)]
    value_parts = [
        straight(value_cuts[turn], turn, by)
        for by in range(1, before + 1)
        for turn in range(rounds)
    ]
    weight_parts = []
    for offset in range(1, planes):
        turned = [(g, (g + head_size - cores * offset) % head_size) for g in range(head_size)]
        weight_parts.append(lax.ppermute(pieces[offset - 1], "head", turned))
    parts = exchange(packed)

    end, tail, far, even, pair_map, group_map, mixed, away = call(
        functools.partial(keys_kernel, blocks),
        [
            array((units, *tile)),
            array((units, *tile)),
            array((units, *tile)),
            array((pairs, 2, *tile)),
            array((pairs, 2, *tile)),
            array((2, *tile)),
            array((units, BLOCK, 2 * BLOCK)),
            array((units, HEAD_DIM), jnp.int32),
        ],
        [VMEM],
        400 * cubes,
    )(parts)
    far_parts = [onward(far, by) for by in range(1, before + 1)]
    map_parts = [onward(group_map, by) for by in range(1, before)]
    *cut, stay, hand = call(
        functools.partial(cut_kernel, axes, heads, len(value_parts)),
        [array((tokens, HEAD_DIM))] * (heads + 1)
        + [array((1 + len(value_parts), tokens, HEAD_DIM))],
        [ANY] * (2 + len(value_parts) + len(own_parts) + 1),
        2000 * cubes,
        [
            pltpu.SemaphoreType.DMA((heads,)),
            pltpu.SemaphoreType.DMA((2 + len(value_parts),)),
        ],
    )(queries, values, *value_parts, *own_parts, away)
    query_parts = [crossed(cut[turn], turn) for turn in range(heads)]
    own_parts = [stay, crossed(hand, 1), *own_parts]
    inner, moving = call(
        functools.partial(queries_kernel, axes, blocks),
        [array((units, BLOCK, BLOCK), F32), array((units, pairs + 1, *tile))],
        [VMEM] * 4 + [ANY] * heads,
        0,
        [pltpu.VMEM((heads, tokens, HEAD_DIM), BF16), pltpu.SemaphoreType.DMA((heads,))],
    )(parts, mixed, even, pair_map, *query_parts)
    weights = call(
        functools.partial(weights_kernel, before),
        array((units, BLOCK, TOPK * BLOCK)),
        [SMEM] + [VMEM] * (4 + before + len(map_parts)),
        0,
    )(away, moving, inner, end, tail, *far_parts, *map_parts)
    attended, *weight_parts = call(
        functools.partial(blend_kernel, axes, before, blocks),
        [array((heads, planes, blocks, *tile))] + [array(part.shape) for part in weight_parts],
        [SMEM, VMEM] + [ANY] * (heads + len(value_parts) + len(weight_parts)),
        0,
        [
            pltpu.VMEM((1 + before, units * BLOCK, HEAD_DIM), BF16),
            pltpu.SemaphoreType.DMA((1 + before, heads)),
            pltpu.SemaphoreType.DMA((planes,)),
        ],
    )(away, weights, *own_parts, *value_parts, *weight_parts)

    returns = [
        [
            (group * heads + place) * head_size + p * cores + core
            for place in range(heads)
            for p in range(planes)
        ]
        for group in range(groups)
        for core in range(cores)
    ]
    local = lax.all_to_all(
        attended.reshape(heads * planes, blocks, *tile),
        axes, 0, 0, axis_index_groups=returns, tiled=True,
    ).reshape(heads, planes, blocks, *tile)

    def projected(other, kind):
        return call(
            functools.partial(project_kernel, axes, other, cores),
            array((tokens, width // cores), kind),
            [VMEM] * (1 + planes),
            128 * cubes,
        )(local, out_weight, *weight_parts)

    arrived = lax.ppermute(projected(1, BF16), "head", partners)
    return (projected(0, F32) + arrived.astype(F32)).astype(BF16)


def solution(mesh):
    in_specs = (
        P("ctx", "head"),
        P("ctx", "head"),
        P("ctx", "head"),
        P("ctx", "head"),
        P("head", "ctx"),
        P("ctx", None),
        P("head", None),
    )
    out_specs = P("ctx", "head")
    return jax.shard_map(
        functools.partial(body, mesh.shape["ctx"], mesh.shape["head"]),
        mesh=mesh,
        in_specs=in_specs,
        out_specs=out_specs,
        check_vma=False,
    )
```

```python
import functools

import jax
import jax.numpy as jnp
from jax import lax
from jax.experimental import pallas as pl
from jax.experimental.pallas import tpu as pltpu
from jax.sharding import PartitionSpec as P

HEAD_DIM = 128
BLOCK = 128
LOOK = 7
TOPK = 4
BASE = 16
EXTRA = 16
TERMS = 3
BF16 = jnp.bfloat16
F32 = jnp.float32
VMEM = pl.BlockSpec(memory_space=pltpu.VMEM)
SMEM = pl.BlockSpec(memory_space=pltpu.SMEM)
ANY = pl.BlockSpec(memory_space=pl.ANY)


def dot(left, right, left_dim, right_dim):
    return lax.dot_general(
        left, right, (((left_dim,), (right_dim,)), ((), ())), preferred_element_type=F32
    )


def nn(left, right):
    return dot(left, right, 1, 0)


def nt(left, right):
    return dot(left, right, 1, 1)


def tn(left, right):
    return dot(left, right, 0, 0)


def split(value):
    high = value.astype(BF16)
    return high, (value - high.astype(F32)).astype(BF16)


def triple(product, left, right):
    rows = left[0].shape[0]
    first = product(jnp.concatenate(left, 0), right[0])
    return first[:rows] + (first[rows:] + product(left[0], right[1]))


def square_iotas():
    rows = lax.broadcasted_iota(jnp.int32, (BLOCK, BLOCK), 0)
    columns = lax.broadcasted_iota(jnp.int32, (BLOCK, BLOCK), 1)
    return rows, columns


def fetched(sources, targets, sems):
    copies = []
    for index, (source, target) in enumerate(zip(sources, targets)):
        copies.append(pltpu.make_async_copy(source, target, sems.at[index]))
        copies[-1].start()
    return copies


def pack_kernel(axes, cores, d_ref, k_ref, rates_hbm, selected_hbm, values_ref, weight_ref,
                *refs):
    tokens = d_ref.shape[0]
    heads = d_ref.shape[1] // HEAD_DIM
    blocks = tokens // BLOCK
    (parts_ref, rates_ref, selected_ref, cut_ref, piece_ref, sems, few_sems, out_sems, cut_sems,
     cut_out_sems, piece_sems) = refs[-11:]
    out_ref, cut_outs, piece_outs = refs[0], refs[1:1 + heads], refs[1 + heads:-11]
    planes = len(piece_outs) + 1
    width = weight_ref.shape[1] // planes
    device = lax.axis_index(axes[0])
    place = lax.rem(device, heads)
    plane = lax.axis_index(axes[1]) // cores
    first_block = device * blocks
    few_copies = fetched([rates_hbm, selected_hbm], [rates_ref, selected_ref], few_sems)
    sources = (d_ref, k_ref)
    copies = []
    for head in range(heads):
        columns = pl.ds(head * HEAD_DIM, HEAD_DIM)
        for kind, source in enumerate(sources):
            copies.append(
                pltpu.make_async_copy(
                    source.at[:, columns],
                    parts_ref.at[head, pl.ds(kind * tokens, tokens)],
                    sems.at[head, kind],
                )
            )
            copies[-1].start()
    cuts = [
        pl.multiple_of(lax.bitwise_xor(place, turn) * HEAD_DIM, HEAD_DIM) for turn in range(heads)
    ]
    cut_copies = fetched(
        [values_ref.at[:, pl.ds(cut, HEAD_DIM)] for cut in cuts],
        [cut_ref.at[turn] for turn in range(heads)],
        cut_sems,
    )
    piece_copies = []
    for offset in range(1, planes):
        start = pl.multiple_of(lax.rem(plane + planes - offset, planes) * width, width)
        piece_copies += fetched(
            [weight_ref.at[:, pl.ds(start, width)]],
            [piece_ref.at[offset - 1]],
            piece_sems.at[0, pl.ds(offset - 1, 1)],
        )
    for copy in few_copies:
        copy.wait()
    row = lax.broadcasted_iota(jnp.int32, (EXTRA, HEAD_DIM), 0)
    lane = lax.broadcasted_iota(jnp.int32, (EXTRA, HEAD_DIM), 1)
    away = jnp.zeros((EXTRA, HEAD_DIM), jnp.int32)
    for block in range(blocks):
        for entry in range(TOPK):
            distance = first_block + block - selected_ref[block, entry]
            away = jnp.where((row == TERMS * blocks + block) & (lane == entry), distance, away)
    away = away.astype(F32)
    terms = []
    rest = rates_ref[...]
    for _ in range(TERMS):
        terms.append(rest.astype(BF16).astype(F32))
        rest = rest - terms[-1]
    out_copies = []
    for head in range(heads):
        extra = away
        for block in range(blocks):
            for index, term in enumerate(terms):
                piece = term[head:head + 1, block * BLOCK:(block + 1) * BLOCK]
                extra = jnp.where(row == TERMS * block + index, piece, extra)
        parts_ref[head, len(sources) * tokens:] = extra.astype(BF16)
        for copy in copies[len(sources) * head:len(sources) * (head + 1)]:
            copy.wait()
        out_copies.append(
            pltpu.make_async_copy(parts_ref.at[head], out_ref.at[head], out_sems.at[head])
        )
        out_copies[-1].start()
    for turn in range(heads):
        cut_copies[turn].wait()
        out_copies += fetched(
            [cut_ref.at[turn]], [cut_outs[turn]], cut_out_sems.at[pl.ds(turn, 1)]
        )
    for index, copy in enumerate(piece_copies):
        copy.wait()
        out_copies += fetched(
            [piece_ref.at[index]], [piece_outs[index]], piece_sems.at[1, pl.ds(index, 1)]
        )
    for copy in out_copies:
        copy.wait()


def cut_kernel(axes, queries_ref, values_ref, *refs):
    sems = refs[-1]
    heads = sems.shape[1]
    outs = refs[-1 - 2 * heads:-1]
    place = lax.rem(lax.axis_index(axes[0]), heads)
    cuts = [
        pl.multiple_of(lax.bitwise_xor(place, turn) * HEAD_DIM, HEAD_DIM) for turn in range(heads)
    ]
    copies = []
    for kind, source in enumerate((queries_ref, values_ref)):
        copies += fetched(
            [source.at[:, pl.ds(cut, HEAD_DIM)] for cut in cuts],
            outs[kind * heads:(kind + 1) * heads],
            sems.at[kind],
        )
    for copy in copies:
        copy.wait()


def rows_of(ref, blocks, unit, kind):
    start = (kind * blocks + unit % blocks) * BLOCK
    return ref[unit // blocks, start:start + BLOCK]


def base_inverse(strict):
    count = BLOCK // BASE
    moved = [
        pltpu.roll(strict[b * BASE:(b + 1) * BASE], (BLOCK - b * BASE) % BLOCK, 1)
        if b else strict[:BASE]
        for b in range(count)
    ]
    lanes = lax.broadcasted_iota(jnp.int32, (BASE // 2, BLOCK), 1)
    rows = lax.broadcasted_iota(jnp.int32, (BASE // 2, BLOCK), 0)
    half = BASE // 2
    parts = []
    for b in range(count):
        upper = (lanes == rows + b * BASE).astype(F32)
        lower = (lanes == rows + b * BASE + half).astype(F32)
        for step in range(BASE - 1):
            if step < half:
                source = upper[step:step + 1]
                if step < half - 1:
                    upper = upper - moved[b][:half, step:step + 1] * source
            else:
                source = lower[step - half:step - half + 1]
            lower = lower - moved[b][half:, step:step + 1] * source
        parts += [upper, lower]
    return jnp.concatenate(parts, 0)


def halves(value, size):
    parts = value.reshape(BLOCK // (2 * size), 2, size, BLOCK)
    return parts[:, 0].reshape(BLOCK // 2, BLOCK), parts[:, 1].reshape(BLOCK // 2, BLOCK)


def joined(first, second, size):
    shape = (BLOCK // (2 * size), 1, size, BLOCK)
    return jnp.concatenate([first.reshape(shape), second.reshape(shape)], 1).reshape(BLOCK, BLOCK)


def interleaved(steps, lag):
    running = list(steps)
    tick = 0
    while any(step is not None for step in running):
        for index, step in enumerate(running):
            if step is not None and tick >= index * lag:
                try:
                    next(step)
                except StopIteration:
                    running[index] = None
        tick += 1


def keys_kernel(blocks, part_ref, end_ref, tail_ref, far_ref, even_ref, pair_ref, mixed_ref,
                away_ref, *group_refs):
    units = part_ref.shape[0] * blocks
    rows, columns = square_iotas()
    diagonal = rows == columns
    identity = diagonal.astype(F32)
    row = lax.broadcasted_iota(jnp.int32, (BLOCK // 2, BLOCK), 0)
    column = lax.broadcasted_iota(jnp.int32, (BLOCK // 2, BLOCK), 1)
    ends, maps = [None] * units, [None] * units

    def terms(unit):
        direction = rows_of(part_ref, blocks, unit, 0)
        key = rows_of(part_ref, blocks, unit, 1)
        extra = part_ref[unit // blocks, 2 * blocks * BLOCK:].astype(F32)
        first = TERMS * (unit % blocks)
        rate = extra[first:first + 1] + extra[first + 1:first + 2] + extra[first + 2:first + 3]
        listed = TERMS * blocks + unit % blocks
        away_ref[unit:unit + 1] = extra[listed:listed + 1].astype(jnp.int32)
        gram = nt(direction, direction)
        key_proj = jnp.where(rows > columns, nt(direction, key), 0.0).astype(BF16)
        squares = jnp.sum(jnp.where(diagonal, gram, 0.0), 0, keepdims=True)
        scale = lax.rsqrt(squares + 1e-06)
        scaled_rate = rate * scale
        scale_column = jnp.sum(jnp.where(diagonal, scale, 0.0), 1, keepdims=True)
        rate_column = jnp.sum(jnp.where(diagonal, scaled_rate, 0.0), 1, keepdims=True)
        strict = jnp.where(rows > columns, rate_column * gram * scale, 0.0)
        yield
        inverse = base_inverse(strict)
        yield
        size = BASE
        while size < BLOCK:
            inside = (row // size == column // (2 * size)) & (lax.rem(column, 2 * size) < size)
            corner = jnp.where(inside, halves(strict, size)[1], 0.0)
            below = triple(nn, split(corner), split(inverse))
            yield
            first_half, second = halves(inverse, size)
            padded = joined(jnp.zeros_like(below), below, size)
            second = second - triple(nn, split(second), split(padded))
            inverse = joined(first_half, second, size)
            size *= 2
            yield
        mixing = split(scale_column * inverse * scaled_rate)
        mixed = nn(mixing[0], jnp.concatenate([direction, key_proj], 1))
        mixed_map = split(mixed[:, :BLOCK] + nn(mixing[1], direction))
        mixed = jnp.concatenate([mixed_map[0], mixed[:, BLOCK:].astype(BF16)], 1)
        mixed_ref[unit] = mixed
        yield
        behind = tn(jnp.concatenate([mixed, mixed_map[1]], 1), direction)
        ends[unit] = key.astype(F32) - behind[BLOCK:2 * BLOCK]
        maps[unit] = split(identity - (behind[:BLOCK] + behind[2 * BLOCK:]))
        end_ref[unit] = ends[unit].astype(BF16)

    onward = []

    def pair_terms(pair):
        even, odd = 2 * pair, 2 * pair + 1
        running = [terms(even), terms(odd)]
        while running:
            for step in list(running):
                if next(step, running) is running:
                    running.remove(step)
            yield
        even_ref[pair, 0] = maps[even][0]
        even_ref[pair, 1] = maps[even][1]
        left = jnp.concatenate([ends[even].astype(BF16), *maps[even]], 0)
        both = nn(left, maps[odd][0])
        tail_even, tail_odd = both[:BLOCK].astype(BF16), ends[odd].astype(BF16)
        tail_ref[even] = tail_even
        tail_ref[odd] = tail_odd
        low = both[2 * BLOCK:] + nn(maps[even][0], maps[odd][1])
        pair_map = split(both[BLOCK:2 * BLOCK] + low)
        pair_ref[pair, 0] = pair_map[0]
        pair_ref[pair, 1] = pair_map[1]
        yield
        if onward:
            far = nn(jnp.concatenate([tail_even, tail_odd], 0), onward[-1][0]).astype(BF16)
            far_ref[even] = far[:BLOCK]
            far_ref[odd] = far[BLOCK:]
            if pair or group_refs:
                pair_map = split(triple(nn, pair_map, onward[-1]))
        else:
            far_ref[even] = tail_even
            far_ref[odd] = tail_odd
        onward.append(pair_map)

    interleaved([pair_terms(pair) for pair in reversed(range(units // 2))], 1)
    for group_ref in group_refs:
        group_ref[0] = onward[-1][0]
        group_ref[1] = onward[-1][1]


def queries_kernel(axes, blocks, part_ref, mixed_ref, even_ref, pair_ref, *refs):
    heads = part_ref.shape[0]
    units = heads * blocks
    inner_ref, moving_ref, query_ref, sems = refs[heads:]
    place = lax.rem(lax.axis_index(axes[0]), heads)
    copies = fetched(
        refs[:heads],
        [query_ref.at[lax.bitwise_xor(place, turn)] for turn in range(heads)],
        sems,
    )
    for copy in copies:
        copy.wait()
    rows, columns = square_iotas()
    current = []
    for unit in range(units):
        direction = rows_of(part_ref, blocks, unit, 0)
        key = rows_of(part_ref, blocks, unit, 1)
        query = rows_of(query_ref, blocks, unit, 0)
        query_proj = split(jnp.where(rows >= columns, nt(query, direction), 0.0))
        ahead = nn(jnp.concatenate(query_proj, 0), mixed_ref[unit])
        ahead = ahead[:BLOCK] + ahead[BLOCK:]
        inner_ref[unit] = nt(query, key) - ahead[:, HEAD_DIM:]
        start = split(query.astype(F32) - ahead[:, :HEAD_DIM])
        moving_ref[unit, 0] = start[0]
        if unit % 2:
            pair = unit // 2
            start = split(triple(nt, start, (even_ref[pair, 0], even_ref[pair, 1])))
        moving_ref[unit, 1] = start[0]
        current.append(start)
    pairs = units // 2
    current = [
        tuple(jnp.concatenate([current[2 * pair][part], current[2 * pair + 1][part]], 0)
              for part in range(2))
        for pair in range(pairs)
    ]
    for step in range(2, pairs + 1):
        for pair in range(step - 1, pairs):
            passed = pair - step + 1
            current[pair] = split(
                triple(nt, current[pair], (pair_ref[passed, 0], pair_ref[passed, 1]))
            )
            moving_ref[2 * pair, step] = current[pair][0][:BLOCK]
            moving_ref[2 * pair + 1, step] = current[pair][0][BLOCK:]


def listed_block(away_ref, unit, entry):
    away = away_ref[unit, entry]
    new = away > 0
    for other in range(1, entry):
        new = new & (away_ref[unit, other] != away)
    return unit - away, new


def earlier(source, ahead, units):
    return jnp.clip(source + ahead * units, 0, units - 1), source < (1 - ahead) * units


def weights_kernel(before, away_ref, moving_ref, inner_ref, end_ref, tail_ref, *refs):
    far_keys, group_maps, weights_ref = refs[:before], refs[before:-1], refs[-1]
    units = inner_ref.shape[0]
    rows, columns = square_iotas()
    scale = HEAD_DIM ** (-0.5)

    def steps(unit):
        pair = unit // 2
        fronts = [moving_ref[unit, pair + 1]]
        for group_map in group_maps:
            passed = nt(fronts[-1], group_map[0]) + nt(fronts[-1], group_map[1])
            fronts.append(passed.astype(BF16))
        score_list = [jnp.where(rows >= columns, inner_ref[unit] * scale, -1e30)]
        for entry in range(1, TOPK):
            source, new = listed_block(away_ref, unit, entry)
            inside = jnp.maximum(source, 0)
            step = jnp.maximum(pair - inside // 2, 0)
            query = moving_ref[unit, step]
            key = jnp.where(step == 0, end_ref[inside], tail_ref[inside])
            for ahead in range(1, before + 1):
                place, here = earlier(source, ahead, units)
                query = jnp.where(here, fronts[ahead - 1], query)
                key = jnp.where(here, far_keys[ahead - 1][place], key)
            score_list.append(jnp.where(new, nt(query, key) * scale, -1e30))
        yield
        scores = jnp.concatenate(score_list, 1)
        expos = jnp.exp(scores - jnp.max(scores, 1, keepdims=True))
        weights_ref[unit] = (expos * (1.0 / jnp.sum(expos, 1, keepdims=True))).astype(BF16)

    interleaved([steps(unit) for unit in range(units)], 1)


def blend_kernel(axes, before, blocks, away_ref, weights_ref, *refs):
    units = weights_ref.shape[0]
    heads = units // blocks
    count = (len(refs) - 4 - heads * (1 + before)) // 2
    arrived = refs[:heads * (1 + before)]
    out_ref, (values_ref, value_sems, sems) = refs[-4 - count], refs[-3:]
    place = lax.rem(lax.axis_index(axes[0]), heads)
    value_copies = []
    for kind in range(1 + before):
        for turn in range(heads):
            start = pl.multiple_of(lax.bitwise_xor(place, turn) * blocks * BLOCK, BLOCK)
            value_copies += fetched(
                [arrived[kind * heads + turn]],
                [values_ref.at[kind, pl.ds(start, blocks * BLOCK)]],
                value_sems.at[kind, pl.ds(turn, 1)],
            )
    copies = fetched(
        refs[heads * (1 + before):heads * (1 + before) + count], refs[-3 - count:-3], sems
    )
    for copy in value_copies:
        copy.wait()

    def value_of(kind, block):
        return values_ref[kind, pl.ds(pl.multiple_of(block * BLOCK, BLOCK), BLOCK)]

    for unit in range(units):
        value_list = [value_of(0, unit)]
        for entry in range(1, TOPK):
            source, _ = listed_block(away_ref, unit, entry)
            kind, block = 0, jnp.maximum(source, 0)
            for ahead in range(1, before + 1):
                other, here = earlier(source, ahead, units)
                kind = jnp.where(here, ahead, kind)
                block = jnp.where(here, other, block)
            value_list.append(value_of(kind, block))
        blended = nn(weights_ref[unit], jnp.concatenate(value_list, 0)).astype(BF16)
        for plane in range(out_ref.shape[1]):
            out_ref[unit // blocks, plane, unit % blocks] = blended
    for copy in copies:
        copy.wait()


def project_kernel(axes, other, cores, attended_ref, own_ref, *refs):
    other_refs, out_ref = refs[:-1], refs[-1]
    heads, planes, blocks = attended_ref.shape[:3]
    index = lax.axis_index(axes[1])
    core, plane = lax.rem(index + other, cores), index // cores
    width = out_ref.shape[1]
    total = None
    for offset in range(planes):
        source = lax.rem(plane + offset, planes)
        attended = jnp.concatenate(
            [
                jnp.concatenate(
                    [attended_ref[head, source, block] for head in range(heads)], 1
                )
                for block in range(blocks)
            ],
            0,
        )
        if offset:
            start = pl.multiple_of(core * width, width)
            weight = other_refs[offset - 1][:, pl.ds(start, width)]
        else:
            start = pl.multiple_of((plane * cores + core) * width, width)
            weight = own_ref[:, pl.ds(start, width)]
        product = nn(attended, weight)
        total = product if total is None else total + product
    out_ref[...] = total.astype(out_ref.dtype)


def call(kernel, outs, specs, flops, scratch=(), places=None, space=32):
    if places is None:
        places = [VMEM] * len(outs) if isinstance(outs, list) else VMEM
    return pl.pallas_call(
        kernel,
        out_shape=outs,
        in_specs=specs,
        out_specs=places,
        scratch_shapes=list(scratch),
        compiler_params=pltpu.CompilerParams(vmem_limit_bytes=space * 2 ** 20),
        cost_estimate=pl.CostEstimate(flops=flops, bytes_accessed=2 ** 21, transcendentals=0),
    )


def body(ctx_size, head_size, queries, keys, values, directions, rates, selected, out_weight):
    tokens = queries.shape[0]
    blocks = tokens // BLOCK
    heads = queries.shape[1] // HEAD_DIM
    units = heads * blocks
    pairs = units // 2
    groups = ctx_size // heads
    before = min(groups - 1, -(-LOOK // heads))
    cores = 2
    planes = head_size // cores
    axes = ("ctx", "head")
    members = [[group * heads + place for place in range(heads)] for group in range(groups)]
    partners = [(g, g + 1 - 2 * (g % cores)) for g in range(head_size)]
    cubes = 2 * BLOCK ** 3
    tile = (BLOCK, HEAD_DIM)

    def exchange(value):
        return lax.all_to_all(value, "ctx", 0, 0, axis_index_groups=members, tiled=True)

    def onward(value, by):
        shift = by * heads
        return lax.ppermute(value, "ctx", [(i, i + shift) for i in range(ctx_size - shift)])

    def crossed(value, turn):
        pairs = [(i, i - i % heads + (i % heads ^ turn)) for i in range(ctx_size)]
        return lax.ppermute(value, "ctx", pairs) if turn else value

    def straight(value, turn, by):
        shift = by * heads
        pairs = [(i, i - i % heads + (i % heads ^ turn) + shift) for i in range(ctx_size - shift)]
        return lax.ppermute(value, "ctx", pairs)

    def array(shape, kind=BF16):
        return jax.ShapeDtypeStruct(shape, kind)

    part_shape = (heads, 2 * tokens + EXTRA, HEAD_DIM)
    width = out_weight.shape[1] // planes
    piece_shape = (out_weight.shape[0], width)
    packed, *rest = call(
        functools.partial(pack_kernel, axes, cores),
        [array(part_shape)]
        + [array((tokens, HEAD_DIM))] * heads
        + [array(piece_shape)] * (planes - 1),
        [ANY] * 6,
        cubes,
        [
            pltpu.VMEM(part_shape, BF16),
            pltpu.VMEM(rates.shape, F32),
            pltpu.SMEM(selected.shape, jnp.int32),
            pltpu.VMEM((heads, tokens, HEAD_DIM), BF16),
            pltpu.VMEM((max(planes - 1, 1), *piece_shape), BF16),
            pltpu.SemaphoreType.DMA((heads, 2)),
            pltpu.SemaphoreType.DMA((2,)),
            pltpu.SemaphoreType.DMA((heads,)),
            pltpu.SemaphoreType.DMA((heads,)),
            pltpu.SemaphoreType.DMA((heads,)),
            pltpu.SemaphoreType.DMA((2, planes)),
        ],
        [ANY] * (heads + planes),
        56,
    )(directions, keys, rates, selected, values, out_weight)
    value_cuts, pieces = rest[:heads], rest[heads:]
    value_parts = [
        straight(value_cuts[turn], turn, by) for by in range(1, before + 1) for turn in range(heads)
    ]
    weight_parts = []
    for offset in range(1, planes):
        turned = [(g, (g + head_size - cores * offset) % head_size) for g in range(head_size)]
        weight_parts.append(lax.ppermute(pieces[offset - 1], "head", turned))
    parts = exchange(packed)

    end, tail, far, even, pair_map, mixed, away, *group_maps = call(
        functools.partial(keys_kernel, blocks),
        [
            array((units, *tile)),
            array((units, *tile)),
            array((units, *tile)),
            array((pairs, 2, *tile)),
            array((pairs, 2, *tile)),
            array((units, BLOCK, 2 * BLOCK)),
            array((units, HEAD_DIM), jnp.int32),
        ]
        + [array((2, *tile))] * (before > 1),
        [VMEM],
        400 * cubes,
    )(parts)
    far_parts = [onward(far, by) for by in range(1, before + 1)]
    map_parts = [onward(group_maps[0], by) for by in range(1, before)]
    cut = call(
        functools.partial(cut_kernel, axes),
        [array((tokens, HEAD_DIM))] * (2 * heads),
        [ANY] * (len(value_parts) + 3),
        2000 * cubes,
        [pltpu.SemaphoreType.DMA((2, heads))],
    )(queries, values, *value_parts, away)
    query_parts = [crossed(cut[turn], turn) for turn in range(heads)]
    own_parts = [crossed(cut[heads + turn], turn) for turn in range(heads)]
    inner, moving = call(
        functools.partial(queries_kernel, axes, blocks),
        [array((units, BLOCK, BLOCK), F32), array((units, pairs + 1, *tile))],
        [VMEM] * 4 + [ANY] * heads,
        0,
        [pltpu.VMEM((heads, tokens, HEAD_DIM), BF16), pltpu.SemaphoreType.DMA((heads,))],
    )(parts, mixed, even, pair_map, *query_parts)
    weights = call(
        functools.partial(weights_kernel, before),
        array((units, BLOCK, TOPK * BLOCK)),
        [SMEM] + [VMEM] * (4 + before + len(map_parts)),
        0,
    )(away, moving, inner, end, tail, *far_parts, *map_parts)
    attended, *weight_parts = call(
        functools.partial(blend_kernel, axes, before, blocks),
        [array((heads, planes, blocks, *tile))] + [array(part.shape) for part in weight_parts],
        [SMEM, VMEM] + [ANY] * (heads * (1 + before) + len(weight_parts)),
        0,
        [
            pltpu.VMEM((1 + before, units * BLOCK, HEAD_DIM), BF16),
            pltpu.SemaphoreType.DMA((1 + before, heads)),
            pltpu.SemaphoreType.DMA((planes,)),
        ],
    )(away, weights, *own_parts, *value_parts, *weight_parts)

    returns = [
        [
            (group * heads + place) * head_size + p * cores + core
            for place in range(heads)
            for p in range(planes)
        ]
        for group in range(groups)
        for core in range(cores)
    ]
    local = lax.all_to_all(
        attended.reshape(heads * planes, blocks, *tile),
        axes, 0, 0, axis_index_groups=returns, tiled=True,
    ).reshape(heads, planes, blocks, *tile)

    def projected(other, kind):
        return call(
            functools.partial(project_kernel, axes, other, cores),
            array((tokens, width // cores), kind),
            [VMEM] * (1 + planes),
            128 * cubes,
        )(local, out_weight, *weight_parts)

    arrived = lax.ppermute(projected(1, BF16), "head", partners)
    return (projected(0, F32) + arrived.astype(F32)).astype(BF16)


def solution(mesh):
    in_specs = (
        P("ctx", "head"),
        P("ctx", "head"),
        P("ctx", "head"),
        P("ctx", "head"),
        P("head", "ctx"),
        P("ctx", None),
        P("head", None),
    )
    out_specs = P("ctx", "head")
    return jax.shard_map(
        functools.partial(body, mesh.shape["ctx"], mesh.shape["head"]),
        mesh=mesh,
        in_specs=in_specs,
        out_specs=out_specs,
        check_vma=False,
    )
```

```python
import functools

import jax
import jax.numpy as jnp
from jax import lax
from jax.experimental import pallas as pl
from jax.experimental.pallas import tpu as pltpu
from jax.sharding import PartitionSpec as P

HEAD_DIM = 128
BLOCK = 128
LOOK = 7
TOPK = 4
BASE = 16
EXTRA = 16
TERMS = 3
BF16 = jnp.bfloat16
F32 = jnp.float32
VMEM = pl.BlockSpec(memory_space=pltpu.VMEM)
SMEM = pl.BlockSpec(memory_space=pltpu.SMEM)
ANY = pl.BlockSpec(memory_space=pl.ANY)


def dot(left, right, left_dim, right_dim):
    return lax.dot_general(
        left, right, (((left_dim,), (right_dim,)), ((), ())), preferred_element_type=F32
    )


def nn(left, right):
    return dot(left, right, 1, 0)


def nt(left, right):
    return dot(left, right, 1, 1)


def tn(left, right):
    return dot(left, right, 0, 0)


def split(value):
    high = value.astype(BF16)
    return high, (value - high.astype(F32)).astype(BF16)


def triple(product, left, right):
    rows = left[0].shape[0]
    first = product(jnp.concatenate(left, 0), right[0])
    return first[:rows] + (first[rows:] + product(left[0], right[1]))


def square_iotas():
    rows = lax.broadcasted_iota(jnp.int32, (BLOCK, BLOCK), 0)
    columns = lax.broadcasted_iota(jnp.int32, (BLOCK, BLOCK), 1)
    return rows, columns


def fetched(sources, targets, sems):
    copies = []
    for index, (source, target) in enumerate(zip(sources, targets)):
        copies.append(pltpu.make_async_copy(source, target, sems.at[index]))
        copies[-1].start()
    return copies


def pack_kernel(axes, cores, d_ref, k_ref, rates_hbm, selected_hbm, values_ref, weight_ref,
                *refs):
    tokens = d_ref.shape[0]
    heads = d_ref.shape[1] // HEAD_DIM
    blocks = tokens // BLOCK
    (parts_ref, rates_ref, selected_ref, cut_ref, piece_ref, sems, few_sems, out_sems, cut_sems,
     cut_out_sems, piece_sems) = refs[-11:]
    out_ref, cut_outs, piece_outs = refs[0], refs[1:1 + heads], refs[1 + heads:-11]
    planes = len(piece_outs) + 1
    width = weight_ref.shape[1] // planes
    device = lax.axis_index(axes[0])
    place = lax.rem(device, heads)
    plane = lax.axis_index(axes[1]) // cores
    first_block = device * blocks
    few_copies = fetched([rates_hbm, selected_hbm], [rates_ref, selected_ref], few_sems)
    sources = (d_ref, k_ref)
    copies = []
    for head in range(heads):
        columns = pl.ds(head * HEAD_DIM, HEAD_DIM)
        for kind, source in enumerate(sources):
            copies.append(
                pltpu.make_async_copy(
                    source.at[:, columns],
                    parts_ref.at[head, pl.ds(kind * tokens, tokens)],
                    sems.at[head, kind],
                )
            )
            copies[-1].start()
    cuts = [
        pl.multiple_of(lax.bitwise_xor(place, turn) * HEAD_DIM, HEAD_DIM) for turn in range(heads)
    ]
    cut_copies = fetched(
        [values_ref.at[:, pl.ds(cut, HEAD_DIM)] for cut in cuts],
        [cut_ref.at[turn] for turn in range(heads)],
        cut_sems,
    )
    piece_copies = []
    for offset in range(1, planes):
        start = pl.multiple_of(lax.rem(plane + planes - offset, planes) * width, width)
        piece_copies += fetched(
            [weight_ref.at[:, pl.ds(start, width)]],
            [piece_ref.at[offset - 1]],
            piece_sems.at[0, pl.ds(offset - 1, 1)],
        )
    for copy in few_copies:
        copy.wait()
    row = lax.broadcasted_iota(jnp.int32, (EXTRA, HEAD_DIM), 0)
    lane = lax.broadcasted_iota(jnp.int32, (EXTRA, HEAD_DIM), 1)
    away = jnp.zeros((EXTRA, HEAD_DIM), jnp.int32)
    for block in range(blocks):
        for entry in range(TOPK):
            distance = first_block + block - selected_ref[block, entry]
            away = jnp.where((row == TERMS * blocks + block) & (lane == entry), distance, away)
    away = away.astype(F32)
    terms = []
    rest = rates_ref[...]
    for _ in range(TERMS):
        terms.append(rest.astype(BF16).astype(F32))
        rest = rest - terms[-1]
    out_copies = []
    for head in range(heads):
        extra = away
        for block in range(blocks):
            for index, term in enumerate(terms):
                piece = term[head:head + 1, block * BLOCK:(block + 1) * BLOCK]
                extra = jnp.where(row == TERMS * block + index, piece, extra)
        parts_ref[head, len(sources) * tokens:] = extra.astype(BF16)
        for copy in copies[len(sources) * head:len(sources) * (head + 1)]:
            copy.wait()
        out_copies.append(
            pltpu.make_async_copy(parts_ref.at[head], out_ref.at[head], out_sems.at[head])
        )
        out_copies[-1].start()
    for turn in range(heads):
        cut_copies[turn].wait()
        out_copies += fetched(
            [cut_ref.at[turn]], [cut_outs[turn]], cut_out_sems.at[pl.ds(turn, 1)]
        )
    for index, copy in enumerate(piece_copies):
        copy.wait()
        out_copies += fetched(
            [piece_ref.at[index]], [piece_outs[index]], piece_sems.at[1, pl.ds(index, 1)]
        )
    for copy in out_copies:
        copy.wait()


def cut_kernel(axes, queries_ref, values_ref, *refs):
    sems = refs[-1]
    heads = sems.shape[1]
    outs = refs[-1 - 2 * heads:-1]
    place = lax.rem(lax.axis_index(axes[0]), heads)
    cuts = [
        pl.multiple_of(lax.bitwise_xor(place, turn) * HEAD_DIM, HEAD_DIM) for turn in range(heads)
    ]
    copies = []
    for kind, source in enumerate((queries_ref, values_ref)):
        copies += fetched(
            [source.at[:, pl.ds(cut, HEAD_DIM)] for cut in cuts],
            outs[kind * heads:(kind + 1) * heads],
            sems.at[kind],
        )
    for copy in copies:
        copy.wait()


def rows_of(ref, blocks, unit, kind):
    start = (kind * blocks + unit % blocks) * BLOCK
    return ref[unit // blocks, start:start + BLOCK]


def base_inverse(strict):
    count = BLOCK // BASE
    moved = [
        pltpu.roll(strict[b * BASE:(b + 1) * BASE], (BLOCK - b * BASE) % BLOCK, 1)
        if b else strict[:BASE]
        for b in range(count)
    ]
    lanes = lax.broadcasted_iota(jnp.int32, (BASE // 2, BLOCK), 1)
    rows = lax.broadcasted_iota(jnp.int32, (BASE // 2, BLOCK), 0)
    half = BASE // 2
    parts = []
    for b in range(count):
        upper = (lanes == rows + b * BASE).astype(F32)
        lower = (lanes == rows + b * BASE + half).astype(F32)
        for step in range(BASE - 1):
            if step < half:
                source = upper[step:step + 1]
                if step < half - 1:
                    upper = upper - moved[b][:half, step:step + 1] * source
            else:
                source = lower[step - half:step - half + 1]
            lower = lower - moved[b][half:, step:step + 1] * source
        parts += [upper, lower]
    return jnp.concatenate(parts, 0)


def halves(value, size):
    parts = value.reshape(BLOCK // (2 * size), 2, size, BLOCK)
    return parts[:, 0].reshape(BLOCK // 2, BLOCK), parts[:, 1].reshape(BLOCK // 2, BLOCK)


def joined(first, second, size):
    shape = (BLOCK // (2 * size), 1, size, BLOCK)
    return jnp.concatenate([first.reshape(shape), second.reshape(shape)], 1).reshape(BLOCK, BLOCK)


def interleaved(steps, lag):
    running = list(steps)
    tick = 0
    while any(step is not None for step in running):
        for index, step in enumerate(running):
            if step is not None and tick >= index * lag:
                try:
                    next(step)
                except StopIteration:
                    running[index] = None
        tick += 1


def keys_kernel(blocks, part_ref, end_ref, tail_ref, far_ref, even_ref, pair_ref, mixed_ref,
                away_ref, *group_refs):
    units = part_ref.shape[0] * blocks
    rows, columns = square_iotas()
    diagonal = rows == columns
    identity = diagonal.astype(F32)
    row = lax.broadcasted_iota(jnp.int32, (BLOCK // 2, BLOCK), 0)
    column = lax.broadcasted_iota(jnp.int32, (BLOCK // 2, BLOCK), 1)
    ends, maps = [None] * units, [None] * units

    def terms(unit):
        direction = rows_of(part_ref, blocks, unit, 0)
        key = rows_of(part_ref, blocks, unit, 1)
        extra = part_ref[unit // blocks, 2 * blocks * BLOCK:].astype(F32)
        first = TERMS * (unit % blocks)
        rate = extra[first:first + 1] + extra[first + 1:first + 2] + extra[first + 2:first + 3]
        listed = TERMS * blocks + unit % blocks
        away_ref[unit:unit + 1] = extra[listed:listed + 1].astype(jnp.int32)
        gram = nt(direction, direction)
        key_proj = jnp.where(rows > columns, nt(direction, key), 0.0).astype(BF16)
        squares = jnp.sum(jnp.where(diagonal, gram, 0.0), 0, keepdims=True)
        scale = lax.rsqrt(squares + 1e-06)
        scaled_rate = rate * scale
        scale_column = jnp.sum(jnp.where(diagonal, scale, 0.0), 1, keepdims=True)
        rate_column = jnp.sum(jnp.where(diagonal, scaled_rate, 0.0), 1, keepdims=True)
        strict = jnp.where(rows > columns, rate_column * gram * scale, 0.0)
        yield
        inverse = base_inverse(strict)
        yield
        size = BASE
        while size < BLOCK:
            inside = (row // size == column // (2 * size)) & (lax.rem(column, 2 * size) < size)
            corner = jnp.where(inside, halves(strict, size)[1], 0.0)
            below = triple(nn, split(corner), split(inverse))
            yield
            first_half, second = halves(inverse, size)
            padded = joined(jnp.zeros_like(below), below, size)
            second = second - triple(nn, split(second), split(padded))
            inverse = joined(first_half, second, size)
            size *= 2
            yield
        mixing = split(scale_column * inverse * scaled_rate)
        mixed = nn(mixing[0], jnp.concatenate([direction, key_proj], 1))
        mixed_map = split(mixed[:, :BLOCK] + nn(mixing[1], direction))
        mixed = jnp.concatenate([mixed_map[0], mixed[:, BLOCK:].astype(BF16)], 1)
        mixed_ref[unit] = mixed
        yield
        behind = tn(jnp.concatenate([mixed, mixed_map[1]], 1), direction)
        ends[unit] = key.astype(F32) - behind[BLOCK:2 * BLOCK]
        maps[unit] = split(identity - (behind[:BLOCK] + behind[2 * BLOCK:]))
        end_ref[unit] = ends[unit].astype(BF16)

    onward = []

    def pair_terms(pair):
        even, odd = 2 * pair, 2 * pair + 1
        running = [terms(even), terms(odd)]
        while running:
            for step in list(running):
                if next(step, running) is running:
                    running.remove(step)
            yield
        even_ref[pair, 0] = maps[even][0]
        even_ref[pair, 1] = maps[even][1]
        left = jnp.concatenate([ends[even].astype(BF16), *maps[even]], 0)
        both = nn(left, maps[odd][0])
        tail_even, tail_odd = both[:BLOCK].astype(BF16), ends[odd].astype(BF16)
        tail_ref[even] = tail_even
        tail_ref[odd] = tail_odd
        low = both[2 * BLOCK:] + nn(maps[even][0], maps[odd][1])
        pair_map = split(both[BLOCK:2 * BLOCK] + low)
        pair_ref[pair, 0] = pair_map[0]
        pair_ref[pair, 1] = pair_map[1]
        yield
        if onward:
            far = nn(jnp.concatenate([tail_even, tail_odd], 0), onward[-1][0]).astype(BF16)
            far_ref[even] = far[:BLOCK]
            far_ref[odd] = far[BLOCK:]
            if pair or group_refs:
                pair_map = split(triple(nn, pair_map, onward[-1]))
        else:
            far_ref[even] = tail_even
            far_ref[odd] = tail_odd
        onward.append(pair_map)

    interleaved([pair_terms(pair) for pair in reversed(range(units // 2))], 2)
    for group_ref in group_refs:
        group_ref[0] = onward[-1][0]
        group_ref[1] = onward[-1][1]


def queries_kernel(axes, blocks, part_ref, mixed_ref, even_ref, pair_ref, *refs):
    heads = part_ref.shape[0]
    units = heads * blocks
    inner_ref, moving_ref, query_ref, sems = refs[heads:]
    place = lax.rem(lax.axis_index(axes[0]), heads)
    copies = fetched(
        refs[:heads],
        [query_ref.at[lax.bitwise_xor(place, turn)] for turn in range(heads)],
        sems,
    )
    for copy in copies:
        copy.wait()
    rows, columns = square_iotas()
    current = []
    for unit in range(units):
        direction = rows_of(part_ref, blocks, unit, 0)
        key = rows_of(part_ref, blocks, unit, 1)
        query = rows_of(query_ref, blocks, unit, 0)
        query_proj = split(jnp.where(rows >= columns, nt(query, direction), 0.0))
        ahead = nn(jnp.concatenate(query_proj, 0), mixed_ref[unit])
        ahead = ahead[:BLOCK] + ahead[BLOCK:]
        inner_ref[unit] = nt(query, key) - ahead[:, HEAD_DIM:]
        start = split(query.astype(F32) - ahead[:, :HEAD_DIM])
        moving_ref[unit, 0] = start[0]
        if unit % 2:
            pair = unit // 2
            start = split(triple(nt, start, (even_ref[pair, 0], even_ref[pair, 1])))
        moving_ref[unit, 1] = start[0]
        current.append(start)
    pairs = units // 2
    current = [
        tuple(jnp.concatenate([current[2 * pair][part], current[2 * pair + 1][part]], 0)
              for part in range(2))
        for pair in range(pairs)
    ]
    for step in range(2, pairs + 1):
        for pair in range(step - 1, pairs):
            passed = pair - step + 1
            current[pair] = split(
                triple(nt, current[pair], (pair_ref[passed, 0], pair_ref[passed, 1]))
            )
            moving_ref[2 * pair, step] = current[pair][0][:BLOCK]
            moving_ref[2 * pair + 1, step] = current[pair][0][BLOCK:]


def listed_block(away_ref, unit, entry):
    away = away_ref[unit, entry]
    new = away > 0
    for other in range(1, entry):
        new = new & (away_ref[unit, other] != away)
    return unit - away, new


def earlier(source, ahead, units):
    return jnp.clip(source + ahead * units, 0, units - 1), source < (1 - ahead) * units


def attend_kernel(axes, before, blocks, away_ref, moving_ref, inner_ref, end_ref, tail_ref,
                  *refs):
    units = inner_ref.shape[0]
    heads = units // blocks
    maps = max(before - 1, 0)
    far_keys, group_maps = refs[:before], refs[before:before + maps]
    refs = refs[before + maps:]
    count = (len(refs) - 4 - heads * (1 + before)) // 2
    arrived = refs[:heads * (1 + before)]
    out_ref, (values_ref, value_sems, sems) = refs[-4 - count], refs[-3:]
    place_here = lax.rem(lax.axis_index(axes[0]), heads)
    value_copies = []
    for kind in range(1 + before):
        for turn in range(heads):
            start = pl.multiple_of(lax.bitwise_xor(place_here, turn) * blocks * BLOCK, BLOCK)
            value_copies += fetched(
                [arrived[kind * heads + turn]],
                [values_ref.at[kind, pl.ds(start, blocks * BLOCK)]],
                value_sems.at[kind, pl.ds(turn, 1)],
            )
    copies = fetched(
        refs[heads * (1 + before):heads * (1 + before) + count], refs[-3 - count:-3], sems
    )
    rows, columns = square_iotas()
    scale = HEAD_DIM ** (-0.5)

    def value_of(kind, block):
        return values_ref[kind, pl.ds(pl.multiple_of(block * BLOCK, BLOCK), BLOCK)]

    def steps(unit):
        pair = unit // 2
        fronts = [moving_ref[unit, pair + 1]]
        for group_map in group_maps:
            passed = nt(fronts[-1], group_map[0]) + nt(fronts[-1], group_map[1])
            fronts.append(passed.astype(BF16))
        score_list = [jnp.where(rows >= columns, inner_ref[unit] * scale, -1e30)]
        sources = [(0, unit)]
        for entry in range(1, TOPK):
            source, new = listed_block(away_ref, unit, entry)
            inside = jnp.maximum(source, 0)
            step = jnp.maximum(pair - inside // 2, 0)
            query = moving_ref[unit, step]
            key = jnp.where(step == 0, end_ref[inside], tail_ref[inside])
            kind, block = 0, inside
            for ahead in range(1, before + 1):
                place, here = earlier(source, ahead, units)
                query = jnp.where(here, fronts[ahead - 1], query)
                key = jnp.where(here, far_keys[ahead - 1][place], key)
                kind = jnp.where(here, ahead, kind)
                block = jnp.where(here, place, block)
            score_list.append(jnp.where(new, nt(query, key) * scale, -1e30))
            sources.append((kind, block))
        yield
        scores = jnp.concatenate(score_list, 1)
        expos = jnp.exp(scores - jnp.max(scores, 1, keepdims=True))
        weights = (expos * (1.0 / jnp.sum(expos, 1, keepdims=True))).astype(BF16)
        yield
        if unit == 0:
            for copy in value_copies:
                copy.wait()
        value_list = [value_of(kind, block) for kind, block in sources]
        blended = nn(weights, jnp.concatenate(value_list, 0)).astype(BF16)
        for plane in range(out_ref.shape[1]):
            out_ref[unit // blocks, plane, unit % blocks] = blended

    interleaved([steps(unit) for unit in range(units)], 1)
    for copy in copies:
        copy.wait()


def project_kernel(axes, other, cores, attended_ref, own_ref, *refs):
    other_refs, out_ref = refs[:-1], refs[-1]
    heads, planes, blocks = attended_ref.shape[:3]
    index = lax.axis_index(axes[1])
    core, plane = lax.rem(index + other, cores), index // cores
    width = out_ref.shape[1]
    total = None
    for offset in range(planes):
        source = lax.rem(plane + offset, planes)
        attended = jnp.concatenate(
            [
                jnp.concatenate(
                    [attended_ref[head, source, block] for head in range(heads)], 1
                )
                for block in range(blocks)
            ],
            0,
        )
        if offset:
            start = pl.multiple_of(core * width, width)
            weight = other_refs[offset - 1][:, pl.ds(start, width)]
        else:
            start = pl.multiple_of((plane * cores + core) * width, width)
            weight = own_ref[:, pl.ds(start, width)]
        product = nn(attended, weight)
        total = product if total is None else total + product
    out_ref[...] = total.astype(out_ref.dtype)


def call(kernel, outs, specs, flops, scratch=(), places=None, space=32):
    if places is None:
        places = [VMEM] * len(outs) if isinstance(outs, list) else VMEM
    return pl.pallas_call(
        kernel,
        out_shape=outs,
        in_specs=specs,
        out_specs=places,
        scratch_shapes=list(scratch),
        compiler_params=pltpu.CompilerParams(vmem_limit_bytes=space * 2 ** 20),
        cost_estimate=pl.CostEstimate(flops=flops, bytes_accessed=2 ** 21, transcendentals=0),
    )


def body(ctx_size, head_size, queries, keys, values, directions, rates, selected, out_weight):
    tokens = queries.shape[0]
    blocks = tokens // BLOCK
    heads = queries.shape[1] // HEAD_DIM
    units = heads * blocks
    pairs = units // 2
    groups = ctx_size // heads
    before = min(groups - 1, -(-LOOK // heads))
    cores = 2
    planes = head_size // cores
    axes = ("ctx", "head")
    members = [[group * heads + place for place in range(heads)] for group in range(groups)]
    partners = [(g, g + 1 - 2 * (g % cores)) for g in range(head_size)]
    cubes = 2 * BLOCK ** 3
    tile = (BLOCK, HEAD_DIM)

    def exchange(value):
        return lax.all_to_all(value, "ctx", 0, 0, axis_index_groups=members, tiled=True)

    def onward(value, by):
        shift = by * heads
        return lax.ppermute(value, "ctx", [(i, i + shift) for i in range(ctx_size - shift)])

    def crossed(value, turn):
        pairs = [(i, i - i % heads + (i % heads ^ turn)) for i in range(ctx_size)]
        return lax.ppermute(value, "ctx", pairs) if turn else value

    def straight(value, turn, by):
        shift = by * heads
        pairs = [(i, i - i % heads + (i % heads ^ turn) + shift) for i in range(ctx_size - shift)]
        return lax.ppermute(value, "ctx", pairs)

    def array(shape, kind=BF16):
        return jax.ShapeDtypeStruct(shape, kind)

    part_shape = (heads, 2 * tokens + EXTRA, HEAD_DIM)
    width = out_weight.shape[1] // planes
    piece_shape = (out_weight.shape[0], width)
    packed, *rest = call(
        functools.partial(pack_kernel, axes, cores),
        [array(part_shape)]
        + [array((tokens, HEAD_DIM))] * heads
        + [array(piece_shape)] * (planes - 1),
        [ANY] * 6,
        cubes,
        [
            pltpu.VMEM(part_shape, BF16),
            pltpu.VMEM(rates.shape, F32),
            pltpu.SMEM(selected.shape, jnp.int32),
            pltpu.VMEM((heads, tokens, HEAD_DIM), BF16),
            pltpu.VMEM((max(planes - 1, 1), *piece_shape), BF16),
            pltpu.SemaphoreType.DMA((heads, 2)),
            pltpu.SemaphoreType.DMA((2,)),
            pltpu.SemaphoreType.DMA((heads,)),
            pltpu.SemaphoreType.DMA((heads,)),
            pltpu.SemaphoreType.DMA((heads,)),
            pltpu.SemaphoreType.DMA((2, planes)),
        ],
        [ANY] * (heads + planes),
        56,
    )(directions, keys, rates, selected, values, out_weight)
    value_cuts, pieces = rest[:heads], rest[heads:]
    value_parts = [
        straight(value_cuts[turn], turn, by) for by in range(1, before + 1) for turn in range(heads)
    ]
    weight_parts = []
    for offset in range(1, planes):
        turned = [(g, (g + head_size - cores * offset) % head_size) for g in range(head_size)]
        weight_parts.append(lax.ppermute(pieces[offset - 1], "head", turned))
    parts = exchange(packed)

    end, tail, far, even, pair_map, mixed, away, *group_maps = call(
        functools.partial(keys_kernel, blocks),
        [
            array((units, *tile)),
            array((units, *tile)),
            array((units, *tile)),
            array((pairs, 2, *tile)),
            array((pairs, 2, *tile)),
            array((units, BLOCK, 2 * BLOCK)),
            array((units, HEAD_DIM), jnp.int32),
        ]
        + [array((2, *tile))] * (before > 1),
        [VMEM],
        400 * cubes,
    )(parts)
    far_parts = [onward(far, by) for by in range(1, before + 1)]
    map_parts = [onward(group_maps[0], by) for by in range(1, before)]
    cut = call(
        functools.partial(cut_kernel, axes),
        [array((tokens, HEAD_DIM))] * (2 * heads),
        [ANY] * (len(value_parts) + 3),
        2000 * cubes,
        [pltpu.SemaphoreType.DMA((2, heads))],
    )(queries, values, *value_parts, away)
    query_parts = [crossed(cut[turn], turn) for turn in range(heads)]
    own_parts = [crossed(cut[heads + turn], turn) for turn in range(heads)]
    inner, moving = call(
        functools.partial(queries_kernel, axes, blocks),
        [array((units, BLOCK, BLOCK), F32), array((units, pairs + 1, *tile))],
        [VMEM] * 4 + [ANY] * heads,
        0,
        [pltpu.VMEM((heads, tokens, HEAD_DIM), BF16), pltpu.SemaphoreType.DMA((heads,))],
    )(parts, mixed, even, pair_map, *query_parts)
    attended, *weight_parts = call(
        functools.partial(attend_kernel, axes, before, blocks),
        [array((heads, planes, blocks, *tile))] + [array(part.shape) for part in weight_parts],
        [SMEM]
        + [VMEM] * (4 + before + len(map_parts))
        + [ANY] * (heads * (1 + before) + len(weight_parts)),
        0,
        [
            pltpu.VMEM((1 + before, units * BLOCK, HEAD_DIM), BF16),
            pltpu.SemaphoreType.DMA((1 + before, heads)),
            pltpu.SemaphoreType.DMA((planes,)),
        ],
    )(
        away, moving, inner, end, tail, *far_parts, *map_parts, *own_parts, *value_parts,
        *weight_parts,
    )

    returns = [
        [
            (group * heads + place) * head_size + p * cores + core
            for place in range(heads)
            for p in range(planes)
        ]
        for group in range(groups)
        for core in range(cores)
    ]
    local = lax.all_to_all(
        attended.reshape(heads * planes, blocks, *tile),
        axes, 0, 0, axis_index_groups=returns, tiled=True,
    ).reshape(heads, planes, blocks, *tile)

    def projected(other, kind):
        return call(
            functools.partial(project_kernel, axes, other, cores),
            array((tokens, width // cores), kind),
            [VMEM] * (1 + planes),
            128 * cubes,
        )(local, out_weight, *weight_parts)

    arrived = lax.ppermute(projected(1, BF16), "head", partners)
    return (projected(0, F32) + arrived.astype(F32)).astype(BF16)


def solution(mesh):
    in_specs = (
        P("ctx", "head"),
        P("ctx", "head"),
        P("ctx", "head"),
        P("ctx", "head"),
        P("head", "ctx"),
        P("ctx", None),
        P("head", None),
    )
    out_specs = P("ctx", "head")
    return jax.shard_map(
        functools.partial(body, mesh.shape["ctx"], mesh.shape["head"]),
        mesh=mesh,
        in_specs=in_specs,
        out_specs=out_specs,
        check_vma=False,
    )
```

```python
import functools

import jax
import jax.numpy as jnp
from jax import lax
from jax.experimental import pallas as pl
from jax.experimental.pallas import tpu as pltpu
from jax.sharding import PartitionSpec as P

HEAD_DIM = 128
BLOCK = 128
LOOK = 7
TOPK = 4
BASE = 16
EXTRA = 16
TERMS = 3
BF16 = jnp.bfloat16
F32 = jnp.float32
VMEM = pl.BlockSpec(memory_space=pltpu.VMEM)
SMEM = pl.BlockSpec(memory_space=pltpu.SMEM)
ANY = pl.BlockSpec(memory_space=pl.ANY)


def dot(left, right, left_dim, right_dim):
    return lax.dot_general(
        left, right, (((left_dim,), (right_dim,)), ((), ())), preferred_element_type=F32
    )


def nn(left, right):
    return dot(left, right, 1, 0)


def nt(left, right):
    return dot(left, right, 1, 1)


def tn(left, right):
    return dot(left, right, 0, 0)


def split(value):
    high = value.astype(BF16)
    return high, (value - high.astype(F32)).astype(BF16)


def triple(product, left, right):
    rows = left[0].shape[0]
    first = product(jnp.concatenate(left, 0), right[0])
    return first[:rows] + (first[rows:] + product(left[0], right[1]))


def square_iotas():
    rows = lax.broadcasted_iota(jnp.int32, (BLOCK, BLOCK), 0)
    columns = lax.broadcasted_iota(jnp.int32, (BLOCK, BLOCK), 1)
    return rows, columns


def fetched(sources, targets, sems):
    copies = []
    for index, (source, target) in enumerate(zip(sources, targets)):
        copies.append(pltpu.make_async_copy(source, target, sems.at[index]))
        copies[-1].start()
    return copies


def pack_kernel(axes, cores, d_ref, k_ref, rates_hbm, selected_hbm, values_ref, weight_ref,
                *refs):
    tokens = d_ref.shape[0]
    heads = d_ref.shape[1] // HEAD_DIM
    blocks = tokens // BLOCK
    (parts_ref, rates_ref, selected_ref, cut_ref, piece_ref, sems, few_sems, out_sems, cut_sems,
     cut_out_sems, piece_sems) = refs[-11:]
    out_ref, cut_outs, piece_outs = refs[0], refs[1:1 + heads], refs[1 + heads:-11]
    planes = len(piece_outs) + 1
    width = weight_ref.shape[1] // planes
    device = lax.axis_index(axes[0])
    place = lax.rem(device, heads)
    plane = lax.axis_index(axes[1]) // cores
    first_block = device * blocks
    few_copies = fetched([rates_hbm, selected_hbm], [rates_ref, selected_ref], few_sems)
    sources = (d_ref, k_ref)
    copies = []
    for head in range(heads):
        columns = pl.ds(head * HEAD_DIM, HEAD_DIM)
        for kind, source in enumerate(sources):
            copies.append(
                pltpu.make_async_copy(
                    source.at[:, columns],
                    parts_ref.at[head, pl.ds(kind * tokens, tokens)],
                    sems.at[head, kind],
                )
            )
            copies[-1].start()
    cuts = [
        pl.multiple_of(lax.bitwise_xor(place, turn) * HEAD_DIM, HEAD_DIM) for turn in range(heads)
    ]
    cut_copies = fetched(
        [values_ref.at[:, pl.ds(cut, HEAD_DIM)] for cut in cuts],
        [cut_ref.at[turn] for turn in range(heads)],
        cut_sems,
    )
    piece_copies = []
    for offset in range(1, planes):
        start = pl.multiple_of(lax.rem(plane + planes - offset, planes) * width, width)
        piece_copies += fetched(
            [weight_ref.at[:, pl.ds(start, width)]],
            [piece_ref.at[offset - 1]],
            piece_sems.at[0, pl.ds(offset - 1, 1)],
        )
    for copy in few_copies:
        copy.wait()
    row = lax.broadcasted_iota(jnp.int32, (EXTRA, HEAD_DIM), 0)
    lane = lax.broadcasted_iota(jnp.int32, (EXTRA, HEAD_DIM), 1)
    away = jnp.zeros((EXTRA, HEAD_DIM), jnp.int32)
    for block in range(blocks):
        for entry in range(TOPK):
            distance = first_block + block - selected_ref[block, entry]
            away = jnp.where((row == TERMS * blocks + block) & (lane == entry), distance, away)
    away = away.astype(F32)
    terms = []
    rest = rates_ref[...]
    for _ in range(TERMS):
        terms.append(rest.astype(BF16).astype(F32))
        rest = rest - terms[-1]
    out_copies = []
    for head in range(heads):
        extra = away
        for block in range(blocks):
            for index, term in enumerate(terms):
                piece = term[head:head + 1, block * BLOCK:(block + 1) * BLOCK]
                extra = jnp.where(row == TERMS * block + index, piece, extra)
        parts_ref[head, len(sources) * tokens:] = extra.astype(BF16)
        for copy in copies[len(sources) * head:len(sources) * (head + 1)]:
            copy.wait()
        out_copies.append(
            pltpu.make_async_copy(parts_ref.at[head], out_ref.at[head], out_sems.at[head])
        )
        out_copies[-1].start()
    for turn in range(heads):
        cut_copies[turn].wait()
        out_copies += fetched(
            [cut_ref.at[turn]], [cut_outs[turn]], cut_out_sems.at[pl.ds(turn, 1)]
        )
    for index, copy in enumerate(piece_copies):
        copy.wait()
        out_copies += fetched(
            [piece_ref.at[index]], [piece_outs[index]], piece_sems.at[1, pl.ds(index, 1)]
        )
    for copy in out_copies:
        copy.wait()


def cut_kernel(axes, heads, queries_ref, values_ref, *refs):
    sems = refs[-1]
    first, outs = refs[-2 * heads], refs[1 - 2 * heads:-1]
    query_outs, value_outs = list(outs[:heads - 1]), list(outs[heads - 1:])
    query_outs.insert(1, first.at[0])
    value_outs.insert(1, first.at[1])
    place = lax.rem(lax.axis_index(axes[0]), heads)
    cuts = [
        pl.multiple_of(lax.bitwise_xor(place, turn) * HEAD_DIM, HEAD_DIM) for turn in range(heads)
    ]
    copies = []
    for kind, (source, targets) in enumerate(
        ((queries_ref, query_outs), (values_ref, value_outs))
    ):
        copies += fetched(
            [source.at[:, pl.ds(cut, HEAD_DIM)] for cut in cuts], targets, sems.at[kind]
        )
    for copy in copies:
        copy.wait()


def rows_of(ref, blocks, unit, kind):
    start = (kind * blocks + unit % blocks) * BLOCK
    return ref[unit // blocks, start:start + BLOCK]


def base_inverse(strict):
    count = BLOCK // BASE
    moved = [
        pltpu.roll(strict[b * BASE:(b + 1) * BASE], (BLOCK - b * BASE) % BLOCK, 1)
        if b else strict[:BASE]
        for b in range(count)
    ]
    lanes = lax.broadcasted_iota(jnp.int32, (BASE // 2, BLOCK), 1)
    rows = lax.broadcasted_iota(jnp.int32, (BASE // 2, BLOCK), 0)
    half = BASE // 2
    parts = []
    for b in range(count):
        upper = (lanes == rows + b * BASE).astype(F32)
        lower = (lanes == rows + b * BASE + half).astype(F32)
        for step in range(BASE - 1):
            if step < half:
                source = upper[step:step + 1]
                if step < half - 1:
                    upper = upper - moved[b][:half, step:step + 1] * source
            else:
                source = lower[step - half:step - half + 1]
            lower = lower - moved[b][half:, step:step + 1] * source
        parts += [upper, lower]
    return jnp.concatenate(parts, 0)


def halves(value, size):
    parts = value.reshape(BLOCK // (2 * size), 2, size, BLOCK)
    return parts[:, 0].reshape(BLOCK // 2, BLOCK), parts[:, 1].reshape(BLOCK // 2, BLOCK)


def joined(first, second, size):
    shape = (BLOCK // (2 * size), 1, size, BLOCK)
    return jnp.concatenate([first.reshape(shape), second.reshape(shape)], 1).reshape(BLOCK, BLOCK)


def interleaved(steps, lag):
    running = list(steps)
    tick = 0
    while any(step is not None for step in running):
        for index, step in enumerate(running):
            if step is not None and tick >= index * lag:
                try:
                    next(step)
                except StopIteration:
                    running[index] = None
        tick += 1


def keys_kernel(blocks, part_ref, end_ref, tail_ref, far_ref, even_ref, pair_ref, mixed_ref,
                away_ref, *group_refs):
    units = part_ref.shape[0] * blocks
    rows, columns = square_iotas()
    diagonal = rows == columns
    identity = diagonal.astype(F32)
    row = lax.broadcasted_iota(jnp.int32, (BLOCK // 2, BLOCK), 0)
    column = lax.broadcasted_iota(jnp.int32, (BLOCK // 2, BLOCK), 1)
    ends, maps = [None] * units, [None] * units

    def terms(unit):
        direction = rows_of(part_ref, blocks, unit, 0)
        key = rows_of(part_ref, blocks, unit, 1)
        extra = part_ref[unit // blocks, 2 * blocks * BLOCK:].astype(F32)
        first = TERMS * (unit % blocks)
        rate = extra[first:first + 1] + extra[first + 1:first + 2] + extra[first + 2:first + 3]
        listed = TERMS * blocks + unit % blocks
        away_ref[unit:unit + 1] = extra[listed:listed + 1].astype(jnp.int32)
        gram = nt(direction, direction)
        key_proj = jnp.where(rows > columns, nt(direction, key), 0.0).astype(BF16)
        squares = jnp.sum(jnp.where(diagonal, gram, 0.0), 0, keepdims=True)
        scale = lax.rsqrt(squares + 1e-06)
        scaled_rate = rate * scale
        scale_column = jnp.sum(jnp.where(diagonal, scale, 0.0), 1, keepdims=True)
        rate_column = jnp.sum(jnp.where(diagonal, scaled_rate, 0.0), 1, keepdims=True)
        strict = jnp.where(rows > columns, rate_column * gram * scale, 0.0)
        yield
        inverse = base_inverse(strict)
        yield
        size = BASE
        while size < BLOCK:
            inside = (row // size == column // (2 * size)) & (lax.rem(column, 2 * size) < size)
            corner = jnp.where(inside, halves(strict, size)[1], 0.0)
            below = triple(nn, split(corner), split(inverse))
            yield
            first_half, second = halves(inverse, size)
            padded = joined(jnp.zeros_like(below), below, size)
            second = second - triple(nn, split(second), split(padded))
            inverse = joined(first_half, second, size)
            size *= 2
            yield
        mixing = split(scale_column * inverse * scaled_rate)
        mixed = nn(mixing[0], jnp.concatenate([direction, key_proj], 1))
        mixed_map = split(mixed[:, :BLOCK] + nn(mixing[1], direction))
        mixed = jnp.concatenate([mixed_map[0], mixed[:, BLOCK:].astype(BF16)], 1)
        mixed_ref[unit] = mixed
        yield
        behind = tn(jnp.concatenate([mixed, mixed_map[1]], 1), direction)
        ends[unit] = key.astype(F32) - behind[BLOCK:2 * BLOCK]
        maps[unit] = split(identity - (behind[:BLOCK] + behind[2 * BLOCK:]))
        end_ref[unit] = ends[unit].astype(BF16)

    onward = []

    def pair_terms(pair):
        even, odd = 2 * pair, 2 * pair + 1
        running = [terms(even), terms(odd)]
        while running:
            for step in list(running):
                if next(step, running) is running:
                    running.remove(step)
            yield
        even_ref[pair, 0] = maps[even][0]
        even_ref[pair, 1] = maps[even][1]
        left = jnp.concatenate([ends[even].astype(BF16), *maps[even]], 0)
        both = nn(left, maps[odd][0])
        tail_even, tail_odd = both[:BLOCK].astype(BF16), ends[odd].astype(BF16)
        tail_ref[even] = tail_even
        tail_ref[odd] = tail_odd
        low = both[2 * BLOCK:] + nn(maps[even][0], maps[odd][1])
        pair_map = split(both[BLOCK:2 * BLOCK] + low)
        pair_ref[pair, 0] = pair_map[0]
        pair_ref[pair, 1] = pair_map[1]
        yield
        if onward:
            far = nn(jnp.concatenate([tail_even, tail_odd], 0), onward[-1][0]).astype(BF16)
            far_ref[even] = far[:BLOCK]
            far_ref[odd] = far[BLOCK:]
            if pair or group_refs:
                pair_map = split(triple(nn, pair_map, onward[-1]))
        else:
            far_ref[even] = tail_even
            far_ref[odd] = tail_odd
        onward.append(pair_map)

    interleaved([pair_terms(pair) for pair in reversed(range(units // 2))], 1)
    for group_ref in group_refs:
        group_ref[0] = onward[-1][0]
        group_ref[1] = onward[-1][1]


def queries_kernel(axes, blocks, part_ref, mixed_ref, even_ref, pair_ref, *refs):
    heads = part_ref.shape[0]
    units = heads * blocks
    inner_ref, moving_ref, query_ref, sems = refs[heads:]
    place = lax.rem(lax.axis_index(axes[0]), heads)
    copies = fetched(
        [refs[turn].at[0] if turn == 1 else refs[turn] for turn in range(heads)],
        [query_ref.at[lax.bitwise_xor(place, turn)] for turn in range(heads)],
        sems,
    )
    for copy in copies:
        copy.wait()
    rows, columns = square_iotas()
    current = []
    for unit in range(units):
        direction = rows_of(part_ref, blocks, unit, 0)
        key = rows_of(part_ref, blocks, unit, 1)
        query = rows_of(query_ref, blocks, unit, 0)
        query_proj = split(jnp.where(rows >= columns, nt(query, direction), 0.0))
        ahead = nn(jnp.concatenate(query_proj, 0), mixed_ref[unit])
        ahead = ahead[:BLOCK] + ahead[BLOCK:]
        inner_ref[unit] = nt(query, key) - ahead[:, HEAD_DIM:]
        start = split(query.astype(F32) - ahead[:, :HEAD_DIM])
        moving_ref[unit, 0] = start[0]
        if unit % 2:
            pair = unit // 2
            start = split(triple(nt, start, (even_ref[pair, 0], even_ref[pair, 1])))
        moving_ref[unit, 1] = start[0]
        current.append(start)
    pairs = units // 2
    current = [
        tuple(jnp.concatenate([current[2 * pair][part], current[2 * pair + 1][part]], 0)
              for part in range(2))
        for pair in range(pairs)
    ]
    for step in range(2, pairs + 1):
        for pair in range(step - 1, pairs):
            passed = pair - step + 1
            current[pair] = split(
                triple(nt, current[pair], (pair_ref[passed, 0], pair_ref[passed, 1]))
            )
            moving_ref[2 * pair, step] = current[pair][0][:BLOCK]
            moving_ref[2 * pair + 1, step] = current[pair][0][BLOCK:]


def listed_block(away_ref, unit, entry):
    away = away_ref[unit, entry]
    new = away > 0
    for other in range(1, entry):
        new = new & (away_ref[unit, other] != away)
    return unit - away, new


def earlier(source, ahead, units):
    return jnp.clip(source + ahead * units, 0, units - 1), source < (1 - ahead) * units


def weights_kernel(before, away_ref, moving_ref, inner_ref, end_ref, tail_ref, *refs):
    far_keys, group_maps, weights_ref = refs[:before], refs[before:-1], refs[-1]
    units = inner_ref.shape[0]
    rows, columns = square_iotas()
    scale = HEAD_DIM ** (-0.5)

    def steps(unit):
        pair = unit // 2
        fronts = [moving_ref[unit, pair + 1]]
        for group_map in group_maps:
            passed = nt(fronts[-1], group_map[0]) + nt(fronts[-1], group_map[1])
            fronts.append(passed.astype(BF16))
        score_list = [jnp.where(rows >= columns, inner_ref[unit] * scale, -1e30)]
        for entry in range(1, TOPK):
            source, new = listed_block(away_ref, unit, entry)
            inside = jnp.maximum(source, 0)
            step = jnp.maximum(pair - inside // 2, 0)
            query = moving_ref[unit, step]
            key = jnp.where(step == 0, end_ref[inside], tail_ref[inside])
            for ahead in range(1, before + 1):
                place, here = earlier(source, ahead, units)
                query = jnp.where(here, fronts[ahead - 1], query)
                key = jnp.where(here, far_keys[ahead - 1][place], key)
            score_list.append(jnp.where(new, nt(query, key) * scale, -1e30))
        yield
        scores = jnp.concatenate(score_list, 1)
        expos = jnp.exp(scores - jnp.max(scores, 1, keepdims=True))
        weights_ref[unit] = (expos * (1.0 / jnp.sum(expos, 1, keepdims=True))).astype(BF16)

    interleaved([steps(unit) for unit in range(units)], 1)


def blend_kernel(axes, before, blocks, away_ref, weights_ref, *refs):
    units = weights_ref.shape[0]
    heads = units // blocks
    count = (len(refs) - 4 - heads * (1 + before)) // 2
    arrived = refs[:heads * (1 + before)]
    out_ref, (values_ref, value_sems, sems) = refs[-4 - count], refs[-3:]
    place = lax.rem(lax.axis_index(axes[0]), heads)
    value_copies = []
    for kind in range(1 + before):
        for turn in range(heads):
            start = pl.multiple_of(lax.bitwise_xor(place, turn) * blocks * BLOCK, BLOCK)
            source = arrived[kind * heads + turn]
            value_copies += fetched(
                [source if kind or turn != 1 else source.at[1]],
                [values_ref.at[kind, pl.ds(start, blocks * BLOCK)]],
                value_sems.at[kind, pl.ds(turn, 1)],
            )
    copies = fetched(
        refs[heads * (1 + before):heads * (1 + before) + count], refs[-3 - count:-3], sems
    )
    for copy in value_copies:
        copy.wait()

    def value_of(kind, block):
        return values_ref[kind, pl.ds(pl.multiple_of(block * BLOCK, BLOCK), BLOCK)]

    for unit in range(units):
        value_list = [value_of(0, unit)]
        for entry in range(1, TOPK):
            source, _ = listed_block(away_ref, unit, entry)
            kind, block = 0, jnp.maximum(source, 0)
            for ahead in range(1, before + 1):
                other, here = earlier(source, ahead, units)
                kind = jnp.where(here, ahead, kind)
                block = jnp.where(here, other, block)
            value_list.append(value_of(kind, block))
        blended = nn(weights_ref[unit], jnp.concatenate(value_list, 0)).astype(BF16)
        for plane in range(out_ref.shape[1]):
            out_ref[unit // blocks, plane, unit % blocks] = blended
    for copy in copies:
        copy.wait()


def project_kernel(axes, other, cores, attended_ref, own_ref, *refs):
    other_refs, out_ref = refs[:-1], refs[-1]
    heads, planes, blocks = attended_ref.shape[:3]
    index = lax.axis_index(axes[1])
    core, plane = lax.rem(index + other, cores), index // cores
    width = out_ref.shape[1]
    total = None
    for offset in range(planes):
        source = lax.rem(plane + offset, planes)
        attended = jnp.concatenate(
            [
                jnp.concatenate(
                    [attended_ref[head, source, block] for head in range(heads)], 1
                )
                for block in range(blocks)
            ],
            0,
        )
        if offset:
            start = pl.multiple_of(core * width, width)
            weight = other_refs[offset - 1][:, pl.ds(start, width)]
        else:
            start = pl.multiple_of((plane * cores + core) * width, width)
            weight = own_ref[:, pl.ds(start, width)]
        product = nn(attended, weight)
        total = product if total is None else total + product
    out_ref[...] = total.astype(out_ref.dtype)


def call(kernel, outs, specs, flops, scratch=(), places=None, space=32):
    if places is None:
        places = [VMEM] * len(outs) if isinstance(outs, list) else VMEM
    return pl.pallas_call(
        kernel,
        out_shape=outs,
        in_specs=specs,
        out_specs=places,
        scratch_shapes=list(scratch),
        compiler_params=pltpu.CompilerParams(vmem_limit_bytes=space * 2 ** 20),
        cost_estimate=pl.CostEstimate(flops=flops, bytes_accessed=2 ** 21, transcendentals=0),
    )


def body(ctx_size, head_size, queries, keys, values, directions, rates, selected, out_weight):
    tokens = queries.shape[0]
    blocks = tokens // BLOCK
    heads = queries.shape[1] // HEAD_DIM
    units = heads * blocks
    pairs = units // 2
    groups = ctx_size // heads
    before = min(groups - 1, -(-LOOK // heads))
    cores = 2
    planes = head_size // cores
    axes = ("ctx", "head")
    members = [[group * heads + place for place in range(heads)] for group in range(groups)]
    partners = [(g, g + 1 - 2 * (g % cores)) for g in range(head_size)]
    cubes = 2 * BLOCK ** 3
    tile = (BLOCK, HEAD_DIM)

    def exchange(value):
        return lax.all_to_all(value, "ctx", 0, 0, axis_index_groups=members, tiled=True)

    def onward(value, by):
        shift = by * heads
        return lax.ppermute(value, "ctx", [(i, i + shift) for i in range(ctx_size - shift)])

    def crossed(value, turn):
        pairs = [(i, i - i % heads + (i % heads ^ turn)) for i in range(ctx_size)]
        return lax.ppermute(value, "ctx", pairs) if turn else value

    def straight(value, turn, by):
        shift = by * heads
        pairs = [(i, i - i % heads + (i % heads ^ turn) + shift) for i in range(ctx_size - shift)]
        return lax.ppermute(value, "ctx", pairs)

    def array(shape, kind=BF16):
        return jax.ShapeDtypeStruct(shape, kind)

    part_shape = (heads, 2 * tokens + EXTRA, HEAD_DIM)
    width = out_weight.shape[1] // planes
    piece_shape = (out_weight.shape[0], width)
    packed, *rest = call(
        functools.partial(pack_kernel, axes, cores),
        [array(part_shape)]
        + [array((tokens, HEAD_DIM))] * heads
        + [array(piece_shape)] * (planes - 1),
        [ANY] * 6,
        cubes,
        [
            pltpu.VMEM(part_shape, BF16),
            pltpu.VMEM(rates.shape, F32),
            pltpu.SMEM(selected.shape, jnp.int32),
            pltpu.VMEM((heads, tokens, HEAD_DIM), BF16),
            pltpu.VMEM((max(planes - 1, 1), *piece_shape), BF16),
            pltpu.SemaphoreType.DMA((heads, 2)),
            pltpu.SemaphoreType.DMA((2,)),
            pltpu.SemaphoreType.DMA((heads,)),
            pltpu.SemaphoreType.DMA((heads,)),
            pltpu.SemaphoreType.DMA((heads,)),
            pltpu.SemaphoreType.DMA((2, planes)),
        ],
        [ANY] * (heads + planes),
        56,
    )(directions, keys, rates, selected, values, out_weight)
    value_cuts, pieces = rest[:heads], rest[heads:]
    value_parts = [
        straight(value_cuts[turn], turn, by) for by in range(1, before + 1) for turn in range(heads)
    ]
    weight_parts = []
    for offset in range(1, planes):
        turned = [(g, (g + head_size - cores * offset) % head_size) for g in range(head_size)]
        weight_parts.append(lax.ppermute(pieces[offset - 1], "head", turned))
    parts = exchange(packed)

    end, tail, far, even, pair_map, mixed, away, *group_maps = call(
        functools.partial(keys_kernel, blocks),
        [
            array((units, *tile)),
            array((units, *tile)),
            array((units, *tile)),
            array((pairs, 2, *tile)),
            array((pairs, 2, *tile)),
            array((units, BLOCK, 2 * BLOCK)),
            array((units, HEAD_DIM), jnp.int32),
        ]
        + [array((2, *tile))] * (before > 1),
        [VMEM],
        400 * cubes,
    )(parts)
    far_parts = [onward(far, by) for by in range(1, before + 1)]
    map_parts = [onward(group_maps[0], by) for by in range(1, before)]
    first, *cut = call(
        functools.partial(cut_kernel, axes, heads),
        [array((2, tokens, HEAD_DIM))] + [array((tokens, HEAD_DIM))] * (2 * heads - 2),
        [ANY] * (len(value_parts) + 3),
        2000 * cubes,
        [pltpu.SemaphoreType.DMA((2, heads))],
    )(queries, values, *value_parts, away)
    first = crossed(first, 1)
    turns = [0, *range(2, heads)]
    query_parts = [crossed(part, turn) for part, turn in zip(cut[:heads - 1], turns)]
    own_parts = [crossed(part, turn) for part, turn in zip(cut[heads - 1:], turns)]
    query_parts.insert(1, first)
    own_parts.insert(1, first)
    inner, moving = call(
        functools.partial(queries_kernel, axes, blocks),
        [array((units, BLOCK, BLOCK), F32), array((units, pairs + 1, *tile))],
        [VMEM] * 4 + [ANY] * heads,
        0,
        [pltpu.VMEM((heads, tokens, HEAD_DIM), BF16), pltpu.SemaphoreType.DMA((heads,))],
    )(parts, mixed, even, pair_map, *query_parts)
    weights = call(
        functools.partial(weights_kernel, before),
        array((units, BLOCK, TOPK * BLOCK)),
        [SMEM] + [VMEM] * (4 + before + len(map_parts)),
        0,
    )(away, moving, inner, end, tail, *far_parts, *map_parts)
    attended, *weight_parts = call(
        functools.partial(blend_kernel, axes, before, blocks),
        [array((heads, planes, blocks, *tile))] + [array(part.shape) for part in weight_parts],
        [SMEM, VMEM] + [ANY] * (heads * (1 + before) + len(weight_parts)),
        0,
        [
            pltpu.VMEM((1 + before, units * BLOCK, HEAD_DIM), BF16),
            pltpu.SemaphoreType.DMA((1 + before, heads)),
            pltpu.SemaphoreType.DMA((planes,)),
        ],
    )(away, weights, *own_parts, *value_parts, *weight_parts)

    returns = [
        [
            (group * heads + place) * head_size + p * cores + core
            for place in range(heads)
            for p in range(planes)
        ]
        for group in range(groups)
        for core in range(cores)
    ]
    local = lax.all_to_all(
        attended.reshape(heads * planes, blocks, *tile),
        axes, 0, 0, axis_index_groups=returns, tiled=True,
    ).reshape(heads, planes, blocks, *tile)

    def projected(other, kind):
        return call(
            functools.partial(project_kernel, axes, other, cores),
            array((tokens, width // cores), kind),
            [VMEM] * (1 + planes),
            128 * cubes,
        )(local, out_weight, *weight_parts)

    arrived = lax.ppermute(projected(1, BF16), "head", partners)
    return (projected(0, F32) + arrived.astype(F32)).astype(BF16)


def solution(mesh):
    in_specs = (
        P("ctx", "head"),
        P("ctx", "head"),
        P("ctx", "head"),
        P("ctx", "head"),
        P("head", "ctx"),
        P("ctx", None),
        P("head", None),
    )
    out_specs = P("ctx", "head")
    return jax.shard_map(
        functools.partial(body, mesh.shape["ctx"], mesh.shape["head"]),
        mesh=mesh,
        in_specs=in_specs,
        out_specs=out_specs,
        check_vma=False,
    )
```

```python
import functools

import jax
import jax.numpy as jnp
from jax import lax
from jax.experimental import pallas as pl
from jax.experimental.pallas import tpu as pltpu
from jax.sharding import PartitionSpec as P

HEAD_DIM = 128
BLOCK = 128
LOOK = 7
TOPK = 4
BASE = 16
EXTRA = 16
TERMS = 3
BF16 = jnp.bfloat16
F32 = jnp.float32
VMEM = pl.BlockSpec(memory_space=pltpu.VMEM)
SMEM = pl.BlockSpec(memory_space=pltpu.SMEM)
ANY = pl.BlockSpec(memory_space=pl.ANY)


def dot(left, right, left_dim, right_dim):
    return lax.dot_general(
        left, right, (((left_dim,), (right_dim,)), ((), ())), preferred_element_type=F32
    )


def nn(left, right):
    return dot(left, right, 1, 0)


def nt(left, right):
    return dot(left, right, 1, 1)


def tn(left, right):
    return dot(left, right, 0, 0)


def split(value):
    high = value.astype(BF16)
    return high, (value - high.astype(F32)).astype(BF16)


def triple(product, left, right):
    rows = left[0].shape[0]
    first = product(jnp.concatenate(left, 0), right[0])
    return first[:rows] + (first[rows:] + product(left[0], right[1]))


def square_iotas():
    rows = lax.broadcasted_iota(jnp.int32, (BLOCK, BLOCK), 0)
    columns = lax.broadcasted_iota(jnp.int32, (BLOCK, BLOCK), 1)
    return rows, columns


def fetched(sources, targets, sems):
    copies = []
    for index, (source, target) in enumerate(zip(sources, targets)):
        copies.append(pltpu.make_async_copy(source, target, sems.at[index]))
        copies[-1].start()
    return copies


def pack_kernel(axes, cores, d_ref, k_ref, rates_hbm, selected_hbm, values_ref, weight_ref,
                *refs):
    tokens = d_ref.shape[0]
    heads = d_ref.shape[1] // HEAD_DIM
    blocks = tokens // BLOCK
    (parts_ref, rates_ref, selected_ref, cut_ref, piece_ref, sems, few_sems, out_sems, cut_sems,
     cut_out_sems, piece_sems) = refs[-11:]
    out_ref, cut_outs, piece_outs = refs[0], refs[1:1 + heads], refs[1 + heads:-11]
    planes = len(piece_outs) + 1
    width = weight_ref.shape[1] // planes
    device = lax.axis_index(axes[0])
    place = lax.rem(device, heads)
    plane = lax.axis_index(axes[1]) // cores
    first_block = device * blocks
    few_copies = fetched([rates_hbm, selected_hbm], [rates_ref, selected_ref], few_sems)
    sources = (d_ref, k_ref)
    copies = []
    for head in range(heads):
        columns = pl.ds(head * HEAD_DIM, HEAD_DIM)
        for kind, source in enumerate(sources):
            copies.append(
                pltpu.make_async_copy(
                    source.at[:, columns],
                    parts_ref.at[head, pl.ds(kind * tokens, tokens)],
                    sems.at[head, kind],
                )
            )
            copies[-1].start()
    cuts = [
        pl.multiple_of(lax.bitwise_xor(place, turn) * HEAD_DIM, HEAD_DIM) for turn in range(heads)
    ]
    cut_copies = fetched(
        [values_ref.at[:, pl.ds(cut, HEAD_DIM)] for cut in cuts],
        [cut_ref.at[turn] for turn in range(heads)],
        cut_sems,
    )
    piece_copies = []
    for offset in range(1, planes):
        start = pl.multiple_of(lax.rem(plane + planes - offset, planes) * width, width)
        piece_copies += fetched(
            [weight_ref.at[:, pl.ds(start, width)]],
            [piece_ref.at[offset - 1]],
            piece_sems.at[0, pl.ds(offset - 1, 1)],
        )
    for copy in few_copies:
        copy.wait()
    row = lax.broadcasted_iota(jnp.int32, (EXTRA, HEAD_DIM), 0)
    lane = lax.broadcasted_iota(jnp.int32, (EXTRA, HEAD_DIM), 1)
    away = jnp.zeros((EXTRA, HEAD_DIM), jnp.int32)
    for block in range(blocks):
        for entry in range(TOPK):
            distance = first_block + block - selected_ref[block, entry]
            away = jnp.where((row == TERMS * blocks + block) & (lane == entry), distance, away)
    away = away.astype(F32)
    terms = []
    rest = rates_ref[...]
    for _ in range(TERMS):
        terms.append(rest.astype(BF16).astype(F32))
        rest = rest - terms[-1]
    out_copies = []
    for head in range(heads):
        extra = away
        for block in range(blocks):
            for index, term in enumerate(terms):
                piece = term[head:head + 1, block * BLOCK:(block + 1) * BLOCK]
                extra = jnp.where(row == TERMS * block + index, piece, extra)
        parts_ref[head, len(sources) * tokens:] = extra.astype(BF16)
        for copy in copies[len(sources) * head:len(sources) * (head + 1)]:
            copy.wait()
        out_copies.append(
            pltpu.make_async_copy(parts_ref.at[head], out_ref.at[head], out_sems.at[head])
        )
        out_copies[-1].start()
    for turn in range(heads):
        cut_copies[turn].wait()
        out_copies += fetched(
            [cut_ref.at[turn]], [cut_outs[turn]], cut_out_sems.at[pl.ds(turn, 1)]
        )
    for index, copy in enumerate(piece_copies):
        copy.wait()
        out_copies += fetched(
            [piece_ref.at[index]], [piece_outs[index]], piece_sems.at[1, pl.ds(index, 1)]
        )
    for copy in out_copies:
        copy.wait()


def cut_kernel(axes, heads, queries_ref, values_ref, *refs):
    sems = refs[-1]
    first, outs = refs[-2 * heads], refs[1 - 2 * heads:-1]
    query_outs, value_outs = list(outs[:heads - 1]), list(outs[heads - 1:])
    query_outs.insert(1, first.at[0])
    value_outs.insert(1, first.at[1])
    place = lax.rem(lax.axis_index(axes[0]), heads)
    cuts = [
        pl.multiple_of(lax.bitwise_xor(place, turn) * HEAD_DIM, HEAD_DIM) for turn in range(heads)
    ]
    copies = []
    for kind, (source, targets) in enumerate(
        ((queries_ref, query_outs), (values_ref, value_outs))
    ):
        copies += fetched(
            [source.at[:, pl.ds(cut, HEAD_DIM)] for cut in cuts], targets, sems.at[kind]
        )
    for copy in copies:
        copy.wait()


def rows_of(ref, blocks, unit, kind):
    start = (kind * blocks + unit % blocks) * BLOCK
    return ref[unit // blocks, start:start + BLOCK]


def base_inverse(strict):
    count = BLOCK // BASE
    moved = [
        pltpu.roll(strict[b * BASE:(b + 1) * BASE], (BLOCK - b * BASE) % BLOCK, 1)
        if b else strict[:BASE]
        for b in range(count)
    ]
    lanes = lax.broadcasted_iota(jnp.int32, (BASE // 2, BLOCK), 1)
    rows = lax.broadcasted_iota(jnp.int32, (BASE // 2, BLOCK), 0)
    half = BASE // 2
    parts = []
    for b in range(count):
        upper = (lanes == rows + b * BASE).astype(F32)
        lower = (lanes == rows + b * BASE + half).astype(F32)
        for step in range(BASE - 1):
            if step < half:
                source = upper[step:step + 1]
                if step < half - 1:
                    upper = upper - moved[b][:half, step:step + 1] * source
            else:
                source = lower[step - half:step - half + 1]
            lower = lower - moved[b][half:, step:step + 1] * source
        parts += [upper, lower]
    return jnp.concatenate(parts, 0)


def halves(value, size):
    parts = value.reshape(BLOCK // (2 * size), 2, size, BLOCK)
    return parts[:, 0].reshape(BLOCK // 2, BLOCK), parts[:, 1].reshape(BLOCK // 2, BLOCK)


def joined(first, second, size):
    shape = (BLOCK // (2 * size), 1, size, BLOCK)
    return jnp.concatenate([first.reshape(shape), second.reshape(shape)], 1).reshape(BLOCK, BLOCK)


def interleaved(steps, lag):
    running = list(steps)
    tick = 0
    while any(step is not None for step in running):
        for index, step in enumerate(running):
            if step is not None and tick >= index * lag:
                try:
                    next(step)
                except StopIteration:
                    running[index] = None
        tick += 1


def keys_kernel(blocks, part_ref, end_ref, tail_ref, far_ref, even_ref, pair_ref, mixed_ref,
                away_ref, *group_refs):
    units = part_ref.shape[0] * blocks
    rows, columns = square_iotas()
    diagonal = rows == columns
    identity = diagonal.astype(F32)
    row = lax.broadcasted_iota(jnp.int32, (BLOCK // 2, BLOCK), 0)
    column = lax.broadcasted_iota(jnp.int32, (BLOCK // 2, BLOCK), 1)
    ends, maps = [None] * units, [None] * units

    def terms(unit):
        direction = rows_of(part_ref, blocks, unit, 0)
        key = rows_of(part_ref, blocks, unit, 1)
        extra = part_ref[unit // blocks, 2 * blocks * BLOCK:].astype(F32)
        first = TERMS * (unit % blocks)
        rate = extra[first:first + 1] + extra[first + 1:first + 2] + extra[first + 2:first + 3]
        listed = TERMS * blocks + unit % blocks
        away_ref[unit:unit + 1] = extra[listed:listed + 1].astype(jnp.int32)
        gram = nt(direction, direction)
        key_proj = jnp.where(rows > columns, nt(direction, key), 0.0).astype(BF16)
        squares = jnp.sum(jnp.where(diagonal, gram, 0.0), 0, keepdims=True)
        scale = lax.rsqrt(squares + 1e-06)
        scaled_rate = rate * scale
        scale_column = jnp.sum(jnp.where(diagonal, scale, 0.0), 1, keepdims=True)
        rate_column = jnp.sum(jnp.where(diagonal, scaled_rate, 0.0), 1, keepdims=True)
        strict = jnp.where(rows > columns, rate_column * gram * scale, 0.0)
        yield
        inverse = base_inverse(strict)
        yield
        size = BASE
        while size < BLOCK:
            inside = (row // size == column // (2 * size)) & (lax.rem(column, 2 * size) < size)
            corner = jnp.where(inside, halves(strict, size)[1], 0.0)
            below = triple(nn, split(corner), split(inverse))
            yield
            first_half, second = halves(inverse, size)
            padded = joined(jnp.zeros_like(below), below, size)
            second = second - triple(nn, split(second), split(padded))
            inverse = joined(first_half, second, size)
            size *= 2
            yield
        mixing = split(scale_column * inverse * scaled_rate)
        mixed = nn(mixing[0], jnp.concatenate([direction, key_proj], 1))
        mixed_map = split(mixed[:, :BLOCK] + nn(mixing[1], direction))
        mixed = jnp.concatenate([mixed_map[0], mixed[:, BLOCK:].astype(BF16)], 1)
        mixed_ref[unit] = mixed
        yield
        behind = tn(jnp.concatenate([mixed, mixed_map[1]], 1), direction)
        ends[unit] = key.astype(F32) - behind[BLOCK:2 * BLOCK]
        maps[unit] = split(identity - (behind[:BLOCK] + behind[2 * BLOCK:]))
        end_ref[unit] = ends[unit].astype(BF16)

    onward = []

    def pair_terms(pair):
        even, odd = 2 * pair, 2 * pair + 1
        running = [terms(even), terms(odd)]
        while running:
            for step in list(running):
                if next(step, running) is running:
                    running.remove(step)
            yield
        even_ref[pair, 0] = maps[even][0]
        even_ref[pair, 1] = maps[even][1]
        left = jnp.concatenate([ends[even].astype(BF16), *maps[even]], 0)
        both = nn(left, maps[odd][0])
        tail_even, tail_odd = both[:BLOCK].astype(BF16), ends[odd].astype(BF16)
        tail_ref[even] = tail_even
        tail_ref[odd] = tail_odd
        low = both[2 * BLOCK:] + nn(maps[even][0], maps[odd][1])
        pair_map = split(both[BLOCK:2 * BLOCK] + low)
        pair_ref[pair, 0] = pair_map[0]
        pair_ref[pair, 1] = pair_map[1]
        yield
        if onward:
            far = nn(jnp.concatenate([tail_even, tail_odd], 0), onward[-1][0]).astype(BF16)
            far_ref[even] = far[:BLOCK]
            far_ref[odd] = far[BLOCK:]
            if pair or group_refs:
                pair_map = split(triple(nn, pair_map, onward[-1]))
        else:
            far_ref[even] = tail_even
            far_ref[odd] = tail_odd
        onward.append(pair_map)

    interleaved([pair_terms(pair) for pair in reversed(range(units // 2))], 1)
    for group_ref in group_refs:
        group_ref[0] = onward[-1][0]
        group_ref[1] = onward[-1][1]


def queries_kernel(axes, blocks, part_ref, mixed_ref, even_ref, pair_ref, *refs):
    heads = part_ref.shape[0]
    units = heads * blocks
    inner_ref, moving_ref, query_ref, sems = refs[heads:]
    place = lax.rem(lax.axis_index(axes[0]), heads)
    copies = fetched(
        [refs[turn].at[0] if turn == 1 else refs[turn] for turn in range(heads)],
        [query_ref.at[lax.bitwise_xor(place, turn)] for turn in range(heads)],
        sems,
    )
    for copy in copies:
        copy.wait()
    rows, columns = square_iotas()
    current = []
    for unit in range(units):
        direction = rows_of(part_ref, blocks, unit, 0)
        key = rows_of(part_ref, blocks, unit, 1)
        query = rows_of(query_ref, blocks, unit, 0)
        query_proj = split(jnp.where(rows >= columns, nt(query, direction), 0.0))
        ahead = nn(jnp.concatenate(query_proj, 0), mixed_ref[unit])
        ahead = ahead[:BLOCK] + ahead[BLOCK:]
        inner_ref[unit] = nt(query, key) - ahead[:, HEAD_DIM:]
        start = split(query.astype(F32) - ahead[:, :HEAD_DIM])
        moving_ref[unit, 0] = start[0]
        if unit % 2:
            pair = unit // 2
            start = split(triple(nt, start, (even_ref[pair, 0], even_ref[pair, 1])))
        moving_ref[unit, 1] = start[0]
        current.append(start)
    pairs = units // 2
    current = [
        tuple(jnp.concatenate([current[2 * pair][part], current[2 * pair + 1][part]], 0)
              for part in range(2))
        for pair in range(pairs)
    ]
    for step in range(2, pairs + 1):
        for pair in range(step - 1, pairs):
            passed = pair - step + 1
            current[pair] = split(
                triple(nt, current[pair], (pair_ref[passed, 0], pair_ref[passed, 1]))
            )
            moving_ref[2 * pair, step] = current[pair][0][:BLOCK]
            moving_ref[2 * pair + 1, step] = current[pair][0][BLOCK:]


def listed_block(away_ref, unit, entry):
    away = away_ref[unit, entry]
    new = away > 0
    for other in range(1, entry):
        new = new & (away_ref[unit, other] != away)
    return unit - away, new


def earlier(source, ahead, units):
    return jnp.clip(source + ahead * units, 0, units - 1), source < (1 - ahead) * units


def softmax(scores):
    expos = jnp.exp(scores - jnp.max(scores, 1, keepdims=True))
    return (expos * (1.0 / jnp.sum(expos, 1, keepdims=True))).astype(BF16)


def weights_kernel(before, away_ref, moving_ref, inner_ref, end_ref, tail_ref, *refs):
    far_keys, group_maps = refs[:before], refs[before:-2]
    weights_ref, scores_ref = refs[-2:]
    units = inner_ref.shape[0]
    ready = weights_ref.shape[0]
    rows, columns = square_iotas()
    scale = HEAD_DIM ** (-0.5)

    def steps(unit):
        pair = unit // 2
        fronts = [moving_ref[unit, pair + 1]]
        for group_map in group_maps:
            passed = nt(fronts[-1], group_map[0]) + nt(fronts[-1], group_map[1])
            fronts.append(passed.astype(BF16))
        score_list = [jnp.where(rows >= columns, inner_ref[unit] * scale, -1e30)]
        for entry in range(1, TOPK):
            source, new = listed_block(away_ref, unit, entry)
            inside = jnp.maximum(source, 0)
            step = jnp.maximum(pair - inside // 2, 0)
            query = moving_ref[unit, step]
            key = jnp.where(step == 0, end_ref[inside], tail_ref[inside])
            for ahead in range(1, before + 1):
                place, here = earlier(source, ahead, units)
                query = jnp.where(here, fronts[ahead - 1], query)
                key = jnp.where(here, far_keys[ahead - 1][place], key)
            score_list.append(jnp.where(new, nt(query, key) * scale, -1e30))
        yield
        scores = jnp.concatenate(score_list, 1)
        if unit < ready:
            weights_ref[unit] = softmax(scores)
        else:
            scores_ref[unit - ready] = scores

    interleaved([steps(unit) for unit in range(units)], 1)


def blend_kernel(axes, before, blocks, away_ref, weights_ref, scores_ref, *refs):
    ready, late = weights_ref.shape[0], scores_ref.shape[0]
    units = ready + late
    heads = units // blocks
    count = (len(refs) - 4 - heads * (1 + before)) // 2
    arrived = refs[:heads * (1 + before)]
    out_ref, (values_ref, value_sems, sems) = refs[-4 - count], refs[-3:]
    place = lax.rem(lax.axis_index(axes[0]), heads)
    value_copies = []
    for kind in range(1 + before):
        for turn in range(heads):
            start = pl.multiple_of(lax.bitwise_xor(place, turn) * blocks * BLOCK, BLOCK)
            source = arrived[kind * heads + turn]
            value_copies += fetched(
                [source if kind or turn != 1 else source.at[1]],
                [values_ref.at[kind, pl.ds(start, blocks * BLOCK)]],
                value_sems.at[kind, pl.ds(turn, 1)],
            )
    copies = fetched(
        refs[heads * (1 + before):heads * (1 + before) + count], refs[-3 - count:-3], sems
    )
    late_weights = [softmax(scores_ref[unit]) for unit in range(late)]
    for copy in value_copies:
        copy.wait()

    def value_of(kind, block):
        return values_ref[kind, pl.ds(pl.multiple_of(block * BLOCK, BLOCK), BLOCK)]

    for unit in range(units):
        value_list = [value_of(0, unit)]
        for entry in range(1, TOPK):
            source, _ = listed_block(away_ref, unit, entry)
            kind, block = 0, jnp.maximum(source, 0)
            for ahead in range(1, before + 1):
                other, here = earlier(source, ahead, units)
                kind = jnp.where(here, ahead, kind)
                block = jnp.where(here, other, block)
            value_list.append(value_of(kind, block))
        weights = weights_ref[unit] if unit < ready else late_weights[unit - ready]
        blended = nn(weights, jnp.concatenate(value_list, 0)).astype(BF16)
        for plane in range(out_ref.shape[1]):
            out_ref[unit // blocks, plane, unit % blocks] = blended
    for copy in copies:
        copy.wait()


def project_kernel(axes, other, cores, attended_ref, own_ref, *refs):
    other_refs, out_ref = refs[:-1], refs[-1]
    heads, planes, blocks = attended_ref.shape[:3]
    index = lax.axis_index(axes[1])
    core, plane = lax.rem(index + other, cores), index // cores
    width = out_ref.shape[1]
    total = None
    for offset in range(planes):
        source = lax.rem(plane + offset, planes)
        attended = jnp.concatenate(
            [
                jnp.concatenate(
                    [attended_ref[head, source, block] for head in range(heads)], 1
                )
                for block in range(blocks)
            ],
            0,
        )
        if offset:
            start = pl.multiple_of(core * width, width)
            weight = other_refs[offset - 1][:, pl.ds(start, width)]
        else:
            start = pl.multiple_of((plane * cores + core) * width, width)
            weight = own_ref[:, pl.ds(start, width)]
        product = nn(attended, weight)
        total = product if total is None else total + product
    out_ref[...] = total.astype(out_ref.dtype)


def call(kernel, outs, specs, flops, scratch=(), places=None, space=32):
    if places is None:
        places = [VMEM] * len(outs) if isinstance(outs, list) else VMEM
    return pl.pallas_call(
        kernel,
        out_shape=outs,
        in_specs=specs,
        out_specs=places,
        scratch_shapes=list(scratch),
        compiler_params=pltpu.CompilerParams(vmem_limit_bytes=space * 2 ** 20),
        cost_estimate=pl.CostEstimate(flops=flops, bytes_accessed=2 ** 21, transcendentals=0),
    )


def body(ctx_size, head_size, queries, keys, values, directions, rates, selected, out_weight):
    tokens = queries.shape[0]
    blocks = tokens // BLOCK
    heads = queries.shape[1] // HEAD_DIM
    units = heads * blocks
    pairs = units // 2
    groups = ctx_size // heads
    before = min(groups - 1, -(-LOOK // heads))
    cores = 2
    planes = head_size // cores
    axes = ("ctx", "head")
    members = [[group * heads + place for place in range(heads)] for group in range(groups)]
    partners = [(g, g + 1 - 2 * (g % cores)) for g in range(head_size)]
    cubes = 2 * BLOCK ** 3
    tile = (BLOCK, HEAD_DIM)

    def exchange(value):
        return lax.all_to_all(value, "ctx", 0, 0, axis_index_groups=members, tiled=True)

    def onward(value, by):
        shift = by * heads
        return lax.ppermute(value, "ctx", [(i, i + shift) for i in range(ctx_size - shift)])

    def crossed(value, turn):
        pairs = [(i, i - i % heads + (i % heads ^ turn)) for i in range(ctx_size)]
        return lax.ppermute(value, "ctx", pairs) if turn else value

    def straight(value, turn, by):
        shift = by * heads
        pairs = [(i, i - i % heads + (i % heads ^ turn) + shift) for i in range(ctx_size - shift)]
        return lax.ppermute(value, "ctx", pairs)

    def array(shape, kind=BF16):
        return jax.ShapeDtypeStruct(shape, kind)

    part_shape = (heads, 2 * tokens + EXTRA, HEAD_DIM)
    width = out_weight.shape[1] // planes
    piece_shape = (out_weight.shape[0], width)
    packed, *rest = call(
        functools.partial(pack_kernel, axes, cores),
        [array(part_shape)]
        + [array((tokens, HEAD_DIM))] * heads
        + [array(piece_shape)] * (planes - 1),
        [ANY] * 6,
        cubes,
        [
            pltpu.VMEM(part_shape, BF16),
            pltpu.VMEM(rates.shape, F32),
            pltpu.SMEM(selected.shape, jnp.int32),
            pltpu.VMEM((heads, tokens, HEAD_DIM), BF16),
            pltpu.VMEM((max(planes - 1, 1), *piece_shape), BF16),
            pltpu.SemaphoreType.DMA((heads, 2)),
            pltpu.SemaphoreType.DMA((2,)),
            pltpu.SemaphoreType.DMA((heads,)),
            pltpu.SemaphoreType.DMA((heads,)),
            pltpu.SemaphoreType.DMA((heads,)),
            pltpu.SemaphoreType.DMA((2, planes)),
        ],
        [ANY] * (heads + planes),
        56,
    )(directions, keys, rates, selected, values, out_weight)
    value_cuts, pieces = rest[:heads], rest[heads:]
    value_parts = [
        straight(value_cuts[turn], turn, by) for by in range(1, before + 1) for turn in range(heads)
    ]
    weight_parts = []
    for offset in range(1, planes):
        turned = [(g, (g + head_size - cores * offset) % head_size) for g in range(head_size)]
        weight_parts.append(lax.ppermute(pieces[offset - 1], "head", turned))
    parts = exchange(packed)

    end, tail, far, even, pair_map, mixed, away, *group_maps = call(
        functools.partial(keys_kernel, blocks),
        [
            array((units, *tile)),
            array((units, *tile)),
            array((units, *tile)),
            array((pairs, 2, *tile)),
            array((pairs, 2, *tile)),
            array((units, BLOCK, 2 * BLOCK)),
            array((units, HEAD_DIM), jnp.int32),
        ]
        + [array((2, *tile))] * (before > 1),
        [VMEM],
        400 * cubes,
    )(parts)
    far_parts = [onward(far, by) for by in range(1, before + 1)]
    map_parts = [onward(group_maps[0], by) for by in range(1, before)]
    first, *cut = call(
        functools.partial(cut_kernel, axes, heads),
        [array((2, tokens, HEAD_DIM))] + [array((tokens, HEAD_DIM))] * (2 * heads - 2),
        [ANY] * (len(value_parts) + 3),
        2000 * cubes,
        [pltpu.SemaphoreType.DMA((2, heads))],
    )(queries, values, *value_parts, away)
    first = crossed(first, 1)
    turns = [0, *range(2, heads)]
    query_parts = [crossed(part, turn) for part, turn in zip(cut[:heads - 1], turns)]
    own_parts = [crossed(part, turn) for part, turn in zip(cut[heads - 1:], turns)]
    query_parts.insert(1, first)
    own_parts.insert(1, first)
    inner, moving = call(
        functools.partial(queries_kernel, axes, blocks),
        [array((units, BLOCK, BLOCK), F32), array((units, pairs + 1, *tile))],
        [VMEM] * 4 + [ANY] * heads,
        0,
        [pltpu.VMEM((heads, tokens, HEAD_DIM), BF16), pltpu.SemaphoreType.DMA((heads,))],
    )(parts, mixed, even, pair_map, *query_parts)
    weights, scores = call(
        functools.partial(weights_kernel, before),
        [
            array((units - units // 2, BLOCK, TOPK * BLOCK)),
            array((units // 2, BLOCK, TOPK * BLOCK), F32),
        ],
        [SMEM] + [VMEM] * (4 + before + len(map_parts)),
        0,
    )(away, moving, inner, end, tail, *far_parts, *map_parts)
    attended, *weight_parts = call(
        functools.partial(blend_kernel, axes, before, blocks),
        [array((heads, planes, blocks, *tile))] + [array(part.shape) for part in weight_parts],
        [SMEM, VMEM, VMEM] + [ANY] * (heads * (1 + before) + len(weight_parts)),
        0,
        [
            pltpu.VMEM((1 + before, units * BLOCK, HEAD_DIM), BF16),
            pltpu.SemaphoreType.DMA((1 + before, heads)),
            pltpu.SemaphoreType.DMA((planes,)),
        ],
    )(away, weights, scores, *own_parts, *value_parts, *weight_parts)

    returns = [
        [
            (group * heads + place) * head_size + p * cores + core
            for place in range(heads)
            for p in range(planes)
        ]
        for group in range(groups)
        for core in range(cores)
    ]
    local = lax.all_to_all(
        attended.reshape(heads * planes, blocks, *tile),
        axes, 0, 0, axis_index_groups=returns, tiled=True,
    ).reshape(heads, planes, blocks, *tile)

    def projected(other, kind):
        return call(
            functools.partial(project_kernel, axes, other, cores),
            array((tokens, width // cores), kind),
            [VMEM] * (1 + planes),
            128 * cubes,
        )(local, out_weight, *weight_parts)

    arrived = lax.ppermute(projected(1, BF16), "head", partners)
    return (projected(0, F32) + arrived.astype(F32)).astype(BF16)


def solution(mesh):
    in_specs = (
        P("ctx", "head"),
        P("ctx", "head"),
        P("ctx", "head"),
        P("ctx", "head"),
        P("head", "ctx"),
        P("ctx", None),
        P("head", None),
    )
    out_specs = P("ctx", "head")
    return jax.shard_map(
        functools.partial(body, mesh.shape["ctx"], mesh.shape["head"]),
        mesh=mesh,
        in_specs=in_specs,
        out_specs=out_specs,
        check_vma=False,
    )
```

```python
import functools

import jax
import jax.numpy as jnp
from jax import lax
from jax.experimental import pallas as pl
from jax.experimental.pallas import tpu as pltpu
from jax.sharding import PartitionSpec as P

HEAD_DIM = 128
BLOCK = 128
LOOK = 7
TOPK = 4
BASE = 16
EXTRA = 16
TERMS = 3
BF16 = jnp.bfloat16
F32 = jnp.float32
VMEM = pl.BlockSpec(memory_space=pltpu.VMEM)
SMEM = pl.BlockSpec(memory_space=pltpu.SMEM)
ANY = pl.BlockSpec(memory_space=pl.ANY)


def dot(left, right, left_dim, right_dim):
    return lax.dot_general(
        left, right, (((left_dim,), (right_dim,)), ((), ())), preferred_element_type=F32
    )


def nn(left, right):
    return dot(left, right, 1, 0)


def nt(left, right):
    return dot(left, right, 1, 1)


def tn(left, right):
    return dot(left, right, 0, 0)


def split(value):
    high = value.astype(BF16)
    return high, (value - high.astype(F32)).astype(BF16)


def triple(product, left, right):
    rows = left[0].shape[0]
    first = product(jnp.concatenate(left, 0), right[0])
    return first[:rows] + (first[rows:] + product(left[0], right[1]))


def square_iotas():
    rows = lax.broadcasted_iota(jnp.int32, (BLOCK, BLOCK), 0)
    columns = lax.broadcasted_iota(jnp.int32, (BLOCK, BLOCK), 1)
    return rows, columns


def fetched(sources, targets, sems):
    copies = []
    for index, (source, target) in enumerate(zip(sources, targets)):
        copies.append(pltpu.make_async_copy(source, target, sems.at[index]))
        copies[-1].start()
    return copies


def pack_kernel(axes, cores, d_ref, k_ref, rates_hbm, selected_hbm, values_ref, weight_ref,
                *refs):
    tokens = d_ref.shape[0]
    heads = d_ref.shape[1] // HEAD_DIM
    blocks = tokens // BLOCK
    (parts_ref, rates_ref, selected_ref, cut_ref, piece_ref, sems, few_sems, out_sems, cut_sems,
     cut_out_sems, piece_sems) = refs[-11:]
    out_ref, cut_outs, piece_outs = refs[0], refs[1:1 + heads], refs[1 + heads:-11]
    planes = len(piece_outs) + 1
    width = weight_ref.shape[1] // planes
    device = lax.axis_index(axes[0])
    place = lax.rem(device, heads)
    plane = lax.axis_index(axes[1]) // cores
    first_block = device * blocks
    few_copies = fetched([rates_hbm, selected_hbm], [rates_ref, selected_ref], few_sems)
    sources = (d_ref, k_ref)
    copies = []
    for head in range(heads):
        columns = pl.ds(head * HEAD_DIM, HEAD_DIM)
        for kind, source in enumerate(sources):
            copies.append(
                pltpu.make_async_copy(
                    source.at[:, columns],
                    parts_ref.at[head, pl.ds(kind * tokens, tokens)],
                    sems.at[head, kind],
                )
            )
            copies[-1].start()
    cuts = [
        pl.multiple_of(lax.bitwise_xor(place, turn) * HEAD_DIM, HEAD_DIM) for turn in range(heads)
    ]
    cut_copies = fetched(
        [values_ref.at[:, pl.ds(cut, HEAD_DIM)] for cut in cuts],
        [cut_ref.at[turn] for turn in range(heads)],
        cut_sems,
    )
    piece_copies = []
    for offset in range(1, planes):
        start = pl.multiple_of(lax.rem(plane + planes - offset, planes) * width, width)
        piece_copies += fetched(
            [weight_ref.at[:, pl.ds(start, width)]],
            [piece_ref.at[offset - 1]],
            piece_sems.at[0, pl.ds(offset - 1, 1)],
        )
    for copy in few_copies:
        copy.wait()
    row = lax.broadcasted_iota(jnp.int32, (EXTRA, HEAD_DIM), 0)
    lane = lax.broadcasted_iota(jnp.int32, (EXTRA, HEAD_DIM), 1)
    away = jnp.zeros((EXTRA, HEAD_DIM), jnp.int32)
    for block in range(blocks):
        for entry in range(TOPK):
            distance = first_block + block - selected_ref[block, entry]
            away = jnp.where((row == TERMS * blocks + block) & (lane == entry), distance, away)
    away = away.astype(F32)
    terms = []
    rest = rates_ref[...]
    for _ in range(TERMS):
        terms.append(rest.astype(BF16).astype(F32))
        rest = rest - terms[-1]
    out_copies = []
    for head in range(heads):
        extra = away
        for block in range(blocks):
            for index, term in enumerate(terms):
                piece = term[head:head + 1, block * BLOCK:(block + 1) * BLOCK]
                extra = jnp.where(row == TERMS * block + index, piece, extra)
        parts_ref[head, len(sources) * tokens:] = extra.astype(BF16)
        for copy in copies[len(sources) * head:len(sources) * (head + 1)]:
            copy.wait()
        out_copies.append(
            pltpu.make_async_copy(parts_ref.at[head], out_ref.at[head], out_sems.at[head])
        )
        out_copies[-1].start()
    for turn in range(heads):
        cut_copies[turn].wait()
        out_copies += fetched(
            [cut_ref.at[turn]], [cut_outs[turn]], cut_out_sems.at[pl.ds(turn, 1)]
        )
    for index, copy in enumerate(piece_copies):
        copy.wait()
        out_copies += fetched(
            [piece_ref.at[index]], [piece_outs[index]], piece_sems.at[1, pl.ds(index, 1)]
        )
    for copy in out_copies:
        copy.wait()


def cut_kernel(axes, heads, queries_ref, values_ref, *refs):
    sems = refs[-1]
    first, outs = refs[-2 * heads], refs[1 - 2 * heads:-1]
    query_outs, value_outs = list(outs[:heads - 1]), list(outs[heads - 1:])
    query_outs.insert(1, first.at[0])
    value_outs.insert(1, first.at[1])
    place = lax.rem(lax.axis_index(axes[0]), heads)
    cuts = [
        pl.multiple_of(lax.bitwise_xor(place, turn) * HEAD_DIM, HEAD_DIM) for turn in range(heads)
    ]
    copies = []
    for kind, (source, targets) in enumerate(
        ((queries_ref, query_outs), (values_ref, value_outs))
    ):
        copies += fetched(
            [source.at[:, pl.ds(cut, HEAD_DIM)] for cut in cuts], targets, sems.at[kind]
        )
    for copy in copies:
        copy.wait()


def rows_of(ref, blocks, unit, kind):
    start = (kind * blocks + unit % blocks) * BLOCK
    return ref[unit // blocks, start:start + BLOCK]


def base_inverse(strict):
    count = BLOCK // BASE
    moved = [
        pltpu.roll(strict[b * BASE:(b + 1) * BASE], (BLOCK - b * BASE) % BLOCK, 1)
        if b else strict[:BASE]
        for b in range(count)
    ]
    lanes = lax.broadcasted_iota(jnp.int32, (BASE // 2, BLOCK), 1)
    rows = lax.broadcasted_iota(jnp.int32, (BASE // 2, BLOCK), 0)
    half = BASE // 2
    parts = []
    for b in range(count):
        upper = (lanes == rows + b * BASE).astype(F32)
        lower = (lanes == rows + b * BASE + half).astype(F32)
        for step in range(BASE - 1):
            if step < half:
                source = upper[step:step + 1]
                if step < half - 1:
                    upper = upper - moved[b][:half, step:step + 1] * source
            else:
                source = lower[step - half:step - half + 1]
            lower = lower - moved[b][half:, step:step + 1] * source
        parts += [upper, lower]
    return jnp.concatenate(parts, 0)


def halves(value, size):
    parts = value.reshape(BLOCK // (2 * size), 2, size, BLOCK)
    return parts[:, 0].reshape(BLOCK // 2, BLOCK), parts[:, 1].reshape(BLOCK // 2, BLOCK)


def joined(first, second, size):
    shape = (BLOCK // (2 * size), 1, size, BLOCK)
    return jnp.concatenate([first.reshape(shape), second.reshape(shape)], 1).reshape(BLOCK, BLOCK)


def interleaved(steps, lag):
    running = list(steps)
    tick = 0
    while any(step is not None for step in running):
        for index, step in enumerate(running):
            if step is not None and tick >= index * lag:
                try:
                    next(step)
                except StopIteration:
                    running[index] = None
        tick += 1


def keys_kernel(blocks, part_ref, end_ref, tail_ref, far_ref, even_ref, pair_ref, mixed_ref,
                away_ref, *group_refs):
    units = part_ref.shape[0] * blocks
    rows, columns = square_iotas()
    diagonal = rows == columns
    identity = diagonal.astype(F32)
    row = lax.broadcasted_iota(jnp.int32, (BLOCK // 2, BLOCK), 0)
    column = lax.broadcasted_iota(jnp.int32, (BLOCK // 2, BLOCK), 1)
    ends, maps = [None] * units, [None] * units

    def terms(unit):
        direction = rows_of(part_ref, blocks, unit, 0)
        key = rows_of(part_ref, blocks, unit, 1)
        extra = part_ref[unit // blocks, 2 * blocks * BLOCK:].astype(F32)
        first = TERMS * (unit % blocks)
        rate = extra[first:first + 1] + extra[first + 1:first + 2] + extra[first + 2:first + 3]
        listed = TERMS * blocks + unit % blocks
        away_ref[unit:unit + 1] = extra[listed:listed + 1].astype(jnp.int32)
        gram = nt(direction, direction)
        key_proj = jnp.where(rows > columns, nt(direction, key), 0.0).astype(BF16)
        squares = jnp.sum(jnp.where(diagonal, gram, 0.0), 0, keepdims=True)
        scale = lax.rsqrt(squares + 1e-06)
        scaled_rate = rate * scale
        scale_column = jnp.sum(jnp.where(diagonal, scale, 0.0), 1, keepdims=True)
        rate_column = jnp.sum(jnp.where(diagonal, scaled_rate, 0.0), 1, keepdims=True)
        strict = jnp.where(rows > columns, rate_column * gram * scale, 0.0)
        yield
        inverse = base_inverse(strict)
        yield
        size = BASE
        while size < BLOCK:
            inside = (row // size == column // (2 * size)) & (lax.rem(column, 2 * size) < size)
            corner = jnp.where(inside, halves(strict, size)[1], 0.0)
            below = triple(nn, split(corner), split(inverse))
            yield
            first_half, second = halves(inverse, size)
            padded = joined(jnp.zeros_like(below), below, size)
            second = second - triple(nn, split(second), split(padded))
            inverse = joined(first_half, second, size)
            size *= 2
            yield
        mixing = split(scale_column * inverse * scaled_rate)
        mixed = nn(mixing[0], jnp.concatenate([direction, key_proj], 1))
        mixed_map = split(mixed[:, :BLOCK] + nn(mixing[1], direction))
        mixed = jnp.concatenate([mixed_map[0], mixed[:, BLOCK:].astype(BF16)], 1)
        mixed_ref[unit] = mixed
        yield
        behind = tn(jnp.concatenate([mixed, mixed_map[1]], 1), direction)
        ends[unit] = key.astype(F32) - behind[BLOCK:2 * BLOCK]
        maps[unit] = split(identity - (behind[:BLOCK] + behind[2 * BLOCK:]))
        end_ref[unit] = ends[unit].astype(BF16)

    onward = []

    def pair_terms(pair):
        even, odd = 2 * pair, 2 * pair + 1
        running = [terms(even), terms(odd)]
        while running:
            for step in list(running):
                if next(step, running) is running:
                    running.remove(step)
            yield
        even_ref[pair, 0] = maps[even][0]
        even_ref[pair, 1] = maps[even][1]
        left = jnp.concatenate([ends[even].astype(BF16), *maps[even]], 0)
        both = nn(left, maps[odd][0])
        tail_even, tail_odd = both[:BLOCK].astype(BF16), ends[odd].astype(BF16)
        tail_ref[even] = tail_even
        tail_ref[odd] = tail_odd
        low = both[2 * BLOCK:] + nn(maps[even][0], maps[odd][1])
        pair_map = split(both[BLOCK:2 * BLOCK] + low)
        pair_ref[pair, 0] = pair_map[0]
        pair_ref[pair, 1] = pair_map[1]
        yield
        if onward:
            far = nn(jnp.concatenate([tail_even, tail_odd], 0), onward[-1][0]).astype(BF16)
            far_ref[even] = far[:BLOCK]
            far_ref[odd] = far[BLOCK:]
            if pair or group_refs:
                pair_map = split(triple(nn, pair_map, onward[-1]))
        else:
            far_ref[even] = tail_even
            far_ref[odd] = tail_odd
        onward.append(pair_map)

    interleaved([pair_terms(pair) for pair in reversed(range(units // 2))], 1)
    for group_ref in group_refs:
        group_ref[0] = onward[-1][0]
        group_ref[1] = onward[-1][1]


def queries_kernel(axes, blocks, part_ref, mixed_ref, even_ref, pair_ref, *refs):
    heads = part_ref.shape[0]
    units = heads * blocks
    inner_ref, moving_ref, query_ref, sems = refs[heads:]
    place = lax.rem(lax.axis_index(axes[0]), heads)
    copies = fetched(
        [refs[turn].at[0] if turn == 1 else refs[turn] for turn in range(heads)],
        [query_ref.at[lax.bitwise_xor(place, turn)] for turn in range(heads)],
        sems,
    )
    for copy in copies:
        copy.wait()
    rows, columns = square_iotas()

    def pair_steps(pair):
        projs, fronts = [], []
        for unit in (2 * pair, 2 * pair + 1):
            direction = rows_of(part_ref, blocks, unit, 0)
            query = rows_of(query_ref, blocks, unit, 0)
            projs.append(split(jnp.where(rows >= columns, nt(query, direction), 0.0)))
        yield
        for unit in (2 * pair, 2 * pair + 1):
            key = rows_of(part_ref, blocks, unit, 1)
            query = rows_of(query_ref, blocks, unit, 0)
            ahead = nn(jnp.concatenate(projs[unit % 2], 0), mixed_ref[unit])
            ahead = ahead[:BLOCK] + ahead[BLOCK:]
            inner_ref[unit] = nt(query, key) - ahead[:, HEAD_DIM:]
            fronts.append(split(query.astype(F32) - ahead[:, :HEAD_DIM]))
            moving_ref[unit, 0] = fronts[-1][0]
        yield
        fronts[1] = split(triple(nt, fronts[1], (even_ref[pair, 0], even_ref[pair, 1])))
        current = tuple(
            jnp.concatenate([fronts[0][part], fronts[1][part]], 0) for part in range(2)
        )
        for step in range(1, pair + 2):
            if step > 1:
                passed = pair - step + 1
                current = split(
                    triple(nt, current, (pair_ref[passed, 0], pair_ref[passed, 1]))
                )
            moving_ref[2 * pair, step] = current[0][:BLOCK]
            moving_ref[2 * pair + 1, step] = current[0][BLOCK:]
            yield

    interleaved([pair_steps(pair) for pair in reversed(range(units // 2))], 1)


def listed_block(away_ref, unit, entry):
    away = away_ref[unit, entry]
    new = away > 0
    for other in range(1, entry):
        new = new & (away_ref[unit, other] != away)
    return unit - away, new


def earlier(source, ahead, units):
    return jnp.clip(source + ahead * units, 0, units - 1), source < (1 - ahead) * units


def weights_kernel(before, away_ref, moving_ref, inner_ref, end_ref, tail_ref, *refs):
    far_keys, group_maps, weights_ref = refs[:before], refs[before:-1], refs[-1]
    units = inner_ref.shape[0]
    rows, columns = square_iotas()
    scale = HEAD_DIM ** (-0.5)

    def steps(unit):
        pair = unit // 2
        fronts = [moving_ref[unit, pair + 1]]
        for group_map in group_maps:
            passed = nt(fronts[-1], group_map[0]) + nt(fronts[-1], group_map[1])
            fronts.append(passed.astype(BF16))
        score_list = [jnp.where(rows >= columns, inner_ref[unit] * scale, -1e30)]
        for entry in range(1, TOPK):
            source, new = listed_block(away_ref, unit, entry)
            inside = jnp.maximum(source, 0)
            step = jnp.maximum(pair - inside // 2, 0)
            query = moving_ref[unit, step]
            key = jnp.where(step == 0, end_ref[inside], tail_ref[inside])
            for ahead in range(1, before + 1):
                place, here = earlier(source, ahead, units)
                query = jnp.where(here, fronts[ahead - 1], query)
                key = jnp.where(here, far_keys[ahead - 1][place], key)
            score_list.append(jnp.where(new, nt(query, key) * scale, -1e30))
        yield
        scores = jnp.concatenate(score_list, 1)
        expos = jnp.exp(scores - jnp.max(scores, 1, keepdims=True))
        weights_ref[unit] = (expos * (1.0 / jnp.sum(expos, 1, keepdims=True))).astype(BF16)

    interleaved([steps(unit) for unit in range(units)], 1)


def blend_kernel(axes, before, blocks, away_ref, weights_ref, *refs):
    units = weights_ref.shape[0]
    heads = units // blocks
    count = (len(refs) - 4 - heads * (1 + before)) // 2
    arrived = refs[:heads * (1 + before)]
    out_ref, (values_ref, value_sems, sems) = refs[-4 - count], refs[-3:]
    place = lax.rem(lax.axis_index(axes[0]), heads)
    value_copies = []
    for kind in range(1 + before):
        for turn in range(heads):
            start = pl.multiple_of(lax.bitwise_xor(place, turn) * blocks * BLOCK, BLOCK)
            source = arrived[kind * heads + turn]
            value_copies += fetched(
                [source if kind or turn != 1 else source.at[1]],
                [values_ref.at[kind, pl.ds(start, blocks * BLOCK)]],
                value_sems.at[kind, pl.ds(turn, 1)],
            )
    copies = fetched(
        refs[heads * (1 + before):heads * (1 + before) + count], refs[-3 - count:-3], sems
    )
    for copy in value_copies:
        copy.wait()

    def value_of(kind, block):
        return values_ref[kind, pl.ds(pl.multiple_of(block * BLOCK, BLOCK), BLOCK)]

    for unit in range(units):
        value_list = [value_of(0, unit)]
        for entry in range(1, TOPK):
            source, _ = listed_block(away_ref, unit, entry)
            kind, block = 0, jnp.maximum(source, 0)
            for ahead in range(1, before + 1):
                other, here = earlier(source, ahead, units)
                kind = jnp.where(here, ahead, kind)
                block = jnp.where(here, other, block)
            value_list.append(value_of(kind, block))
        blended = nn(weights_ref[unit], jnp.concatenate(value_list, 0)).astype(BF16)
        for plane in range(out_ref.shape[1]):
            out_ref[unit // blocks, plane, unit % blocks] = blended
    for copy in copies:
        copy.wait()


def project_kernel(axes, other, cores, attended_ref, own_ref, *refs):
    other_refs, out_ref = refs[:-1], refs[-1]
    heads, planes, blocks = attended_ref.shape[:3]
    index = lax.axis_index(axes[1])
    core, plane = lax.rem(index + other, cores), index // cores
    width = out_ref.shape[1]
    total = None
    for offset in range(planes):
        source = lax.rem(plane + offset, planes)
        attended = jnp.concatenate(
            [
                jnp.concatenate(
                    [attended_ref[head, source, block] for head in range(heads)], 1
                )
                for block in range(blocks)
            ],
            0,
        )
        if offset:
            start = pl.multiple_of(core * width, width)
            weight = other_refs[offset - 1][:, pl.ds(start, width)]
        else:
            start = pl.multiple_of((plane * cores + core) * width, width)
            weight = own_ref[:, pl.ds(start, width)]
        product = nn(attended, weight)
        total = product if total is None else total + product
    out_ref[...] = total.astype(out_ref.dtype)


def call(kernel, outs, specs, flops, scratch=(), places=None, space=32):
    if places is None:
        places = [VMEM] * len(outs) if isinstance(outs, list) else VMEM
    return pl.pallas_call(
        kernel,
        out_shape=outs,
        in_specs=specs,
        out_specs=places,
        scratch_shapes=list(scratch),
        compiler_params=pltpu.CompilerParams(vmem_limit_bytes=space * 2 ** 20),
        cost_estimate=pl.CostEstimate(flops=flops, bytes_accessed=2 ** 21, transcendentals=0),
    )


def body(ctx_size, head_size, queries, keys, values, directions, rates, selected, out_weight):
    tokens = queries.shape[0]
    blocks = tokens // BLOCK
    heads = queries.shape[1] // HEAD_DIM
    units = heads * blocks
    pairs = units // 2
    groups = ctx_size // heads
    before = min(groups - 1, -(-LOOK // heads))
    cores = 2
    planes = head_size // cores
    axes = ("ctx", "head")
    members = [[group * heads + place for place in range(heads)] for group in range(groups)]
    partners = [(g, g + 1 - 2 * (g % cores)) for g in range(head_size)]
    cubes = 2 * BLOCK ** 3
    tile = (BLOCK, HEAD_DIM)

    def exchange(value):
        return lax.all_to_all(value, "ctx", 0, 0, axis_index_groups=members, tiled=True)

    def onward(value, by):
        shift = by * heads
        return lax.ppermute(value, "ctx", [(i, i + shift) for i in range(ctx_size - shift)])

    def crossed(value, turn):
        pairs = [(i, i - i % heads + (i % heads ^ turn)) for i in range(ctx_size)]
        return lax.ppermute(value, "ctx", pairs) if turn else value

    def straight(value, turn, by):
        shift = by * heads
        pairs = [(i, i - i % heads + (i % heads ^ turn) + shift) for i in range(ctx_size - shift)]
        return lax.ppermute(value, "ctx", pairs)

    def array(shape, kind=BF16):
        return jax.ShapeDtypeStruct(shape, kind)

    part_shape = (heads, 2 * tokens + EXTRA, HEAD_DIM)
    width = out_weight.shape[1] // planes
    piece_shape = (out_weight.shape[0], width)
    packed, *rest = call(
        functools.partial(pack_kernel, axes, cores),
        [array(part_shape)]
        + [array((tokens, HEAD_DIM))] * heads
        + [array(piece_shape)] * (planes - 1),
        [ANY] * 6,
        cubes,
        [
            pltpu.VMEM(part_shape, BF16),
            pltpu.VMEM(rates.shape, F32),
            pltpu.SMEM(selected.shape, jnp.int32),
            pltpu.VMEM((heads, tokens, HEAD_DIM), BF16),
            pltpu.VMEM((max(planes - 1, 1), *piece_shape), BF16),
            pltpu.SemaphoreType.DMA((heads, 2)),
            pltpu.SemaphoreType.DMA((2,)),
            pltpu.SemaphoreType.DMA((heads,)),
            pltpu.SemaphoreType.DMA((heads,)),
            pltpu.SemaphoreType.DMA((heads,)),
            pltpu.SemaphoreType.DMA((2, planes)),
        ],
        [ANY] * (heads + planes),
        56,
    )(directions, keys, rates, selected, values, out_weight)
    value_cuts, pieces = rest[:heads], rest[heads:]
    value_parts = [
        straight(value_cuts[turn], turn, by) for by in range(1, before + 1) for turn in range(heads)
    ]
    weight_parts = []
    for offset in range(1, planes):
        turned = [(g, (g + head_size - cores * offset) % head_size) for g in range(head_size)]
        weight_parts.append(lax.ppermute(pieces[offset - 1], "head", turned))
    parts = exchange(packed)

    end, tail, far, even, pair_map, mixed, away, *group_maps = call(
        functools.partial(keys_kernel, blocks),
        [
            array((units, *tile)),
            array((units, *tile)),
            array((units, *tile)),
            array((pairs, 2, *tile)),
            array((pairs, 2, *tile)),
            array((units, BLOCK, 2 * BLOCK)),
            array((units, HEAD_DIM), jnp.int32),
        ]
        + [array((2, *tile))] * (before > 1),
        [VMEM],
        400 * cubes,
    )(parts)
    far_parts = [onward(far, by) for by in range(1, before + 1)]
    map_parts = [onward(group_maps[0], by) for by in range(1, before)]
    first, *cut = call(
        functools.partial(cut_kernel, axes, heads),
        [array((2, tokens, HEAD_DIM))] + [array((tokens, HEAD_DIM))] * (2 * heads - 2),
        [ANY] * (len(value_parts) + 3),
        2000 * cubes,
        [pltpu.SemaphoreType.DMA((2, heads))],
    )(queries, values, *value_parts, away)
    first = crossed(first, 1)
    turns = [0, *range(2, heads)]
    query_parts = [crossed(part, turn) for part, turn in zip(cut[:heads - 1], turns)]
    own_parts = [crossed(part, turn) for part, turn in zip(cut[heads - 1:], turns)]
    query_parts.insert(1, first)
    own_parts.insert(1, first)
    inner, moving = call(
        functools.partial(queries_kernel, axes, blocks),
        [array((units, BLOCK, BLOCK), F32), array((units, pairs + 1, *tile))],
        [VMEM] * 4 + [ANY] * heads,
        0,
        [pltpu.VMEM((heads, tokens, HEAD_DIM), BF16), pltpu.SemaphoreType.DMA((heads,))],
    )(parts, mixed, even, pair_map, *query_parts)
    weights = call(
        functools.partial(weights_kernel, before),
        array((units, BLOCK, TOPK * BLOCK)),
        [SMEM] + [VMEM] * (4 + before + len(map_parts)),
        0,
    )(away, moving, inner, end, tail, *far_parts, *map_parts)
    attended, *weight_parts = call(
        functools.partial(blend_kernel, axes, before, blocks),
        [array((heads, planes, blocks, *tile))] + [array(part.shape) for part in weight_parts],
        [SMEM, VMEM] + [ANY] * (heads * (1 + before) + len(weight_parts)),
        0,
        [
            pltpu.VMEM((1 + before, units * BLOCK, HEAD_DIM), BF16),
            pltpu.SemaphoreType.DMA((1 + before, heads)),
            pltpu.SemaphoreType.DMA((planes,)),
        ],
    )(away, weights, *own_parts, *value_parts, *weight_parts)

    returns = [
        [
            (group * heads + place) * head_size + p * cores + core
            for place in range(heads)
            for p in range(planes)
        ]
        for group in range(groups)
        for core in range(cores)
    ]
    local = lax.all_to_all(
        attended.reshape(heads * planes, blocks, *tile),
        axes, 0, 0, axis_index_groups=returns, tiled=True,
    ).reshape(heads, planes, blocks, *tile)

    def projected(other, kind):
        return call(
            functools.partial(project_kernel, axes, other, cores),
            array((tokens, width // cores), kind),
            [VMEM] * (1 + planes),
            128 * cubes,
        )(local, out_weight, *weight_parts)

    arrived = lax.ppermute(projected(1, BF16), "head", partners)
    return (projected(0, F32) + arrived.astype(F32)).astype(BF16)


def solution(mesh):
    in_specs = (
        P("ctx", "head"),
        P("ctx", "head"),
        P("ctx", "head"),
        P("ctx", "head"),
        P("head", "ctx"),
        P("ctx", None),
        P("head", None),
    )
    out_specs = P("ctx", "head")
    return jax.shard_map(
        functools.partial(body, mesh.shape["ctx"], mesh.shape["head"]),
        mesh=mesh,
        in_specs=in_specs,
        out_specs=out_specs,
        check_vma=False,
    )
```

```python
import functools

import jax
import jax.numpy as jnp
from jax import lax
from jax.experimental import pallas as pl
from jax.experimental.pallas import tpu as pltpu
from jax.sharding import PartitionSpec as P

HEAD_DIM = 128
BLOCK = 128
LOOK = 7
TOPK = 4
BASE = 16
EXTRA = 16
TERMS = 3
BF16 = jnp.bfloat16
F32 = jnp.float32
VMEM = pl.BlockSpec(memory_space=pltpu.VMEM)
SMEM = pl.BlockSpec(memory_space=pltpu.SMEM)
ANY = pl.BlockSpec(memory_space=pl.ANY)


def dot(left, right, left_dim, right_dim):
    return lax.dot_general(
        left, right, (((left_dim,), (right_dim,)), ((), ())), preferred_element_type=F32
    )


def nn(left, right):
    return dot(left, right, 1, 0)


def nt(left, right):
    return dot(left, right, 1, 1)


def tn(left, right):
    return dot(left, right, 0, 0)


def split(value):
    high = value.astype(BF16)
    return high, (value - high.astype(F32)).astype(BF16)


def triple(product, left, right):
    rows = left[0].shape[0]
    first = product(jnp.concatenate(left, 0), right[0])
    return first[:rows] + (first[rows:] + product(left[0], right[1]))


def square_iotas():
    rows = lax.broadcasted_iota(jnp.int32, (BLOCK, BLOCK), 0)
    columns = lax.broadcasted_iota(jnp.int32, (BLOCK, BLOCK), 1)
    return rows, columns


def fetched(sources, targets, sems):
    copies = []
    for index, (source, target) in enumerate(zip(sources, targets)):
        copies.append(pltpu.make_async_copy(source, target, sems.at[index]))
        copies[-1].start()
    return copies


def pack_kernel(axes, cores, d_ref, k_ref, rates_hbm, selected_hbm, values_ref, weight_ref,
                *refs):
    tokens = d_ref.shape[0]
    heads = d_ref.shape[1] // HEAD_DIM
    blocks = tokens // BLOCK
    (parts_ref, rates_ref, selected_ref, cut_ref, piece_ref, sems, few_sems, out_sems, cut_sems,
     cut_out_sems, piece_sems) = refs[-11:]
    out_ref, cut_outs, piece_outs = refs[0], refs[1:1 + heads], refs[1 + heads:-11]
    planes = len(piece_outs) + 1
    width = weight_ref.shape[1] // planes
    device = lax.axis_index(axes[0])
    place = lax.rem(device, heads)
    plane = lax.axis_index(axes[1]) // cores
    first_block = device * blocks
    few_copies = fetched([rates_hbm, selected_hbm], [rates_ref, selected_ref], few_sems)
    sources = (d_ref, k_ref)
    copies = []
    for head in range(heads):
        columns = pl.ds(head * HEAD_DIM, HEAD_DIM)
        for kind, source in enumerate(sources):
            copies.append(
                pltpu.make_async_copy(
                    source.at[:, columns],
                    parts_ref.at[head, pl.ds(kind * tokens, tokens)],
                    sems.at[head, kind],
                )
            )
            copies[-1].start()
    cuts = [
        pl.multiple_of(lax.bitwise_xor(place, turn) * HEAD_DIM, HEAD_DIM) for turn in range(heads)
    ]
    cut_copies = fetched(
        [values_ref.at[:, pl.ds(cut, HEAD_DIM)] for cut in cuts],
        [cut_ref.at[turn] for turn in range(heads)],
        cut_sems,
    )
    piece_copies = []
    for offset in range(1, planes):
        start = pl.multiple_of(lax.rem(plane + planes - offset, planes) * width, width)
        piece_copies += fetched(
            [weight_ref.at[:, pl.ds(start, width)]],
            [piece_ref.at[offset - 1]],
            piece_sems.at[0, pl.ds(offset - 1, 1)],
        )
    for copy in few_copies:
        copy.wait()
    row = lax.broadcasted_iota(jnp.int32, (EXTRA, HEAD_DIM), 0)
    lane = lax.broadcasted_iota(jnp.int32, (EXTRA, HEAD_DIM), 1)
    away = jnp.zeros((EXTRA, HEAD_DIM), jnp.int32)
    for block in range(blocks):
        for entry in range(TOPK):
            distance = first_block + block - selected_ref[block, entry]
            away = jnp.where((row == TERMS * blocks + block) & (lane == entry), distance, away)
    away = away.astype(F32)
    terms = []
    rest = rates_ref[...]
    for _ in range(TERMS):
        terms.append(rest.astype(BF16).astype(F32))
        rest = rest - terms[-1]
    out_copies = []
    for head in range(heads):
        extra = away
        for block in range(blocks):
            for index, term in enumerate(terms):
                piece = term[head:head + 1, block * BLOCK:(block + 1) * BLOCK]
                extra = jnp.where(row == TERMS * block + index, piece, extra)
        parts_ref[head, len(sources) * tokens:] = extra.astype(BF16)
        for copy in copies[len(sources) * head:len(sources) * (head + 1)]:
            copy.wait()
        out_copies.append(
            pltpu.make_async_copy(parts_ref.at[head], out_ref.at[head], out_sems.at[head])
        )
        out_copies[-1].start()
    for turn in range(heads):
        cut_copies[turn].wait()
        out_copies += fetched(
            [cut_ref.at[turn]], [cut_outs[turn]], cut_out_sems.at[pl.ds(turn, 1)]
        )
    for index, copy in enumerate(piece_copies):
        copy.wait()
        out_copies += fetched(
            [piece_ref.at[index]], [piece_outs[index]], piece_sems.at[1, pl.ds(index, 1)]
        )
    for copy in out_copies:
        copy.wait()


def cut_kernel(axes, heads, queries_ref, values_ref, *refs):
    sems = refs[-1]
    first, outs = refs[-2 * heads], refs[1 - 2 * heads:-1]
    query_outs, value_outs = list(outs[:heads - 1]), list(outs[heads - 1:])
    query_outs.insert(1, first.at[0])
    value_outs.insert(1, first.at[1])
    place = lax.rem(lax.axis_index(axes[0]), heads)
    cuts = [
        pl.multiple_of(lax.bitwise_xor(place, turn) * HEAD_DIM, HEAD_DIM) for turn in range(heads)
    ]
    copies = []
    for kind, (source, targets) in enumerate(
        ((queries_ref, query_outs), (values_ref, value_outs))
    ):
        copies += fetched(
            [source.at[:, pl.ds(cut, HEAD_DIM)] for cut in cuts], targets, sems.at[kind]
        )
    for copy in copies:
        copy.wait()


def rows_of(ref, blocks, unit, kind):
    start = (kind * blocks + unit % blocks) * BLOCK
    return ref[unit // blocks, start:start + BLOCK]


def base_inverse(strict):
    count = BLOCK // BASE
    moved = [
        pltpu.roll(strict[b * BASE:(b + 1) * BASE], (BLOCK - b * BASE) % BLOCK, 1)
        if b else strict[:BASE]
        for b in range(count)
    ]
    lanes = lax.broadcasted_iota(jnp.int32, (BASE // 2, BLOCK), 1)
    rows = lax.broadcasted_iota(jnp.int32, (BASE // 2, BLOCK), 0)
    half = BASE // 2
    parts = []
    for b in range(count):
        upper = (lanes == rows + b * BASE).astype(F32)
        lower = (lanes == rows + b * BASE + half).astype(F32)
        for step in range(BASE - 1):
            if step < half:
                source = upper[step:step + 1]
                if step < half - 1:
                    upper = upper - moved[b][:half, step:step + 1] * source
            else:
                source = lower[step - half:step - half + 1]
            lower = lower - moved[b][half:, step:step + 1] * source
        parts += [upper, lower]
    return jnp.concatenate(parts, 0)


def halves(value, size):
    parts = value.reshape(BLOCK // (2 * size), 2, size, BLOCK)
    return parts[:, 0].reshape(BLOCK // 2, BLOCK), parts[:, 1].reshape(BLOCK // 2, BLOCK)


def joined(first, second, size):
    shape = (BLOCK // (2 * size), 1, size, BLOCK)
    return jnp.concatenate([first.reshape(shape), second.reshape(shape)], 1).reshape(BLOCK, BLOCK)


def interleaved(steps, lag):
    running = list(steps)
    tick = 0
    while any(step is not None for step in running):
        for index, step in enumerate(running):
            if step is not None and tick >= index * lag:
                try:
                    next(step)
                except StopIteration:
                    running[index] = None
        tick += 1


def keys_kernel(blocks, part_ref, end_ref, tail_ref, far_ref, even_ref, pair_ref, mixed_ref,
                away_ref, *group_refs):
    units = part_ref.shape[0] * blocks
    rows, columns = square_iotas()
    diagonal = rows == columns
    identity = diagonal.astype(F32)
    row = lax.broadcasted_iota(jnp.int32, (BLOCK // 2, BLOCK), 0)
    column = lax.broadcasted_iota(jnp.int32, (BLOCK // 2, BLOCK), 1)
    ends, maps = [None] * units, [None] * units

    def terms(unit):
        direction = rows_of(part_ref, blocks, unit, 0)
        key = rows_of(part_ref, blocks, unit, 1)
        extra = part_ref[unit // blocks, 2 * blocks * BLOCK:].astype(F32)
        first = TERMS * (unit % blocks)
        rate = extra[first:first + 1] + extra[first + 1:first + 2] + extra[first + 2:first + 3]
        listed = TERMS * blocks + unit % blocks
        away_ref[unit:unit + 1] = extra[listed:listed + 1].astype(jnp.int32)
        gram = nt(direction, direction)
        key_proj = jnp.where(rows > columns, nt(direction, key), 0.0).astype(BF16)
        squares = jnp.sum(jnp.where(diagonal, gram, 0.0), 0, keepdims=True)
        scale = lax.rsqrt(squares + 1e-06)
        scaled_rate = rate * scale
        scale_column = jnp.sum(jnp.where(diagonal, scale, 0.0), 1, keepdims=True)
        rate_column = jnp.sum(jnp.where(diagonal, scaled_rate, 0.0), 1, keepdims=True)
        strict = jnp.where(rows > columns, rate_column * gram * scale, 0.0)
        yield
        inverse = base_inverse(strict)
        yield
        size = BASE
        while size < BLOCK:
            inside = (row // size == column // (2 * size)) & (lax.rem(column, 2 * size) < size)
            corner = jnp.where(inside, halves(strict, size)[1], 0.0)
            below = triple(nn, split(corner), split(inverse))
            yield
            first_half, second = halves(inverse, size)
            padded = joined(jnp.zeros_like(below), below, size)
            second = second - triple(nn, split(second), split(padded))
            inverse = joined(first_half, second, size)
            size *= 2
            yield
        mixing = split(scale_column * inverse * scaled_rate)
        mixed = nn(mixing[0], jnp.concatenate([direction, key_proj], 1))
        mixed_map = split(mixed[:, :BLOCK] + nn(mixing[1], direction))
        mixed = jnp.concatenate([mixed_map[0], mixed[:, BLOCK:].astype(BF16)], 1)
        mixed_ref[unit] = mixed
        yield
        behind = tn(jnp.concatenate([mixed, mixed_map[1]], 1), direction)
        ends[unit] = key.astype(F32) - behind[BLOCK:2 * BLOCK]
        maps[unit] = split(identity - (behind[:BLOCK] + behind[2 * BLOCK:]))
        end_ref[unit] = ends[unit].astype(BF16)

    onward = []

    def pair_terms(pair):
        even, odd = 2 * pair, 2 * pair + 1
        running = [terms(even), terms(odd)]
        while running:
            for step in list(running):
                if next(step, running) is running:
                    running.remove(step)
            yield
        even_ref[pair, 0] = maps[even][0]
        even_ref[pair, 1] = maps[even][1]
        left = jnp.concatenate([ends[even].astype(BF16), *maps[even]], 0)
        both = nn(left, maps[odd][0])
        tail_even, tail_odd = both[:BLOCK].astype(BF16), ends[odd].astype(BF16)
        tail_ref[even] = tail_even
        tail_ref[odd] = tail_odd
        low = both[2 * BLOCK:] + nn(maps[even][0], maps[odd][1])
        pair_map = split(both[BLOCK:2 * BLOCK] + low)
        pair_ref[pair, 0] = pair_map[0]
        pair_ref[pair, 1] = pair_map[1]
        yield
        if onward:
            far = nn(jnp.concatenate([tail_even, tail_odd], 0), onward[-1][0]).astype(BF16)
            far_ref[even] = far[:BLOCK]
            far_ref[odd] = far[BLOCK:]
            if pair or group_refs:
                pair_map = split(triple(nn, pair_map, onward[-1]))
        else:
            far_ref[even] = tail_even
            far_ref[odd] = tail_odd
        onward.append(pair_map)

    interleaved([pair_terms(pair) for pair in reversed(range(units // 2))], 1)
    for group_ref in group_refs:
        group_ref[0] = onward[-1][0]
        group_ref[1] = onward[-1][1]


def queries_kernel(axes, blocks, part_ref, mixed_ref, even_ref, pair_ref, *refs):
    heads = part_ref.shape[0]
    units = heads * blocks
    inner_ref, moving_ref, query_ref = refs[heads:]
    place = lax.rem(lax.axis_index(axes[0]), heads)
    for turn in range(heads):
        query_ref[lax.bitwise_xor(place, turn)] = refs[1][0] if turn == 1 else refs[turn][...]
    rows, columns = square_iotas()

    def pair_steps(pair):
        projs, fronts = [], []
        for unit in (2 * pair, 2 * pair + 1):
            direction = rows_of(part_ref, blocks, unit, 0)
            query = rows_of(query_ref, blocks, unit, 0)
            projs.append(split(jnp.where(rows >= columns, nt(query, direction), 0.0)))
        yield
        for unit in (2 * pair, 2 * pair + 1):
            key = rows_of(part_ref, blocks, unit, 1)
            query = rows_of(query_ref, blocks, unit, 0)
            ahead = nn(jnp.concatenate(projs[unit % 2], 0), mixed_ref[unit])
            ahead = ahead[:BLOCK] + ahead[BLOCK:]
            inner_ref[unit] = nt(query, key) - ahead[:, HEAD_DIM:]
            fronts.append(split(query.astype(F32) - ahead[:, :HEAD_DIM]))
            moving_ref[unit, 0] = fronts[-1][0]
        yield
        fronts[1] = split(triple(nt, fronts[1], (even_ref[pair, 0], even_ref[pair, 1])))
        current = tuple(
            jnp.concatenate([fronts[0][part], fronts[1][part]], 0) for part in range(2)
        )
        for step in range(1, pair + 2):
            if step > 1:
                passed = pair - step + 1
                current = split(
                    triple(nt, current, (pair_ref[passed, 0], pair_ref[passed, 1]))
                )
            moving_ref[2 * pair, step] = current[0][:BLOCK]
            moving_ref[2 * pair + 1, step] = current[0][BLOCK:]
            yield

    interleaved([pair_steps(pair) for pair in reversed(range(units // 2))], 1)


def listed_block(away_ref, unit, entry):
    away = away_ref[unit, entry]
    new = away > 0
    for other in range(1, entry):
        new = new & (away_ref[unit, other] != away)
    return unit - away, new


def earlier(source, ahead, units):
    return jnp.clip(source + ahead * units, 0, units - 1), source < (1 - ahead) * units


def weights_kernel(before, away_ref, moving_ref, inner_ref, end_ref, tail_ref, *refs):
    far_keys, group_maps, weights_ref = refs[:before], refs[before:-1], refs[-1]
    units = inner_ref.shape[0]
    rows, columns = square_iotas()
    scale = HEAD_DIM ** (-0.5)

    def steps(unit):
        pair = unit // 2
        fronts = [moving_ref[unit, pair + 1]]
        for group_map in group_maps:
            passed = nt(fronts[-1], group_map[0]) + nt(fronts[-1], group_map[1])
            fronts.append(passed.astype(BF16))
        score_list = [jnp.where(rows >= columns, inner_ref[unit] * scale, -1e30)]
        for entry in range(1, TOPK):
            source, new = listed_block(away_ref, unit, entry)
            inside = jnp.maximum(source, 0)
            step = jnp.maximum(pair - inside // 2, 0)
            query = moving_ref[unit, step]
            key = jnp.where(step == 0, end_ref[inside], tail_ref[inside])
            for ahead in range(1, before + 1):
                place, here = earlier(source, ahead, units)
                query = jnp.where(here, fronts[ahead - 1], query)
                key = jnp.where(here, far_keys[ahead - 1][place], key)
            score_list.append(jnp.where(new, nt(query, key) * scale, -1e30))
        yield
        scores = jnp.concatenate(score_list, 1)
        expos = jnp.exp(scores - jnp.max(scores, 1, keepdims=True))
        weights_ref[unit] = (expos * (1.0 / jnp.sum(expos, 1, keepdims=True))).astype(BF16)

    interleaved([steps(unit) for unit in range(units)], 1)


def blend_kernel(axes, before, blocks, away_ref, weights_ref, *refs):
    units = weights_ref.shape[0]
    heads = units // blocks
    count = (len(refs) - 3 - heads * (1 + before)) // 2
    arrived = refs[:heads * (1 + before)]
    out_ref, (values_ref, sems) = refs[-3 - count], refs[-2:]
    copies = fetched(
        refs[heads * (1 + before):heads * (1 + before) + count], refs[-2 - count:-2], sems
    )
    place = lax.rem(lax.axis_index(axes[0]), heads)
    for kind in range(1 + before):
        for turn in range(heads):
            start = pl.multiple_of(lax.bitwise_xor(place, turn) * blocks * BLOCK, BLOCK)
            source = arrived[kind * heads + turn]
            values_ref[kind, pl.ds(start, blocks * BLOCK)] = (
                source[...] if kind or turn != 1 else source[1]
            )

    def value_of(kind, block):
        return values_ref[kind, pl.ds(pl.multiple_of(block * BLOCK, BLOCK), BLOCK)]

    for unit in range(units):
        value_list = [value_of(0, unit)]
        for entry in range(1, TOPK):
            source, _ = listed_block(away_ref, unit, entry)
            kind, block = 0, jnp.maximum(source, 0)
            for ahead in range(1, before + 1):
                other, here = earlier(source, ahead, units)
                kind = jnp.where(here, ahead, kind)
                block = jnp.where(here, other, block)
            value_list.append(value_of(kind, block))
        blended = nn(weights_ref[unit], jnp.concatenate(value_list, 0)).astype(BF16)
        for plane in range(out_ref.shape[1]):
            out_ref[unit // blocks, plane, unit % blocks] = blended
    for copy in copies:
        copy.wait()


def project_kernel(axes, other, cores, attended_ref, own_ref, *refs):
    other_refs, out_ref = refs[:-1], refs[-1]
    heads, planes, blocks = attended_ref.shape[:3]
    index = lax.axis_index(axes[1])
    core, plane = lax.rem(index + other, cores), index // cores
    width = out_ref.shape[1]
    total = None
    for offset in range(planes):
        source = lax.rem(plane + offset, planes)
        attended = jnp.concatenate(
            [
                jnp.concatenate(
                    [attended_ref[head, source, block] for head in range(heads)], 1
                )
                for block in range(blocks)
            ],
            0,
        )
        if offset:
            start = pl.multiple_of(core * width, width)
            weight = other_refs[offset - 1][:, pl.ds(start, width)]
        else:
            start = pl.multiple_of((plane * cores + core) * width, width)
            weight = own_ref[:, pl.ds(start, width)]
        product = nn(attended, weight)
        total = product if total is None else total + product
    out_ref[...] = total.astype(out_ref.dtype)


def call(kernel, outs, specs, flops, scratch=(), places=None, space=32):
    if places is None:
        places = [VMEM] * len(outs) if isinstance(outs, list) else VMEM
    return pl.pallas_call(
        kernel,
        out_shape=outs,
        in_specs=specs,
        out_specs=places,
        scratch_shapes=list(scratch),
        compiler_params=pltpu.CompilerParams(vmem_limit_bytes=space * 2 ** 20),
        cost_estimate=pl.CostEstimate(flops=flops, bytes_accessed=2 ** 21, transcendentals=0),
    )


def body(ctx_size, head_size, queries, keys, values, directions, rates, selected, out_weight):
    tokens = queries.shape[0]
    blocks = tokens // BLOCK
    heads = queries.shape[1] // HEAD_DIM
    units = heads * blocks
    pairs = units // 2
    groups = ctx_size // heads
    before = min(groups - 1, -(-LOOK // heads))
    cores = 2
    planes = head_size // cores
    axes = ("ctx", "head")
    members = [[group * heads + place for place in range(heads)] for group in range(groups)]
    partners = [(g, g + 1 - 2 * (g % cores)) for g in range(head_size)]
    cubes = 2 * BLOCK ** 3
    tile = (BLOCK, HEAD_DIM)

    def exchange(value):
        return lax.all_to_all(value, "ctx", 0, 0, axis_index_groups=members, tiled=True)

    def onward(value, by):
        shift = by * heads
        return lax.ppermute(value, "ctx", [(i, i + shift) for i in range(ctx_size - shift)])

    def crossed(value, turn):
        pairs = [(i, i - i % heads + (i % heads ^ turn)) for i in range(ctx_size)]
        return lax.ppermute(value, "ctx", pairs) if turn else value

    def straight(value, turn, by):
        shift = by * heads
        pairs = [(i, i - i % heads + (i % heads ^ turn) + shift) for i in range(ctx_size - shift)]
        return lax.ppermute(value, "ctx", pairs)

    def array(shape, kind=BF16):
        return jax.ShapeDtypeStruct(shape, kind)

    part_shape = (heads, 2 * tokens + EXTRA, HEAD_DIM)
    width = out_weight.shape[1] // planes
    piece_shape = (out_weight.shape[0], width)
    packed, *rest = call(
        functools.partial(pack_kernel, axes, cores),
        [array(part_shape)]
        + [array((tokens, HEAD_DIM))] * heads
        + [array(piece_shape)] * (planes - 1),
        [ANY] * 6,
        cubes,
        [
            pltpu.VMEM(part_shape, BF16),
            pltpu.VMEM(rates.shape, F32),
            pltpu.SMEM(selected.shape, jnp.int32),
            pltpu.VMEM((heads, tokens, HEAD_DIM), BF16),
            pltpu.VMEM((max(planes - 1, 1), *piece_shape), BF16),
            pltpu.SemaphoreType.DMA((heads, 2)),
            pltpu.SemaphoreType.DMA((2,)),
            pltpu.SemaphoreType.DMA((heads,)),
            pltpu.SemaphoreType.DMA((heads,)),
            pltpu.SemaphoreType.DMA((heads,)),
            pltpu.SemaphoreType.DMA((2, planes)),
        ],
        [ANY] * (heads + planes),
        56,
    )(directions, keys, rates, selected, values, out_weight)
    value_cuts, pieces = rest[:heads], rest[heads:]
    value_parts = [
        straight(value_cuts[turn], turn, by) for by in range(1, before + 1) for turn in range(heads)
    ]
    weight_parts = []
    for offset in range(1, planes):
        turned = [(g, (g + head_size - cores * offset) % head_size) for g in range(head_size)]
        weight_parts.append(lax.ppermute(pieces[offset - 1], "head", turned))
    parts = exchange(packed)

    end, tail, far, even, pair_map, mixed, away, *group_maps = call(
        functools.partial(keys_kernel, blocks),
        [
            array((units, *tile)),
            array((units, *tile)),
            array((units, *tile)),
            array((pairs, 2, *tile)),
            array((pairs, 2, *tile)),
            array((units, BLOCK, 2 * BLOCK)),
            array((units, HEAD_DIM), jnp.int32),
        ]
        + [array((2, *tile))] * (before > 1),
        [VMEM],
        400 * cubes,
    )(parts)
    far_parts = [onward(far, by) for by in range(1, before + 1)]
    map_parts = [onward(group_maps[0], by) for by in range(1, before)]
    first, *cut = call(
        functools.partial(cut_kernel, axes, heads),
        [array((2, tokens, HEAD_DIM))] + [array((tokens, HEAD_DIM))] * (2 * heads - 2),
        [ANY] * (len(value_parts) + 3),
        2000 * cubes,
        [pltpu.SemaphoreType.DMA((2, heads))],
    )(queries, values, *value_parts, away)
    first = crossed(first, 1)
    turns = [0, *range(2, heads)]
    query_parts = [crossed(part, turn) for part, turn in zip(cut[:heads - 1], turns)]
    own_parts = [crossed(part, turn) for part, turn in zip(cut[heads - 1:], turns)]
    query_parts.insert(1, first)
    own_parts.insert(1, first)
    inner, moving = call(
        functools.partial(queries_kernel, axes, blocks),
        [array((units, BLOCK, BLOCK), F32), array((units, pairs + 1, *tile))],
        [VMEM] * (4 + heads),
        0,
        [pltpu.VMEM((heads, tokens, HEAD_DIM), BF16)],
    )(parts, mixed, even, pair_map, *query_parts)
    weights = call(
        functools.partial(weights_kernel, before),
        array((units, BLOCK, TOPK * BLOCK)),
        [SMEM] + [VMEM] * (4 + before + len(map_parts)),
        0,
    )(away, moving, inner, end, tail, *far_parts, *map_parts)
    attended, *weight_parts = call(
        functools.partial(blend_kernel, axes, before, blocks),
        [array((heads, planes, blocks, *tile))] + [array(part.shape) for part in weight_parts],
        [SMEM] + [VMEM] * (1 + heads * (1 + before)) + [ANY] * len(weight_parts),
        0,
        [
            pltpu.VMEM((1 + before, units * BLOCK, HEAD_DIM), BF16),
            pltpu.SemaphoreType.DMA((planes,)),
        ],
    )(away, weights, *own_parts, *value_parts, *weight_parts)

    returns = [
        [
            (group * heads + place) * head_size + p * cores + core
            for place in range(heads)
            for p in range(planes)
        ]
        for group in range(groups)
        for core in range(cores)
    ]
    local = lax.all_to_all(
        attended.reshape(heads * planes, blocks, *tile),
        axes, 0, 0, axis_index_groups=returns, tiled=True,
    ).reshape(heads, planes, blocks, *tile)

    def projected(other, kind):
        return call(
            functools.partial(project_kernel, axes, other, cores),
            array((tokens, width // cores), kind),
            [VMEM] * (1 + planes),
            128 * cubes,
        )(local, out_weight, *weight_parts)

    arrived = lax.ppermute(projected(1, BF16), "head", partners)
    return (projected(0, F32) + arrived.astype(F32)).astype(BF16)


def solution(mesh):
    in_specs = (
        P("ctx", "head"),
        P("ctx", "head"),
        P("ctx", "head"),
        P("ctx", "head"),
        P("head", "ctx"),
        P("ctx", None),
        P("head", None),
    )
    out_specs = P("ctx", "head")
    return jax.shard_map(
        functools.partial(body, mesh.shape["ctx"], mesh.shape["head"]),
        mesh=mesh,
        in_specs=in_specs,
        out_specs=out_specs,
        check_vma=False,
    )
```

```python
import functools

import jax
import jax.numpy as jnp
from jax import lax
from jax.experimental import pallas as pl
from jax.experimental.pallas import tpu as pltpu
from jax.sharding import PartitionSpec as P

HEAD_DIM = 128
BLOCK = 128
LOOK = 7
TOPK = 4
BASE = 16
EXTRA = 16
TERMS = 3
BF16 = jnp.bfloat16
F32 = jnp.float32
VMEM = pl.BlockSpec(memory_space=pltpu.VMEM)
SMEM = pl.BlockSpec(memory_space=pltpu.SMEM)
ANY = pl.BlockSpec(memory_space=pl.ANY)


def dot(left, right, left_dim, right_dim):
    return lax.dot_general(
        left, right, (((left_dim,), (right_dim,)), ((), ())), preferred_element_type=F32
    )


def nn(left, right):
    return dot(left, right, 1, 0)


def nt(left, right):
    return dot(left, right, 1, 1)


def tn(left, right):
    return dot(left, right, 0, 0)


def split(value):
    high = value.astype(BF16)
    return high, (value - high.astype(F32)).astype(BF16)


def triple(product, left, right):
    rows = left[0].shape[0]
    first = product(jnp.concatenate(left, 0), right[0])
    return first[:rows] + (first[rows:] + product(left[0], right[1]))


def square_iotas():
    rows = lax.broadcasted_iota(jnp.int32, (BLOCK, BLOCK), 0)
    columns = lax.broadcasted_iota(jnp.int32, (BLOCK, BLOCK), 1)
    return rows, columns


def fetched(sources, targets, sems):
    copies = []
    for index, (source, target) in enumerate(zip(sources, targets)):
        copies.append(pltpu.make_async_copy(source, target, sems.at[index]))
        copies[-1].start()
    return copies


def pack_kernel(axes, cores, d_ref, k_ref, rates_hbm, selected_hbm, values_ref, weight_ref,
                *refs):
    tokens = d_ref.shape[0]
    heads = d_ref.shape[1] // HEAD_DIM
    blocks = tokens // BLOCK
    (parts_ref, rates_ref, selected_ref, cut_ref, piece_ref, sems, few_sems, out_sems, cut_sems,
     cut_out_sems, piece_sems) = refs[-11:]
    out_ref, cut_outs, piece_outs = refs[0], refs[1:1 + heads], refs[1 + heads:-11]
    planes = len(piece_outs) + 1
    width = weight_ref.shape[1] // planes
    device = lax.axis_index(axes[0])
    place = lax.rem(device, heads)
    plane = lax.axis_index(axes[1]) // cores
    first_block = device * blocks
    few_copies = fetched([rates_hbm, selected_hbm], [rates_ref, selected_ref], few_sems)
    sources = (d_ref, k_ref)
    copies = []
    for head in range(heads):
        columns = pl.ds(head * HEAD_DIM, HEAD_DIM)
        for kind, source in enumerate(sources):
            copies.append(
                pltpu.make_async_copy(
                    source.at[:, columns],
                    parts_ref.at[head, pl.ds(kind * tokens, tokens)],
                    sems.at[head, kind],
                )
            )
            copies[-1].start()
    cuts = [
        pl.multiple_of(lax.bitwise_xor(place, turn) * HEAD_DIM, HEAD_DIM) for turn in range(heads)
    ]
    cut_copies = fetched(
        [values_ref.at[:, pl.ds(cut, HEAD_DIM)] for cut in cuts],
        [cut_ref.at[turn] for turn in range(heads)],
        cut_sems,
    )
    piece_copies = []
    for offset in range(1, planes):
        start = pl.multiple_of(lax.rem(plane + planes - offset, planes) * width, width)
        piece_copies += fetched(
            [weight_ref.at[:, pl.ds(start, width)]],
            [piece_ref.at[offset - 1]],
            piece_sems.at[0, pl.ds(offset - 1, 1)],
        )
    for copy in few_copies:
        copy.wait()
    row = lax.broadcasted_iota(jnp.int32, (EXTRA, HEAD_DIM), 0)
    lane = lax.broadcasted_iota(jnp.int32, (EXTRA, HEAD_DIM), 1)
    away = jnp.zeros((EXTRA, HEAD_DIM), jnp.int32)
    for block in range(blocks):
        for entry in range(TOPK):
            distance = first_block + block - selected_ref[block, entry]
            away = jnp.where((row == TERMS * blocks + block) & (lane == entry), distance, away)
    away = away.astype(F32)
    terms = []
    rest = rates_ref[...]
    for _ in range(TERMS):
        terms.append(rest.astype(BF16).astype(F32))
        rest = rest - terms[-1]
    out_copies = []
    for head in range(heads):
        extra = away
        for block in range(blocks):
            for index, term in enumerate(terms):
                piece = term[head:head + 1, block * BLOCK:(block + 1) * BLOCK]
                extra = jnp.where(row == TERMS * block + index, piece, extra)
        parts_ref[head, len(sources) * tokens:] = extra.astype(BF16)
        for copy in copies[len(sources) * head:len(sources) * (head + 1)]:
            copy.wait()
        out_copies.append(
            pltpu.make_async_copy(parts_ref.at[head], out_ref.at[head], out_sems.at[head])
        )
        out_copies[-1].start()
    for turn in range(heads):
        cut_copies[turn].wait()
        out_copies += fetched(
            [cut_ref.at[turn]], [cut_outs[turn]], cut_out_sems.at[pl.ds(turn, 1)]
        )
    for index, copy in enumerate(piece_copies):
        copy.wait()
        out_copies += fetched(
            [piece_ref.at[index]], [piece_outs[index]], piece_sems.at[1, pl.ds(index, 1)]
        )
    for copy in out_copies:
        copy.wait()


def cut_kernel(axes, heads, queries_ref, values_ref, *refs):
    sems = refs[-1]
    first, outs = refs[-2 * heads], refs[1 - 2 * heads:-1]
    query_outs, value_outs = list(outs[:heads - 1]), list(outs[heads - 1:])
    query_outs.insert(1, first.at[0])
    value_outs.insert(1, first.at[1])
    place = lax.rem(lax.axis_index(axes[0]), heads)
    cuts = [
        pl.multiple_of(lax.bitwise_xor(place, turn) * HEAD_DIM, HEAD_DIM) for turn in range(heads)
    ]
    copies = []
    for kind, (source, targets) in enumerate(
        ((queries_ref, query_outs), (values_ref, value_outs))
    ):
        copies += fetched(
            [source.at[:, pl.ds(cut, HEAD_DIM)] for cut in cuts], targets, sems.at[kind]
        )
    for copy in copies:
        copy.wait()


def rows_of(ref, blocks, unit, kind):
    start = (kind * blocks + unit % blocks) * BLOCK
    return ref[unit // blocks, start:start + BLOCK]


def base_inverse(strict, first, last):
    count = BLOCK // BASE
    moved = [
        pltpu.roll(strict[b * BASE:(b + 1) * BASE], (BLOCK - b * BASE) % BLOCK, 1)
        if b else strict[:BASE]
        for b in range(count)
    ]
    lanes = lax.broadcasted_iota(jnp.int32, (BASE // 2, BLOCK), 1)
    rows = lax.broadcasted_iota(jnp.int32, (BASE // 2, BLOCK), 0)
    half = BASE // 2
    parts = []
    for b in range(first, last):
        upper = (lanes == rows + b * BASE).astype(F32)
        lower = (lanes == rows + b * BASE + half).astype(F32)
        for step in range(BASE - 1):
            if step < half:
                source = upper[step:step + 1]
                if step < half - 1:
                    upper = upper - moved[b][:half, step:step + 1] * source
            else:
                source = lower[step - half:step - half + 1]
            lower = lower - moved[b][half:, step:step + 1] * source
        parts += [upper, lower]
    return jnp.concatenate(parts, 0)


def halves(value, size):
    parts = value.reshape(BLOCK // (2 * size), 2, size, BLOCK)
    return parts[:, 0].reshape(BLOCK // 2, BLOCK), parts[:, 1].reshape(BLOCK // 2, BLOCK)


def joined(first, second, size):
    shape = (BLOCK // (2 * size), 1, size, BLOCK)
    return jnp.concatenate([first.reshape(shape), second.reshape(shape)], 1).reshape(BLOCK, BLOCK)


def interleaved(steps, lag):
    running = list(steps)
    tick = 0
    while any(step is not None for step in running):
        for index, step in enumerate(running):
            if step is not None and tick >= index * lag:
                try:
                    next(step)
                except StopIteration:
                    running[index] = None
        tick += 1


def keys_kernel(blocks, part_ref, end_ref, tail_ref, far_ref, even_ref, pair_ref, mixed_ref,
                away_ref, *group_refs):
    units = part_ref.shape[0] * blocks
    rows, columns = square_iotas()
    diagonal = rows == columns
    identity = diagonal.astype(F32)
    row = lax.broadcasted_iota(jnp.int32, (BLOCK // 2, BLOCK), 0)
    column = lax.broadcasted_iota(jnp.int32, (BLOCK // 2, BLOCK), 1)
    ends, maps = [None] * units, [None] * units

    def terms(unit):
        direction = rows_of(part_ref, blocks, unit, 0)
        key = rows_of(part_ref, blocks, unit, 1)
        extra = part_ref[unit // blocks, 2 * blocks * BLOCK:].astype(F32)
        first = TERMS * (unit % blocks)
        rate = extra[first:first + 1] + extra[first + 1:first + 2] + extra[first + 2:first + 3]
        listed = TERMS * blocks + unit % blocks
        away_ref[unit:unit + 1] = extra[listed:listed + 1].astype(jnp.int32)
        gram = nt(direction, direction)
        key_proj = jnp.where(rows > columns, nt(direction, key), 0.0).astype(BF16)
        squares = jnp.sum(jnp.where(diagonal, gram, 0.0), 0, keepdims=True)
        scale = lax.rsqrt(squares + 1e-06)
        scaled_rate = rate * scale
        scale_column = jnp.sum(jnp.where(diagonal, scale, 0.0), 1, keepdims=True)
        rate_column = jnp.sum(jnp.where(diagonal, scaled_rate, 0.0), 1, keepdims=True)
        strict = jnp.where(rows > columns, rate_column * gram * scale, 0.0)
        yield
        middle = BLOCK // BASE // 2
        upper_part = base_inverse(strict, 0, middle)
        yield
        inverse = jnp.concatenate([upper_part, base_inverse(strict, middle, 2 * middle)], 0)
        yield
        size = BASE
        while size < BLOCK:
            inside = (row // size == column // (2 * size)) & (lax.rem(column, 2 * size) < size)
            corner = jnp.where(inside, halves(strict, size)[1], 0.0)
            below = triple(nn, split(corner), split(inverse))
            yield
            first_half, second = halves(inverse, size)
            padded = joined(jnp.zeros_like(below), below, size)
            second = second - triple(nn, split(second), split(padded))
            inverse = joined(first_half, second, size)
            size *= 2
            yield
        mixing = split(scale_column * inverse * scaled_rate)
        mixed = nn(mixing[0], jnp.concatenate([direction, key_proj], 1))
        mixed_map = split(mixed[:, :BLOCK] + nn(mixing[1], direction))
        mixed = jnp.concatenate([mixed_map[0], mixed[:, BLOCK:].astype(BF16)], 1)
        mixed_ref[unit] = mixed
        yield
        behind = tn(jnp.concatenate([mixed, mixed_map[1]], 1), direction)
        ends[unit] = key.astype(F32) - behind[BLOCK:2 * BLOCK]
        maps[unit] = split(identity - (behind[:BLOCK] + behind[2 * BLOCK:]))
        end_ref[unit] = ends[unit].astype(BF16)

    onward = []

    def pair_terms(pair):
        even, odd = 2 * pair, 2 * pair + 1
        running = [terms(even), terms(odd)]
        while running:
            for step in list(running):
                if next(step, running) is running:
                    running.remove(step)
            yield
        even_ref[pair, 0] = maps[even][0]
        even_ref[pair, 1] = maps[even][1]
        left = jnp.concatenate([ends[even].astype(BF16), *maps[even]], 0)
        both = nn(left, maps[odd][0])
        tail_even, tail_odd = both[:BLOCK].astype(BF16), ends[odd].astype(BF16)
        tail_ref[even] = tail_even
        tail_ref[odd] = tail_odd
        low = both[2 * BLOCK:] + nn(maps[even][0], maps[odd][1])
        pair_map = split(both[BLOCK:2 * BLOCK] + low)
        pair_ref[pair, 0] = pair_map[0]
        pair_ref[pair, 1] = pair_map[1]
        yield
        if onward:
            far = nn(jnp.concatenate([tail_even, tail_odd], 0), onward[-1][0]).astype(BF16)
            far_ref[even] = far[:BLOCK]
            far_ref[odd] = far[BLOCK:]
            if pair or group_refs:
                pair_map = split(triple(nn, pair_map, onward[-1]))
        else:
            far_ref[even] = tail_even
            far_ref[odd] = tail_odd
        onward.append(pair_map)

    interleaved([pair_terms(pair) for pair in reversed(range(units // 2))], 1)
    for group_ref in group_refs:
        group_ref[0] = onward[-1][0]
        group_ref[1] = onward[-1][1]


def queries_kernel(axes, blocks, part_ref, mixed_ref, even_ref, pair_ref, *refs):
    heads = part_ref.shape[0]
    units = heads * blocks
    inner_ref, moving_ref, query_ref = refs[heads:]
    place = lax.rem(lax.axis_index(axes[0]), heads)
    for turn in range(heads):
        query_ref[lax.bitwise_xor(place, turn)] = refs[1][0] if turn == 1 else refs[turn][...]
    rows, columns = square_iotas()

    def pair_steps(pair):
        projs, fronts = [], []
        for unit in (2 * pair, 2 * pair + 1):
            direction = rows_of(part_ref, blocks, unit, 0)
            query = rows_of(query_ref, blocks, unit, 0)
            projs.append(split(jnp.where(rows >= columns, nt(query, direction), 0.0)))
        yield
        for unit in (2 * pair, 2 * pair + 1):
            key = rows_of(part_ref, blocks, unit, 1)
            query = rows_of(query_ref, blocks, unit, 0)
            ahead = nn(jnp.concatenate(projs[unit % 2], 0), mixed_ref[unit])
            ahead = ahead[:BLOCK] + ahead[BLOCK:]
            inner_ref[unit] = nt(query, key) - ahead[:, HEAD_DIM:]
            fronts.append(split(query.astype(F32) - ahead[:, :HEAD_DIM]))
            moving_ref[unit, 0] = fronts[-1][0]
        yield
        fronts[1] = split(triple(nt, fronts[1], (even_ref[pair, 0], even_ref[pair, 1])))
        current = tuple(
            jnp.concatenate([fronts[0][part], fronts[1][part]], 0) for part in range(2)
        )
        for step in range(1, pair + 2):
            if step > 1:
                passed = pair - step + 1
                current = split(
                    triple(nt, current, (pair_ref[passed, 0], pair_ref[passed, 1]))
                )
            moving_ref[2 * pair, step] = current[0][:BLOCK]
            moving_ref[2 * pair + 1, step] = current[0][BLOCK:]
            yield

    interleaved([pair_steps(pair) for pair in reversed(range(units // 2))], 1)


def listed_block(away_ref, unit, entry):
    away = away_ref[unit, entry]
    new = away > 0
    for other in range(1, entry):
        new = new & (away_ref[unit, other] != away)
    return unit - away, new


def earlier(source, ahead, units):
    return jnp.clip(source + ahead * units, 0, units - 1), source < (1 - ahead) * units


def weights_kernel(before, away_ref, moving_ref, inner_ref, end_ref, tail_ref, *refs):
    far_keys, group_maps, weights_ref = refs[:before], refs[before:-1], refs[-1]
    units = inner_ref.shape[0]
    rows, columns = square_iotas()
    scale = HEAD_DIM ** (-0.5)

    def steps(unit):
        pair = unit // 2
        fronts = [moving_ref[unit, pair + 1]]
        for group_map in group_maps:
            passed = nt(fronts[-1], group_map[0]) + nt(fronts[-1], group_map[1])
            fronts.append(passed.astype(BF16))
        score_list = [jnp.where(rows >= columns, inner_ref[unit] * scale, -1e30)]
        for entry in range(1, TOPK):
            source, new = listed_block(away_ref, unit, entry)
            inside = jnp.maximum(source, 0)
            step = jnp.maximum(pair - inside // 2, 0)
            query = moving_ref[unit, step]
            key = jnp.where(step == 0, end_ref[inside], tail_ref[inside])
            for ahead in range(1, before + 1):
                place, here = earlier(source, ahead, units)
                query = jnp.where(here, fronts[ahead - 1], query)
                key = jnp.where(here, far_keys[ahead - 1][place], key)
            score_list.append(jnp.where(new, nt(query, key) * scale, -1e30))
        yield
        scores = jnp.concatenate(score_list, 1)
        expos = jnp.exp(scores - jnp.max(scores, 1, keepdims=True))
        yield
        weights_ref[unit] = (expos * (1.0 / jnp.sum(expos, 1, keepdims=True))).astype(BF16)

    interleaved([steps(unit) for unit in range(units)], 1)


def blend_kernel(axes, before, blocks, away_ref, weights_ref, *refs):
    units = weights_ref.shape[0]
    heads = units // blocks
    count = (len(refs) - 3 - heads * (1 + before)) // 2
    arrived = refs[:heads * (1 + before)]
    out_ref, (values_ref, sems) = refs[-3 - count], refs[-2:]
    copies = fetched(
        refs[heads * (1 + before):heads * (1 + before) + count], refs[-2 - count:-2], sems
    )
    place = lax.rem(lax.axis_index(axes[0]), heads)
    for kind in range(1 + before):
        for turn in range(heads):
            start = pl.multiple_of(lax.bitwise_xor(place, turn) * blocks * BLOCK, BLOCK)
            source = arrived[kind * heads + turn]
            values_ref[kind, pl.ds(start, blocks * BLOCK)] = (
                source[...] if kind or turn != 1 else source[1]
            )

    def value_of(kind, block):
        return values_ref[kind, pl.ds(pl.multiple_of(block * BLOCK, BLOCK), BLOCK)]

    for unit in range(units):
        value_list = [value_of(0, unit)]
        for entry in range(1, TOPK):
            source, _ = listed_block(away_ref, unit, entry)
            kind, block = 0, jnp.maximum(source, 0)
            for ahead in range(1, before + 1):
                other, here = earlier(source, ahead, units)
                kind = jnp.where(here, ahead, kind)
                block = jnp.where(here, other, block)
            value_list.append(value_of(kind, block))
        blended = nn(weights_ref[unit], jnp.concatenate(value_list, 0)).astype(BF16)
        for plane in range(out_ref.shape[1]):
            out_ref[unit // blocks, plane, unit % blocks] = blended
    for copy in copies:
        copy.wait()


def project_kernel(axes, other, cores, attended_ref, own_ref, *refs):
    other_refs, out_ref = refs[:-1], refs[-1]
    heads, planes, blocks = attended_ref.shape[:3]
    index = lax.axis_index(axes[1])
    core, plane = lax.rem(index + other, cores), index // cores
    width = out_ref.shape[1]
    total = None
    for offset in range(planes):
        source = lax.rem(plane + offset, planes)
        attended = jnp.concatenate(
            [
                jnp.concatenate(
                    [attended_ref[head, source, block] for head in range(heads)], 1
                )
                for block in range(blocks)
            ],
            0,
        )
        if offset:
            start = pl.multiple_of(core * width, width)
            weight = other_refs[offset - 1][:, pl.ds(start, width)]
        else:
            start = pl.multiple_of((plane * cores + core) * width, width)
            weight = own_ref[:, pl.ds(start, width)]
        product = nn(attended, weight)
        total = product if total is None else total + product
    out_ref[...] = total.astype(out_ref.dtype)


def call(kernel, outs, specs, flops, scratch=(), places=None, space=32):
    if places is None:
        places = [VMEM] * len(outs) if isinstance(outs, list) else VMEM
    return pl.pallas_call(
        kernel,
        out_shape=outs,
        in_specs=specs,
        out_specs=places,
        scratch_shapes=list(scratch),
        compiler_params=pltpu.CompilerParams(vmem_limit_bytes=space * 2 ** 20),
        cost_estimate=pl.CostEstimate(flops=flops, bytes_accessed=2 ** 21, transcendentals=0),
    )


def body(ctx_size, head_size, queries, keys, values, directions, rates, selected, out_weight):
    tokens = queries.shape[0]
    blocks = tokens // BLOCK
    heads = queries.shape[1] // HEAD_DIM
    units = heads * blocks
    pairs = units // 2
    groups = ctx_size // heads
    before = min(groups - 1, -(-LOOK // heads))
    cores = 2
    planes = head_size // cores
    axes = ("ctx", "head")
    members = [[group * heads + place for place in range(heads)] for group in range(groups)]
    partners = [(g, g + 1 - 2 * (g % cores)) for g in range(head_size)]
    cubes = 2 * BLOCK ** 3
    tile = (BLOCK, HEAD_DIM)

    def exchange(value):
        return lax.all_to_all(value, "ctx", 0, 0, axis_index_groups=members, tiled=True)

    def onward(value, by):
        shift = by * heads
        return lax.ppermute(value, "ctx", [(i, i + shift) for i in range(ctx_size - shift)])

    def crossed(value, turn):
        pairs = [(i, i - i % heads + (i % heads ^ turn)) for i in range(ctx_size)]
        return lax.ppermute(value, "ctx", pairs) if turn else value

    def straight(value, turn, by):
        shift = by * heads
        pairs = [(i, i - i % heads + (i % heads ^ turn) + shift) for i in range(ctx_size - shift)]
        return lax.ppermute(value, "ctx", pairs)

    def array(shape, kind=BF16):
        return jax.ShapeDtypeStruct(shape, kind)

    part_shape = (heads, 2 * tokens + EXTRA, HEAD_DIM)
    width = out_weight.shape[1] // planes
    piece_shape = (out_weight.shape[0], width)
    packed, *rest = call(
        functools.partial(pack_kernel, axes, cores),
        [array(part_shape)]
        + [array((tokens, HEAD_DIM))] * heads
        + [array(piece_shape)] * (planes - 1),
        [ANY] * 6,
        cubes,
        [
            pltpu.VMEM(part_shape, BF16),
            pltpu.VMEM(rates.shape, F32),
            pltpu.SMEM(selected.shape, jnp.int32),
            pltpu.VMEM((heads, tokens, HEAD_DIM), BF16),
            pltpu.VMEM((max(planes - 1, 1), *piece_shape), BF16),
            pltpu.SemaphoreType.DMA((heads, 2)),
            pltpu.SemaphoreType.DMA((2,)),
            pltpu.SemaphoreType.DMA((heads,)),
            pltpu.SemaphoreType.DMA((heads,)),
            pltpu.SemaphoreType.DMA((heads,)),
            pltpu.SemaphoreType.DMA((2, planes)),
        ],
        [ANY] * (heads + planes),
        56,
    )(directions, keys, rates, selected, values, out_weight)
    value_cuts, pieces = rest[:heads], rest[heads:]
    value_parts = [
        straight(value_cuts[turn], turn, by) for by in range(1, before + 1) for turn in range(heads)
    ]
    weight_parts = []
    for offset in range(1, planes):
        turned = [(g, (g + head_size - cores * offset) % head_size) for g in range(head_size)]
        weight_parts.append(lax.ppermute(pieces[offset - 1], "head", turned))
    parts = exchange(packed)

    end, tail, far, even, pair_map, mixed, away, *group_maps = call(
        functools.partial(keys_kernel, blocks),
        [
            array((units, *tile)),
            array((units, *tile)),
            array((units, *tile)),
            array((pairs, 2, *tile)),
            array((pairs, 2, *tile)),
            array((units, BLOCK, 2 * BLOCK)),
            array((units, HEAD_DIM), jnp.int32),
        ]
        + [array((2, *tile))] * (before > 1),
        [VMEM],
        400 * cubes,
    )(parts)
    far_parts = [onward(far, by) for by in range(1, before + 1)]
    map_parts = [onward(group_maps[0], by) for by in range(1, before)]
    first, *cut = call(
        functools.partial(cut_kernel, axes, heads),
        [array((2, tokens, HEAD_DIM))] + [array((tokens, HEAD_DIM))] * (2 * heads - 2),
        [ANY] * (len(value_parts) + 3),
        2000 * cubes,
        [pltpu.SemaphoreType.DMA((2, heads))],
    )(queries, values, *value_parts, away)
    first = crossed(first, 1)
    turns = [0, *range(2, heads)]
    query_parts = [crossed(part, turn) for part, turn in zip(cut[:heads - 1], turns)]
    own_parts = [crossed(part, turn) for part, turn in zip(cut[heads - 1:], turns)]
    query_parts.insert(1, first)
    own_parts.insert(1, first)
    inner, moving = call(
        functools.partial(queries_kernel, axes, blocks),
        [array((units, BLOCK, BLOCK), F32), array((units, pairs + 1, *tile))],
        [VMEM] * (4 + heads),
        0,
        [pltpu.VMEM((heads, tokens, HEAD_DIM), BF16)],
    )(parts, mixed, even, pair_map, *query_parts)
    weights = call(
        functools.partial(weights_kernel, before),
        array((units, BLOCK, TOPK * BLOCK)),
        [SMEM] + [VMEM] * (4 + before + len(map_parts)),
        0,
    )(away, moving, inner, end, tail, *far_parts, *map_parts)
    attended, *weight_parts = call(
        functools.partial(blend_kernel, axes, before, blocks),
        [array((heads, planes, blocks, *tile))] + [array(part.shape) for part in weight_parts],
        [SMEM] + [VMEM] * (1 + heads * (1 + before)) + [ANY] * len(weight_parts),
        0,
        [
            pltpu.VMEM((1 + before, units * BLOCK, HEAD_DIM), BF16),
            pltpu.SemaphoreType.DMA((planes,)),
        ],
    )(away, weights, *own_parts, *value_parts, *weight_parts)

    returns = [
        [
            (group * heads + place) * head_size + p * cores + core
            for place in range(heads)
            for p in range(planes)
        ]
        for group in range(groups)
        for core in range(cores)
    ]
    local = lax.all_to_all(
        attended.reshape(heads * planes, blocks, *tile),
        axes, 0, 0, axis_index_groups=returns, tiled=True,
    ).reshape(heads, planes, blocks, *tile)

    def projected(other, kind):
        return call(
            functools.partial(project_kernel, axes, other, cores),
            array((tokens, width // cores), kind),
            [VMEM] * (1 + planes),
            128 * cubes,
        )(local, out_weight, *weight_parts)

    arrived = lax.ppermute(projected(1, BF16), "head", partners)
    return (projected(0, F32) + arrived.astype(F32)).astype(BF16)


def solution(mesh):
    in_specs = (
        P("ctx", "head"),
        P("ctx", "head"),
        P("ctx", "head"),
        P("ctx", "head"),
        P("head", "ctx"),
        P("ctx", None),
        P("head", None),
    )
    out_specs = P("ctx", "head")
    return jax.shard_map(
        functools.partial(body, mesh.shape["ctx"], mesh.shape["head"]),
        mesh=mesh,
        in_specs=in_specs,
        out_specs=out_specs,
        check_vma=False,
    )
```

```python
import functools

import jax
import jax.numpy as jnp
from jax import lax
from jax.experimental import pallas as pl
from jax.experimental.pallas import tpu as pltpu
from jax.sharding import PartitionSpec as P

HEAD_DIM = 128
BLOCK = 128
LOOK = 7
TOPK = 4
BASE = 16
EXTRA = 16
TERMS = 3
BF16 = jnp.bfloat16
F32 = jnp.float32
VMEM = pl.BlockSpec(memory_space=pltpu.VMEM)
SMEM = pl.BlockSpec(memory_space=pltpu.SMEM)
ANY = pl.BlockSpec(memory_space=pl.ANY)


def dot(left, right, left_dim, right_dim):
    return lax.dot_general(
        left, right, (((left_dim,), (right_dim,)), ((), ())), preferred_element_type=F32
    )


def nn(left, right):
    return dot(left, right, 1, 0)


def nt(left, right):
    return dot(left, right, 1, 1)


def tn(left, right):
    return dot(left, right, 0, 0)


def split(value):
    high = value.astype(BF16)
    return high, (value - high.astype(F32)).astype(BF16)


def triple(product, left, right):
    rows = left[0].shape[0]
    first = product(jnp.concatenate(left, 0), right[0])
    return first[:rows] + (first[rows:] + product(left[0], right[1]))


def square_iotas():
    rows = lax.broadcasted_iota(jnp.int32, (BLOCK, BLOCK), 0)
    columns = lax.broadcasted_iota(jnp.int32, (BLOCK, BLOCK), 1)
    return rows, columns


def fetched(sources, targets, sems):
    copies = []
    for index, (source, target) in enumerate(zip(sources, targets)):
        copies.append(pltpu.make_async_copy(source, target, sems.at[index]))
        copies[-1].start()
    return copies


def pack_kernel(axes, cores, d_ref, k_ref, rates_hbm, selected_hbm, values_ref, weight_ref,
                *refs):
    tokens = d_ref.shape[0]
    heads = d_ref.shape[1] // HEAD_DIM
    blocks = tokens // BLOCK
    (parts_ref, rates_ref, selected_ref, cut_ref, piece_ref, sems, few_sems, out_sems, cut_sems,
     cut_out_sems, piece_sems) = refs[-11:]
    out_ref, cut_outs, piece_outs = refs[0], refs[1:1 + heads], refs[1 + heads:-11]
    planes = len(piece_outs) + 1
    width = weight_ref.shape[1] // planes
    device = lax.axis_index(axes[0])
    place = lax.rem(device, heads)
    plane = lax.axis_index(axes[1]) // cores
    first_block = device * blocks
    few_copies = fetched([rates_hbm, selected_hbm], [rates_ref, selected_ref], few_sems)
    sources = (d_ref, k_ref)
    copies = []
    for head in range(heads):
        columns = pl.ds(head * HEAD_DIM, HEAD_DIM)
        for kind, source in enumerate(sources):
            copies.append(
                pltpu.make_async_copy(
                    source.at[:, columns],
                    parts_ref.at[head, pl.ds(kind * tokens, tokens)],
                    sems.at[head, kind],
                )
            )
            copies[-1].start()
    cuts = [
        pl.multiple_of(lax.bitwise_xor(place, turn) * HEAD_DIM, HEAD_DIM) for turn in range(heads)
    ]
    cut_copies = fetched(
        [values_ref.at[:, pl.ds(cut, HEAD_DIM)] for cut in cuts],
        [cut_ref.at[turn] for turn in range(heads)],
        cut_sems,
    )
    piece_copies = []
    for offset in range(1, planes):
        start = pl.multiple_of(lax.rem(plane + planes - offset, planes) * width, width)
        piece_copies += fetched(
            [weight_ref.at[:, pl.ds(start, width)]],
            [piece_ref.at[offset - 1]],
            piece_sems.at[0, pl.ds(offset - 1, 1)],
        )
    for copy in few_copies:
        copy.wait()
    row = lax.broadcasted_iota(jnp.int32, (EXTRA, HEAD_DIM), 0)
    lane = lax.broadcasted_iota(jnp.int32, (EXTRA, HEAD_DIM), 1)
    away = jnp.zeros((EXTRA, HEAD_DIM), jnp.int32)
    for block in range(blocks):
        for entry in range(TOPK):
            distance = first_block + block - selected_ref[block, entry]
            away = jnp.where((row == TERMS * blocks + block) & (lane == entry), distance, away)
    away = away.astype(F32)
    terms = []
    rest = rates_ref[...]
    for _ in range(TERMS):
        terms.append(rest.astype(BF16).astype(F32))
        rest = rest - terms[-1]
    out_copies = []
    for head in range(heads):
        extra = away
        for block in range(blocks):
            for index, term in enumerate(terms):
                piece = term[head:head + 1, block * BLOCK:(block + 1) * BLOCK]
                extra = jnp.where(row == TERMS * block + index, piece, extra)
        parts_ref[head, len(sources) * tokens:] = extra.astype(BF16)
        for copy in copies[len(sources) * head:len(sources) * (head + 1)]:
            copy.wait()
        out_copies.append(
            pltpu.make_async_copy(parts_ref.at[head], out_ref.at[head], out_sems.at[head])
        )
        out_copies[-1].start()
    for turn in range(heads):
        cut_copies[turn].wait()
        out_copies += fetched(
            [cut_ref.at[turn]], [cut_outs[turn]], cut_out_sems.at[pl.ds(turn, 1)]
        )
    for index, copy in enumerate(piece_copies):
        copy.wait()
        out_copies += fetched(
            [piece_ref.at[index]], [piece_outs[index]], piece_sems.at[1, pl.ds(index, 1)]
        )
    for copy in out_copies:
        copy.wait()


def cut_kernel(axes, heads, queries_ref, values_ref, *refs):
    sems = refs[-1]
    first, outs = refs[-2 * heads], refs[1 - 2 * heads:-1]
    query_outs, value_outs = list(outs[:heads - 1]), list(outs[heads - 1:])
    query_outs.insert(1, first.at[0])
    value_outs.insert(1, first.at[1])
    place = lax.rem(lax.axis_index(axes[0]), heads)
    cuts = [
        pl.multiple_of(lax.bitwise_xor(place, turn) * HEAD_DIM, HEAD_DIM) for turn in range(heads)
    ]
    copies = []
    for kind, (source, targets) in enumerate(
        ((queries_ref, query_outs), (values_ref, value_outs))
    ):
        copies += fetched(
            [source.at[:, pl.ds(cut, HEAD_DIM)] for cut in cuts], targets, sems.at[kind]
        )
    for copy in copies:
        copy.wait()


def rows_of(ref, blocks, unit, kind):
    start = (kind * blocks + unit % blocks) * BLOCK
    return ref[unit // blocks, start:start + BLOCK]


def base_inverse(strict):
    count = BLOCK // BASE
    moved = [
        pltpu.roll(strict[b * BASE:(b + 1) * BASE], (BLOCK - b * BASE) % BLOCK, 1)
        if b else strict[:BASE]
        for b in range(count)
    ]
    lanes = lax.broadcasted_iota(jnp.int32, (BASE // 2, BLOCK), 1)
    rows = lax.broadcasted_iota(jnp.int32, (BASE // 2, BLOCK), 0)
    half = BASE // 2
    parts = []
    for b in range(count):
        upper = (lanes == rows + b * BASE).astype(F32)
        lower = (lanes == rows + b * BASE + half).astype(F32)
        for step in range(BASE - 1):
            if step < half:
                source = upper[step:step + 1]
                if step < half - 1:
                    upper = upper - moved[b][:half, step:step + 1] * source
            else:
                source = lower[step - half:step - half + 1]
            lower = lower - moved[b][half:, step:step + 1] * source
        parts += [upper, lower]
    return jnp.concatenate(parts, 0)


def halves(value, size):
    parts = value.reshape(BLOCK // (2 * size), 2, size, BLOCK)
    return parts[:, 0].reshape(BLOCK // 2, BLOCK), parts[:, 1].reshape(BLOCK // 2, BLOCK)


def joined(first, second, size):
    shape = (BLOCK // (2 * size), 1, size, BLOCK)
    return jnp.concatenate([first.reshape(shape), second.reshape(shape)], 1).reshape(BLOCK, BLOCK)


def interleaved(steps, lag):
    running = list(steps)
    tick = 0
    while any(step is not None for step in running):
        for index, step in enumerate(running):
            if step is not None and tick >= index * lag:
                try:
                    next(step)
                except StopIteration:
                    running[index] = None
        tick += 1


def keys_kernel(blocks, part_ref, end_ref, tail_ref, far_ref, even_ref, pair_ref, mixed_ref,
                away_ref, *group_refs):
    units = part_ref.shape[0] * blocks
    rows, columns = square_iotas()
    diagonal = rows == columns
    identity = diagonal.astype(F32)
    row = lax.broadcasted_iota(jnp.int32, (BLOCK // 2, BLOCK), 0)
    column = lax.broadcasted_iota(jnp.int32, (BLOCK // 2, BLOCK), 1)
    ends, maps = [None] * units, [None] * units

    def terms(unit):
        direction = rows_of(part_ref, blocks, unit, 0)
        key = rows_of(part_ref, blocks, unit, 1)
        extra = part_ref[unit // blocks, 2 * blocks * BLOCK:].astype(F32)
        first = TERMS * (unit % blocks)
        rate = extra[first:first + 1] + extra[first + 1:first + 2] + extra[first + 2:first + 3]
        listed = TERMS * blocks + unit % blocks
        away_ref[unit:unit + 1] = extra[listed:listed + 1].astype(jnp.int32)
        gram = nt(direction, direction)
        key_proj = jnp.where(rows > columns, nt(direction, key), 0.0).astype(BF16)
        squares = jnp.sum(jnp.where(diagonal, gram, 0.0), 0, keepdims=True)
        scale = lax.rsqrt(squares + 1e-06)
        scaled_rate = rate * scale
        scale_column = jnp.sum(jnp.where(diagonal, scale, 0.0), 1, keepdims=True)
        rate_column = jnp.sum(jnp.where(diagonal, scaled_rate, 0.0), 1, keepdims=True)
        strict = jnp.where(rows > columns, rate_column * gram * scale, 0.0)
        yield
        inverse = base_inverse(strict)
        yield
        size = BASE
        while size < BLOCK:
            inside = (row // size == column // (2 * size)) & (lax.rem(column, 2 * size) < size)
            corner = jnp.where(inside, halves(strict, size)[1], 0.0)
            below = triple(nn, split(corner), split(inverse))
            yield
            first_half, second = halves(inverse, size)
            padded = joined(jnp.zeros_like(below), below, size)
            second = second - triple(nn, split(second), split(padded))
            inverse = joined(first_half, second, size)
            size *= 2
            yield
        mixing = split(scale_column * inverse * scaled_rate)
        mixed = nn(mixing[0], jnp.concatenate([direction, key_proj], 1))
        mixed_map = split(mixed[:, :BLOCK] + nn(mixing[1], direction))
        mixed = jnp.concatenate([mixed_map[0], mixed[:, BLOCK:].astype(BF16)], 1)
        mixed_ref[unit] = mixed
        yield
        behind = tn(jnp.concatenate([mixed, mixed_map[1]], 1), direction)
        ends[unit] = key.astype(F32) - behind[BLOCK:2 * BLOCK]
        maps[unit] = split(identity - (behind[:BLOCK] + behind[2 * BLOCK:]))
        end_ref[unit] = ends[unit].astype(BF16)

    onward = []

    def pair_terms(pair):
        even, odd = 2 * pair, 2 * pair + 1
        running = [terms(even), terms(odd)]
        while running:
            for step in list(running):
                if next(step, running) is running:
                    running.remove(step)
            yield
        even_ref[pair, 0] = maps[even][0]
        even_ref[pair, 1] = maps[even][1]
        left = jnp.concatenate([ends[even].astype(BF16), *maps[even]], 0)
        both = nn(left, maps[odd][0])
        tail_even, tail_odd = both[:BLOCK].astype(BF16), ends[odd].astype(BF16)
        tail_ref[even] = tail_even
        tail_ref[odd] = tail_odd
        low = both[2 * BLOCK:] + nn(maps[even][0], maps[odd][1])
        pair_map = split(both[BLOCK:2 * BLOCK] + low)
        pair_ref[pair, 0] = pair_map[0]
        pair_ref[pair, 1] = pair_map[1]
        yield
        if onward:
            far = nn(jnp.concatenate([tail_even, tail_odd], 0), onward[-1][0]).astype(BF16)
            far_ref[even] = far[:BLOCK]
            far_ref[odd] = far[BLOCK:]
            if pair or group_refs:
                pair_map = split(triple(nn, pair_map, onward[-1]))
        else:
            far_ref[even] = tail_even
            far_ref[odd] = tail_odd
        onward.append(pair_map)

    interleaved([pair_terms(pair) for pair in reversed(range(units // 2))], 1)
    for group_ref in group_refs:
        group_ref[0] = onward[-1][0]
        group_ref[1] = onward[-1][1]


def queries_kernel(axes, blocks, part_ref, mixed_ref, even_ref, pair_ref, *refs):
    heads = part_ref.shape[0]
    units = heads * blocks
    inner_ref, moving_ref, query_ref = refs[heads:]
    place = lax.rem(lax.axis_index(axes[0]), heads)
    for turn in range(heads):
        query_ref[lax.bitwise_xor(place, turn)] = refs[1][0] if turn == 1 else refs[turn][...]
    rows, columns = square_iotas()

    def pair_steps(pair):
        projs, fronts = [], []
        for unit in (2 * pair, 2 * pair + 1):
            direction = rows_of(part_ref, blocks, unit, 0)
            query = rows_of(query_ref, blocks, unit, 0)
            projs.append(split(jnp.where(rows >= columns, nt(query, direction), 0.0)))
        yield
        for unit in (2 * pair, 2 * pair + 1):
            key = rows_of(part_ref, blocks, unit, 1)
            query = rows_of(query_ref, blocks, unit, 0)
            ahead = nn(jnp.concatenate(projs[unit % 2], 0), mixed_ref[unit])
            ahead = ahead[:BLOCK] + ahead[BLOCK:]
            inner_ref[unit] = nt(query, key) - ahead[:, HEAD_DIM:]
            fronts.append(split(query.astype(F32) - ahead[:, :HEAD_DIM]))
            moving_ref[unit, 0] = fronts[-1][0]
        yield
        fronts[1] = split(triple(nt, fronts[1], (even_ref[pair, 0], even_ref[pair, 1])))
        current = tuple(
            jnp.concatenate([fronts[0][part], fronts[1][part]], 0) for part in range(2)
        )
        for step in range(1, pair + 2):
            if step > 1:
                passed = pair - step + 1
                current = split(
                    triple(nt, current, (pair_ref[passed, 0], pair_ref[passed, 1]))
                )
            moving_ref[2 * pair, step] = current[0][:BLOCK]
            moving_ref[2 * pair + 1, step] = current[0][BLOCK:]
            yield

    interleaved([pair_steps(pair) for pair in reversed(range(units // 2))], 1)


def listed_block(away_ref, unit, entry):
    away = away_ref[unit, entry]
    new = away > 0
    for other in range(1, entry):
        new = new & (away_ref[unit, other] != away)
    return unit - away, new


def earlier(source, ahead, units):
    return jnp.clip(source + ahead * units, 0, units - 1), source < (1 - ahead) * units


def weights_kernel(before, away_ref, moving_ref, inner_ref, end_ref, tail_ref, *refs):
    far_keys, group_maps, weights_ref = refs[:before], refs[before:-1], refs[-1]
    units = inner_ref.shape[0]
    rows, columns = square_iotas()
    scale = HEAD_DIM ** (-0.5)

    def steps(unit):
        pair = unit // 2
        fronts = [moving_ref[unit, pair + 1]]
        for group_map in group_maps:
            passed = nt(fronts[-1], group_map[0]) + nt(fronts[-1], group_map[1])
            fronts.append(passed.astype(BF16))
        score_list = [jnp.where(rows >= columns, inner_ref[unit] * scale, -1e30)]
        for entry in range(1, TOPK):
            source, new = listed_block(away_ref, unit, entry)
            inside = jnp.maximum(source, 0)
            step = jnp.maximum(pair - inside // 2, 0)
            query = moving_ref[unit, step]
            key = jnp.where(step == 0, end_ref[inside], tail_ref[inside])
            for ahead in range(1, before + 1):
                place, here = earlier(source, ahead, units)
                query = jnp.where(here, fronts[ahead - 1], query)
                key = jnp.where(here, far_keys[ahead - 1][place], key)
            score_list.append(jnp.where(new, nt(query, key) * scale, -1e30))
        yield
        scores = jnp.concatenate(score_list, 1)
        expos = jnp.exp(scores - jnp.max(scores, 1, keepdims=True))
        weights_ref[unit] = (expos * (1.0 / jnp.sum(expos, 1, keepdims=True))).astype(BF16)

    interleaved([steps(unit) for unit in range(units)], 1)


def blend_kernel(axes, before, blocks, away_ref, weights_ref, *refs):
    units = weights_ref.shape[0]
    heads = units // blocks
    arrived = refs[:heads * (1 + before)]
    out_ref, values_ref = refs[-2:]
    place = lax.rem(lax.axis_index(axes[0]), heads)
    for kind in range(1 + before):
        for turn in range(heads):
            start = pl.multiple_of(lax.bitwise_xor(place, turn) * blocks * BLOCK, BLOCK)
            source = arrived[kind * heads + turn]
            values_ref[kind, pl.ds(start, blocks * BLOCK)] = (
                source[...] if kind or turn != 1 else source[1]
            )

    def value_of(kind, block):
        return values_ref[kind, pl.ds(pl.multiple_of(block * BLOCK, BLOCK), BLOCK)]

    for unit in range(units):
        value_list = [value_of(0, unit)]
        for entry in range(1, TOPK):
            source, _ = listed_block(away_ref, unit, entry)
            kind, block = 0, jnp.maximum(source, 0)
            for ahead in range(1, before + 1):
                other, here = earlier(source, ahead, units)
                kind = jnp.where(here, ahead, kind)
                block = jnp.where(here, other, block)
            value_list.append(value_of(kind, block))
        blended = nn(weights_ref[unit], jnp.concatenate(value_list, 0)).astype(BF16)
        for plane in range(out_ref.shape[1]):
            out_ref[unit // blocks, plane, unit % blocks] = blended


def project_kernel(axes, other, cores, attended_ref, own_ref, *refs):
    other_refs, out_ref = refs[:-1], refs[-1]
    heads, planes, blocks = attended_ref.shape[:3]
    index = lax.axis_index(axes[1])
    core, plane = lax.rem(index + other, cores), index // cores
    width = out_ref.shape[1]
    total = None
    for offset in range(planes):
        source = lax.rem(plane + offset, planes)
        attended = jnp.concatenate(
            [
                jnp.concatenate(
                    [attended_ref[head, source, block] for head in range(heads)], 1
                )
                for block in range(blocks)
            ],
            0,
        )
        if offset:
            start = pl.multiple_of(core * width, width)
            weight = other_refs[offset - 1][:, pl.ds(start, width)]
        else:
            start = pl.multiple_of((plane * cores + core) * width, width)
            weight = own_ref[:, pl.ds(start, width)]
        product = nn(attended, weight)
        total = product if total is None else total + product
    out_ref[...] = total.astype(out_ref.dtype)


def call(kernel, outs, specs, flops, scratch=(), places=None, space=32):
    if places is None:
        places = [VMEM] * len(outs) if isinstance(outs, list) else VMEM
    return pl.pallas_call(
        kernel,
        out_shape=outs,
        in_specs=specs,
        out_specs=places,
        scratch_shapes=list(scratch),
        compiler_params=pltpu.CompilerParams(vmem_limit_bytes=space * 2 ** 20),
        cost_estimate=pl.CostEstimate(flops=flops, bytes_accessed=2 ** 21, transcendentals=0),
    )


def body(ctx_size, head_size, queries, keys, values, directions, rates, selected, out_weight):
    tokens = queries.shape[0]
    blocks = tokens // BLOCK
    heads = queries.shape[1] // HEAD_DIM
    units = heads * blocks
    pairs = units // 2
    groups = ctx_size // heads
    before = min(groups - 1, -(-LOOK // heads))
    cores = 2
    planes = head_size // cores
    axes = ("ctx", "head")
    members = [[group * heads + place for place in range(heads)] for group in range(groups)]
    partners = [(g, g + 1 - 2 * (g % cores)) for g in range(head_size)]
    cubes = 2 * BLOCK ** 3
    tile = (BLOCK, HEAD_DIM)

    def exchange(value):
        return lax.all_to_all(value, "ctx", 0, 0, axis_index_groups=members, tiled=True)

    def onward(value, by):
        shift = by * heads
        return lax.ppermute(value, "ctx", [(i, i + shift) for i in range(ctx_size - shift)])

    def crossed(value, turn):
        pairs = [(i, i - i % heads + (i % heads ^ turn)) for i in range(ctx_size)]
        return lax.ppermute(value, "ctx", pairs) if turn else value

    def straight(value, turn, by):
        shift = by * heads
        pairs = [(i, i - i % heads + (i % heads ^ turn) + shift) for i in range(ctx_size - shift)]
        return lax.ppermute(value, "ctx", pairs)

    def array(shape, kind=BF16):
        return jax.ShapeDtypeStruct(shape, kind)

    part_shape = (heads, 2 * tokens + EXTRA, HEAD_DIM)
    width = out_weight.shape[1] // planes
    piece_shape = (out_weight.shape[0], width)
    packed, *rest = call(
        functools.partial(pack_kernel, axes, cores),
        [array(part_shape)]
        + [array((tokens, HEAD_DIM))] * heads
        + [array(piece_shape)] * (planes - 1),
        [ANY] * 6,
        cubes,
        [
            pltpu.VMEM(part_shape, BF16),
            pltpu.VMEM(rates.shape, F32),
            pltpu.SMEM(selected.shape, jnp.int32),
            pltpu.VMEM((heads, tokens, HEAD_DIM), BF16),
            pltpu.VMEM((max(planes - 1, 1), *piece_shape), BF16),
            pltpu.SemaphoreType.DMA((heads, 2)),
            pltpu.SemaphoreType.DMA((2,)),
            pltpu.SemaphoreType.DMA((heads,)),
            pltpu.SemaphoreType.DMA((heads,)),
            pltpu.SemaphoreType.DMA((heads,)),
            pltpu.SemaphoreType.DMA((2, planes)),
        ],
        [ANY] * (heads + planes),
        56,
    )(directions, keys, rates, selected, values, out_weight)
    value_cuts, pieces = rest[:heads], rest[heads:]
    value_parts = [
        straight(value_cuts[turn], turn, by) for by in range(1, before + 1) for turn in range(heads)
    ]
    weight_parts = []
    for offset in range(1, planes):
        turned = [(g, (g + head_size - cores * offset) % head_size) for g in range(head_size)]
        weight_parts.append(lax.ppermute(pieces[offset - 1], "head", turned))
    parts = exchange(packed)

    end, tail, far, even, pair_map, mixed, away, *group_maps = call(
        functools.partial(keys_kernel, blocks),
        [
            array((units, *tile)),
            array((units, *tile)),
            array((units, *tile)),
            array((pairs, 2, *tile)),
            array((pairs, 2, *tile)),
            array((units, BLOCK, 2 * BLOCK)),
            array((units, HEAD_DIM), jnp.int32),
        ]
        + [array((2, *tile))] * (before > 1),
        [VMEM],
        400 * cubes,
    )(parts)
    far_parts = [onward(far, by) for by in range(1, before + 1)]
    map_parts = [onward(group_maps[0], by) for by in range(1, before)]
    first, *cut = call(
        functools.partial(cut_kernel, axes, heads),
        [array((2, tokens, HEAD_DIM))] + [array((tokens, HEAD_DIM))] * (2 * heads - 2),
        [ANY] * (len(value_parts) + 3),
        2000 * cubes,
        [pltpu.SemaphoreType.DMA((2, heads))],
    )(queries, values, *value_parts, away)
    first = crossed(first, 1)
    turns = [0, *range(2, heads)]
    query_parts = [crossed(part, turn) for part, turn in zip(cut[:heads - 1], turns)]
    own_parts = [crossed(part, turn) for part, turn in zip(cut[heads - 1:], turns)]
    query_parts.insert(1, first)
    own_parts.insert(1, first)
    inner, moving = call(
        functools.partial(queries_kernel, axes, blocks),
        [array((units, BLOCK, BLOCK), F32), array((units, pairs + 1, *tile))],
        [VMEM] * (4 + heads),
        0,
        [pltpu.VMEM((heads, tokens, HEAD_DIM), BF16)],
    )(parts, mixed, even, pair_map, *query_parts)
    weights = call(
        functools.partial(weights_kernel, before),
        array((units, BLOCK, TOPK * BLOCK)),
        [SMEM] + [VMEM] * (4 + before + len(map_parts)),
        0,
    )(away, moving, inner, end, tail, *far_parts, *map_parts)
    attended = call(
        functools.partial(blend_kernel, axes, before, blocks),
        array((heads, planes, blocks, *tile)),
        [SMEM] + [VMEM] * (1 + heads * (1 + before)) + [ANY] * len(weight_parts),
        0,
        [
            pltpu.VMEM((1 + before, units * BLOCK, HEAD_DIM), BF16),
        ],
    )(away, weights, *own_parts, *value_parts, *weight_parts)

    returns = [
        [
            (group * heads + place) * head_size + p * cores + core
            for place in range(heads)
            for p in range(planes)
        ]
        for group in range(groups)
        for core in range(cores)
    ]
    local = lax.all_to_all(
        attended.reshape(heads * planes, blocks, *tile),
        axes, 0, 0, axis_index_groups=returns, tiled=True,
    ).reshape(heads, planes, blocks, *tile)

    def projected(other, kind):
        return call(
            functools.partial(project_kernel, axes, other, cores),
            array((tokens, width // cores), kind),
            [VMEM] * (1 + planes),
            128 * cubes,
        )(local, out_weight, *weight_parts)

    arrived = lax.ppermute(projected(1, BF16), "head", partners)
    return (projected(0, F32) + arrived.astype(F32)).astype(BF16)


def solution(mesh):
    in_specs = (
        P("ctx", "head"),
        P("ctx", "head"),
        P("ctx", "head"),
        P("ctx", "head"),
        P("head", "ctx"),
        P("ctx", None),
        P("head", None),
    )
    out_specs = P("ctx", "head")
    return jax.shard_map(
        functools.partial(body, mesh.shape["ctx"], mesh.shape["head"]),
        mesh=mesh,
        in_specs=in_specs,
        out_specs=out_specs,
        check_vma=False,
    )
```
